32 devices in a mesh: freq: 4 (over x, core), frames: 8 (over z, y).
Axes of the slice: x: 2, y: 2, z: 4, core: 2. Of those that a mesh axis runs over, the one named last changes fastest.
Arguments:
- signal: float32 [8, 4, 1048576], P('frames', 'freq'), may hold values from -6 to 6
- templates: float32 [64, 32768], P(None, ('freq', 'frames')), may hold values from 0.03 to 3.6, as said below
- activations: float32 [64, 1024], P('freq', 'frames'), may hold values from 0.3 to 36, as said below
Outputs:
- final_activations: float32 [64, 1024], P('freq', 'frames')
- final_templates: float32 [64, 32768], P(None, ('freq', 'frames'))
The draws below stay inside these ranges and needn't reach their ends.
Inputs may be any that keep to these rules, and one draw needn't show every extreme that they name: `templates`: all entries are positive. `activations`: all entries are positive.
All inputs are finite; a program needn't handle non-finite values.
Results may differ from the reference program's by a relative error of at most 0.00011.
Values sent between devices are 32-bit elements; how exact they have to be, the bound alone decides.
No kernel may reach another device: no remote copies, remote signals or barrier semaphores. Data moves between devices by JAX's collectives and lax.ppermute only.
A program may use at most 64 MiB of HBM per device.

```python
import math
import jax
import jax.numpy as jnp
from jax import lax

FRAME_LEN = 65536
SPLIT = 256
RANK = 64
FR_DEV = 32
BINS = 32768
BLK = 128
FRAMES = 1024
BLOCKS = 8
SUBS = 4


def positive_field(seed_key, row_count, column_count, low_value, high_value):
    values = jnp.exp(jax.random.uniform(seed_key, (row_count, column_count), jnp.float32, math.log(low_value), math.log(high_value)))
    rising = jnp.exp(math.log(3.0) * jnp.arange(column_count, dtype=jnp.int32).astype(jnp.float32) / column_count)
    return values * rising[None, :]


def draw_signal(key, part):
    hop_len = FRAME_LEN // 2
    row_count = BLOCKS * SUBS * FR_DEV
    piece_count = BLOCKS * SUBS
    note_count = 32
    harmonics = 4
    period = 4 * FRAME_LEN
    base_pitch = jax.random.randint(jax.random.fold_in(key, 31), (note_count,), 8, period // (2 * harmonics), jnp.int32)
    orders = jnp.arange(1, harmonics + 1, dtype=jnp.int32)
    pitch = (base_pitch[:, None] * orders[None, :]).reshape(note_count * harmonics)
    start_phase = jax.random.uniform(jax.random.fold_in(key, 32), (note_count * harmonics,), jnp.float32, 0.0, 2.0 * math.pi)
    positions = jnp.arange(hop_len, dtype=jnp.int32)
    low_part = positions % 256
    high_part = positions // 256
    inner = (pitch[:, None] * high_part[None, :] % period * 256 + pitch[:, None] * low_part[None, :]) % period
    inner_angle = 2.0 * math.pi / period * inner.astype(jnp.float32)
    table = jnp.concatenate([jnp.cos(inner_angle), jnp.sin(inner_angle)], 0)
    rows = jnp.arange(row_count, dtype=jnp.int32)
    row_turn = (pitch % 8)[None, :] * (rows % 8)[:, None] % 8
    theta = start_phase[None, :] + 2.0 * math.pi / 8.0 * row_turn.astype(jnp.float32)
    envelope = jnp.exp(jax.random.uniform(jax.random.fold_in(key, 33), (piece_count, note_count), jnp.float32, math.log(0.02), math.log(0.4)))
    harmonic_weight = jax.random.uniform(jax.random.fold_in(key, 34), (note_count, harmonics), jnp.float32, 0.4, 1.0) / orders[None, :].astype(jnp.float32)
    amplitude = (jnp.repeat(envelope, FR_DEV, axis=0)[:, :, None] * harmonic_weight[None, :, :]).reshape(row_count, note_count * harmonics)
    coefficient = jnp.concatenate([amplitude * jnp.sin(theta), amplitude * jnp.cos(theta)], 1)
    tone = jnp.dot(coefficient, table, precision=lax.Precision.HIGHEST, preferred_element_type=jnp.float32)
    noise = jax.random.normal(jax.random.fold_in(key, 35), (row_count, hop_len), jnp.float32)
    tilt = jax.random.uniform(jax.random.fold_in(key, 36), (piece_count,), jnp.float32, -0.8, 0.8)
    noise_gain = jnp.exp(jax.random.uniform(jax.random.fold_in(key, 37), (piece_count,), jnp.float32, math.log(0.25), math.log(0.75)))
    row_tilt = jnp.repeat(tilt, FR_DEV)[:, None]
    row_gain = jnp.repeat(noise_gain, FR_DEV)[:, None]
    shifted = jnp.concatenate([jnp.zeros((row_count, 1), jnp.float32), noise[:, :-1]], 1)
    colored = (noise + row_tilt * shifted) * row_gain
    values = jnp.clip(tone + colored, -6.0, 6.0)
    return values.reshape(BLOCKS, SUBS, FR_DEV * hop_len)


def draw_templates(key, part):
    values = positive_field(jax.random.fold_in(key, 11), RANK, BINS, 0.03, 0.3)
    return values


def draw_activations(key, part):
    values = positive_field(jax.random.fold_in(key, 21), RANK, FRAMES, 0.3, 3.0)
    return values


def setup_inputs(seed: int = 0) -> dict:
    keys = jax.random.split(jax.random.key(seed), 4)
    return {
        "signal": draw_signal(jax.random.fold_in(keys[3], 71), 0),
        "templates": draw_templates(jax.random.fold_in(keys[3], 71), 0),
        "activations": draw_activations(jax.random.fold_in(keys[3], 71), 0),
    }


PRECISE = lax.Precision.HIGHEST

def hann_window():
    positions = jnp.arange(FRAME_LEN, dtype=jnp.int32).astype(jnp.float32)
    return 0.5 - 0.5 * jnp.cos(2.0 * math.pi / FRAME_LEN * positions)

def magnitudes(signal):
    hop_len = FRAME_LEN // 2
    sample_rows = jnp.concatenate([signal.reshape(FRAMES, hop_len), jnp.zeros((1, hop_len), signal.dtype)], 0)
    window = hann_window()
    group_size = math.gcd(FRAMES, 64)

    def per_block(offset):
        first_half = lax.dynamic_slice_in_dim(sample_rows, offset, group_size, 0)
        second_half = lax.dynamic_slice_in_dim(sample_rows, offset + 1, group_size, 0)
        frames = jnp.concatenate([first_half, second_half], 1) * window
        transform = jnp.fft.rfft(frames, axis=1)[:, :BINS]
        real_part = jnp.real(transform)
        imag_part = jnp.imag(transform)
        magnitude = jnp.sqrt(real_part * real_part + imag_part * imag_part) * (8.0 / SPLIT)
        return magnitude.astype(jnp.float32)
    offsets = jnp.arange(FRAMES // group_size, dtype=jnp.int32) * group_size
    return lax.map(per_block, offsets).reshape(FRAMES, BINS)

def quotient(spectrum_rows, basis, act_block):
    approx = lax.dot_general(act_block, basis, (((0,), (0,)), ((), ())), precision=PRECISE, preferred_element_type=jnp.float32)
    return spectrum_rows / approx

def update_activity(spectrum, basis, activity):
    totals = lax.optimization_barrier(jnp.sum(basis, axis=1))

    def per_block(offset):
        act_block = lax.dynamic_slice_in_dim(activity, offset, BLK, 1)
        spectrum_rows = lax.dynamic_slice_in_dim(spectrum, offset, BLK, 0)
        ratio_rows = quotient(spectrum_rows, basis, act_block)
        numerator = lax.dot_general(basis, ratio_rows, (((1,), (1,)), ((), ())), precision=PRECISE, preferred_element_type=jnp.float32)
        return act_block * (numerator / totals[:, None])
    offsets = jnp.arange(FRAMES // BLK, dtype=jnp.int32) * BLK
    blocks = lax.map(per_block, offsets)
    return jnp.transpose(blocks, (1, 0, 2)).reshape(RANK, FRAMES)

def update_basis(spectrum, basis, activity):

    def accumulate(running, offset):
        act_block = lax.dynamic_slice_in_dim(activity, offset, BLK, 1)
        spectrum_rows = lax.dynamic_slice_in_dim(spectrum, offset, BLK, 0)
        ratio_rows = quotient(spectrum_rows, basis, act_block)
        return (running + jnp.dot(act_block, ratio_rows, precision=PRECISE, preferred_element_type=jnp.float32), None)
    offsets = jnp.arange(FRAMES // BLK, dtype=jnp.int32) * BLK
    numerator, unused = lax.scan(accumulate, jnp.zeros((RANK, BINS), jnp.float32), offsets)
    totals = lax.optimization_barrier(jnp.sum(activity, axis=1))
    return basis * (numerator / totals[:, None])

def reference(signal, templates, activations):
    spectrum = magnitudes(signal)
    middle = update_activity(spectrum, templates, activations)
    final_templates = update_basis(spectrum, templates, middle)
    final_activations = update_activity(spectrum, final_templates, middle)
    return (final_activations, final_templates)
```

```python
import functools
import math

import jax
import jax.numpy as jnp
import ml_dtypes
import numpy as np
from jax import lax
from jax.experimental import pallas as pl
from jax.experimental.pallas import tpu as pltpu
from jax.sharding import Mesh
from jax.sharding import PartitionSpec as P

FRAME_LEN = 65536
SPLIT = 256
LANES = 128
GROUP = 8
HOP_ROWS = FRAME_LEN // 2 // LANES
VMEM = 56 * 1024 * 1024
NT = (((1,), (1,)), ((), ()))


def high_low(values):
    high = values.astype(np.float32).astype(ml_dtypes.bfloat16)
    low = (values - high.astype(np.float64)).astype(ml_dtypes.bfloat16)
    return high, low


def for_three_products(values):
    high, low = high_low(values)
    return np.concatenate([high, low, high], 1)


def units_of_member(units_here, member_blocks):
    order = list(range(units_here))
    if units_here % 8 == 0:
        order.sort(key=lambda r: (row_of_unit(r) % 2, r))
    kept = [(block, r) for block in member_blocks for r in order]
    if units_here % 8 == 0:
        kept.sort(key=lambda pair: row_of_unit(pair[1]) % 2)
    return kept


def row_of_unit(unit):
    return unit // 2 if unit % 2 == 0 else SPLIT - 1 - unit // 2


@functools.lru_cache(maxsize=None)
def tables(unit_order):
    half = SPLIT // 2
    index = np.arange(SPLIT, dtype=np.float64)
    slot = np.arange(half, dtype=np.float64)
    angle = 2.0 * np.pi / SPLIT * np.mod(np.outer(np.arange(half + 1), np.arange(SPLIT)), SPLIT)
    cosine, sine = np.cos(angle), np.sin(angle)
    first = np.concatenate([cosine[:half], cosine[half:], -sine[1:half]], 0)
    turn = 2.0 * np.pi / (SPLIT * SPLIT) * np.outer(slot, index)
    twiddle_cos, twiddle_sin = np.cos(turn), np.sin(turn)
    masked_cos = twiddle_cos.copy()
    masked_cos[0] = 0.0
    twiddle = np.stack([twiddle_cos, twiddle_sin, masked_cos]).astype(np.float32)
    middle = 2.0 * np.pi / (SPLIT * SPLIT) * half * index
    odd = 2.0 * np.pi / SPLIT * slot
    rows = np.zeros((8, SPLIT), np.float32)
    rows[0], rows[1] = np.cos(middle), -np.sin(middle)
    rows[2, :half], rows[3, :half] = np.cos(odd), np.sin(odd)
    seconds, mirrored, places = [], [], []
    for parity in range(2):
        here = [place for place, unit in enumerate(unit_order) if row_of_unit(unit) % 2 == parity]
        turns = np.array([row_of_unit(unit_order[place]) // 2 for place in here])
        phase = 2.0 * np.pi / half * np.mod(np.outer(turns, np.arange(half)), half)
        c, s = np.cos(phase), np.sin(phase)
        seconds.append(
            for_three_products(np.concatenate([np.concatenate([c, s], 1), np.concatenate([-s, c], 1)], 0))
        )
        flags = np.zeros((half, LANES), np.float32)
        flags[:, 0] = [unit_order[place] % 2 for place in here]
        mirrored.append(flags)
        places.append(tuple(here))
    position = np.arange(FRAME_LEN, dtype=np.float64)
    window = (0.5 - 0.5 * np.cos(2.0 * np.pi / FRAME_LEN * position)).astype(np.float32)
    window = window.reshape(SPLIT, 2, LANES).transpose(1, 0, 2)
    return (
        np.ascontiguousarray(window),
        for_three_products(first),
        twiddle,
        rows,
        np.stack(seconds),
        np.stack(mirrored),
        tuple(places),
    )


def split_values(values):
    high = values.astype(jnp.bfloat16)
    low = (values - high.astype(jnp.float32)).astype(jnp.bfloat16)
    return high, low


def dot(left, right):
    return jnp.dot(left, right, preferred_element_type=jnp.float32)


def dot_nt(left, right):
    return lax.dot_general(left, right, NT, preferred_element_type=jnp.float32)


def spectrum_kernel(
    places,
    per_member,
    main_ref,
    next_ref,
    window_ref,
    first_ref,
    twiddle_ref,
    rows_ref,
    second_ref,
    mirrored_ref,
    *rest,
):
    out_ref, parts_ref, middle_ref = rest[-3:]
    half = SPLIT // 2
    middle_ref[...] = jnp.zeros_like(middle_ref)

    def even_odd(real, imag):
        even = jnp.concatenate([real[:, :half] + real[:, half:], imag[:, :half] + imag[:, half:]], 1)
        real = real[:, :half] - real[:, half:]
        imag = imag[:, :half] - imag[:, half:]
        c, s = rows_ref[2:3, :half], rows_ref[3:4, :half]
        odd = jnp.concatenate([real * c + imag * s, imag * c - real * s], 1)
        return even, odd

    def three(values):
        high, low = split_values(values)
        return jnp.concatenate([high, high, low], 1)

    for g in range(GROUP):
        columns = []
        for side in range(2):
            top = main_ref[pl.ds(g * HOP_ROWS + side, half, stride=2), :]
            if g + 1 < GROUP:
                bottom = main_ref[pl.ds((g + 1) * HOP_ROWS + side, half, stride=2), :]
            else:
                bottom = next_ref[pl.ds(side, half, stride=2), :]
            columns.append(jnp.concatenate([top, bottom], 0) * window_ref[side])
        high, low = split_values(jnp.concatenate(columns, 1))
        section = dot(first_ref[...], jnp.concatenate([high, high, low], 0))
        a, b = section[:half], section[half:]
        real = a * twiddle_ref[0] + b * twiddle_ref[1]
        imag = b * twiddle_ref[2] - a * twiddle_ref[1]
        for parity, values in enumerate(even_odd(real, imag)):
            parts_ref[parity, g * half : (g + 1) * half, :] = three(values)
        nyquist = section[half : half + 1]
        for parity, values in enumerate(even_odd(nyquist * rows_ref[0:1], nyquist * rows_ref[1:2])):
            middle_ref[parity, g : g + 1, :] = values

    def magnitude(values):
        real, imag = values[:half], values[half:]
        return jnp.sqrt(real * real + imag * imag) * (8.0 / SPLIT)

    for parity in range(2):
        middle = magnitude(dot_nt(second_ref[parity], three(middle_ref[parity])))
        is_middle = mirrored_ref[parity] > 0.0
        for pair in range(GROUP // 2):
            values = magnitude(
                dot_nt(second_ref[parity], parts_ref[parity, pair * SPLIT : (pair + 1) * SPLIT, :])
            )
            for lane in range(2):
                g = 2 * pair + lane
                block = jnp.where(
                    is_middle, middle[:, g : g + 1], values[:, lane * LANES : (lane + 1) * LANES]
                )
                start = 0
                while start < half:
                    stop = start + 1
                    place = places[parity][start]
                    while (
                        stop < half
                        and stop - start < 8
                        and places[parity][stop] == place + stop - start
                        and places[parity][stop] // per_member == place // per_member
                    ):
                        stop += 1
                    member, row = divmod(place, per_member)
                    out_ref[member, 0, pl.ds(row * GROUP + g, stop - start, stride=GROUP), :] = block[start:stop]
                    start = stop


def spectrum_blocks(samples, trailing, unit_order, members):
    window, first, twiddle, rows, second, mirrored, places = tables(unit_order)
    per_member = SPLIT // members
    chunks = samples.shape[0] // (GROUP * HOP_ROWS)
    constants = [jnp.asarray(t) for t in (window, first, twiddle, rows, second, mirrored)]
    out_shape = jax.ShapeDtypeStruct((members, chunks, per_member * GROUP, LANES), jnp.float32)
    whole = [pl.BlockSpec(t.shape, lambda s, n=t.ndim: (0,) * n) for t in constants]
    kernel = functools.partial(spectrum_kernel, places, per_member)

    def call(first_chunk, count, following, following_spec, earlier):
        extra = [] if earlier is None else [earlier]
        return pl.pallas_call(
            kernel,
            grid=(count,),
            in_specs=[
                pl.BlockSpec((GROUP * HOP_ROWS, LANES), lambda s: (s + first_chunk, 0)),
                following_spec,
                *whole,
                *[pl.BlockSpec(memory_space=pl.ANY) for _ in extra],
            ],
            out_specs=pl.BlockSpec(
                (members, 1, per_member * GROUP, LANES), lambda s: (0, s + first_chunk, 0, 0)
            ),
            out_shape=out_shape,
            scratch_shapes=[
                pltpu.VMEM((2, GROUP * LANES, 3 * SPLIT), jnp.bfloat16),
                pltpu.VMEM((2, 16, SPLIT), jnp.float32),
            ],
            input_output_aliases={2 + len(constants): 0} if extra else {},
            compiler_params=pltpu.CompilerParams(vmem_limit_bytes=VMEM),
            cost_estimate=pl.CostEstimate(
                flops=count * GROUP * 6 * SPLIT * SPLIT * SPLIT * 2,
                bytes_accessed=count * GROUP * FRAME_LEN * 4,
                transcendentals=0,
            ),
        )(samples, following, *constants, *extra)

    ahead = pl.BlockSpec((HOP_ROWS, LANES), lambda s: (GROUP * (s + 1), 0))
    result = call(0, chunks - 1, samples, ahead, None)
    return call(chunks - 1, 1, trailing, pl.BlockSpec((HOP_ROWS, LANES), lambda s: (0, 0)), result)


def lanes_of_activity(activity):
    high, low = split_values(activity)
    return jnp.concatenate([high, high, low, low], 1)


def ratio_of(spectrum_ref, activity_lanes, basis):
    frames = activity_lanes.shape[0]
    splits = [split_values(block) for block in basis]
    stacked = jnp.concatenate([jnp.concatenate([h, l, h, l], 0) for h, l in splits], 1)
    approx = dot(activity_lanes, stacked)
    count = len(basis)
    values = jnp.concatenate(
        [
            spectrum_ref[:, :, row * GROUP : (row + 1) * GROUP, :].reshape(frames, LANES)
            for row in range(count)
        ],
        1,
    )
    return values / approx, splits


def add_to_activity(total_ref, ratio, splits):
    high, low = split_values(ratio)
    basis = jnp.concatenate([jnp.concatenate([h, l], 0) for h, l in splits], 1)
    total_ref[...] += dot_nt(jnp.concatenate([high, low], 1), jnp.concatenate([basis, basis], 1))


def first_kernel(rows, spectrum_ref, basis_ref, activity_ref, out_ref, lanes_ref, total_ref, sums_ref):
    step = pl.program_id(0)
    rank = activity_ref.shape[1]

    @pl.when(step == 0)
    def _():
        lanes_ref[...] = lanes_of_activity(activity_ref[...])
        total_ref[...] = jnp.zeros_like(total_ref)
        sums_ref[...] = jnp.zeros_like(sums_ref)

    basis = [basis_ref[row] for row in range(rows)]
    ratio, splits = ratio_of(spectrum_ref, lanes_ref[...], basis)
    add_to_activity(total_ref, ratio, splits)
    sums_ref[...] += sum(basis)

    @pl.when(step == pl.num_programs(0) - 1)
    def _():
        total = total_ref[...]
        total = total[:, :rank] + total[:, rank:]
        half = total.shape[0] // 2
        out_ref[:half, :] = jnp.concatenate([total[:half], total[half:]], 1)
        sums = jnp.sum(jnp.transpose(sums_ref[...]), axis=0, keepdims=True)
        out_ref[half:, :] = jnp.broadcast_to(jnp.concatenate([sums, sums], 1), (8, 2 * rank))


def by_owner(values, shape):
    subs, members, ranks, width = shape
    local = width // subs
    blocks = []
    for member in range(members):
        rows = [
            values[(sub * members + member) * local : (sub * members + member + 1) * local]
            for sub in range(subs)
        ]
        blocks.append(jnp.transpose(jnp.concatenate(rows, 0)).reshape(subs, ranks, width))
    return blocks


def second_kernel(
    rows, spectrum_ref, basis_ref, activity_ref, sums_ref, middle_ref, owned_ref, out_ref, lanes_ref, turned_ref
):
    step = pl.program_id(0)
    rank = activity_ref.shape[1]

    @pl.when(step == 0)
    def _():
        half = activity_ref.shape[0] // 2
        scale = sums_ref[:half, :] / sums_ref[half : half + 1, :]
        middle = activity_ref[...] * jnp.concatenate([scale[:, :rank], scale[:, rank:]], 0)
        middle_ref[...] = middle
        lanes_ref[...] = lanes_of_activity(middle)
        turned = jnp.transpose(middle)
        high, low = split_values(turned)
        turned_ref[...] = jnp.concatenate([high, low], 0)
        totals = jnp.sum(turned, axis=1, keepdims=True)
        out_ref[out_ref.shape[0] - 1] = jnp.broadcast_to(totals, (rank, LANES))
        subs, members, ranks, width = owned_ref.shape
        for member, block in enumerate(by_owner(middle, owned_ref.shape)):
            owned_ref[:, member] = block

    basis = [basis_ref[row] for row in range(rows)]
    ratio, _ = ratio_of(spectrum_ref, lanes_ref[...], basis)
    high, low = split_values(ratio)
    turned = turned_ref[...]
    total = dot(turned, high) + dot(turned, low)
    total = total[:rank] + total[rank:]
    for row in range(rows):
        out_ref[step * rows + row] = total[:, row * LANES : (row + 1) * LANES]


def third_kernel(
    rows,
    sources,
    spectrum_ref,
    basis_ref,
    middle_ref,
    *rest,
):
    numerators = rest[:sources]
    totals = rest[sources : 2 * sources]
    new_ref, out_ref, lanes_ref, total_ref, sums_ref = rest[2 * sources :]
    step = pl.program_id(0)
    rank = middle_ref.shape[1]

    @pl.when(step == 0)
    def _():
        lanes_ref[...] = lanes_of_activity(middle_ref[...])
        total_ref[...] = jnp.zeros_like(total_ref)
        sums_ref[...] = jnp.zeros_like(sums_ref)

    total = sum(ref[0] for ref in totals)
    basis = []
    for row in range(rows):
        block = basis_ref[row] * (sum(ref[row] for ref in numerators) / total)
        new_ref[row] = block
        basis.append(block)
    ratio, splits = ratio_of(spectrum_ref, lanes_ref[...], basis)
    add_to_activity(total_ref, ratio, splits)
    sums_ref[...] += sum(basis)

    @pl.when(step == pl.num_programs(0) - 1)
    def _():
        total = total_ref[...]
        total = total[:, :rank] + total[:, rank:]
        subs, members, _, ranks, width = out_ref.shape
        shape = (subs, members, ranks, width)
        sums = jnp.sum(sums_ref[...], axis=1, keepdims=True)
        sums = jnp.broadcast_to(sums, (rank, width)).reshape(subs, ranks, width)
        for member, block in enumerate(by_owner(total, shape)):
            out_ref[:, member, 0] = block
            out_ref[:, member, 1] = sums


def step_rows(per_member):
    return 2 if per_member % 2 == 0 else 1


def spectrum_spec(spectrum, rows):
    members, chunks = spectrum.shape[:2]
    return pl.BlockSpec((members, chunks, rows * GROUP, LANES), lambda s: (0, 0, s, 0))


def full(shape):
    return pl.BlockSpec(shape, lambda s: (0,) * len(shape))


def out_rank(operands):
    return operands[1].shape[1]


def update_call(kernel, spectrum, per_member, in_specs, out_specs, out_shape, scratch, operands):
    rows = step_rows(per_member)
    rank = out_rank(operands)
    return pl.pallas_call(
        kernel,
        grid=(per_member // rows,),
        in_specs=in_specs,
        out_specs=out_specs,
        out_shape=out_shape,
        scratch_shapes=scratch,
        compiler_params=pltpu.CompilerParams(vmem_limit_bytes=VMEM),
        cost_estimate=pl.CostEstimate(
            flops=spectrum.size * rank * 16, bytes_accessed=spectrum.size * 4, transcendentals=0
        ),
    )(*operands)


def turned_lanes(values):
    return jnp.roll(jnp.flip(values, -1), 1, -1)


def swap_by(value, axis, mask):
    count = lax.axis_size(axis)
    return lax.ppermute(value, axis, [(i, i ^ mask) for i in range(count)])


def sum_over(value, axes):
    for axis in axes:
        count = lax.axis_size(axis)
        if count & (count - 1):
            value = lax.psum(value, axis)
            continue
        mask = 1
        while mask < count:
            value = value + swap_by(value, axis, mask)
            mask *= 2
    return value


def on_device(signal, templates, activations):
    subs, groups, members = (lax.axis_size(axis) for axis in ("freq", "group", "member"))
    blocks = groups * members
    rank, bins_here = templates.shape
    ranks_here, width = activations.shape
    units_here = bins_here // LANES
    exchange = ("freq", "member")
    partners = subs * members
    per_member = units_here * groups
    rows = step_rows(per_member)
    me_sub, me_group, me_member = (lax.axis_index(axis) for axis in ("freq", "group", "member"))

    kept = units_of_member(units_here, range(groups))
    unit_order = tuple(
        units_here * (sub * blocks + group * members + member) + r
        for sub in range(subs)
        for member in range(members)
        for group, r in kept
    )

    samples = signal.reshape(-1, LANES)
    route = [
        (((sub + 1) % subs) * blocks + block + (sub + 1) // subs, sub * blocks + block)
        for sub in range(subs)
        for block in range(blocks)
        if block + (sub + 1) // subs < blocks
    ]
    trailing = lax.ppermute(samples[:HOP_ROWS], ("freq", "group", "member"), route)
    gathered = lax.all_gather(activations, exchange)
    other = [swap_by(templates, "group", 1)] if groups == 2 else []

    spectrum = spectrum_blocks(samples, trailing, unit_order, partners)
    spectrum, gathered, other, templates = lax.optimization_barrier(
        (spectrum, gathered, other, templates)
    )
    spectrum = lax.all_to_all(spectrum, exchange, 0, 0, tiled=True)

    local = width // subs
    activity = gathered.reshape(subs, members, ranks_here, subs, local)
    activity = activity.transpose(3, 1, 4, 0, 2).reshape(partners * local, rank)
    frames = partners * local

    own = templates.reshape(rank, units_here, LANES).transpose(1, 0, 2)
    if other:
        remote = other[0].reshape(rank, units_here, LANES).transpose(1, 0, 2)
        by_group = jnp.where(me_group == 0, jnp.stack([own, remote]), jnp.stack([remote, own]))
    else:
        by_group = own[None]
    unit_index = units_here * (
        me_sub * blocks + jnp.arange(groups)[:, None] * members + me_member
    ) + jnp.arange(units_here)[None, :]
    is_turned = (unit_index % 2 == 1)[:, :, None, None]
    by_group = jnp.where(is_turned, turned_lanes(by_group), by_group)
    basis = jnp.concatenate([by_group[group, r][None] for group, r in kept], 0)

    specs = spectrum_spec(spectrum, rows)
    basis_spec = pl.BlockSpec((rows, rank, LANES), lambda s: (s, 0, 0))
    lanes_scratch = pltpu.VMEM((frames, 4 * rank), jnp.bfloat16)
    total_scratch = pltpu.VMEM((frames, 2 * rank), jnp.float32)
    sums_scratch = pltpu.VMEM((rank, LANES), jnp.float32)
    sums_shape = (frames // 2 + 8, 2 * rank)
    sums = update_call(
        functools.partial(first_kernel, rows),
        spectrum,
        per_member,
        [specs, basis_spec, full((frames, rank))],
        full(sums_shape),
        jax.ShapeDtypeStruct(sums_shape, jnp.float32),
        [lanes_scratch, total_scratch, sums_scratch],
        (spectrum, basis, activity),
    )
    sums = sum_over(sums, exchange)

    owned_shape = (subs, members, ranks_here, width)
    numerator_shape = (per_member + 1, rank, LANES)
    middle, owned, numerator = update_call(
        functools.partial(second_kernel, rows),
        spectrum,
        per_member,
        [specs, basis_spec, full((frames, rank)), full(sums_shape)],
        [full((frames, rank)), full(owned_shape), full(numerator_shape)],
        [
            jax.ShapeDtypeStruct((frames, rank), jnp.float32),
            jax.ShapeDtypeStruct(owned_shape, jnp.float32),
            jax.ShapeDtypeStruct(numerator_shape, jnp.float32),
        ],
        [lanes_scratch, pltpu.VMEM((2 * rank, frames), jnp.bfloat16)],
        (spectrum, basis, activity, sums),
    )
    numerators = [numerator]
    if groups == 2:
        numerators.append(swap_by(numerator, "group", 1))
    payload_shape = (subs, members, 2, ranks_here, width)
    total_spec = pl.BlockSpec((1, rank, LANES), lambda s: (per_member, 0, 0))
    new_basis, payload = update_call(
        functools.partial(third_kernel, rows, len(numerators)),
        spectrum,
        per_member,
        [specs, basis_spec, full((frames, rank))]
        + [basis_spec] * len(numerators)
        + [total_spec] * len(numerators),
        [basis_spec, full(payload_shape)],
        [
            jax.ShapeDtypeStruct((per_member, rank, LANES), jnp.float32),
            jax.ShapeDtypeStruct(payload_shape, jnp.float32),
        ],
        [lanes_scratch, total_scratch, sums_scratch],
        (spectrum, basis, middle, *numerators, *numerators),
    )
    received = lax.all_to_all(
        payload.reshape(partners, 2, ranks_here, width), exchange, 0, 0, tiled=True
    )
    summed = jnp.sum(received, axis=0)
    mine = lax.dynamic_slice(
        owned, (me_sub, me_member, 0, 0), (1, 1, ranks_here, width)
    ).reshape(ranks_here, width)
    final_activations = mine * (summed[0] / summed[1])

    back = jnp.stack(
        [
            jnp.stack([new_basis[kept.index((group, r))] for r in range(units_here)])
            for group in range(groups)
        ]
    )
    back = lax.dynamic_index_in_dim(back, me_group, 0, keepdims=False)
    turned_here = lax.dynamic_index_in_dim(is_turned, me_group, 0, keepdims=False)
    back = jnp.where(turned_here, turned_lanes(back), back)
    final_templates = back.transpose(1, 0, 2).reshape(rank, bins_here)
    return (final_activations, final_templates)


def solution(mesh):
    subs, blocks = mesh.devices.shape
    groups = 2 if blocks % 2 == 0 else 1
    grid = Mesh(
        mesh.devices.reshape(subs, groups, blocks // groups), ("freq", "group", "member")
    )
    frames = ("group", "member")
    return jax.shard_map(
        on_device,
        mesh=grid,
        in_specs=(P(frames, "freq", None), P(None, ("freq", *frames)), P("freq", frames)),
        out_specs=(P("freq", frames), P(None, ("freq", *frames))),
        check_vma=False,
    )
```

```python
import functools
import math

import jax
import jax.numpy as jnp
import ml_dtypes
import numpy as np
from jax import lax
from jax.experimental import pallas as pl
from jax.experimental.pallas import tpu as pltpu
from jax.sharding import Mesh
from jax.sharding import PartitionSpec as P

FRAME_LEN = 65536
SPLIT = 256
LANES = 128
GROUP = 8
HOP_ROWS = FRAME_LEN // 2 // LANES
SPECTRUM_VMEM = 24 * 1024 * 1024
UPDATE_VMEM = 24 * 1024 * 1024
NT = (((1,), (1,)), ((), ()))


def high_low(values):
    high = values.astype(np.float32).astype(ml_dtypes.bfloat16)
    low = (values - high.astype(np.float64)).astype(ml_dtypes.bfloat16)
    return high, low


def for_three_products(values):
    high, low = high_low(values)
    return np.concatenate([high, low, high], 1)


def units_of_member(units_here, member_blocks):
    order = list(range(units_here))
    if units_here % 8 == 0:
        order.sort(key=lambda r: (row_of_unit(r) % 2, r))
    kept = [(block, r) for block in member_blocks for r in order]
    if units_here % 8 == 0:
        kept.sort(key=lambda pair: row_of_unit(pair[1]) % 2)
    return kept


def row_of_unit(unit):
    return unit // 2 if unit % 2 == 0 else SPLIT - 1 - unit // 2


@functools.lru_cache(maxsize=None)
def tables(unit_order):
    half = SPLIT // 2
    index = np.arange(SPLIT, dtype=np.float64)
    slot = np.arange(half, dtype=np.float64)
    angle = 2.0 * np.pi / SPLIT * np.mod(np.outer(np.arange(half + 1), np.arange(SPLIT)), SPLIT)
    cosine, sine = np.cos(angle), np.sin(angle)
    first = np.concatenate([cosine[:half], cosine[half:], -sine[1:half]], 0)
    turn = 2.0 * np.pi / (SPLIT * SPLIT) * np.outer(slot, index)
    twiddle_cos, twiddle_sin = np.cos(turn), np.sin(turn)
    masked_cos = twiddle_cos.copy()
    masked_cos[0] = 0.0
    twiddle = np.stack([twiddle_cos, twiddle_sin, masked_cos]).astype(np.float32)
    middle = 2.0 * np.pi / (SPLIT * SPLIT) * half * index
    odd = 2.0 * np.pi / SPLIT * slot
    rows = np.zeros((8, SPLIT), np.float32)
    rows[0], rows[1] = np.cos(middle), -np.sin(middle)
    rows[2, :half], rows[3, :half] = np.cos(odd), np.sin(odd)
    seconds, mirrored, places = [], [], []
    for parity in range(2):
        here = [place for place, unit in enumerate(unit_order) if row_of_unit(unit) % 2 == parity]
        turns = np.array([row_of_unit(unit_order[place]) // 2 for place in here])
        phase = 2.0 * np.pi / half * np.mod(np.outer(turns, np.arange(half)), half)
        c, s = np.cos(phase), np.sin(phase)
        seconds.append(
            for_three_products(np.concatenate([np.concatenate([c, s], 1), np.concatenate([-s, c], 1)], 0))
        )
        flags = np.zeros((half, LANES), np.float32)
        flags[:, 0] = [unit_order[place] % 2 for place in here]
        mirrored.append(flags)
        places.append(tuple(here))
    position = np.arange(FRAME_LEN, dtype=np.float64)
    window = (0.5 - 0.5 * np.cos(2.0 * np.pi / FRAME_LEN * position)).astype(np.float32)
    window = window.reshape(SPLIT, 2, LANES).transpose(1, 0, 2)
    return (
        np.ascontiguousarray(window),
        for_three_products(first),
        twiddle,
        rows,
        np.stack(seconds),
        np.stack(mirrored),
        tuple(places),
    )


def split_values(values):
    high = values.astype(jnp.bfloat16)
    low = (values - high.astype(jnp.float32)).astype(jnp.bfloat16)
    return high, low


def dot(left, right):
    return jnp.dot(left, right, preferred_element_type=jnp.float32)


def dot_nt(left, right):
    return lax.dot_general(left, right, NT, preferred_element_type=jnp.float32)


def spectrum_kernel(
    places,
    per_member,
    main_ref,
    next_ref,
    trailing_ref,
    window_ref,
    first_ref,
    twiddle_ref,
    rows_ref,
    second_ref,
    mirrored_ref,
    out_ref,
    parts_ref,
    middle_ref,
):
    half = SPLIT // 2
    middle_ref[...] = jnp.zeros_like(middle_ref)

    def even_odd(real, imag):
        even = jnp.concatenate([real[:, :half] + real[:, half:], imag[:, :half] + imag[:, half:]], 1)
        real = real[:, :half] - real[:, half:]
        imag = imag[:, :half] - imag[:, half:]
        c, s = rows_ref[2:3, :half], rows_ref[3:4, :half]
        odd = jnp.concatenate([real * c + imag * s, imag * c - real * s], 1)
        return even, odd

    def three(values):
        high, low = split_values(values)
        return jnp.concatenate([high, high, low], 1)

    for g in range(GROUP):
        columns = []
        for side in range(2):
            top = main_ref[pl.ds(g * HOP_ROWS + side, half, stride=2), :]
            if g + 1 < GROUP:
                bottom = main_ref[pl.ds((g + 1) * HOP_ROWS + side, half, stride=2), :]
            else:
                bottom = jnp.where(
                    pl.program_id(0) == pl.num_programs(0) - 1,
                    trailing_ref[pl.ds(side, half, stride=2), :],
                    next_ref[pl.ds(side, half, stride=2), :],
                )
            columns.append(jnp.concatenate([top, bottom], 0) * window_ref[side])
        high, low = split_values(jnp.concatenate(columns, 1))
        section = dot(first_ref[...], jnp.concatenate([high, high, low], 0))
        a, b = section[:half], section[half:]
        real = a * twiddle_ref[0] + b * twiddle_ref[1]
        imag = b * twiddle_ref[2] - a * twiddle_ref[1]
        for parity, values in enumerate(even_odd(real, imag)):
            parts_ref[parity, g * half : (g + 1) * half, :] = three(values)
        nyquist = section[half : half + 1]
        for parity, values in enumerate(even_odd(nyquist * rows_ref[0:1], nyquist * rows_ref[1:2])):
            middle_ref[parity, g : g + 1, :] = values

    def magnitude(values):
        real, imag = values[:half], values[half:]
        return jnp.sqrt(real * real + imag * imag) * (8.0 / SPLIT)

    for parity in range(2):
        middle = magnitude(dot_nt(second_ref[parity], three(middle_ref[parity])))
        is_middle = mirrored_ref[parity] > 0.0
        for pair in range(GROUP // 2):
            values = magnitude(
                dot_nt(second_ref[parity], parts_ref[parity, pair * SPLIT : (pair + 1) * SPLIT, :])
            )
            for lane in range(2):
                g = 2 * pair + lane
                block = jnp.where(
                    is_middle, middle[:, g : g + 1], values[:, lane * LANES : (lane + 1) * LANES]
                )
                start = 0
                while start < half:
                    stop = start + 1
                    place = places[parity][start]
                    while (
                        stop < half
                        and stop - start < 8
                        and places[parity][stop] == place + stop - start
                        and places[parity][stop] // per_member == place // per_member
                    ):
                        stop += 1
                    member, row = divmod(place, per_member)
                    out_ref[member, 0, pl.ds(row * GROUP + g, stop - start, stride=GROUP), :] = block[start:stop]
                    start = stop


def spectrum_blocks(samples, trailing, unit_order, members):
    window, first, twiddle, rows, second, mirrored, places = tables(unit_order)
    per_member = SPLIT // members
    chunks = samples.shape[0] // (GROUP * HOP_ROWS)
    constants = [jnp.asarray(t) for t in (window, first, twiddle, rows, second, mirrored)]
    out_shape = jax.ShapeDtypeStruct((members, chunks, per_member * GROUP, LANES), jnp.float32)
    whole = [pl.BlockSpec(t.shape, lambda s, n=t.ndim: (0,) * n) for t in constants]
    kernel = functools.partial(spectrum_kernel, places, per_member)

    last = chunks * GROUP - 1
    return pl.pallas_call(
        functools.partial(spectrum_kernel, places, per_member),
        grid=(chunks,),
        in_specs=[
            pl.BlockSpec((GROUP * HOP_ROWS, LANES), lambda s: (s, 0)),
            pl.BlockSpec((HOP_ROWS, LANES), lambda s: (jnp.minimum(GROUP * (s + 1), last), 0)),
            pl.BlockSpec((HOP_ROWS, LANES), lambda s: (0, 0)),
            *whole,
        ],
        out_specs=pl.BlockSpec((members, 1, per_member * GROUP, LANES), lambda s: (0, s, 0, 0)),
        out_shape=out_shape,
        scratch_shapes=[
            pltpu.VMEM((2, GROUP * LANES, 3 * SPLIT), jnp.bfloat16),
            pltpu.VMEM((2, 16, SPLIT), jnp.float32),
        ],
        compiler_params=pltpu.CompilerParams(vmem_limit_bytes=SPECTRUM_VMEM),
        cost_estimate=pl.CostEstimate(
            flops=chunks * GROUP * 6 * SPLIT * SPLIT * SPLIT * 2,
            bytes_accessed=chunks * GROUP * FRAME_LEN * 4,
            transcendentals=0,
        ),
    )(samples, samples, trailing, *constants)


def lanes_of_activity(activity):
    high, low = split_values(activity)
    return jnp.concatenate([high, high, low, low], 1)


def ratio_of(spectrum_ref, start, activity_lanes, basis):
    frames = activity_lanes.shape[0]
    splits = [split_values(block) for block in basis]
    stacked = jnp.concatenate([jnp.concatenate([h, l, h, l], 0) for h, l in splits], 1)
    approx = dot(activity_lanes, stacked)
    values = jnp.concatenate(
        [
            spectrum_ref[:, :, (start + row) * GROUP : (start + row + 1) * GROUP, :].reshape(frames, LANES)
            for row in range(len(basis))
        ],
        1,
    )
    return values / approx, splits


def for_activity(ratio, splits):
    high, low = split_values(ratio)
    basis = jnp.concatenate([jnp.concatenate([h, l], 0) for h, l in splits], 1)
    return dot_nt(jnp.concatenate([high, low], 1), jnp.concatenate([basis, basis], 1))


def row_steps(per_member):
    rows = math.gcd(per_member, 8)
    return [range(start, start + rows) for start in range(0, per_member, rows)]


def packed(values):
    half = values.shape[0] // 2
    return jnp.concatenate([values[:half], values[half:]], 1)


def unpacked(values):
    half = values.shape[1] // 2
    return jnp.concatenate([values[:, :half], values[:, half:]], 0)


def first_kernel(side_ref, spectrum_ref, basis_ref, activity_ref, mine_ref, other_ref, lanes_ref, total_ref):
    rank = activity_ref.shape[1]
    lanes_ref[...] = lanes_of_activity(activity_ref[...])
    sums = jnp.zeros((rank, LANES), jnp.float32)
    for step, rows in enumerate(row_steps(basis_ref.shape[0])):
        basis = [basis_ref[row] for row in rows]
        ratio, splits = ratio_of(spectrum_ref, rows[0], lanes_ref[...], basis)
        part = for_activity(ratio, splits)
        if step == 0:
            total_ref[...] = part
        else:
            total_ref[...] += part
        sums += sum(basis)
    total = total_ref[...]
    total = total[:, :rank] + total[:, rank:]
    half = total.shape[0] // 2
    quarter = half // 2
    early, late = packed(total[:half]), packed(total[half:])
    first = side_ref[0] == 0
    mine_ref[:quarter, :] = jnp.where(first, early, late)
    other_ref[:quarter, :] = jnp.where(first, late, early)
    sums = jnp.sum(jnp.transpose(sums), axis=0, keepdims=True)
    sums = jnp.broadcast_to(jnp.concatenate([sums, sums], 1), (8, 2 * rank))
    mine_ref[quarter:, :] = sums
    other_ref[quarter:, :] = sums


def by_owner(values, shape):
    subs, members, ranks, width = shape
    local = width // subs
    blocks = []
    for member in range(members):
        rows = [
            values[(sub * members + member) * local : (sub * members + member + 1) * local]
            for sub in range(subs)
        ]
        blocks.append(jnp.transpose(jnp.concatenate(rows, 0)).reshape(subs, ranks, width))
    return blocks


def second_kernel(
    side_ref, spectrum_ref, basis_ref, activity_ref, mine_ref, other_ref, middle_ref, out_ref, lanes_ref, turned_ref
):
    rank = activity_ref.shape[1]
    quarter = activity_ref.shape[0] // 4
    first = side_ref[0] == 0
    mine = mine_ref[:quarter, :] / mine_ref[quarter : quarter + 1, :]
    other = other_ref[:quarter, :] / other_ref[quarter : quarter + 1, :]
    early, late = jnp.where(first, mine, other), jnp.where(first, other, mine)
    middle = activity_ref[...] * jnp.concatenate([unpacked(early), unpacked(late)], 0)
    middle_ref[...] = middle
    lanes_ref[...] = lanes_of_activity(middle)
    turned = jnp.transpose(middle)
    high, low = split_values(turned)
    turned_ref[...] = jnp.concatenate([high, low], 0)
    totals = jnp.sum(turned, axis=1, keepdims=True)
    out_ref[out_ref.shape[0] - 1] = jnp.broadcast_to(totals, (rank, LANES))
    for rows in row_steps(basis_ref.shape[0]):
        ratio, _ = ratio_of(spectrum_ref, rows[0], lanes_ref[...], [basis_ref[row] for row in rows])
        high, low = split_values(ratio)
        total = dot(turned_ref[...], high) + dot(turned_ref[...], low)
        total = total[:rank] + total[rank:]
        for place, row in enumerate(rows):
            out_ref[row] = total[:, place * LANES : (place + 1) * LANES]


def third_kernel(spectrum_ref, basis_ref, middle_ref, *rest):
    new_ref, out_ref, lanes_ref, total_ref = rest[-4:]
    numerators = rest[:-4]
    rank = middle_ref.shape[1]
    per_member = basis_ref.shape[0]
    lanes_ref[...] = lanes_of_activity(middle_ref[...])
    scale = 1.0 / sum(ref[per_member] for ref in numerators)
    sums = jnp.zeros((rank, LANES), jnp.float32)
    for step, rows in enumerate(row_steps(per_member)):
        basis = [basis_ref[row] * (sum(ref[row] for ref in numerators) * scale) for row in rows]
        for row, block in zip(rows, basis):
            new_ref[row] = block
        ratio, splits = ratio_of(spectrum_ref, rows[0], lanes_ref[...], basis)
        part = for_activity(ratio, splits)
        if step == 0:
            total_ref[...] = part
        else:
            total_ref[...] += part
        sums += sum(basis)
    total = total_ref[...]
    total = total[:, :rank] + total[:, rank:]
    subs, members, _, ranks, width = out_ref.shape
    sums = jnp.sum(sums, axis=1, keepdims=True)
    sums = jnp.broadcast_to(sums, (rank, width)).reshape(subs, ranks, width)
    for member, block in enumerate(by_owner(total, (subs, members, ranks, width))):
        out_ref[:, member, 0] = block
        out_ref[:, member, 1] = sums


def update_call(kernel, spectrum, out_shapes, scratch, operands, scalars=()):
    in_vmem = pl.BlockSpec(memory_space=pltpu.VMEM)
    rank = operands[0].shape[1]
    return pl.pallas_call(
        kernel,
        in_specs=[pl.BlockSpec(memory_space=pltpu.SMEM) for _ in scalars]
        + [in_vmem for _ in range(1 + len(operands))],
        out_specs=[in_vmem for _ in out_shapes],
        out_shape=[jax.ShapeDtypeStruct(shape, jnp.float32) for shape in out_shapes],
        scratch_shapes=scratch,
        compiler_params=pltpu.CompilerParams(vmem_limit_bytes=UPDATE_VMEM),
        cost_estimate=pl.CostEstimate(
            flops=spectrum.size * rank * 16, bytes_accessed=spectrum.size * 4, transcendentals=0
        ),
    )(*scalars, spectrum, *operands)


def turned_lanes(values):
    return jnp.roll(jnp.flip(values, -1), 1, -1)


def swap_by(value, axis, mask):
    count = lax.axis_size(axis)
    return lax.ppermute(value, axis, [(i, i ^ mask) for i in range(count)])


def sum_over(value, axis, mask):
    while mask < lax.axis_size(axis):
        value = value + swap_by(value, axis, mask)
        mask *= 2
    return value


def on_device(signal, templates, activations):
    subs, groups, members = (lax.axis_size(axis) for axis in ("freq", "group", "member"))
    blocks = groups * members
    rank, bins_here = templates.shape
    ranks_here, width = activations.shape
    units_here = bins_here // LANES
    exchange = ("freq", "member")
    partners = subs * members
    per_member = units_here * groups
    me_sub, me_group, me_member = (lax.axis_index(axis) for axis in ("freq", "group", "member"))

    kept = units_of_member(units_here, range(groups))
    unit_order = tuple(
        units_here * (sub * blocks + group * members + member) + r
        for sub in range(subs)
        for member in range(members)
        for group, r in kept
    )

    samples = signal.reshape(-1, LANES)
    route = [
        (((sub + 1) % subs) * blocks + block + (sub + 1) // subs, sub * blocks + block)
        for sub in range(subs)
        for block in range(blocks)
        if block + (sub + 1) // subs < blocks
    ]
    trailing = lax.ppermute(samples[:HOP_ROWS], ("freq", "group", "member"), route)
    gathered = lax.all_to_all(
        jnp.broadcast_to(activations[None], (partners, ranks_here, width)), exchange, 0, 0, tiled=True
    )
    other = [swap_by(templates, "group", 1)] if groups == 2 else []

    spectrum = spectrum_blocks(samples, trailing, unit_order, partners)
    spectrum, gathered, other, templates = lax.optimization_barrier(
        (spectrum, gathered, other, templates)
    )
    spectrum = lax.all_to_all(spectrum, exchange, 0, 0, tiled=True)

    local = width // subs
    activity = gathered.reshape(subs, members, ranks_here, subs, local)
    activity = activity.transpose(3, 1, 4, 0, 2).reshape(partners * local, rank)
    frames = partners * local

    own = templates.reshape(rank, units_here, LANES).transpose(1, 0, 2)
    if other:
        remote = other[0].reshape(rank, units_here, LANES).transpose(1, 0, 2)
        by_group = jnp.where(me_group == 0, jnp.stack([own, remote]), jnp.stack([remote, own]))
    else:
        by_group = own[None]
    unit_index = units_here * (
        me_sub * blocks + jnp.arange(groups)[:, None] * members + me_member
    ) + jnp.arange(units_here)[None, :]
    is_turned = (unit_index % 2 == 1)[:, :, None, None]
    by_group = jnp.where(is_turned, turned_lanes(by_group), by_group)
    basis = jnp.concatenate([by_group[group, r][None] for group, r in kept], 0)

    lanes_scratch = pltpu.VMEM((frames, 4 * rank), jnp.bfloat16)
    total_scratch = pltpu.VMEM((frames, 2 * rank), jnp.float32)
    half_shape = (frames // 4 + 8, 2 * rank)
    side = (me_sub % 2).astype(jnp.int32).reshape(1)
    mine, other = update_call(
        first_kernel, spectrum, [half_shape] * 2, [lanes_scratch, total_scratch], (basis, activity), (side,)
    )
    mine = mine + swap_by(other, "freq", 1)
    mine = sum_over(mine, "freq", 2)
    mine = sum_over(mine, "member", 1)
    other = swap_by(mine, "freq", 1)

    middle, numerator = update_call(
        second_kernel,
        spectrum,
        [(frames, rank), (per_member + 1, rank, LANES)],
        [lanes_scratch, pltpu.VMEM((2 * rank, frames), jnp.bfloat16)],
        (basis, activity, mine, other),
        (side,),
    )
    numerators = [numerator]
    if groups == 2:
        numerators.append(swap_by(numerator, "group", 1))
    new_basis, payload = update_call(
        third_kernel,
        spectrum,
        [(per_member, rank, LANES), (subs, members, 2, ranks_here, width)],
        [lanes_scratch, total_scratch],
        (basis, middle, *numerators),
    )
    received = lax.all_to_all(
        payload.reshape(partners, 2, ranks_here, width), exchange, 0, 0, tiled=True
    )
    summed = jnp.sum(received, axis=0)
    mine = lax.dynamic_slice(
        middle.reshape(subs, members, local, rank),
        (0, me_member, 0, me_sub * ranks_here),
        (subs, 1, local, ranks_here),
    )
    mine = mine.reshape(width, ranks_here).T
    final_activations = mine * (summed[0] / summed[1])

    back = jnp.stack(
        [
            jnp.stack([new_basis[kept.index((group, r))] for r in range(units_here)])
            for group in range(groups)
        ]
    )
    back = lax.dynamic_index_in_dim(back, me_group, 0, keepdims=False)
    turned_here = lax.dynamic_index_in_dim(is_turned, me_group, 0, keepdims=False)
    back = jnp.where(turned_here, turned_lanes(back), back)
    final_templates = back.transpose(1, 0, 2).reshape(rank, bins_here)
    return (final_activations, final_templates)


def solution(mesh):
    subs, blocks = mesh.devices.shape
    groups = 2 if blocks % 2 == 0 else 1
    grid = Mesh(
        mesh.devices.reshape(subs, groups, blocks // groups), ("freq", "group", "member")
    )
    frames = ("group", "member")
    return jax.shard_map(
        on_device,
        mesh=grid,
        in_specs=(P(frames, "freq", None), P(None, ("freq", *frames)), P("freq", frames)),
        out_specs=(P("freq", frames), P(None, ("freq", *frames))),
        check_vma=False,
    )
```

```python
import functools
import math

import jax
import jax.numpy as jnp
import ml_dtypes
import numpy as np
from jax import lax
from jax.experimental import pallas as pl
from jax.experimental.pallas import tpu as pltpu
from jax.sharding import Mesh
from jax.sharding import PartitionSpec as P

FRAME_LEN = 65536
SPLIT = 256
LANES = 128
GROUP = 8
HOP_ROWS = FRAME_LEN // 2 // LANES
SPECTRUM_VMEM = 24 * 1024 * 1024
UPDATE_VMEM = 24 * 1024 * 1024
NT = (((1,), (1,)), ((), ()))


def high_low(values):
    high = values.astype(np.float32).astype(ml_dtypes.bfloat16)
    low = (values - high.astype(np.float64)).astype(ml_dtypes.bfloat16)
    return high, low


def for_three_products(values):
    high, low = high_low(values)
    return np.concatenate([high, low, high], 1)


def units_of_member(units_here, member_blocks):
    order = list(range(units_here))
    if units_here % 8 == 0:
        order.sort(key=lambda r: (row_of_unit(r) % 2, r))
    kept = [(block, r) for block in member_blocks for r in order]
    if units_here % 8 == 0:
        kept.sort(key=lambda pair: row_of_unit(pair[1]) % 2)
    return kept


def row_of_unit(unit):
    return unit // 2 if unit % 2 == 0 else SPLIT - 1 - unit // 2


@functools.lru_cache(maxsize=None)
def tables(unit_order):
    half = SPLIT // 2
    index = np.arange(SPLIT, dtype=np.float64)
    slot = np.arange(half, dtype=np.float64)
    angle = 2.0 * np.pi / SPLIT * np.mod(np.outer(np.arange(half + 1), np.arange(SPLIT)), SPLIT)
    cosine, sine = np.cos(angle), np.sin(angle)
    first = np.concatenate([cosine[:half], cosine[half:], -sine[1:half]], 0)
    turn = 2.0 * np.pi / (SPLIT * SPLIT) * np.outer(slot, index)
    twiddle_cos, twiddle_sin = np.cos(turn), np.sin(turn)
    masked_cos = twiddle_cos.copy()
    masked_cos[0] = 0.0
    twiddle = np.stack([twiddle_cos, twiddle_sin, masked_cos]).astype(np.float32)
    middle = 2.0 * np.pi / (SPLIT * SPLIT) * half * index
    odd = 2.0 * np.pi / SPLIT * slot
    rows = np.zeros((8, SPLIT), np.float32)
    rows[0], rows[1] = np.cos(middle), -np.sin(middle)
    rows[2, :half], rows[3, :half] = np.cos(odd), np.sin(odd)
    seconds, mirrored, places = [], [], []
    for parity in range(2):
        here = [place for place, unit in enumerate(unit_order) if row_of_unit(unit) % 2 == parity]
        turns = np.array([row_of_unit(unit_order[place]) // 2 for place in here])
        phase = 2.0 * np.pi / half * np.mod(np.outer(turns, np.arange(half)), half)
        c, s = np.cos(phase), np.sin(phase)
        seconds.append(
            for_three_products(np.concatenate([np.concatenate([c, s], 1), np.concatenate([-s, c], 1)], 0))
        )
        flags = np.zeros((half, LANES), np.float32)
        flags[:, 0] = [unit_order[place] % 2 for place in here]
        mirrored.append(flags)
        places.append(tuple(here))
    position = np.arange(FRAME_LEN, dtype=np.float64)
    window = (0.5 - 0.5 * np.cos(2.0 * np.pi / FRAME_LEN * position)).astype(np.float32)
    window = window.reshape(SPLIT, 2, LANES).transpose(1, 0, 2)
    return (
        np.ascontiguousarray(window),
        for_three_products(first),
        twiddle,
        rows,
        np.stack(seconds),
        np.stack(mirrored),
        tuple(places),
    )


def split_values(values):
    high = values.astype(jnp.bfloat16)
    low = (values - high.astype(jnp.float32)).astype(jnp.bfloat16)
    return high, low


def dot(left, right):
    return jnp.dot(left, right, preferred_element_type=jnp.float32)


def dot_nt(left, right):
    return lax.dot_general(left, right, NT, preferred_element_type=jnp.float32)


def transform_group(hop_rows, base, stride, places, per_member, table_refs, out_ref, parts_ref, middle_ref, ready):
    window_ref, first_ref, twiddle_ref, rows_ref, second_ref, mirrored_ref = table_refs
    half = SPLIT // 2
    middle_ref[...] = jnp.zeros_like(middle_ref)

    def even_odd(real, imag):
        even = jnp.concatenate([real[:, :half] + real[:, half:], imag[:, :half] + imag[:, half:]], 1)
        real = real[:, :half] - real[:, half:]
        imag = imag[:, :half] - imag[:, half:]
        c, s = rows_ref[2:3, :half], rows_ref[3:4, :half]
        odd = jnp.concatenate([real * c + imag * s, imag * c - real * s], 1)
        return even, odd

    def three(values):
        high, low = split_values(values)
        return jnp.concatenate([high, high, low], 1)

    for g in range(GROUP):
        columns = [
            jnp.concatenate([hop_rows(g, side), hop_rows(g + 1, side)], 0) * window_ref[side]
            for side in range(2)
        ]
        high, low = split_values(jnp.concatenate(columns, 1))
        section = dot(first_ref[...], jnp.concatenate([high, high, low], 0))
        a, b = section[:half], section[half:]
        real = a * twiddle_ref[0] + b * twiddle_ref[1]
        imag = b * twiddle_ref[2] - a * twiddle_ref[1]
        for parity, values in enumerate(even_odd(real, imag)):
            parts_ref[parity, g * half : (g + 1) * half, :] = three(values)
        nyquist = section[half : half + 1]
        for parity, values in enumerate(even_odd(nyquist * rows_ref[0:1], nyquist * rows_ref[1:2])):
            middle_ref[parity, g : g + 1, :] = values

    ready()

    def magnitude(values):
        real, imag = values[:half], values[half:]
        return jnp.sqrt(real * real + imag * imag) * (8.0 / SPLIT)

    for parity in range(2):
        middle = magnitude(dot_nt(second_ref[parity], three(middle_ref[parity])))
        is_middle = mirrored_ref[parity] > 0.0
        for pair in range(GROUP // 2):
            values = magnitude(
                dot_nt(second_ref[parity], parts_ref[parity, pair * SPLIT : (pair + 1) * SPLIT, :])
            )
            for lane in range(2):
                g = 2 * pair + lane
                block = jnp.where(
                    is_middle, middle[:, g : g + 1], values[:, lane * LANES : (lane + 1) * LANES]
                )
                start = 0
                while start < half:
                    stop = start + 1
                    place = places[parity][start]
                    while (
                        stop < half
                        and stop - start < 8
                        and places[parity][stop] == place + stop - start
                        and places[parity][stop] // per_member == place // per_member
                    ):
                        stop += 1
                    member, row = divmod(place, per_member)
                    out_ref[member, pl.ds(row * stride + base + g, stop - start, stride=stride), :] = block[
                        start:stop
                    ]
                    start = stop


def early_kernel(
    places, per_member, frames, samples_ref, *rest
):
    table_refs, (out_ref, tail_ref) = rest[:6], rest[6:8]
    copies_ref, (hops_ref, parts_ref, middle_ref, sem_ref) = rest[8:14], rest[14:]
    groups = frames // GROUP - 1
    group_rows = GROUP * HOP_ROWS
    half = SPLIT // 2

    def fetch(first, count, slot):
        return pltpu.make_async_copy(
            samples_ref.at[pl.ds(first, count), :], hops_ref.at[pl.ds(first, count), :], sem_ref.at[slot]
        )

    tables_in = [
        pltpu.make_async_copy(table_refs[i], copies_ref[i], sem_ref.at[i]) for i in range(len(table_refs))
    ]
    lead = fetch(0, HOP_ROWS, 6)
    tail = pltpu.make_async_copy(
        samples_ref.at[pl.ds(groups * group_rows, group_rows), :], tail_ref, sem_ref.at[7]
    )
    hops = [fetch(HOP_ROWS + i * group_rows, group_rows, 8 + i) for i in range(groups)]
    for copy in [tables_in[1], lead, hops[0], *tables_in[:1], *tables_in[2:], *hops[1:], tail]:
        copy.start()
    lead.wait()
    for copy in tables_in[:4]:
        copy.wait()

    def body(i, carry):
        first = pl.multiple_of(i * group_rows, group_rows)
        pltpu.make_async_copy(
            samples_ref.at[pl.ds(HOP_ROWS + first, group_rows), :],
            hops_ref.at[pl.ds(HOP_ROWS + first, group_rows), :],
            sem_ref.at[8 + i],
        ).wait()

        def ready():
            @pl.when(i == 0)
            def _():
                for copy in tables_in[4:]:
                    copy.wait()

        transform_group(
            lambda hop, side: hops_ref[pl.ds(first + hop * HOP_ROWS + side, half, stride=2), :],
            i * GROUP,
            frames,
            places,
            per_member,
            copies_ref,
            out_ref,
            parts_ref,
            middle_ref,
            ready,
        )
        return carry

    lax.fori_loop(0, groups, body, 0)
    tail.wait()


def late_kernel(places, per_member, frames, tail_ref, trailing_ref, activity_ref, *rest):
    table_refs, (_, out_ref, parts_ref, middle_ref) = rest[:6], rest[6:]

    def hop_rows(hop, side):
        if hop == GROUP:
            return trailing_ref[pl.ds(side, SPLIT // 2, stride=2), :]
        return tail_ref[pl.ds(hop * HOP_ROWS + side, SPLIT // 2, stride=2), :]

    for member in range(out_ref.shape[0]):
        out_ref[member, per_member * frames :, :] = activity_ref[...]
    transform_group(
        hop_rows,
        frames - GROUP,
        frames,
        places,
        per_member,
        table_refs,
        out_ref,
        parts_ref,
        middle_ref,
        lambda: None,
    )


def spectrum_blocks(samples, trailing, activity, unit_order, members):
    *values, places = tables(unit_order)
    per_member = SPLIT // members
    frames = samples.shape[0] // HOP_ROWS
    groups = frames // GROUP - 1
    constants = [jnp.asarray(t) for t in values]
    out_shape = jax.ShapeDtypeStruct((members, per_member * frames + activity.shape[0], LANES), jnp.float32)
    tail_shape = jax.ShapeDtypeStruct((GROUP * HOP_ROWS, LANES), jnp.float32)
    in_vmem = pl.BlockSpec(memory_space=pltpu.VMEM)
    in_hbm = pl.BlockSpec(memory_space=pltpu.HBM)
    scratch = [
        pltpu.VMEM((2, GROUP * LANES, 3 * SPLIT), jnp.bfloat16),
        pltpu.VMEM((2, 16, SPLIT), jnp.float32),
    ]

    def settings(count):
        return dict(
            compiler_params=pltpu.CompilerParams(vmem_limit_bytes=SPECTRUM_VMEM),
            cost_estimate=pl.CostEstimate(
                flops=count * GROUP * 6 * SPLIT * SPLIT * SPLIT * 2,
                bytes_accessed=count * GROUP * FRAME_LEN * 4,
                transcendentals=0,
            ),
        )

    early, tail = pl.pallas_call(
        functools.partial(early_kernel, places, per_member, frames),
        in_specs=[in_hbm] * (1 + len(constants)),
        out_specs=[in_vmem, in_vmem],
        out_shape=[out_shape, tail_shape],
        scratch_shapes=[pltpu.VMEM(t.shape, t.dtype) for t in constants]
        + [pltpu.VMEM(((groups * GROUP + 1) * HOP_ROWS, LANES), jnp.float32)]
        + scratch
        + [pltpu.SemaphoreType.DMA((8 + groups,))],
        **settings(groups),
    )(samples, *constants)
    return pl.pallas_call(
        functools.partial(late_kernel, places, per_member, frames),
        in_specs=[in_vmem] * (4 + len(constants)),
        out_specs=in_vmem,
        out_shape=out_shape,
        scratch_shapes=scratch,
        input_output_aliases={3 + len(constants): 0},
        **settings(1),
    )(tail, trailing, activity, *constants, early)


def lanes_of_activity(activity):
    high, low = split_values(activity)
    return jnp.concatenate([high, high, low, low], 1)


def ratio_of(spectrum_ref, start, activity_lanes, basis):
    frames = activity_lanes.shape[0]
    local = frames // spectrum_ref.shape[0]
    splits = [split_values(block) for block in basis]
    stacked = jnp.concatenate([jnp.concatenate([h, l, h, l], 0) for h, l in splits], 1)
    approx = dot(activity_lanes, stacked)
    values = jnp.concatenate(
        [
            spectrum_ref[:, (start + row) * local : (start + row + 1) * local, :].reshape(frames, LANES)
            for row in range(len(basis))
        ],
        1,
    )
    return values / approx, jnp.concatenate([jnp.concatenate([h, l], 0) for h, l in splits], 1)


def for_activity(ratio, basis):
    high, low = split_values(ratio)
    return dot_nt(high, basis) + dot_nt(low, basis)


def both_parts(values):
    half = values.shape[1] // 2
    return values + pltpu.roll(values, half, 1)


def row_sums(basis):
    return dot_nt(jnp.ones((16, basis.shape[1]), jnp.bfloat16), basis)


def row_steps(per_member):
    rows = math.gcd(per_member, 8)
    return [range(start, start + rows) for start in range(0, per_member, rows)]


def packed(values):
    rows, width = values.shape
    lane = lax.broadcasted_iota(jnp.int32, (rows // 2, width), 1)
    return jnp.where(lane < width // 2, values[: rows // 2], values[rows // 2 :])


def unpacked(values):
    half = values.shape[1] // 2
    return jnp.concatenate([values[:, :half], values[:, half:]], 0)


def gathered_activity(spectrum_ref, shape):
    subs, members, ranks, width = shape
    local = width // subs
    frames_in = width // LANES
    first = spectrum_ref.shape[1] - ranks * frames_in
    pieces = {}
    for member in range(members):
        for part in range(frames_in):
            start = first + part * ranks
            rows = [spectrum_ref[sub * members + member, start : start + ranks, :] for sub in range(subs)]
            block = jnp.transpose(jnp.concatenate(rows, 0))
            for place in range(LANES // local):
                pieces[part * (LANES // local) + place, member] = block[place * local : (place + 1) * local]
    return jnp.concatenate([pieces[sub, member] for sub in range(subs) for member in range(members)], 0)


def first_kernel(shape, side_ref, spectrum_ref, basis_ref, mine_ref, other_ref, activity_ref, lanes_ref, total_ref):
    activity = gathered_activity(spectrum_ref, shape)
    activity_ref[...] = activity
    lanes_ref[...] = lanes_of_activity(activity)
    sums = 0.0
    for step, rows in enumerate(row_steps(basis_ref.shape[0])):
        ratio, basis = ratio_of(spectrum_ref, rows[0], lanes_ref[...], [basis_ref[row] for row in rows])
        part = for_activity(ratio, basis)
        if step == 0:
            total_ref[...] = part
        else:
            total_ref[...] += part
        sums += row_sums(basis)
    total = both_parts(total_ref[...])
    half = total.shape[0] // 2
    quarter = half // 2
    early, late = packed(total[:half]), packed(total[half:])
    first = side_ref[0] == 0
    mine_ref[:quarter, :] = jnp.where(first, early, late)
    other_ref[:quarter, :] = jnp.where(first, late, early)
    sums = both_parts(sums)[:8]
    mine_ref[quarter:, :] = sums
    other_ref[quarter:, :] = sums


def by_owner(values, shape):
    subs, members, ranks, width = shape
    local = width // subs
    blocks = []
    for member in range(members):
        rows = [
            values[(sub * members + member) * local : (sub * members + member + 1) * local]
            for sub in range(subs)
        ]
        blocks.append(jnp.transpose(jnp.concatenate(rows, 0)).reshape(subs, ranks, width))
    return blocks


def second_kernel(
    side_ref, spectrum_ref, basis_ref, activity_ref, mine_ref, other_ref, middle_ref, out_ref, lanes_ref, turned_ref
):
    rank = activity_ref.shape[1]
    quarter = activity_ref.shape[0] // 4
    first = side_ref[0] == 0
    mine = mine_ref[:quarter, :] / mine_ref[quarter : quarter + 1, :]
    other = other_ref[:quarter, :] / other_ref[quarter : quarter + 1, :]
    early, late = jnp.where(first, mine, other), jnp.where(first, other, mine)
    middle = activity_ref[...] * jnp.concatenate([unpacked(early), unpacked(late)], 0)
    middle_ref[...] = middle
    lanes_ref[...] = lanes_of_activity(middle)
    turned = jnp.transpose(middle)
    high, low = split_values(turned)
    turned_ref[...] = jnp.concatenate([high, low], 0)
    totals = jnp.sum(turned, axis=1, keepdims=True)
    out_ref[out_ref.shape[0] - 1] = jnp.broadcast_to(totals, (rank, LANES))
    for rows in row_steps(basis_ref.shape[0]):
        ratio, _ = ratio_of(spectrum_ref, rows[0], lanes_ref[...], [basis_ref[row] for row in rows])
        high, low = split_values(ratio)
        total = dot(turned_ref[...], high) + dot(turned_ref[...], low)
        total = total[:rank] + total[rank:]
        for place, row in enumerate(rows):
            out_ref[row] = total[:, place * LANES : (place + 1) * LANES]


def third_kernel(spectrum_ref, basis_ref, middle_ref, *rest):
    new_ref, out_ref, lanes_ref, total_ref = rest[-4:]
    numerators = rest[:-4]
    rank = middle_ref.shape[1]
    per_member = basis_ref.shape[0]
    lanes_ref[...] = lanes_of_activity(middle_ref[...])
    scale = 1.0 / sum(ref[per_member] for ref in numerators)
    sums = 0.0
    for step, rows in enumerate(row_steps(per_member)):
        blocks = [basis_ref[row] * (sum(ref[row] for ref in numerators) * scale) for row in rows]
        for row, block in zip(rows, blocks):
            new_ref[row] = block
        ratio, basis = ratio_of(spectrum_ref, rows[0], lanes_ref[...], blocks)
        part = for_activity(ratio, basis)
        if step == 0:
            total_ref[...] = part
        else:
            total_ref[...] += part
        sums += row_sums(basis)
    total = both_parts(total_ref[...])[:, :rank]
    subs, members, _, ranks, width = out_ref.shape
    sums = jnp.transpose(jnp.broadcast_to(both_parts(sums)[:1], (LANES, 2 * rank)))[:rank]
    sums = jnp.concatenate([sums] * (width // LANES), 1).reshape(subs, ranks, width)
    for member, block in enumerate(by_owner(total, (subs, members, ranks, width))):
        out_ref[:, member, 0] = block
        out_ref[:, member, 1] = sums


def update_call(kernel, spectrum, out_shapes, scratch, operands, scalars=()):
    in_vmem = pl.BlockSpec(memory_space=pltpu.VMEM)
    rank = operands[0].shape[1]
    return pl.pallas_call(
        kernel,
        in_specs=[pl.BlockSpec(memory_space=pltpu.SMEM) for _ in scalars]
        + [in_vmem for _ in range(1 + len(operands))],
        out_specs=[in_vmem for _ in out_shapes],
        out_shape=[jax.ShapeDtypeStruct(shape, jnp.float32) for shape in out_shapes],
        scratch_shapes=scratch,
        compiler_params=pltpu.CompilerParams(vmem_limit_bytes=UPDATE_VMEM),
        cost_estimate=pl.CostEstimate(
            flops=spectrum.size * rank * 16, bytes_accessed=spectrum.size * 4, transcendentals=0
        ),
    )(*scalars, spectrum, *operands)


def turned_lanes(values):
    return jnp.roll(jnp.flip(values, -1), 1, -1)


def swap_by(value, axis, mask):
    count = lax.axis_size(axis)
    return lax.ppermute(value, axis, [(i, i ^ mask) for i in range(count)])


def sum_over(value, axis, mask):
    while mask < lax.axis_size(axis):
        value = value + swap_by(value, axis, mask)
        mask *= 2
    return value


def on_device(signal, templates, activations):
    subs, groups, members = (lax.axis_size(axis) for axis in ("freq", "group", "member"))
    blocks = groups * members
    rank, bins_here = templates.shape
    ranks_here, width = activations.shape
    units_here = bins_here // LANES
    exchange = ("freq", "member")
    partners = subs * members
    per_member = units_here * groups
    me_sub, me_group, me_member = (lax.axis_index(axis) for axis in ("freq", "group", "member"))

    kept = units_of_member(units_here, range(groups))
    unit_order = tuple(
        units_here * (sub * blocks + group * members + member) + r
        for sub in range(subs)
        for member in range(members)
        for group, r in kept
    )

    samples = signal.reshape(-1, LANES)
    route = [
        (((sub + 1) % subs) * blocks + block + (sub + 1) // subs, sub * blocks + block)
        for sub in range(subs)
        for block in range(blocks)
        if block + (sub + 1) // subs < blocks
    ]
    trailing = lax.ppermute(samples[:HOP_ROWS], ("freq", "group", "member"), route)
    own_rows = activations.reshape(ranks_here, width // LANES, LANES).transpose(1, 0, 2)
    own_rows = own_rows.reshape(ranks_here * width // LANES, LANES)
    spectrum = spectrum_blocks(samples, trailing, own_rows, unit_order, partners)
    spectrum, templates = lax.optimization_barrier((spectrum, templates))
    other = [swap_by(templates, "group", 1)] if groups == 2 else []
    spectrum = lax.all_to_all(spectrum, exchange, 0, 0, tiled=True)
    local = width // subs
    frames = partners * local

    own = templates.reshape(rank, units_here, LANES).transpose(1, 0, 2)
    if other:
        remote = other[0].reshape(rank, units_here, LANES).transpose(1, 0, 2)
        by_group = jnp.where(me_group == 0, jnp.stack([own, remote]), jnp.stack([remote, own]))
    else:
        by_group = own[None]
    unit_index = units_here * (
        me_sub * blocks + jnp.arange(groups)[:, None] * members + me_member
    ) + jnp.arange(units_here)[None, :]
    is_turned = (unit_index % 2 == 1)[:, :, None, None]
    by_group = jnp.where(is_turned, turned_lanes(by_group), by_group)
    basis = jnp.concatenate([by_group[group, r][None] for group, r in kept], 0)

    lanes_scratch = pltpu.VMEM((frames, 4 * rank), jnp.bfloat16)
    total_scratch = pltpu.VMEM((frames, 2 * rank), jnp.float32)
    half_shape = (frames // 4 + 8, 2 * rank)
    side = (me_sub % 2).astype(jnp.int32).reshape(1)
    mine, other, activity = update_call(
        functools.partial(first_kernel, (subs, members, ranks_here, width)),
        spectrum,
        [half_shape, half_shape, (frames, rank)],
        [lanes_scratch, total_scratch],
        (basis,),
        (side,),
    )
    mine = mine + swap_by(other, "freq", 1)
    mine = sum_over(mine, "freq", 2)
    mine = sum_over(mine, "member", 1)
    other = swap_by(mine, "freq", 1)

    middle, numerator = update_call(
        second_kernel,
        spectrum,
        [(frames, rank), (per_member + 1, rank, LANES)],
        [lanes_scratch, pltpu.VMEM((2 * rank, frames), jnp.bfloat16)],
        (basis, activity, mine, other),
        (side,),
    )
    numerators = [numerator]
    if groups == 2:
        numerators.append(swap_by(numerator, "group", 1))
    new_basis, payload = update_call(
        third_kernel,
        spectrum,
        [(per_member, rank, LANES), (subs, members, 2, ranks_here, width)],
        [lanes_scratch, total_scratch],
        (basis, middle, *numerators),
    )
    received = lax.all_to_all(
        payload.reshape(partners, 2, ranks_here, width), exchange, 0, 0, tiled=True
    )
    summed = jnp.sum(received, axis=0)
    mine = lax.dynamic_slice(
        middle.reshape(subs, members, local, rank),
        (0, me_member, 0, me_sub * ranks_here),
        (subs, 1, local, ranks_here),
    )
    mine = mine.reshape(width, ranks_here).T
    final_activations = mine * (summed[0] / summed[1])

    back = jnp.stack(
        [
            jnp.stack([new_basis[kept.index((group, r))] for r in range(units_here)])
            for group in range(groups)
        ]
    )
    back = lax.dynamic_index_in_dim(back, me_group, 0, keepdims=False)
    turned_here = lax.dynamic_index_in_dim(is_turned, me_group, 0, keepdims=False)
    back = jnp.where(turned_here, turned_lanes(back), back)
    final_templates = back.transpose(1, 0, 2).reshape(rank, bins_here)
    return (final_activations, final_templates)


def solution(mesh):
    subs, blocks = mesh.devices.shape
    groups = 2 if blocks % 2 == 0 else 1
    grid = Mesh(
        mesh.devices.reshape(subs, groups, blocks // groups), ("freq", "group", "member")
    )
    frames = ("group", "member")
    return jax.shard_map(
        on_device,
        mesh=grid,
        in_specs=(P(frames, "freq", None), P(None, ("freq", *frames)), P("freq", frames)),
        out_specs=(P("freq", frames), P(None, ("freq", *frames))),
        check_vma=False,
    )
```

```python
import functools
import math

import jax
import jax.numpy as jnp
import ml_dtypes
import numpy as np
from jax import lax
from jax.experimental import pallas as pl
from jax.experimental.pallas import tpu as pltpu
from jax.sharding import Mesh
from jax.sharding import PartitionSpec as P

FRAME_LEN = 65536
SPLIT = 256
LANES = 128
GROUP = 8
HOP_ROWS = FRAME_LEN // 2 // LANES
SPECTRUM_VMEM = 24 * 1024 * 1024
UPDATE_VMEM = 24 * 1024 * 1024
NT = (((1,), (1,)), ((), ()))


def high_low(values):
    high = values.astype(np.float32).astype(ml_dtypes.bfloat16)
    low = (values - high.astype(np.float64)).astype(ml_dtypes.bfloat16)
    return high, low


def for_three_products(values):
    high, low = high_low(values)
    return np.concatenate([high, low, high], 1)


def units_of_member(units_here, member_blocks):
    order = list(range(units_here))
    if units_here % 8 == 0:
        order.sort(key=lambda r: (row_of_unit(r) % 2, r))
    kept = [(block, r) for block in member_blocks for r in order]
    if units_here % 8 == 0:
        kept.sort(key=lambda pair: row_of_unit(pair[1]) % 2)
    return kept


def row_of_unit(unit):
    return unit // 2 if unit % 2 == 0 else SPLIT - 1 - unit // 2


@functools.lru_cache(maxsize=None)
def tables(unit_order):
    half = SPLIT // 2
    index = np.arange(SPLIT, dtype=np.float64)
    slot = np.arange(half, dtype=np.float64)
    angle = 2.0 * np.pi / SPLIT * np.mod(np.outer(np.arange(half + 1), np.arange(SPLIT)), SPLIT)
    cosine, sine = np.cos(angle), np.sin(angle)
    first = np.concatenate([cosine[:half], cosine[half:], -sine[1:half]], 0)
    turn = 2.0 * np.pi / (SPLIT * SPLIT) * np.outer(slot, index)
    twiddle_cos, twiddle_sin = np.cos(turn), np.sin(turn)
    masked_cos = twiddle_cos.copy()
    masked_cos[0] = 0.0
    twiddle = np.stack([twiddle_cos, twiddle_sin, masked_cos]).astype(np.float32)
    middle = 2.0 * np.pi / (SPLIT * SPLIT) * half * index
    odd = 2.0 * np.pi / SPLIT * slot
    rows = np.zeros((8, SPLIT), np.float32)
    rows[0], rows[1] = np.cos(middle), -np.sin(middle)
    rows[2, :half], rows[3, :half] = np.cos(odd), np.sin(odd)
    seconds, mirrored, places = [], [], []
    for parity in range(2):
        here = [place for place, unit in enumerate(unit_order) if row_of_unit(unit) % 2 == parity]
        turns = np.array([row_of_unit(unit_order[place]) // 2 for place in here])
        phase = 2.0 * np.pi / half * np.mod(np.outer(turns, np.arange(half)), half)
        c, s = np.cos(phase), np.sin(phase)
        seconds.append(
            for_three_products(np.concatenate([np.concatenate([c, s], 1), np.concatenate([-s, c], 1)], 0))
        )
        flags = np.zeros((half, LANES), np.float32)
        flags[:, 0] = [unit_order[place] % 2 for place in here]
        mirrored.append(flags)
        places.append(tuple(here))
    position = np.arange(FRAME_LEN, dtype=np.float64)
    window = (0.5 - 0.5 * np.cos(2.0 * np.pi / FRAME_LEN * position)).astype(np.float32)
    window = window.reshape(SPLIT, 2, LANES).transpose(1, 0, 2)
    return (
        np.ascontiguousarray(window),
        for_three_products(first),
        twiddle,
        rows,
        np.stack(seconds),
        np.stack(mirrored),
        tuple(places),
    )


def split_values(values):
    high = values.astype(jnp.bfloat16)
    low = (values - high.astype(jnp.float32)).astype(jnp.bfloat16)
    return high, low


def dot(left, right):
    return jnp.dot(left, right, preferred_element_type=jnp.float32)


def dot_nt(left, right):
    return lax.dot_general(left, right, NT, preferred_element_type=jnp.float32)


def transform_group(hop_rows, base, stride, places, per_member, table_refs, out_ref, parts_ref, middle_ref, ready):
    window_ref, first_ref, twiddle_ref, rows_ref, second_ref, mirrored_ref = table_refs
    half = SPLIT // 2
    middle_ref[...] = jnp.zeros_like(middle_ref)

    def even_odd(real, imag):
        even = jnp.concatenate([real[:, :half] + real[:, half:], imag[:, :half] + imag[:, half:]], 1)
        real = real[:, :half] - real[:, half:]
        imag = imag[:, :half] - imag[:, half:]
        c, s = rows_ref[2:3, :half], rows_ref[3:4, :half]
        odd = jnp.concatenate([real * c + imag * s, imag * c - real * s], 1)
        return even, odd

    def three(values):
        high, low = split_values(values)
        return jnp.concatenate([high, high, low], 1)

    for g in range(GROUP):
        columns = [
            jnp.concatenate([hop_rows(g, side), hop_rows(g + 1, side)], 0) * window_ref[side]
            for side in range(2)
        ]
        high, low = split_values(jnp.concatenate(columns, 1))
        section = dot(first_ref[...], jnp.concatenate([high, high, low], 0))
        a, b = section[:half], section[half:]
        real = a * twiddle_ref[0] + b * twiddle_ref[1]
        imag = b * twiddle_ref[2] - a * twiddle_ref[1]
        for parity, values in enumerate(even_odd(real, imag)):
            parts_ref[parity, g * half : (g + 1) * half, :] = three(values)
        nyquist = section[half : half + 1]
        for parity, values in enumerate(even_odd(nyquist * rows_ref[0:1], nyquist * rows_ref[1:2])):
            middle_ref[parity, g : g + 1, :] = values

    ready()

    def magnitude(values):
        real, imag = values[:half], values[half:]
        return jnp.sqrt(real * real + imag * imag) * (8.0 / SPLIT)

    for parity in range(2):
        middle = magnitude(dot_nt(second_ref[parity], three(middle_ref[parity])))
        is_middle = mirrored_ref[parity] > 0.0
        for pair in range(GROUP // 2):
            values = magnitude(
                dot_nt(second_ref[parity], parts_ref[parity, pair * SPLIT : (pair + 1) * SPLIT, :])
            )
            for lane in range(2):
                g = 2 * pair + lane
                block = jnp.where(
                    is_middle, middle[:, g : g + 1], values[:, lane * LANES : (lane + 1) * LANES]
                )
                start = 0
                while start < half:
                    stop = start + 1
                    place = places[parity][start]
                    while (
                        stop < half
                        and stop - start < 8
                        and places[parity][stop] == place + stop - start
                        and places[parity][stop] // per_member == place // per_member
                    ):
                        stop += 1
                    member, row = divmod(place, per_member)
                    out_ref[member, pl.ds(row * stride + base + g, stop - start, stride=stride), :] = block[
                        start:stop
                    ]
                    start = stop


def early_kernel(
    places, per_member, frames, samples_ref, *rest
):
    table_refs, (out_ref, tail_ref) = rest[:6], rest[6:8]
    copies_ref, (hops_ref, parts_ref, middle_ref, sem_ref) = rest[8:14], rest[14:]
    groups = frames // GROUP - 1
    group_rows = GROUP * HOP_ROWS
    half = SPLIT // 2

    def fetch(first, count, slot):
        return pltpu.make_async_copy(
            samples_ref.at[pl.ds(first, count), :], hops_ref.at[pl.ds(first, count), :], sem_ref.at[slot]
        )

    tables_in = [
        pltpu.make_async_copy(table_refs[i], copies_ref[i], sem_ref.at[i]) for i in range(len(table_refs))
    ]
    lead = fetch(0, HOP_ROWS, 6)
    tail = pltpu.make_async_copy(
        samples_ref.at[pl.ds(groups * group_rows, group_rows), :], tail_ref, sem_ref.at[7]
    )
    hops = [fetch(HOP_ROWS + i * group_rows, group_rows, 8 + i) for i in range(groups)]
    for copy in [tables_in[1], lead, hops[0], *tables_in[:1], *tables_in[2:], *hops[1:], tail]:
        copy.start()
    lead.wait()
    for copy in tables_in[:4]:
        copy.wait()

    def body(i, carry):
        first = pl.multiple_of(i * group_rows, group_rows)
        pltpu.make_async_copy(
            samples_ref.at[pl.ds(HOP_ROWS + first, group_rows), :],
            hops_ref.at[pl.ds(HOP_ROWS + first, group_rows), :],
            sem_ref.at[8 + i],
        ).wait()

        def ready():
            @pl.when(i == 0)
            def _():
                for copy in tables_in[4:]:
                    copy.wait()

        transform_group(
            lambda hop, side: hops_ref[pl.ds(first + hop * HOP_ROWS + side, half, stride=2), :],
            i * GROUP,
            frames,
            places,
            per_member,
            copies_ref,
            out_ref,
            parts_ref,
            middle_ref,
            ready,
        )
        return carry

    lax.fori_loop(0, groups, body, 0)
    tail.wait()


def late_kernel(places, per_member, frames, tail_ref, trailing_ref, activity_ref, *rest):
    table_refs, (_, out_ref, parts_ref, middle_ref) = rest[:6], rest[6:]

    def hop_rows(hop, side):
        if hop == GROUP:
            return trailing_ref[pl.ds(side, SPLIT // 2, stride=2), :]
        return tail_ref[pl.ds(hop * HOP_ROWS + side, SPLIT // 2, stride=2), :]

    for member in range(out_ref.shape[0]):
        out_ref[member, per_member * frames :, :] = activity_ref[...]
    transform_group(
        hop_rows,
        frames - GROUP,
        frames,
        places,
        per_member,
        table_refs,
        out_ref,
        parts_ref,
        middle_ref,
        lambda: None,
    )


def spectrum_blocks(samples, trailing, activity, unit_order, members):
    *values, places = tables(unit_order)
    per_member = SPLIT // members
    frames = samples.shape[0] // HOP_ROWS
    groups = frames // GROUP - 1
    constants = [jnp.asarray(t) for t in values]
    out_shape = jax.ShapeDtypeStruct((members, per_member * frames + activity.shape[0], LANES), jnp.float32)
    tail_shape = jax.ShapeDtypeStruct((GROUP * HOP_ROWS, LANES), jnp.float32)
    in_vmem = pl.BlockSpec(memory_space=pltpu.VMEM)
    in_hbm = pl.BlockSpec(memory_space=pltpu.HBM)
    scratch = [
        pltpu.VMEM((2, GROUP * LANES, 3 * SPLIT), jnp.bfloat16),
        pltpu.VMEM((2, 16, SPLIT), jnp.float32),
    ]

    def settings(count):
        return dict(
            compiler_params=pltpu.CompilerParams(vmem_limit_bytes=SPECTRUM_VMEM),
            cost_estimate=pl.CostEstimate(
                flops=count * GROUP * 6 * SPLIT * SPLIT * SPLIT * 2,
                bytes_accessed=count * GROUP * FRAME_LEN * 4,
                transcendentals=0,
            ),
        )

    early, tail, *copies = pl.pallas_call(
        functools.partial(early_kernel, places, per_member, frames),
        in_specs=[in_hbm] * (1 + len(constants)),
        out_specs=[in_vmem] * (2 + len(constants)),
        out_shape=[out_shape, tail_shape] + [jax.ShapeDtypeStruct(t.shape, t.dtype) for t in constants],
        scratch_shapes=[pltpu.VMEM(((groups * GROUP + 1) * HOP_ROWS, LANES), jnp.float32)]
        + scratch
        + [pltpu.SemaphoreType.DMA((8 + groups,))],
        **settings(groups),
    )(*[pltpu.with_memory_space_constraint(value, pltpu.HBM) for value in (samples, *constants)])
    return pl.pallas_call(
        functools.partial(late_kernel, places, per_member, frames),
        in_specs=[in_vmem] * (4 + len(constants)),
        out_specs=in_vmem,
        out_shape=out_shape,
        scratch_shapes=scratch,
        input_output_aliases={3 + len(constants): 0},
        **settings(1),
    )(tail, trailing, activity, *copies, early)


def lanes_of_activity(activity):
    high, low = split_values(activity)
    return jnp.concatenate([high, high, low, low], 1)


def ratio_of(spectrum_ref, start, activity_lanes, basis):
    frames = activity_lanes.shape[0]
    local = frames // spectrum_ref.shape[0]
    splits = [split_values(block) for block in basis]
    stacked = jnp.concatenate([jnp.concatenate([h, l, h, l], 0) for h, l in splits], 1)
    approx = dot(activity_lanes, stacked)
    values = jnp.concatenate(
        [
            spectrum_ref[:, (start + row) * local : (start + row + 1) * local, :].reshape(frames, LANES)
            for row in range(len(basis))
        ],
        1,
    )
    return values / approx, jnp.concatenate([jnp.concatenate([h, l], 0) for h, l in splits], 1)


def for_activity(ratio, basis):
    high, low = split_values(ratio)
    return dot_nt(high, basis) + dot_nt(low, basis)


def both_parts(values):
    half = values.shape[1] // 2
    return values + pltpu.roll(values, half, 1)


def row_sums(basis):
    return dot_nt(jnp.ones((16, basis.shape[1]), jnp.bfloat16), basis)


def row_steps(per_member):
    rows = math.gcd(per_member, 8)
    return [range(start, start + rows) for start in range(0, per_member, rows)]


def packed(values):
    rows, width = values.shape
    lane = lax.broadcasted_iota(jnp.int32, (rows // 2, width), 1)
    return jnp.where(lane < width // 2, values[: rows // 2], values[rows // 2 :])


def unpacked(values):
    half = values.shape[1] // 2
    return jnp.concatenate([values[:, :half], values[:, half:]], 0)


def gathered_activity(spectrum_ref, shape):
    subs, members, ranks, width = shape
    local = width // subs
    frames_in = width // LANES
    first = spectrum_ref.shape[1] - ranks * frames_in
    pieces = {}
    for member in range(members):
        for part in range(frames_in):
            start = first + part * ranks
            rows = [spectrum_ref[sub * members + member, start : start + ranks, :] for sub in range(subs)]
            block = jnp.transpose(jnp.concatenate(rows, 0))
            for place in range(LANES // local):
                pieces[part * (LANES // local) + place, member] = block[place * local : (place + 1) * local]
    return jnp.concatenate([pieces[sub, member] for sub in range(subs) for member in range(members)], 0)


def first_kernel(shape, side_ref, spectrum_ref, basis_ref, mine_ref, other_ref, activity_ref, lanes_ref, total_ref):
    activity = gathered_activity(spectrum_ref, shape)
    activity_ref[...] = activity
    lanes_ref[...] = lanes_of_activity(activity)
    sums = 0.0
    for step, rows in enumerate(row_steps(basis_ref.shape[0])):
        ratio, basis = ratio_of(spectrum_ref, rows[0], lanes_ref[...], [basis_ref[row] for row in rows])
        part = for_activity(ratio, basis)
        if step == 0:
            total_ref[...] = part
        else:
            total_ref[...] += part
        sums += row_sums(basis)
    total = both_parts(total_ref[...])
    half = total.shape[0] // 2
    quarter = half // 2
    early, late = packed(total[:half]), packed(total[half:])
    first = side_ref[0] == 0
    mine_ref[:quarter, :] = jnp.where(first, early, late)
    other_ref[:quarter, :] = jnp.where(first, late, early)
    sums = both_parts(sums)[:8]
    mine_ref[quarter:, :] = sums
    other_ref[quarter:, :] = sums


def by_owner(values, shape):
    subs, members, ranks, width = shape
    local = width // subs
    blocks = []
    for member in range(members):
        rows = [
            values[(sub * members + member) * local : (sub * members + member + 1) * local]
            for sub in range(subs)
        ]
        blocks.append(jnp.transpose(jnp.concatenate(rows, 0)).reshape(subs, ranks, width))
    return blocks


def second_kernel(
    side_ref, spectrum_ref, basis_ref, activity_ref, mine_ref, other_ref, middle_ref, out_ref, lanes_ref, turned_ref
):
    rank = activity_ref.shape[1]
    quarter = activity_ref.shape[0] // 4
    first = side_ref[0] == 0
    mine = mine_ref[:quarter, :] / mine_ref[quarter : quarter + 1, :]
    other = other_ref[:quarter, :] / other_ref[quarter : quarter + 1, :]
    early, late = jnp.where(first, mine, other), jnp.where(first, other, mine)
    middle = activity_ref[...] * jnp.concatenate([unpacked(early), unpacked(late)], 0)
    middle_ref[...] = middle
    lanes_ref[...] = lanes_of_activity(middle)
    turned = jnp.transpose(middle)
    high, low = split_values(turned)
    turned_ref[...] = jnp.concatenate([high, low], 0)
    totals = jnp.sum(turned, axis=1, keepdims=True)
    out_ref[out_ref.shape[0] - 1] = jnp.broadcast_to(totals, (rank, LANES))
    for rows in row_steps(basis_ref.shape[0]):
        ratio, _ = ratio_of(spectrum_ref, rows[0], lanes_ref[...], [basis_ref[row] for row in rows])
        high, low = split_values(ratio)
        total = dot(turned_ref[...], high) + dot(turned_ref[...], low)
        total = total[:rank] + total[rank:]
        for place, row in enumerate(rows):
            out_ref[row] = total[:, place * LANES : (place + 1) * LANES]


def third_kernel(spectrum_ref, basis_ref, middle_ref, *rest):
    new_ref, out_ref, lanes_ref, total_ref = rest[-4:]
    numerators = rest[:-4]
    rank = middle_ref.shape[1]
    per_member = basis_ref.shape[0]
    lanes_ref[...] = lanes_of_activity(middle_ref[...])
    scale = 1.0 / sum(ref[per_member] for ref in numerators)
    sums = 0.0
    for step, rows in enumerate(row_steps(per_member)):
        blocks = [basis_ref[row] * (sum(ref[row] for ref in numerators) * scale) for row in rows]
        for row, block in zip(rows, blocks):
            new_ref[row] = block
        ratio, basis = ratio_of(spectrum_ref, rows[0], lanes_ref[...], blocks)
        part = for_activity(ratio, basis)
        if step == 0:
            total_ref[...] = part
        else:
            total_ref[...] += part
        sums += row_sums(basis)
    total = both_parts(total_ref[...])[:, :rank]
    subs, members, _, ranks, width = out_ref.shape
    sums = jnp.transpose(jnp.broadcast_to(both_parts(sums)[:1], (LANES, 2 * rank)))[:rank]
    sums = jnp.concatenate([sums] * (width // LANES), 1).reshape(subs, ranks, width)
    for member, block in enumerate(by_owner(total, (subs, members, ranks, width))):
        out_ref[:, member, 0] = block
        out_ref[:, member, 1] = sums


def update_call(kernel, spectrum, out_shapes, scratch, operands, scalars=()):
    in_vmem = pl.BlockSpec(memory_space=pltpu.VMEM)
    rank = operands[0].shape[1]
    return pl.pallas_call(
        kernel,
        in_specs=[pl.BlockSpec(memory_space=pltpu.SMEM) for _ in scalars]
        + [in_vmem for _ in range(1 + len(operands))],
        out_specs=[in_vmem for _ in out_shapes],
        out_shape=[jax.ShapeDtypeStruct(shape, jnp.float32) for shape in out_shapes],
        scratch_shapes=scratch,
        compiler_params=pltpu.CompilerParams(vmem_limit_bytes=UPDATE_VMEM),
        cost_estimate=pl.CostEstimate(
            flops=spectrum.size * rank * 16, bytes_accessed=spectrum.size * 4, transcendentals=0
        ),
    )(*scalars, spectrum, *operands)


def turned_lanes(values):
    return jnp.roll(jnp.flip(values, -1), 1, -1)


def swap_by(value, axis, mask):
    count = lax.axis_size(axis)
    return lax.ppermute(value, axis, [(i, i ^ mask) for i in range(count)])


def sum_over(value, axis, mask):
    while mask < lax.axis_size(axis):
        value = value + swap_by(value, axis, mask)
        mask *= 2
    return value


def on_device(signal, templates, activations):
    subs, groups, members = (lax.axis_size(axis) for axis in ("freq", "group", "member"))
    blocks = groups * members
    rank, bins_here = templates.shape
    ranks_here, width = activations.shape
    units_here = bins_here // LANES
    exchange = ("freq", "member")
    partners = subs * members
    per_member = units_here * groups
    me_sub, me_group, me_member = (lax.axis_index(axis) for axis in ("freq", "group", "member"))

    kept = units_of_member(units_here, range(groups))
    unit_order = tuple(
        units_here * (sub * blocks + group * members + member) + r
        for sub in range(subs)
        for member in range(members)
        for group, r in kept
    )

    samples = signal.reshape(-1, LANES)
    route = [
        (((sub + 1) % subs) * blocks + block + (sub + 1) // subs, sub * blocks + block)
        for sub in range(subs)
        for block in range(blocks)
        if block + (sub + 1) // subs < blocks
    ]
    trailing = lax.ppermute(samples[:HOP_ROWS], ("freq", "group", "member"), route)
    other = [swap_by(templates, "group", 1)] if groups == 2 else []
    own_rows = activations.reshape(ranks_here, width // LANES, LANES).transpose(1, 0, 2)
    own_rows = own_rows.reshape(ranks_here * width // LANES, LANES)
    spectrum = spectrum_blocks(samples, trailing, own_rows, unit_order, partners)
    spectrum, other = lax.optimization_barrier((spectrum, other))
    spectrum = lax.all_to_all(spectrum, exchange, 0, 0, tiled=True)
    local = width // subs
    frames = partners * local

    own = templates.reshape(rank, units_here, LANES).transpose(1, 0, 2)
    if other:
        remote = other[0].reshape(rank, units_here, LANES).transpose(1, 0, 2)
        by_group = jnp.where(me_group == 0, jnp.stack([own, remote]), jnp.stack([remote, own]))
    else:
        by_group = own[None]
    unit_index = units_here * (
        me_sub * blocks + jnp.arange(groups)[:, None] * members + me_member
    ) + jnp.arange(units_here)[None, :]
    is_turned = (unit_index % 2 == 1)[:, :, None, None]
    by_group = jnp.where(is_turned, turned_lanes(by_group), by_group)
    basis = jnp.concatenate([by_group[group, r][None] for group, r in kept], 0)

    lanes_scratch = pltpu.VMEM((frames, 4 * rank), jnp.bfloat16)
    total_scratch = pltpu.VMEM((frames, 2 * rank), jnp.float32)
    half_shape = (frames // 4 + 8, 2 * rank)
    side = (me_sub % 2).astype(jnp.int32).reshape(1)
    mine, other, activity = update_call(
        functools.partial(first_kernel, (subs, members, ranks_here, width)),
        spectrum,
        [half_shape, half_shape, (frames, rank)],
        [lanes_scratch, total_scratch],
        (basis,),
        (side,),
    )
    mine = mine + swap_by(other, "freq", 1)
    mine = sum_over(mine, "freq", 2)
    mine = sum_over(mine, "member", 1)
    other = swap_by(mine, "freq", 1)

    middle, numerator = update_call(
        second_kernel,
        spectrum,
        [(frames, rank), (per_member + 1, rank, LANES)],
        [lanes_scratch, pltpu.VMEM((2 * rank, frames), jnp.bfloat16)],
        (basis, activity, mine, other),
        (side,),
    )
    numerators = [numerator]
    if groups == 2:
        numerators.append(swap_by(numerator, "group", 1))
    new_basis, payload = update_call(
        third_kernel,
        spectrum,
        [(per_member, rank, LANES), (subs, members, 2, ranks_here, width)],
        [lanes_scratch, total_scratch],
        (basis, middle, *numerators),
    )
    received = lax.all_to_all(
        payload.reshape(partners, 2, ranks_here, width), exchange, 0, 0, tiled=True
    )
    summed = jnp.sum(received, axis=0)
    mine = lax.dynamic_slice(
        middle.reshape(subs, members, local, rank),
        (0, me_member, 0, me_sub * ranks_here),
        (subs, 1, local, ranks_here),
    )
    mine = mine.reshape(width, ranks_here).T
    final_activations = mine * (summed[0] / summed[1])

    back = jnp.stack(
        [
            jnp.stack([new_basis[kept.index((group, r))] for r in range(units_here)])
            for group in range(groups)
        ]
    )
    back = lax.dynamic_index_in_dim(back, me_group, 0, keepdims=False)
    turned_here = lax.dynamic_index_in_dim(is_turned, me_group, 0, keepdims=False)
    back = jnp.where(turned_here, turned_lanes(back), back)
    final_templates = back.transpose(1, 0, 2).reshape(rank, bins_here)
    return (final_activations, final_templates)


def solution(mesh):
    subs, blocks = mesh.devices.shape
    groups = 2 if blocks % 2 == 0 else 1
    grid = Mesh(
        mesh.devices.reshape(subs, groups, blocks // groups), ("freq", "group", "member")
    )
    frames = ("group", "member")
    return jax.shard_map(
        on_device,
        mesh=grid,
        in_specs=(P(frames, "freq", None), P(None, ("freq", *frames)), P("freq", frames)),
        out_specs=(P("freq", frames), P(None, ("freq", *frames))),
        check_vma=False,
    )
```

```python
import functools
import math

import jax
import jax.numpy as jnp
import ml_dtypes
import numpy as np
from jax import lax
from jax.experimental import pallas as pl
from jax.experimental.pallas import tpu as pltpu
from jax.sharding import Mesh
from jax.sharding import PartitionSpec as P

FRAME_LEN = 65536
SPLIT = 256
LANES = 128
GROUP = 8
HOP_ROWS = FRAME_LEN // 2 // LANES
SPECTRUM_VMEM = 24 * 1024 * 1024
UPDATE_VMEM = 24 * 1024 * 1024
NT = (((1,), (1,)), ((), ()))


def high_low(values):
    high = values.astype(np.float32).astype(ml_dtypes.bfloat16)
    low = (values - high.astype(np.float64)).astype(ml_dtypes.bfloat16)
    return high, low


def for_three_products(values):
    high, low = high_low(values)
    return np.concatenate([high, low, high], 1)


def units_of_member(units_here, member_blocks):
    order = list(range(units_here))
    if units_here % 8 == 0:
        order.sort(key=lambda r: (row_of_unit(r) % 2, r))
    kept = [(block, r) for block in member_blocks for r in order]
    if units_here % 8 == 0:
        kept.sort(key=lambda pair: row_of_unit(pair[1]) % 2)
    return kept


def row_of_unit(unit):
    return unit // 2 if unit % 2 == 0 else SPLIT - 1 - unit // 2


@functools.lru_cache(maxsize=None)
def tables(unit_order):
    half = SPLIT // 2
    index = np.arange(SPLIT, dtype=np.float64)
    slot = np.arange(half, dtype=np.float64)
    angle = 2.0 * np.pi / SPLIT * np.mod(np.outer(np.arange(half + 1), np.arange(SPLIT)), SPLIT)
    cosine, sine = np.cos(angle), np.sin(angle)
    first = np.concatenate([cosine[:half], cosine[half:], -sine[1:half]], 0)
    turn = 2.0 * np.pi / (SPLIT * SPLIT) * np.outer(slot, index)
    twiddle_cos, twiddle_sin = np.cos(turn), np.sin(turn)
    masked_cos = twiddle_cos.copy()
    masked_cos[0] = 0.0
    twiddle = np.stack([twiddle_cos, twiddle_sin, masked_cos]).astype(np.float32)
    middle = 2.0 * np.pi / (SPLIT * SPLIT) * half * index
    odd = 2.0 * np.pi / SPLIT * slot
    rows = np.zeros((8, SPLIT), np.float32)
    rows[0], rows[1] = np.cos(middle), -np.sin(middle)
    rows[2, :half], rows[3, :half] = np.cos(odd), np.sin(odd)
    seconds, mirrored, places = [], [], []
    for parity in range(2):
        here = [place for place, unit in enumerate(unit_order) if row_of_unit(unit) % 2 == parity]
        turns = np.array([row_of_unit(unit_order[place]) // 2 for place in here])
        phase = 2.0 * np.pi / half * np.mod(np.outer(turns, np.arange(half)), half)
        c, s = np.cos(phase), np.sin(phase)
        seconds.append(
            for_three_products(np.concatenate([np.concatenate([c, s], 1), np.concatenate([-s, c], 1)], 0))
        )
        flags = np.zeros((half, LANES), np.float32)
        flags[:, 0] = [unit_order[place] % 2 for place in here]
        mirrored.append(flags)
        places.append(tuple(here))
    position = np.arange(FRAME_LEN, dtype=np.float64)
    window = (0.5 - 0.5 * np.cos(2.0 * np.pi / FRAME_LEN * position)).astype(np.float32)
    window = window.reshape(SPLIT, 2, LANES).transpose(1, 0, 2)
    return (
        np.ascontiguousarray(window),
        for_three_products(first),
        twiddle,
        rows,
        np.stack(seconds),
        np.stack(mirrored),
        tuple(places),
    )


def split_values(values):
    high = values.astype(jnp.bfloat16)
    low = (values - high.astype(jnp.float32)).astype(jnp.bfloat16)
    return high, low


def dot(left, right):
    return jnp.dot(left, right, preferred_element_type=jnp.float32)


def dot_nt(left, right):
    return lax.dot_general(left, right, NT, preferred_element_type=jnp.float32)


def transform_group(hop_rows, places, per_member, table_refs, out_ref, parts_ref, middle_ref, ready):
    window_ref, first_ref, twiddle_ref, rows_ref, second_ref, mirrored_ref = table_refs
    half = SPLIT // 2
    middle_ref[...] = jnp.zeros_like(middle_ref)

    def even_odd(real, imag):
        even = jnp.concatenate([real[:, :half] + real[:, half:], imag[:, :half] + imag[:, half:]], 1)
        real = real[:, :half] - real[:, half:]
        imag = imag[:, :half] - imag[:, half:]
        c, s = rows_ref[2:3, :half], rows_ref[3:4, :half]
        odd = jnp.concatenate([real * c + imag * s, imag * c - real * s], 1)
        return even, odd

    def three(values):
        high, low = split_values(values)
        return jnp.concatenate([high, high, low], 1)

    for g in range(GROUP):
        columns = [
            jnp.concatenate([hop_rows(g, side), hop_rows(g + 1, side)], 0) * window_ref[side]
            for side in range(2)
        ]
        high, low = split_values(jnp.concatenate(columns, 1))
        section = dot(first_ref[...], jnp.concatenate([high, high, low], 0))
        a, b = section[:half], section[half:]
        real = a * twiddle_ref[0] + b * twiddle_ref[1]
        imag = b * twiddle_ref[2] - a * twiddle_ref[1]
        for parity, values in enumerate(even_odd(real, imag)):
            parts_ref[parity, g * half : (g + 1) * half, :] = three(values)
        nyquist = section[half : half + 1]
        for parity, values in enumerate(even_odd(nyquist * rows_ref[0:1], nyquist * rows_ref[1:2])):
            middle_ref[parity, g : g + 1, :] = values

    ready()

    def magnitude(values):
        real, imag = values[:half], values[half:]
        return jnp.sqrt(real * real + imag * imag) * (8.0 / SPLIT)

    for parity in range(2):
        middle = magnitude(dot_nt(second_ref[parity], three(middle_ref[parity])))
        is_middle = mirrored_ref[parity] > 0.0
        for pair in range(GROUP // 2):
            values = magnitude(
                dot_nt(second_ref[parity], parts_ref[parity, pair * SPLIT : (pair + 1) * SPLIT, :])
            )
            for lane in range(2):
                g = 2 * pair + lane
                block = jnp.where(
                    is_middle, middle[:, g : g + 1], values[:, lane * LANES : (lane + 1) * LANES]
                )
                start = 0
                while start < half:
                    stop = start + 1
                    place = places[parity][start]
                    while (
                        stop < half
                        and stop - start < 8
                        and places[parity][stop] == place + stop - start
                        and places[parity][stop] // per_member == place // per_member
                    ):
                        stop += 1
                    member, row = divmod(place, per_member)
                    out_ref[member, pl.ds(row * GROUP + g, stop - start, stride=GROUP), :] = block[start:stop]
                    start = stop


def early_kernel(
    places, per_member, frames, samples_ref, *rest
):
    table_refs, (out_ref, tail_ref) = rest[:6], rest[6:8]
    copies_ref, (hops_ref, parts_ref, middle_ref, group_ref, sem_ref, out_sem_ref) = rest[8:14], rest[14:]
    groups = frames // GROUP - 1
    group_rows = GROUP * HOP_ROWS
    half = SPLIT // 2

    def fetch(first, count, slot):
        return pltpu.make_async_copy(
            samples_ref.at[pl.ds(first, count), :], hops_ref.at[pl.ds(first, count), :], sem_ref.at[slot]
        )

    tables_in = [
        pltpu.make_async_copy(table_refs[i], copies_ref[i], sem_ref.at[i]) for i in range(len(table_refs))
    ]
    lead = fetch(0, HOP_ROWS, 6)
    tail = pltpu.make_async_copy(
        samples_ref.at[pl.ds(groups * group_rows, group_rows), :], tail_ref, sem_ref.at[7]
    )
    hops = [fetch(HOP_ROWS + i * group_rows, group_rows, 8 + i) for i in range(groups)]
    for copy in [tables_in[1], lead, hops[0], *tables_in[:1], *tables_in[2:], *hops[1:], tail]:
        copy.start()
    lead.wait()
    for copy in tables_in[:4]:
        copy.wait()

    def body(i, carry):
        first = pl.multiple_of(i * group_rows, group_rows)
        pltpu.make_async_copy(
            samples_ref.at[pl.ds(HOP_ROWS + first, group_rows), :],
            hops_ref.at[pl.ds(HOP_ROWS + first, group_rows), :],
            sem_ref.at[8 + i],
        ).wait()

        def ready():
            @pl.when(i == 0)
            def _():
                for copy in tables_in[4:]:
                    copy.wait()

        transform_group(
            lambda hop, side: hops_ref[pl.ds(first + hop * HOP_ROWS + side, half, stride=2), :],
            places,
            per_member,
            copies_ref,
            group_ref.at[i],
            parts_ref,
            middle_ref,
            ready,
        )
        send(i).start()
        return carry

    def send(i):
        count = group_ref.shape[2]
        return pltpu.make_async_copy(
            group_ref.at[i],
            out_ref.at[:, pl.ds(pl.multiple_of(i * count, count), count), :],
            out_sem_ref.at[i],
        )

    lax.fori_loop(0, groups, body, 0)
    tail.wait()
    for i in range(groups):
        send(i).wait()


def late_kernel(places, per_member, frames, tail_ref, trailing_ref, activity_ref, *rest):
    table_refs, (_, out_ref, parts_ref, middle_ref, group_ref, sem_ref) = rest[:6], rest[6:]
    count = per_member * GROUP

    def hop_rows(hop, side):
        if hop == GROUP:
            return trailing_ref[pl.ds(side, SPLIT // 2, stride=2), :]
        return tail_ref[pl.ds(hop * HOP_ROWS + side, SPLIT // 2, stride=2), :]

    for member in range(out_ref.shape[0]):
        group_ref[member, count:, :] = activity_ref[...]
    transform_group(
        hop_rows,
        places,
        per_member,
        table_refs,
        group_ref,
        parts_ref,
        middle_ref,
        lambda: None,
    )
    first = (frames // GROUP - 1) * count
    send = pltpu.make_async_copy(group_ref, out_ref.at[:, pl.ds(first, group_ref.shape[1]), :], sem_ref)
    send.start()
    send.wait()


def spectrum_blocks(samples, trailing, activity, unit_order, members):
    *values, places = tables(unit_order)
    per_member = SPLIT // members
    frames = samples.shape[0] // HOP_ROWS
    groups = frames // GROUP - 1
    constants = [jnp.asarray(t) for t in values]
    group_shape = (members, per_member * GROUP, LANES)
    last_shape = (members, per_member * GROUP + activity.shape[0], LANES)
    out_shape = pltpu.HBM((members, per_member * frames + activity.shape[0], LANES), jnp.float32)
    tail_shape = jax.ShapeDtypeStruct((GROUP * HOP_ROWS, LANES), jnp.float32)
    in_vmem = pl.BlockSpec(memory_space=pltpu.VMEM)
    in_hbm = pl.BlockSpec(memory_space=pltpu.HBM)
    scratch = [
        pltpu.VMEM((2, GROUP * LANES, 3 * SPLIT), jnp.bfloat16),
        pltpu.VMEM((2, 16, SPLIT), jnp.float32),
    ]

    def settings(count):
        return dict(
            compiler_params=pltpu.CompilerParams(vmem_limit_bytes=SPECTRUM_VMEM),
            cost_estimate=pl.CostEstimate(
                flops=count * GROUP * 6 * SPLIT * SPLIT * SPLIT * 2,
                bytes_accessed=count * GROUP * FRAME_LEN * 4,
                transcendentals=0,
            ),
        )

    early, tail, *copies = pl.pallas_call(
        functools.partial(early_kernel, places, per_member, frames),
        in_specs=[in_hbm] * (1 + len(constants)),
        out_specs=[in_hbm] + [in_vmem] * (1 + len(constants)),
        out_shape=[out_shape, tail_shape] + [jax.ShapeDtypeStruct(t.shape, t.dtype) for t in constants],
        scratch_shapes=[pltpu.VMEM(((groups * GROUP + 1) * HOP_ROWS, LANES), jnp.float32)]
        + scratch
        + [
            pltpu.VMEM((groups, *group_shape), jnp.float32),
            pltpu.SemaphoreType.DMA((8 + groups,)),
            pltpu.SemaphoreType.DMA((groups,)),
        ],
        **settings(groups),
    )(*[pltpu.with_memory_space_constraint(value, pltpu.HBM) for value in (samples, *constants)])
    return pl.pallas_call(
        functools.partial(late_kernel, places, per_member, frames),
        in_specs=[in_vmem] * (3 + len(constants)) + [in_hbm],
        out_specs=in_hbm,
        out_shape=out_shape,
        scratch_shapes=scratch + [pltpu.VMEM(last_shape, jnp.float32), pltpu.SemaphoreType.DMA],
        input_output_aliases={3 + len(constants): 0},
        **settings(1),
    )(tail, trailing, activity, *copies, early)


def lanes_of_activity(activity):
    high, low = split_values(activity)
    return jnp.concatenate([high, high, low, low], 1)


def ratio_of(spectrum_ref, start, activity_lanes, basis):
    frames = activity_lanes.shape[0]
    members = spectrum_ref.shape[0]
    groups = frames // (members * GROUP)
    stride = spectrum_ref.shape[1] // groups
    splits = [split_values(block) for block in basis]
    stacked = jnp.concatenate([jnp.concatenate([h, l, h, l], 0) for h, l in splits], 1)
    approx = dot(activity_lanes, stacked)
    values = jnp.concatenate(
        [
            jnp.stack(
                [
                    spectrum_ref[:, pl.ds(group * stride + (start + row) * GROUP, GROUP), :]
                    for group in range(groups)
                ],
                1,
            ).reshape(frames, LANES)
            for row in range(len(basis))
        ],
        1,
    )
    return values / approx, jnp.concatenate([jnp.concatenate([h, l], 0) for h, l in splits], 1)


def for_activity(ratio, basis):
    high, low = split_values(ratio)
    return dot_nt(high, basis) + dot_nt(low, basis)


def both_parts(values):
    half = values.shape[1] // 2
    return values + pltpu.roll(values, half, 1)


def row_sums(basis):
    return dot_nt(jnp.ones((16, basis.shape[1]), jnp.bfloat16), basis)


def row_steps(per_member):
    rows = math.gcd(per_member, 8)
    return [range(start, start + rows) for start in range(0, per_member, rows)]


def packed(values):
    rows, width = values.shape
    lane = lax.broadcasted_iota(jnp.int32, (rows // 2, width), 1)
    return jnp.where(lane < width // 2, values[: rows // 2], values[rows // 2 :])


def unpacked(values):
    half = values.shape[1] // 2
    return jnp.concatenate([values[:, :half], values[:, half:]], 0)


def gathered_activity(rows_ref, shape):
    subs, members, ranks, width = shape
    local = width // subs
    frames_in = width // LANES
    pieces = {}
    for member in range(members):
        for part in range(frames_in):
            start = part * ranks
            rows = [rows_ref[sub * members + member, start : start + ranks, :] for sub in range(subs)]
            block = jnp.transpose(jnp.concatenate(rows, 0))
            for place in range(LANES // local):
                pieces[part * (LANES // local) + place, member] = block[place * local : (place + 1) * local]
    return jnp.concatenate([pieces[sub, member] for sub in range(subs) for member in range(members)], 0)


def first_kernel(
    shape,
    side_ref,
    received_ref,
    basis_ref,
    mine_ref,
    other_ref,
    activity_ref,
    spectrum_ref,
    lanes_ref,
    total_ref,
    rows_ref,
    sem_ref,
):
    per_member = basis_ref.shape[0]
    count = spectrum_ref.shape[1]
    groups = count // (per_member * GROUP)
    steps = row_steps(per_member)

    def fetch(step, group):
        place = pl.ds((group * per_member + steps[step][0]) * GROUP, len(steps[step]) * GROUP)
        return pltpu.make_async_copy(
            received_ref.at[:, place, :], spectrum_ref.at[:, place, :], sem_ref.at[1 + step * groups + group]
        )

    rows_copy = pltpu.make_async_copy(
        received_ref.at[:, pl.ds(count, rows_ref.shape[1]), :], rows_ref, sem_ref.at[0]
    )
    rows_copy.start()
    copies = [[fetch(step, group) for group in range(groups)] for step in range(len(steps))]
    for copy in sum(copies, []):
        copy.start()
    rows_copy.wait()
    activity = gathered_activity(rows_ref, shape)
    activity_ref[...] = activity
    lanes_ref[...] = lanes_of_activity(activity)
    sums = 0.0
    for step, rows in enumerate(steps):
        for copy in copies[step]:
            copy.wait()
        ratio, basis = ratio_of(spectrum_ref, rows[0], lanes_ref[...], [basis_ref[row] for row in rows])
        part = for_activity(ratio, basis)
        if step == 0:
            total_ref[...] = part
        else:
            total_ref[...] += part
        sums += row_sums(basis)
    total = both_parts(total_ref[...])
    half = total.shape[0] // 2
    quarter = half // 2
    early, late = packed(total[:half]), packed(total[half:])
    first = side_ref[0] == 0
    mine_ref[:quarter, :] = jnp.where(first, early, late)
    other_ref[:quarter, :] = jnp.where(first, late, early)
    sums = both_parts(sums)[:8]
    mine_ref[quarter:, :] = sums
    other_ref[quarter:, :] = sums


def by_owner(values, shape):
    subs, members, ranks, width = shape
    local = width // subs
    blocks = []
    for member in range(members):
        rows = [
            values[(sub * members + member) * local : (sub * members + member + 1) * local]
            for sub in range(subs)
        ]
        blocks.append(jnp.transpose(jnp.concatenate(rows, 0)).reshape(subs, ranks, width))
    return blocks


def second_kernel(
    side_ref, spectrum_ref, basis_ref, activity_ref, mine_ref, other_ref, middle_ref, out_ref, lanes_ref, turned_ref
):
    rank = activity_ref.shape[1]
    quarter = activity_ref.shape[0] // 4
    first = side_ref[0] == 0
    mine = mine_ref[:quarter, :] / mine_ref[quarter : quarter + 1, :]
    other = other_ref[:quarter, :] / other_ref[quarter : quarter + 1, :]
    early, late = jnp.where(first, mine, other), jnp.where(first, other, mine)
    middle = activity_ref[...] * jnp.concatenate([unpacked(early), unpacked(late)], 0)
    middle_ref[...] = middle
    lanes_ref[...] = lanes_of_activity(middle)
    turned = jnp.transpose(middle)
    high, low = split_values(turned)
    turned_ref[...] = jnp.concatenate([high, low], 0)
    totals = jnp.sum(turned, axis=1, keepdims=True)
    out_ref[out_ref.shape[0] - 1] = jnp.broadcast_to(totals, (rank, LANES))
    for rows in row_steps(basis_ref.shape[0]):
        ratio, _ = ratio_of(spectrum_ref, rows[0], lanes_ref[...], [basis_ref[row] for row in rows])
        high, low = split_values(ratio)
        total = dot(turned_ref[...], high) + dot(turned_ref[...], low)
        total = total[:rank] + total[rank:]
        for place, row in enumerate(rows):
            out_ref[row] = total[:, place * LANES : (place + 1) * LANES]


def third_kernel(spectrum_ref, basis_ref, middle_ref, *rest):
    new_ref, out_ref, lanes_ref, total_ref = rest[-4:]
    numerators = rest[:-4]
    rank = middle_ref.shape[1]
    per_member = basis_ref.shape[0]
    lanes_ref[...] = lanes_of_activity(middle_ref[...])
    scale = 1.0 / sum(ref[per_member] for ref in numerators)
    sums = 0.0
    for step, rows in enumerate(row_steps(per_member)):
        blocks = [basis_ref[row] * (sum(ref[row] for ref in numerators) * scale) for row in rows]
        for row, block in zip(rows, blocks):
            new_ref[row] = block
        ratio, basis = ratio_of(spectrum_ref, rows[0], lanes_ref[...], blocks)
        part = for_activity(ratio, basis)
        if step == 0:
            total_ref[...] = part
        else:
            total_ref[...] += part
        sums += row_sums(basis)
    total = both_parts(total_ref[...])[:, :rank]
    subs, members, _, ranks, width = out_ref.shape
    sums = jnp.transpose(jnp.broadcast_to(both_parts(sums)[:1], (LANES, 2 * rank)))[:rank]
    sums = jnp.concatenate([sums] * (width // LANES), 1).reshape(subs, ranks, width)
    for member, block in enumerate(by_owner(total, (subs, members, ranks, width))):
        out_ref[:, member, 0] = block
        out_ref[:, member, 1] = sums


def update_call(kernel, spectrum, out_shapes, scratch, operands, scalars=(), place=pltpu.VMEM):
    in_vmem = pl.BlockSpec(memory_space=pltpu.VMEM)
    if place == pltpu.HBM:
        spectrum = pltpu.with_memory_space_constraint(spectrum, place)
    rank = operands[0].shape[1]
    return pl.pallas_call(
        kernel,
        in_specs=[pl.BlockSpec(memory_space=pltpu.SMEM) for _ in scalars]
        + [pl.BlockSpec(memory_space=place)]
        + [in_vmem for _ in operands],
        out_specs=[in_vmem for _ in out_shapes],
        out_shape=[jax.ShapeDtypeStruct(shape, jnp.float32) for shape in out_shapes],
        scratch_shapes=scratch,
        compiler_params=pltpu.CompilerParams(vmem_limit_bytes=UPDATE_VMEM),
        cost_estimate=pl.CostEstimate(
            flops=spectrum.size * rank * 16, bytes_accessed=spectrum.size * 4, transcendentals=0
        ),
    )(*scalars, spectrum, *operands)


def turned_lanes(values):
    return jnp.roll(jnp.flip(values, -1), 1, -1)


def swap_by(value, axis, mask):
    count = lax.axis_size(axis)
    return lax.ppermute(value, axis, [(i, i ^ mask) for i in range(count)])


def sum_over(value, axis, mask):
    count = lax.axis_size(axis)
    while mask < count:
        masks = [mask] if 2 * mask >= count else [mask, 2 * mask, 3 * mask]
        value = sum([swap_by(value, axis, m) for m in masks], value)
        mask *= 2 if len(masks) == 1 else 4
    return value


def on_device(signal, templates, activations):
    subs, groups, members = (lax.axis_size(axis) for axis in ("freq", "group", "member"))
    blocks = groups * members
    rank, bins_here = templates.shape
    ranks_here, width = activations.shape
    units_here = bins_here // LANES
    exchange = ("freq", "member")
    partners = subs * members
    per_member = units_here * groups
    me_sub, me_group, me_member = (lax.axis_index(axis) for axis in ("freq", "group", "member"))

    kept = units_of_member(units_here, range(groups))
    unit_order = tuple(
        units_here * (sub * blocks + group * members + member) + r
        for sub in range(subs)
        for member in range(members)
        for group, r in kept
    )

    samples = signal.reshape(-1, LANES)
    route = [
        (((sub + 1) % subs) * blocks + block + (sub + 1) // subs, sub * blocks + block)
        for sub in range(subs)
        for block in range(blocks)
        if block + (sub + 1) // subs < blocks
    ]
    trailing = lax.ppermute(samples[:HOP_ROWS], ("freq", "group", "member"), route)
    other = [swap_by(templates, "group", 1)] if groups == 2 else []
    own_rows = activations.reshape(ranks_here, width // LANES, LANES).transpose(1, 0, 2)
    own_rows = own_rows.reshape(ranks_here * width // LANES, LANES)
    spectrum = spectrum_blocks(samples, trailing, own_rows, unit_order, partners)
    spectrum, other = lax.optimization_barrier((spectrum, other))
    spectrum = lax.all_to_all(spectrum, exchange, 0, 0, tiled=True)
    local = width // subs
    frames = partners * local

    own = templates.reshape(rank, units_here, LANES).transpose(1, 0, 2)
    if other:
        remote = other[0].reshape(rank, units_here, LANES).transpose(1, 0, 2)
        by_group = jnp.where(me_group == 0, jnp.stack([own, remote]), jnp.stack([remote, own]))
    else:
        by_group = own[None]
    unit_index = units_here * (
        me_sub * blocks + jnp.arange(groups)[:, None] * members + me_member
    ) + jnp.arange(units_here)[None, :]
    is_turned = (unit_index % 2 == 1)[:, :, None, None]
    by_group = jnp.where(is_turned, turned_lanes(by_group), by_group)
    basis = jnp.concatenate([by_group[group, r][None] for group, r in kept], 0)

    lanes_scratch = pltpu.VMEM((frames, 4 * rank), jnp.bfloat16)
    total_scratch = pltpu.VMEM((frames, 2 * rank), jnp.float32)
    half_shape = (frames // 4 + 8, 2 * rank)
    side = (me_sub % 2).astype(jnp.int32).reshape(1)
    extra = ranks_here * width // LANES
    spectrum_rows = spectrum.shape[1] - extra
    row_groups = spectrum_rows // (per_member * GROUP)
    mine, other, activity, spectrum = update_call(
        functools.partial(first_kernel, (subs, members, ranks_here, width)),
        spectrum,
        [half_shape, half_shape, (frames, rank), (partners, spectrum_rows, LANES)],
        [
            lanes_scratch,
            total_scratch,
            pltpu.VMEM((partners, extra, LANES), jnp.float32),
            pltpu.SemaphoreType.DMA((1 + len(row_steps(per_member)) * row_groups,)),
        ],
        (basis,),
        (side,),
        pltpu.HBM,
    )
    mine = mine + swap_by(other, "freq", 1)
    mine = sum_over(mine, "freq", 2)
    mine = sum_over(mine, "member", 1)
    other = swap_by(mine, "freq", 1)

    middle, numerator = update_call(
        second_kernel,
        spectrum,
        [(frames, rank), (per_member + 1, rank, LANES)],
        [lanes_scratch, pltpu.VMEM((2 * rank, frames), jnp.bfloat16)],
        (basis, activity, mine, other),
        (side,),
    )
    numerators = [numerator]
    if groups == 2:
        numerators.append(swap_by(numerator, "group", 1))
    new_basis, payload = update_call(
        third_kernel,
        spectrum,
        [(per_member, rank, LANES), (subs, members, 2, ranks_here, width)],
        [lanes_scratch, total_scratch],
        (basis, middle, *numerators),
    )
    received = lax.all_to_all(
        payload.reshape(partners, 2, ranks_here, width), exchange, 0, 0, tiled=True
    )
    summed = jnp.sum(received, axis=0)
    mine = lax.dynamic_slice(
        middle.reshape(subs, members, local, rank),
        (0, me_member, 0, me_sub * ranks_here),
        (subs, 1, local, ranks_here),
    )
    mine = mine.reshape(width, ranks_here).T
    final_activations = mine * (summed[0] / summed[1])

    back = jnp.stack(
        [
            jnp.stack([new_basis[kept.index((group, r))] for r in range(units_here)])
            for group in range(groups)
        ]
    )
    back = lax.dynamic_index_in_dim(back, me_group, 0, keepdims=False)
    turned_here = lax.dynamic_index_in_dim(is_turned, me_group, 0, keepdims=False)
    back = jnp.where(turned_here, turned_lanes(back), back)
    final_templates = back.transpose(1, 0, 2).reshape(rank, bins_here)
    return (final_activations, final_templates)


def solution(mesh):
    subs, blocks = mesh.devices.shape
    groups = 2 if blocks % 2 == 0 else 1
    grid = Mesh(
        mesh.devices.reshape(subs, groups, blocks // groups), ("freq", "group", "member")
    )
    frames = ("group", "member")
    return jax.shard_map(
        on_device,
        mesh=grid,
        in_specs=(P(frames, "freq", None), P(None, ("freq", *frames)), P("freq", frames)),
        out_specs=(P("freq", frames), P(None, ("freq", *frames))),
        check_vma=False,
    )
```

```python
import functools
import math

import jax
import jax.numpy as jnp
import ml_dtypes
import numpy as np
from jax import lax
from jax.experimental import pallas as pl
from jax.experimental.pallas import tpu as pltpu
from jax.sharding import Mesh
from jax.sharding import PartitionSpec as P

FRAME_LEN = 65536
SPLIT = 256
LANES = 128
GROUP = 8
HOP_ROWS = FRAME_LEN // 2 // LANES
SPECTRUM_VMEM = 24 * 1024 * 1024
UPDATE_VMEM = 24 * 1024 * 1024
NT = (((1,), (1,)), ((), ()))


def high_low(values):
    high = values.astype(np.float32).astype(ml_dtypes.bfloat16)
    low = (values - high.astype(np.float64)).astype(ml_dtypes.bfloat16)
    return high, low


def for_three_products(values):
    high, low = high_low(values)
    return np.concatenate([high, low, high], 1)


def units_of_member(units_here, member_blocks):
    order = list(range(units_here))
    if units_here % 8 == 0:
        order.sort(key=lambda r: (row_of_unit(r) % 2, r))
    kept = [(block, r) for block in member_blocks for r in order]
    if units_here % 8 == 0:
        kept.sort(key=lambda pair: row_of_unit(pair[1]) % 2)
    return kept


def row_of_unit(unit):
    return unit // 2 if unit % 2 == 0 else SPLIT - 1 - unit // 2


@functools.lru_cache(maxsize=None)
def tables(unit_order):
    half = SPLIT // 2
    index = np.arange(SPLIT, dtype=np.float64)
    slot = np.arange(half, dtype=np.float64)
    angle = 2.0 * np.pi / SPLIT * np.mod(np.outer(np.arange(half + 1), np.arange(SPLIT)), SPLIT)
    cosine, sine = np.cos(angle), np.sin(angle)
    first = np.concatenate([cosine[:half], cosine[half:], -sine[1:half]], 0)
    turn = 2.0 * np.pi / (SPLIT * SPLIT) * np.outer(slot, index)
    twiddle_cos, twiddle_sin = np.cos(turn), np.sin(turn)
    masked_cos = twiddle_cos.copy()
    masked_cos[0] = 0.0
    twiddle = np.stack([twiddle_cos, twiddle_sin, masked_cos]).astype(np.float32)
    middle = 2.0 * np.pi / (SPLIT * SPLIT) * half * index
    odd = 2.0 * np.pi / SPLIT * slot
    rows = np.zeros((8, SPLIT), np.float32)
    rows[0], rows[1] = np.cos(middle), -np.sin(middle)
    rows[2, :half], rows[3, :half] = np.cos(odd), np.sin(odd)
    seconds, mirrored, places = [], [], []
    for parity in range(2):
        here = [place for place, unit in enumerate(unit_order) if row_of_unit(unit) % 2 == parity]
        turns = np.array([row_of_unit(unit_order[place]) // 2 for place in here])
        phase = 2.0 * np.pi / half * np.mod(np.outer(turns, np.arange(half)), half)
        c, s = np.cos(phase), np.sin(phase)
        seconds.append(
            for_three_products(np.concatenate([np.concatenate([c, s], 1), np.concatenate([-s, c], 1)], 0))
        )
        flags = np.zeros((half, LANES), np.float32)
        flags[:, 0] = [unit_order[place] % 2 for place in here]
        mirrored.append(flags)
        places.append(tuple(here))
    position = np.arange(FRAME_LEN, dtype=np.float64)
    window = (0.5 - 0.5 * np.cos(2.0 * np.pi / FRAME_LEN * position)).astype(np.float32)
    window = window.reshape(SPLIT, 2, LANES).transpose(1, 0, 2)
    return (
        np.ascontiguousarray(window),
        for_three_products(first),
        twiddle,
        rows,
        np.stack(seconds),
        np.stack(mirrored),
        tuple(places),
    )


def split_values(values):
    high = values.astype(jnp.bfloat16)
    low = (values - high.astype(jnp.float32)).astype(jnp.bfloat16)
    return high, low


def dot(left, right):
    return jnp.dot(left, right, preferred_element_type=jnp.float32)


def dot_nt(left, right):
    return lax.dot_general(left, right, NT, preferred_element_type=jnp.float32)


def transform_group(hop_rows, places, per_member, table_refs, out_ref, parts_ref, middle_ref, ready):
    window_ref, first_ref, twiddle_ref, rows_ref, second_ref, mirrored_ref = table_refs
    half = SPLIT // 2
    middle_ref[...] = jnp.zeros_like(middle_ref)

    def even_odd(real, imag):
        even = jnp.concatenate([real[:, :half] + real[:, half:], imag[:, :half] + imag[:, half:]], 1)
        real = real[:, :half] - real[:, half:]
        imag = imag[:, :half] - imag[:, half:]
        c, s = rows_ref[2:3, :half], rows_ref[3:4, :half]
        odd = jnp.concatenate([real * c + imag * s, imag * c - real * s], 1)
        return even, odd

    def three(values):
        high, low = split_values(values)
        return jnp.concatenate([high, high, low], 1)

    for g in range(GROUP):
        columns = [
            jnp.concatenate([hop_rows(g, side), hop_rows(g + 1, side)], 0) * window_ref[side]
            for side in range(2)
        ]
        high, low = split_values(jnp.concatenate(columns, 1))
        section = dot(first_ref[...], jnp.concatenate([high, high, low], 0))
        a, b = section[:half], section[half:]
        real = a * twiddle_ref[0] + b * twiddle_ref[1]
        imag = b * twiddle_ref[2] - a * twiddle_ref[1]
        for parity, values in enumerate(even_odd(real, imag)):
            parts_ref[parity, g * half : (g + 1) * half, :] = three(values)
        nyquist = section[half : half + 1]
        for parity, values in enumerate(even_odd(nyquist * rows_ref[0:1], nyquist * rows_ref[1:2])):
            middle_ref[parity, g : g + 1, :] = values

    ready()

    def magnitude(values):
        real, imag = values[:half], values[half:]
        return jnp.sqrt(real * real + imag * imag) * (8.0 / SPLIT)

    for parity in range(2):
        middle = magnitude(dot_nt(second_ref[parity], three(middle_ref[parity])))
        is_middle = mirrored_ref[parity] > 0.0
        for pair in range(GROUP // 2):
            values = magnitude(
                dot_nt(second_ref[parity], parts_ref[parity, pair * SPLIT : (pair + 1) * SPLIT, :])
            )
            for lane in range(2):
                g = 2 * pair + lane
                block = jnp.where(
                    is_middle, middle[:, g : g + 1], values[:, lane * LANES : (lane + 1) * LANES]
                )
                start = 0
                while start < half:
                    stop = start + 1
                    place = places[parity][start]
                    while (
                        stop < half
                        and stop - start < 8
                        and places[parity][stop] == place + stop - start
                        and places[parity][stop] // per_member == place // per_member
                    ):
                        stop += 1
                    member, row = divmod(place, per_member)
                    out_ref[member, pl.ds(row * GROUP + g, stop - start, stride=GROUP), :] = block[start:stop]
                    start = stop


def early_kernel(
    places, per_member, frames, samples_ref, *rest
):
    table_refs, (out_ref, tail_ref) = rest[:6], rest[6:8]
    copies_ref, (hops_ref, parts_ref, middle_ref, group_ref, sem_ref, out_sem_ref) = rest[8:14], rest[14:]
    groups = frames // GROUP - 1
    group_rows = GROUP * HOP_ROWS
    half = SPLIT // 2

    def fetch(first, count, slot):
        return pltpu.make_async_copy(
            samples_ref.at[pl.ds(first, count), :], hops_ref.at[pl.ds(first, count), :], sem_ref.at[slot]
        )

    tables_in = [
        pltpu.make_async_copy(table_refs[i], copies_ref[i], sem_ref.at[i]) for i in range(len(table_refs))
    ]
    lead = fetch(0, HOP_ROWS, 6)
    tail = pltpu.make_async_copy(
        samples_ref.at[pl.ds(groups * group_rows, group_rows), :], tail_ref, sem_ref.at[7]
    )
    hops = [fetch(HOP_ROWS + i * group_rows, group_rows, 8 + i) for i in range(groups)]
    for copy in [tables_in[1], lead, hops[0], *tables_in[:1], *tables_in[2:], *hops[1:], tail]:
        copy.start()
    lead.wait()
    for copy in tables_in[:4]:
        copy.wait()

    def body(i, carry):
        first = pl.multiple_of(i * group_rows, group_rows)
        pltpu.make_async_copy(
            samples_ref.at[pl.ds(HOP_ROWS + first, group_rows), :],
            hops_ref.at[pl.ds(HOP_ROWS + first, group_rows), :],
            sem_ref.at[8 + i],
        ).wait()

        def ready():
            @pl.when(i == 0)
            def _():
                for copy in tables_in[4:]:
                    copy.wait()

        transform_group(
            lambda hop, side: hops_ref[pl.ds(first + hop * HOP_ROWS + side, half, stride=2), :],
            places,
            per_member,
            copies_ref,
            group_ref.at[i],
            parts_ref,
            middle_ref,
            ready,
        )
        send(i).start()
        return carry

    def send(i):
        count = group_ref.shape[2]
        return pltpu.make_async_copy(
            group_ref.at[i],
            out_ref.at[:, pl.ds(pl.multiple_of(i * count, count), count), :],
            out_sem_ref.at[i],
        )

    lax.fori_loop(0, groups, body, 0)
    tail.wait()
    for i in range(groups):
        send(i).wait()


def late_kernel(places, per_member, frames, tail_ref, trailing_ref, activity_ref, *rest):
    table_refs, (_, out_ref, parts_ref, middle_ref, group_ref, sem_ref) = rest[:6], rest[6:]
    count = per_member * GROUP

    def hop_rows(hop, side):
        if hop == GROUP:
            return trailing_ref[pl.ds(side, SPLIT // 2, stride=2), :]
        return tail_ref[pl.ds(hop * HOP_ROWS + side, SPLIT // 2, stride=2), :]

    for member in range(out_ref.shape[0]):
        group_ref[member, count:, :] = activity_ref[...]
    transform_group(
        hop_rows,
        places,
        per_member,
        table_refs,
        group_ref,
        parts_ref,
        middle_ref,
        lambda: None,
    )
    first = (frames // GROUP - 1) * count
    send = pltpu.make_async_copy(group_ref, out_ref.at[:, pl.ds(first, group_ref.shape[1]), :], sem_ref)
    send.start()
    send.wait()


def spectrum_blocks(samples, trailing, activity, unit_order, members):
    *values, places = tables(unit_order)
    per_member = SPLIT // members
    frames = samples.shape[0] // HOP_ROWS
    groups = frames // GROUP - 1
    constants = [jnp.asarray(t) for t in values]
    group_shape = (members, per_member * GROUP, LANES)
    last_shape = (members, per_member * GROUP + activity.shape[0], LANES)
    out_shape = pltpu.HBM((members, per_member * frames + activity.shape[0], LANES), jnp.float32)
    tail_shape = jax.ShapeDtypeStruct((GROUP * HOP_ROWS, LANES), jnp.float32)
    in_vmem = pl.BlockSpec(memory_space=pltpu.VMEM)
    in_hbm = pl.BlockSpec(memory_space=pltpu.HBM)
    scratch = [
        pltpu.VMEM((2, GROUP * LANES, 3 * SPLIT), jnp.bfloat16),
        pltpu.VMEM((2, 16, SPLIT), jnp.float32),
    ]

    def settings(count):
        return dict(
            compiler_params=pltpu.CompilerParams(vmem_limit_bytes=SPECTRUM_VMEM),
            cost_estimate=pl.CostEstimate(
                flops=count * GROUP * 6 * SPLIT * SPLIT * SPLIT * 2,
                bytes_accessed=count * GROUP * FRAME_LEN * 4,
                transcendentals=0,
            ),
        )

    early, tail, *copies = pl.pallas_call(
        functools.partial(early_kernel, places, per_member, frames),
        in_specs=[in_hbm] * (1 + len(constants)),
        out_specs=[in_hbm] + [in_vmem] * (1 + len(constants)),
        out_shape=[out_shape, tail_shape] + [jax.ShapeDtypeStruct(t.shape, t.dtype) for t in constants],
        scratch_shapes=[pltpu.VMEM(((groups * GROUP + 1) * HOP_ROWS, LANES), jnp.float32)]
        + scratch
        + [
            pltpu.VMEM((groups, *group_shape), jnp.float32),
            pltpu.SemaphoreType.DMA((8 + groups,)),
            pltpu.SemaphoreType.DMA((groups,)),
        ],
        **settings(groups),
    )(*[pltpu.with_memory_space_constraint(value, pltpu.HBM) for value in (samples, *constants)])
    return pl.pallas_call(
        functools.partial(late_kernel, places, per_member, frames),
        in_specs=[in_vmem] * (3 + len(constants)) + [in_hbm],
        out_specs=in_hbm,
        out_shape=out_shape,
        scratch_shapes=scratch + [pltpu.VMEM(last_shape, jnp.float32), pltpu.SemaphoreType.DMA],
        input_output_aliases={3 + len(constants): 0},
        **settings(1),
    )(tail, trailing, activity, *copies, early)


def lanes_of_activity(activity):
    high, low = split_values(activity)
    return jnp.concatenate([high, high, low, low], 1)


def ratio_of(spectrum_ref, start, activity_lanes, basis):
    frames = activity_lanes.shape[0]
    members = spectrum_ref.shape[0]
    groups = frames // (members * GROUP)
    stride = spectrum_ref.shape[1] // groups
    splits = [split_values(block) for block in basis]
    stacked = jnp.concatenate([jnp.concatenate([h, l, h, l], 0) for h, l in splits], 1)
    approx = dot(activity_lanes, stacked)
    values = jnp.concatenate(
        [
            jnp.stack(
                [
                    spectrum_ref[:, pl.ds(group * stride + (start + row) * GROUP, GROUP), :]
                    for group in range(groups)
                ],
                1,
            ).reshape(frames, LANES)
            for row in range(len(basis))
        ],
        1,
    )
    return values / approx, jnp.concatenate([jnp.concatenate([h, l], 0) for h, l in splits], 1)


def for_activity(ratio, basis):
    high, low = split_values(ratio)
    return dot_nt(high, basis) + dot_nt(low, basis)


def both_parts(values):
    half = values.shape[1] // 2
    return values + pltpu.roll(values, half, 1)


def row_sums(basis):
    return dot_nt(jnp.ones((16, basis.shape[1]), jnp.bfloat16), basis)


def row_steps(per_member):
    rows = math.gcd(per_member, 8)
    return [range(start, start + rows) for start in range(0, per_member, rows)]


def packed(values):
    rows, width = values.shape
    lane = lax.broadcasted_iota(jnp.int32, (rows // 2, width), 1)
    return jnp.where(lane < width // 2, values[: rows // 2], values[rows // 2 :])


def unpacked(values):
    half = values.shape[1] // 2
    return jnp.concatenate([values[:, :half], values[:, half:]], 0)


def gathered_activity(rows_ref, shape):
    subs, members, ranks, width = shape
    local = width // subs
    frames_in = width // LANES
    pieces = {}
    for member in range(members):
        for part in range(frames_in):
            start = part * ranks
            rows = [rows_ref[sub * members + member, start : start + ranks, :] for sub in range(subs)]
            block = jnp.transpose(jnp.concatenate(rows, 0))
            for place in range(LANES // local):
                pieces[part * (LANES // local) + place, member] = block[place * local : (place + 1) * local]
    return jnp.concatenate([pieces[sub, member] for sub in range(subs) for member in range(members)], 0)


def start_fetches(received_ref, spectrum_ref, sem_ref, per_member):
    count = spectrum_ref.shape[1]
    groups = count // (per_member * GROUP)
    copies = []
    for step, rows in enumerate(row_steps(per_member)):
        copies.append([])
        for group in range(groups):
            place = pl.ds((group * per_member + rows[0]) * GROUP, len(rows) * GROUP)
            copies[-1].append(
                pltpu.make_async_copy(
                    received_ref.at[:, place, :], spectrum_ref.at[:, place, :], sem_ref.at[step * groups + group]
                )
            )
            copies[-1][-1].start()
    return copies


def first_kernel(
    shape,
    side_ref,
    received_ref,
    basis_ref,
    mine_ref,
    other_ref,
    activity_ref,
    spectrum_ref,
    lanes_ref,
    total_ref,
    rows_ref,
    rows_sem_ref,
    sem_ref,
):
    steps = row_steps(basis_ref.shape[0])
    count = spectrum_ref.shape[1]
    rows_copy = pltpu.make_async_copy(
        received_ref.at[:, pl.ds(count, rows_ref.shape[1]), :], rows_ref, rows_sem_ref
    )
    rows_copy.start()
    copies = start_fetches(received_ref, spectrum_ref, sem_ref, basis_ref.shape[0])
    rows_copy.wait()
    activity = gathered_activity(rows_ref, shape)
    activity_ref[...] = activity
    lanes_ref[...] = lanes_of_activity(activity)
    sums = 0.0
    for step, rows in enumerate(steps):
        for copy in copies[step]:
            copy.wait()
        ratio, basis = ratio_of(spectrum_ref, rows[0], lanes_ref[...], [basis_ref[row] for row in rows])
        part = for_activity(ratio, basis)
        if step == 0:
            total_ref[...] = part
        else:
            total_ref[...] += part
        sums += row_sums(basis)
    total = both_parts(total_ref[...])
    half = total.shape[0] // 2
    quarter = half // 2
    early, late = packed(total[:half]), packed(total[half:])
    first = side_ref[0] == 0
    mine_ref[:quarter, :] = jnp.where(first, early, late)
    other_ref[:quarter, :] = jnp.where(first, late, early)
    sums = both_parts(sums)[:8]
    mine_ref[quarter:, :] = sums
    other_ref[quarter:, :] = sums


def by_owner(values, shape):
    subs, members, ranks, width = shape
    local = width // subs
    blocks = []
    for member in range(members):
        rows = [
            values[(sub * members + member) * local : (sub * members + member + 1) * local]
            for sub in range(subs)
        ]
        blocks.append(jnp.transpose(jnp.concatenate(rows, 0)).reshape(subs, ranks, width))
    return blocks


def second_kernel(
    side_ref, spectrum_ref, basis_ref, activity_ref, mine_ref, other_ref, middle_ref, out_ref, lanes_ref, turned_ref
):
    rank = activity_ref.shape[1]
    quarter = activity_ref.shape[0] // 4
    first = side_ref[0] == 0
    mine = mine_ref[:quarter, :] / mine_ref[quarter : quarter + 1, :]
    other = other_ref[:quarter, :] / other_ref[quarter : quarter + 1, :]
    early, late = jnp.where(first, mine, other), jnp.where(first, other, mine)
    middle = activity_ref[...] * jnp.concatenate([unpacked(early), unpacked(late)], 0)
    middle_ref[...] = middle
    lanes_ref[...] = lanes_of_activity(middle)
    turned = jnp.transpose(middle)
    high, low = split_values(turned)
    turned_ref[...] = jnp.concatenate([high, low], 0)
    totals = jnp.sum(middle, axis=0, keepdims=True)
    totals = jnp.broadcast_to(jnp.concatenate([totals] * (LANES // rank), 1), (8, LANES))
    out_ref[out_ref.shape[0] - 8 :, :] = totals
    for rows in row_steps(basis_ref.shape[0]):
        ratio, _ = ratio_of(spectrum_ref, rows[0], lanes_ref[...], [basis_ref[row] for row in rows])
        high, low = split_values(ratio)
        total = dot(turned_ref[...], high) + dot(turned_ref[...], low)
        total = total[:rank] + total[rank:]
        for place, row in enumerate(rows):
            out_ref[row * rank : (row + 1) * rank, :] = total[:, place * LANES : (place + 1) * LANES]


def third_kernel(received_ref, basis_ref, middle_ref, *rest):
    new_ref, out_ref, lanes_ref, total_ref, spectrum_ref, sem_ref = rest[-6:]
    numerators = rest[:-6]
    rank = middle_ref.shape[1]
    per_member = basis_ref.shape[0]
    copies = start_fetches(received_ref, spectrum_ref, sem_ref, per_member)
    lanes_ref[...] = lanes_of_activity(middle_ref[...])
    totals = sum(ref[per_member * rank :, :] for ref in numerators)
    totals = jnp.transpose(jnp.concatenate([totals] * (LANES // 8), 0))[:rank]
    scale = 1.0 / totals
    sums = 0.0
    for step, rows in enumerate(row_steps(per_member)):
        blocks = [
            basis_ref[row] * (sum(ref[row * rank : (row + 1) * rank, :] for ref in numerators) * scale)
            for row in rows
        ]
        for row, block in zip(rows, blocks):
            new_ref[row] = block
        for copy in copies[step]:
            copy.wait()
        ratio, basis = ratio_of(spectrum_ref, rows[0], lanes_ref[...], blocks)
        part = for_activity(ratio, basis)
        if step == 0:
            total_ref[...] = part
        else:
            total_ref[...] += part
        sums += row_sums(basis)
    total = both_parts(total_ref[...])[:, :rank]
    subs, members, _, ranks, width = out_ref.shape
    sums = jnp.transpose(jnp.broadcast_to(both_parts(sums)[:1], (LANES, 2 * rank)))[:rank]
    sums = jnp.concatenate([sums] * (width // LANES), 1).reshape(subs, ranks, width)
    for member, block in enumerate(by_owner(total, (subs, members, ranks, width))):
        out_ref[:, member, 0] = block
        out_ref[:, member, 1] = sums


def update_call(kernel, spectrum, out_shapes, scratch, operands, scalars=(), place=pltpu.VMEM):
    in_vmem = pl.BlockSpec(memory_space=pltpu.VMEM)
    if place == pltpu.HBM:
        spectrum = pltpu.with_memory_space_constraint(spectrum, place)
    rank = operands[0].shape[1]
    return pl.pallas_call(
        kernel,
        in_specs=[pl.BlockSpec(memory_space=pltpu.SMEM) for _ in scalars]
        + [pl.BlockSpec(memory_space=place)]
        + [in_vmem for _ in operands],
        out_specs=[in_vmem for _ in out_shapes],
        out_shape=[jax.ShapeDtypeStruct(shape, jnp.float32) for shape in out_shapes],
        scratch_shapes=scratch,
        compiler_params=pltpu.CompilerParams(vmem_limit_bytes=UPDATE_VMEM),
        cost_estimate=pl.CostEstimate(
            flops=spectrum.size * rank * 16, bytes_accessed=spectrum.size * 4, transcendentals=0
        ),
    )(*scalars, spectrum, *operands)


def turned_lanes(values):
    return jnp.roll(jnp.flip(values, -1), 1, -1)


def swap_by(value, axis, mask):
    count = lax.axis_size(axis)
    return lax.ppermute(value, axis, [(i, i ^ mask) for i in range(count)])


def sum_over(value, axis, mask):
    count = lax.axis_size(axis)
    while mask < count:
        masks = [mask] if 2 * mask >= count else [mask, 2 * mask, 3 * mask]
        value = sum([swap_by(value, axis, m) for m in masks], value)
        mask *= 2 if len(masks) == 1 else 4
    return value


def on_device(signal, templates, activations):
    subs, groups, members = (lax.axis_size(axis) for axis in ("freq", "group", "member"))
    blocks = groups * members
    rank, bins_here = templates.shape
    ranks_here, width = activations.shape
    units_here = bins_here // LANES
    exchange = ("freq", "member")
    partners = subs * members
    per_member = units_here * groups
    me_sub, me_group, me_member = (lax.axis_index(axis) for axis in ("freq", "group", "member"))

    kept = units_of_member(units_here, range(groups))
    unit_order = tuple(
        units_here * (sub * blocks + group * members + member) + r
        for sub in range(subs)
        for member in range(members)
        for group, r in kept
    )

    samples = signal.reshape(-1, LANES)
    route = [
        (((sub + 1) % subs) * blocks + block + (sub + 1) // subs, sub * blocks + block)
        for sub in range(subs)
        for block in range(blocks)
        if block + (sub + 1) // subs < blocks
    ]
    trailing = lax.ppermute(samples[:HOP_ROWS], ("freq", "group", "member"), route)
    other = [swap_by(templates, "group", 1)] if groups == 2 else []
    own_rows = activations.reshape(ranks_here, width // LANES, LANES).transpose(1, 0, 2)
    own_rows = own_rows.reshape(ranks_here * width // LANES, LANES)
    spectrum = spectrum_blocks(samples, trailing, own_rows, unit_order, partners)
    spectrum, other = lax.optimization_barrier((spectrum, other))
    spectrum = lax.all_to_all(spectrum, exchange, 0, 0, tiled=True)
    local = width // subs
    frames = partners * local

    own = templates.reshape(rank, units_here, LANES).transpose(1, 0, 2)
    if other:
        remote = other[0].reshape(rank, units_here, LANES).transpose(1, 0, 2)
        by_group = jnp.where(me_group == 0, jnp.stack([own, remote]), jnp.stack([remote, own]))
    else:
        by_group = own[None]
    unit_index = units_here * (
        me_sub * blocks + jnp.arange(groups)[:, None] * members + me_member
    ) + jnp.arange(units_here)[None, :]
    is_turned = (unit_index % 2 == 1)[:, :, None, None]
    by_group = jnp.where(is_turned, turned_lanes(by_group), by_group)
    basis = jnp.concatenate([by_group[group, r][None] for group, r in kept], 0)

    lanes_scratch = pltpu.VMEM((frames, 4 * rank), jnp.bfloat16)
    total_scratch = pltpu.VMEM((frames, 2 * rank), jnp.float32)
    half_shape = (frames // 4 + 8, 2 * rank)
    side = (me_sub % 2).astype(jnp.int32).reshape(1)
    extra = ranks_here * width // LANES
    spectrum_rows = spectrum.shape[1] - extra
    row_groups = spectrum_rows // (per_member * GROUP)
    fetch_sems = pltpu.SemaphoreType.DMA((len(row_steps(per_member)) * row_groups,))
    received = spectrum
    mine, other, activity, spectrum = update_call(
        functools.partial(first_kernel, (subs, members, ranks_here, width)),
        received,
        [half_shape, half_shape, (frames, rank), (partners, spectrum_rows, LANES)],
        [
            lanes_scratch,
            total_scratch,
            pltpu.VMEM((partners, extra, LANES), jnp.float32),
            pltpu.SemaphoreType.DMA,
            fetch_sems,
        ],
        (basis,),
        (side,),
        pltpu.HBM,
    )
    mine = mine + swap_by(other, "freq", 1)
    mine = sum_over(mine, "freq", 2)
    mine = sum_over(mine, "member", 1)
    other = swap_by(mine, "freq", 1)

    middle, numerator = update_call(
        second_kernel,
        spectrum,
        [(frames, rank), (per_member * rank + 8, LANES)],
        [lanes_scratch, pltpu.VMEM((2 * rank, frames), jnp.bfloat16)],
        (basis, activity, mine, other),
        (side,),
    )
    numerators = [numerator]
    if groups == 2:
        numerators.append(swap_by(numerator, "group", 1))
    new_basis, payload = update_call(
        third_kernel,
        received,
        [(per_member, rank, LANES), (subs, members, 2, ranks_here, width)],
        [
            lanes_scratch,
            total_scratch,
            pltpu.VMEM((partners, spectrum_rows, LANES), jnp.float32),
            fetch_sems,
        ],
        (basis, middle, *numerators),
        (),
        pltpu.HBM,
    )
    parts = lax.all_to_all(
        payload.reshape(partners, 2, ranks_here, width), exchange, 0, 0, tiled=True
    )
    summed = jnp.sum(parts, axis=0)
    mine = lax.dynamic_slice(
        middle.reshape(subs, members, local, rank),
        (0, me_member, 0, me_sub * ranks_here),
        (subs, 1, local, ranks_here),
    )
    mine = mine.reshape(width, ranks_here).T
    final_activations = mine * (summed[0] / summed[1])

    back = jnp.stack(
        [
            jnp.stack([new_basis[kept.index((group, r))] for r in range(units_here)])
            for group in range(groups)
        ]
    )
    back = lax.dynamic_index_in_dim(back, me_group, 0, keepdims=False)
    turned_here = lax.dynamic_index_in_dim(is_turned, me_group, 0, keepdims=False)
    back = jnp.where(turned_here, turned_lanes(back), back)
    final_templates = back.transpose(1, 0, 2).reshape(rank, bins_here)
    return (final_activations, final_templates)


def solution(mesh):
    subs, blocks = mesh.devices.shape
    groups = 2 if blocks % 2 == 0 else 1
    grid = Mesh(
        mesh.devices.reshape(subs, groups, blocks // groups), ("freq", "group", "member")
    )
    frames = ("group", "member")
    return jax.shard_map(
        on_device,
        mesh=grid,
        in_specs=(P(frames, "freq", None), P(None, ("freq", *frames)), P("freq", frames)),
        out_specs=(P("freq", frames), P(None, ("freq", *frames))),
        check_vma=False,
    )
```

```python
import functools
import math

import jax
import jax.numpy as jnp
import ml_dtypes
import numpy as np
from jax import lax
from jax.experimental import pallas as pl
from jax.experimental.pallas import tpu as pltpu
from jax.sharding import Mesh
from jax.sharding import PartitionSpec as P

FRAME_LEN = 65536
SPLIT = 256
LANES = 128
GROUP = 8
HOP_ROWS = FRAME_LEN // 2 // LANES
SPECTRUM_VMEM = 24 * 1024 * 1024
UPDATE_VMEM = 24 * 1024 * 1024
NT = (((1,), (1,)), ((), ()))


def high_low(values):
    high = values.astype(np.float32).astype(ml_dtypes.bfloat16)
    low = (values - high.astype(np.float64)).astype(ml_dtypes.bfloat16)
    return high, low


def both_parts_below(values):
    high, low = high_low(values)
    return np.concatenate([high, low], 0)


def units_of_member(units_here, member_blocks):
    order = list(range(units_here))
    if units_here % 8 == 0:
        order.sort(key=lambda r: (row_of_unit(r) % 2, r))
    kept = [(block, r) for block in member_blocks for r in order]
    if units_here % 8 == 0:
        kept.sort(key=lambda pair: row_of_unit(pair[1]) % 2)
    return kept


def row_of_unit(unit):
    return unit // 2 if unit % 2 == 0 else SPLIT - 1 - unit // 2


@functools.lru_cache(maxsize=None)
def tables(unit_order):
    half = SPLIT // 2
    index = np.arange(SPLIT, dtype=np.float64)
    slot = np.arange(half, dtype=np.float64)
    angle = 2.0 * np.pi / SPLIT * np.mod(np.outer(np.arange(half + 1), np.arange(SPLIT)), SPLIT)
    cosine, sine = np.cos(angle), np.sin(angle)
    first = np.concatenate([cosine[:half], cosine[half:], -sine[1:half]], 0)
    turn = 2.0 * np.pi / (SPLIT * SPLIT) * np.outer(slot, index)
    twiddle_cos, twiddle_sin = np.cos(turn), np.sin(turn)
    masked_cos = twiddle_cos.copy()
    masked_cos[0] = 0.0
    twiddle = np.stack([twiddle_cos, twiddle_sin, masked_cos]).astype(np.float32)
    middle = 2.0 * np.pi / (SPLIT * SPLIT) * half * index
    odd = 2.0 * np.pi / SPLIT * slot
    rows = np.zeros((8, SPLIT), np.float32)
    rows[0], rows[1] = np.cos(middle), -np.sin(middle)
    rows[2, :half], rows[3, :half] = np.cos(odd), np.sin(odd)
    seconds, mirrored, places = [], [], []
    for parity in range(2):
        here = [place for place, unit in enumerate(unit_order) if row_of_unit(unit) % 2 == parity]
        turns = np.array([row_of_unit(unit_order[place]) // 2 for place in here])
        phase = 2.0 * np.pi / half * np.mod(np.outer(turns, np.arange(half)), half)
        c, s = np.cos(phase), np.sin(phase)
        seconds.append(
            both_parts_below(np.concatenate([np.concatenate([c, s], 1), np.concatenate([-s, c], 1)], 0))
        )
        flags = np.zeros((half, LANES), np.float32)
        flags[:, 0] = [unit_order[place] % 2 for place in here]
        mirrored.append(flags)
        places.append(tuple(here))
    position = np.arange(FRAME_LEN, dtype=np.float64)
    window = (0.5 - 0.5 * np.cos(2.0 * np.pi / FRAME_LEN * position)).astype(np.float32)
    window = window.reshape(SPLIT, 2, LANES).transpose(1, 0, 2)
    return (
        np.ascontiguousarray(window),
        both_parts_below(first),
        twiddle,
        rows,
        np.stack(seconds),
        np.stack(mirrored),
        tuple(places),
    )


def split_values(values):
    high = values.astype(jnp.bfloat16)
    low = (values - high.astype(jnp.float32)).astype(jnp.bfloat16)
    return high, low


def dot(left, right):
    return jnp.dot(left, right, preferred_element_type=jnp.float32)


def dot_nt(left, right):
    return lax.dot_general(left, right, NT, preferred_element_type=jnp.float32)


def transform_group(hop_rows, places, per_member, table_refs, out_ref, parts_ref, middle_ref, written=None):
    window_ref, first_ref, twiddle_ref, rows_ref, second_ref, mirrored_ref = table_refs
    half = SPLIT // 2
    middle_ref[...] = jnp.zeros_like(middle_ref)

    def even_odd(real, imag):
        even = jnp.concatenate([real[:, :half] + real[:, half:], imag[:, :half] + imag[:, half:]], 1)
        real = real[:, :half] - real[:, half:]
        imag = imag[:, :half] - imag[:, half:]
        c, s = rows_ref[2:3, :half], rows_ref[3:4, :half]
        odd = jnp.concatenate([real * c + imag * s, imag * c - real * s], 1)
        return even, odd

    def in_parts(values):
        return jnp.concatenate(split_values(values), 1)

    def second(parity, parts):
        both = dot_nt(second_ref[parity], parts[:, :SPLIT])
        return both[:SPLIT] + (both[SPLIT:] + dot_nt(second_ref[parity, :SPLIT, :], parts[:, SPLIT:]))

    for g in range(GROUP):
        columns = [
            jnp.concatenate([hop_rows(g, side), hop_rows(g + 1, side)], 0) * window_ref[side]
            for side in range(2)
        ]
        high, low = split_values(jnp.concatenate(columns, 1))
        section = dot(first_ref[...], high)
        section = section[:SPLIT] + (section[SPLIT:] + dot(first_ref[:SPLIT, :], low))
        a, b = section[:half], section[half:]
        real = a * twiddle_ref[0] + b * twiddle_ref[1]
        imag = b * twiddle_ref[2] - a * twiddle_ref[1]
        for parity, values in enumerate(even_odd(real, imag)):
            parts_ref[parity, g * half : (g + 1) * half, :] = in_parts(values)
        nyquist = section[half : half + 1]
        for parity, values in enumerate(even_odd(nyquist * rows_ref[0:1], nyquist * rows_ref[1:2])):
            middle_ref[parity, g : g + 1, :] = values

    def magnitude(values):
        real, imag = values[:half], values[half:]
        return jnp.sqrt(real * real + imag * imag) * (8.0 / SPLIT)

    for parity in range(2):
        middle = magnitude(second(parity, in_parts(middle_ref[parity])))
        is_middle = mirrored_ref[parity] > 0.0
        for pair in range(GROUP // 2):
            values = magnitude(second(parity, parts_ref[parity, pair * SPLIT : (pair + 1) * SPLIT, :]))
            for lane in range(2):
                g = 2 * pair + lane
                block = jnp.where(
                    is_middle, middle[:, g : g + 1], values[:, lane * LANES : (lane + 1) * LANES]
                )
                start = 0
                while start < half:
                    stop = start + 1
                    place = places[parity][start]
                    while (
                        stop < half
                        and stop - start < 8
                        and places[parity][stop] == place + stop - start
                        and places[parity][stop] // per_member == place // per_member
                    ):
                        stop += 1
                    member, row = divmod(place, per_member)
                    out_ref[member, pl.ds(row * GROUP + g, stop - start, stride=GROUP), :] = block[start:stop]
                    start = stop
        if written is not None:
            written(parity)


def early_kernel(
    places, per_member, frames, samples_ref, *rest
):
    table_refs, (out_ref, tail_ref, group_ref) = rest[:6], rest[6:9]
    copies_ref, (hops_ref, parts_ref, middle_ref, sem_ref, out_sem_ref) = rest[9:15], rest[15:]
    groups = frames // GROUP - 1
    group_rows = GROUP * HOP_ROWS
    half = SPLIT // 2

    def fetch(first, count, slot):
        return pltpu.make_async_copy(
            samples_ref.at[pl.ds(first, count), :], hops_ref.at[pl.ds(first, count), :], sem_ref.at[slot]
        )

    tables_in = [
        pltpu.make_async_copy(table_refs[i], copies_ref[i], sem_ref.at[i]) for i in range(len(table_refs))
    ]
    lead = fetch(0, HOP_ROWS, 6)
    tail = pltpu.make_async_copy(
        samples_ref.at[pl.ds(groups * group_rows, group_rows), :], tail_ref, sem_ref.at[7]
    )
    hops = [fetch(HOP_ROWS + i * group_rows, group_rows, 8 + i) for i in range(groups)]
    for copy in [tables_in[1], lead, hops[0], *tables_in[:1], *tables_in[2:], *hops[1:], tail]:
        copy.start()
    lead.wait()
    for copy in tables_in:
        copy.wait()

    def body(i, carry):
        first = pl.multiple_of(i * group_rows, group_rows)
        pltpu.make_async_copy(
            samples_ref.at[pl.ds(HOP_ROWS + first, group_rows), :],
            hops_ref.at[pl.ds(HOP_ROWS + first, group_rows), :],
            sem_ref.at[8 + i],
        ).wait()

        transform_group(
            lambda hop, side: hops_ref[pl.ds(first + hop * HOP_ROWS + side, half, stride=2), :],
            places,
            per_member,
            copies_ref,
            group_ref.at[i],
            parts_ref,
            middle_ref,
        )

        @pl.when(i < groups - 1)
        def _():
            send(i).start()

        return carry

    def send(i):
        count = group_ref.shape[2]
        return pltpu.make_async_copy(
            group_ref.at[i],
            out_ref.at[:, pl.ds(pl.multiple_of(i * count, count), count), :],
            out_sem_ref.at[i],
        )

    lax.fori_loop(0, groups, body, 0)
    tail.wait()
    for i in range(groups - 1):
        send(i).wait()


def late_kernel(places, per_member, frames, done_ref, tail_ref, trailing_ref, activity_ref, *rest):
    table_refs, (_, out_ref, parts_ref, middle_ref, group_ref, sem_ref) = rest[:6], rest[6:]
    count = per_member * GROUP
    before = frames // GROUP - 1
    pass_on = pltpu.make_async_copy(
        done_ref.at[before - 1], out_ref.at[:, pl.ds((before - 1) * count, count), :], sem_ref.at[0]
    )
    pass_on.start()

    def hop_rows(hop, side):
        if hop == GROUP:
            return trailing_ref[pl.ds(side, SPLIT // 2, stride=2), :]
        return tail_ref[pl.ds(hop * HOP_ROWS + side, SPLIT // 2, stride=2), :]

    for member in range(out_ref.shape[0]):
        group_ref[member, count:, :] = activity_ref[...]
    bounds = [0, group_ref.shape[1]]
    if all(place % per_member < per_member // 2 for place in places[0]):
        bounds.insert(1, count // 2)
    sends = []

    def written(parity):
        if parity == 1 or len(bounds) == 3:
            first, last = bounds[len(sends)], bounds[len(sends) + 1]
            sends.append(
                pltpu.make_async_copy(
                    group_ref.at[:, pl.ds(first, last - first), :],
                    out_ref.at[:, pl.ds(before * count + first, last - first), :],
                    sem_ref.at[1 + len(sends)],
                )
            )
            sends[-1].start()

    transform_group(
        hop_rows,
        places,
        per_member,
        table_refs,
        group_ref,
        parts_ref,
        middle_ref,
        written,
    )
    pass_on.wait()
    for send in sends:
        send.wait()


def spectrum_blocks(samples, trailing, activity, unit_order, members):
    *values, places = tables(unit_order)
    per_member = SPLIT // members
    frames = samples.shape[0] // HOP_ROWS
    groups = frames // GROUP - 1
    constants = [jnp.asarray(t) for t in values]
    group_shape = (members, per_member * GROUP, LANES)
    last_shape = (members, per_member * GROUP + activity.shape[0], LANES)
    out_shape = pltpu.HBM((members, per_member * frames + activity.shape[0], LANES), jnp.float32)
    tail_shape = jax.ShapeDtypeStruct((GROUP * HOP_ROWS, LANES), jnp.float32)
    in_vmem = pl.BlockSpec(memory_space=pltpu.VMEM)
    in_hbm = pl.BlockSpec(memory_space=pltpu.HBM)
    scratch = [
        pltpu.VMEM((2, GROUP * LANES, 2 * SPLIT), jnp.bfloat16),
        pltpu.VMEM((2, 16, SPLIT), jnp.float32),
    ]

    def settings(count):
        return dict(
            compiler_params=pltpu.CompilerParams(vmem_limit_bytes=SPECTRUM_VMEM),
            cost_estimate=pl.CostEstimate(
                flops=count * GROUP * 6 * SPLIT * SPLIT * SPLIT * 2,
                bytes_accessed=count * GROUP * FRAME_LEN * 4,
                transcendentals=0,
            ),
        )

    early, tail, done, *copies = pl.pallas_call(
        functools.partial(early_kernel, places, per_member, frames),
        in_specs=[in_hbm] * (1 + len(constants)),
        out_specs=[in_hbm] + [in_vmem] * (2 + len(constants)),
        out_shape=[out_shape, tail_shape, jax.ShapeDtypeStruct((groups, *group_shape), jnp.float32)]
        + [jax.ShapeDtypeStruct(t.shape, t.dtype) for t in constants],
        scratch_shapes=[pltpu.VMEM(((groups * GROUP + 1) * HOP_ROWS, LANES), jnp.float32)]
        + scratch
        + [
            pltpu.SemaphoreType.DMA((8 + groups,)),
            pltpu.SemaphoreType.DMA((groups,)),
        ],
        **settings(groups),
    )(*[pltpu.with_memory_space_constraint(value, pltpu.HBM) for value in (samples, *constants)])
    return pl.pallas_call(
        functools.partial(late_kernel, places, per_member, frames),
        in_specs=[in_vmem] * (4 + len(constants)) + [in_hbm],
        out_specs=in_hbm,
        out_shape=out_shape,
        scratch_shapes=scratch + [pltpu.VMEM(last_shape, jnp.float32), pltpu.SemaphoreType.DMA((3,))],
        input_output_aliases={4 + len(constants): 0},
        **settings(1),
    )(done, tail, trailing, activity, *copies, early)


def lanes_of_activity(activity):
    high, low = split_values(activity)
    return jnp.concatenate([high, high, low, low], 1)


def ratio_of(spectrum_ref, start, activity_lanes, basis):
    frames = activity_lanes.shape[0]
    members = spectrum_ref.shape[0]
    groups = frames // (members * GROUP)
    stride = spectrum_ref.shape[1] // groups
    splits = [split_values(block) for block in basis]
    stacked = jnp.concatenate([jnp.concatenate([h, l, h, l], 0) for h, l in splits], 1)
    approx = dot(activity_lanes, stacked)
    values = jnp.concatenate(
        [
            jnp.stack(
                [
                    spectrum_ref[:, pl.ds(group * stride + (start + row) * GROUP, GROUP), :]
                    for group in range(groups)
                ],
                1,
            ).reshape(frames, LANES)
            for row in range(len(basis))
        ],
        1,
    )
    return values / approx, jnp.concatenate([jnp.concatenate([h, l], 0) for h, l in splits], 1)


def for_activity(ratio, basis):
    high, low = split_values(ratio)
    return dot_nt(high, basis) + dot_nt(low, basis)


def both_parts(values):
    half = values.shape[1] // 2
    return values + pltpu.roll(values, half, 1)


def row_sums(basis):
    return dot_nt(jnp.ones((16, basis.shape[1]), jnp.bfloat16), basis)


def row_steps(per_member, most=8):
    rows = math.gcd(per_member, most)
    return [range(start, start + rows) for start in range(0, per_member, rows)]


def packed(values):
    rows, width = values.shape
    lane = lax.broadcasted_iota(jnp.int32, (rows // 2, width), 1)
    return jnp.where(lane < width // 2, values[: rows // 2], values[rows // 2 :])


def unpacked(values):
    half = values.shape[1] // 2
    return jnp.concatenate([values[:, :half], values[:, half:]], 0)


def gathered_activity(rows_ref, shape):
    subs, members, ranks, width = shape
    local = width // subs
    frames_in = width // LANES
    pieces = {}
    for member in range(members):
        for part in range(frames_in):
            start = part * ranks
            rows = [rows_ref[sub * members + member, start : start + ranks, :] for sub in range(subs)]
            block = jnp.transpose(jnp.concatenate(rows, 0))
            for place in range(LANES // local):
                pieces[part * (LANES // local) + place, member] = block[place * local : (place + 1) * local]
    return jnp.concatenate([pieces[sub, member] for sub in range(subs) for member in range(members)], 0)


def start_fetches(received_ref, spectrum_ref, sem_ref, per_member, steps):
    count = spectrum_ref.shape[1]
    groups = count // (per_member * GROUP)
    copies = []
    for step, rows in enumerate(steps):
        copies.append([])
        for group in range(groups):
            place = pl.ds((group * per_member + rows[0]) * GROUP, len(rows) * GROUP)
            copies[-1].append(
                pltpu.make_async_copy(
                    received_ref.at[:, place, :], spectrum_ref.at[:, place, :], sem_ref.at[step * groups + group]
                )
            )
            copies[-1][-1].start()
    return copies


def first_kernel(
    shape,
    side_ref,
    received_ref,
    basis_ref,
    mine_ref,
    other_ref,
    activity_ref,
    spectrum_ref,
    lanes_ref,
    total_ref,
    rows_ref,
    rows_sem_ref,
    sem_ref,
):
    steps = row_steps(basis_ref.shape[0], 16)
    count = spectrum_ref.shape[1]
    rows_copy = pltpu.make_async_copy(
        received_ref.at[:, pl.ds(count, rows_ref.shape[1]), :], rows_ref, rows_sem_ref
    )
    rows_copy.start()
    copies = start_fetches(received_ref, spectrum_ref, sem_ref, basis_ref.shape[0], steps)
    rows_copy.wait()
    activity = gathered_activity(rows_ref, shape)
    activity_ref[...] = activity
    lanes_ref[...] = lanes_of_activity(activity)
    sums = 0.0
    for step, rows in enumerate(steps):
        for copy in copies[step]:
            copy.wait()
        ratio, basis = ratio_of(spectrum_ref, rows[0], lanes_ref[...], [basis_ref[row] for row in rows])
        part = for_activity(ratio, basis)
        if step == 0:
            total_ref[...] = part
        else:
            total_ref[...] += part
        sums += row_sums(basis)
    total = both_parts(total_ref[...])
    half = total.shape[0] // 2
    quarter = half // 2
    early, late = packed(total[:half]), packed(total[half:])
    first = side_ref[0] == 0
    mine_ref[:quarter, :] = jnp.where(first, early, late)
    other_ref[:quarter, :] = jnp.where(first, late, early)
    sums = both_parts(sums)[:8]
    mine_ref[quarter:, :] = sums
    other_ref[quarter:, :] = sums


def by_owner(values, shape):
    subs, members, ranks, width = shape
    local = width // subs
    blocks = []
    for member in range(members):
        rows = [
            values[(sub * members + member) * local : (sub * members + member + 1) * local]
            for sub in range(subs)
        ]
        blocks.append(jnp.transpose(jnp.concatenate(rows, 0)).reshape(subs, ranks, width))
    return blocks


def second_kernel(
    side_ref, spectrum_ref, basis_ref, activity_ref, mine_ref, other_ref, middle_ref, out_ref, lanes_ref, turned_ref
):
    rank = activity_ref.shape[1]
    quarter = activity_ref.shape[0] // 4
    first = side_ref[0] == 0
    mine = mine_ref[:quarter, :] / mine_ref[quarter : quarter + 1, :]
    other = other_ref[:quarter, :] / other_ref[quarter : quarter + 1, :]
    early, late = jnp.where(first, mine, other), jnp.where(first, other, mine)
    middle = activity_ref[...] * jnp.concatenate([unpacked(early), unpacked(late)], 0)
    middle_ref[...] = middle
    lanes_ref[...] = lanes_of_activity(middle)
    turned = jnp.transpose(middle)
    high, low = split_values(turned)
    turned_ref[...] = jnp.concatenate([high, low], 0)
    totals = jnp.sum(middle, axis=0, keepdims=True)
    totals = jnp.broadcast_to(jnp.concatenate([totals] * (LANES // rank), 1), (8, LANES))
    out_ref[out_ref.shape[0] - 8 :, :] = totals
    for rows in row_steps(basis_ref.shape[0]):
        ratio, _ = ratio_of(spectrum_ref, rows[0], lanes_ref[...], [basis_ref[row] for row in rows])
        high, low = split_values(ratio)
        total = dot(turned_ref[...], high) + dot(turned_ref[...], low)
        total = total[:rank] + total[rank:]
        for place, row in enumerate(rows):
            out_ref[row * rank : (row + 1) * rank, :] = total[:, place * LANES : (place + 1) * LANES]


def third_kernel(received_ref, basis_ref, middle_ref, *rest):
    new_ref, out_ref, lanes_ref, total_ref, spectrum_ref, sem_ref = rest[-6:]
    numerators = rest[:-6]
    rank = middle_ref.shape[1]
    per_member = basis_ref.shape[0]
    steps = row_steps(per_member)
    copies = start_fetches(received_ref, spectrum_ref, sem_ref, per_member, steps)
    lanes_ref[...] = lanes_of_activity(middle_ref[...])
    totals = sum(ref[per_member * rank :, :] for ref in numerators)
    totals = jnp.transpose(jnp.concatenate([totals] * (LANES // 8), 0))[:rank]
    scale = 1.0 / totals
    sums = 0.0
    for step, rows in enumerate(steps):
        blocks = [
            basis_ref[row] * (sum(ref[row * rank : (row + 1) * rank, :] for ref in numerators) * scale)
            for row in rows
        ]
        for row, block in zip(rows, blocks):
            new_ref[row] = block
        for copy in copies[step]:
            copy.wait()
        ratio, basis = ratio_of(spectrum_ref, rows[0], lanes_ref[...], blocks)
        part = for_activity(ratio, basis)
        if step == 0:
            total_ref[...] = part
        else:
            total_ref[...] += part
        sums += row_sums(basis)
    total = both_parts(total_ref[...])[:, :rank]
    subs, members, _, ranks, width = out_ref.shape
    sums = jnp.transpose(jnp.broadcast_to(both_parts(sums)[:1], (LANES, 2 * rank)))[:rank]
    sums = jnp.concatenate([sums] * (width // LANES), 1).reshape(subs, ranks, width)
    for member, block in enumerate(by_owner(total, (subs, members, ranks, width))):
        out_ref[:, member, 0] = block
        out_ref[:, member, 1] = sums


def update_call(kernel, spectrum, out_shapes, scratch, operands, scalars=(), place=pltpu.VMEM):
    in_vmem = pl.BlockSpec(memory_space=pltpu.VMEM)
    if place == pltpu.HBM:
        spectrum = pltpu.with_memory_space_constraint(spectrum, place)
    rank = operands[0].shape[1]
    return pl.pallas_call(
        kernel,
        in_specs=[pl.BlockSpec(memory_space=pltpu.SMEM) for _ in scalars]
        + [pl.BlockSpec(memory_space=place)]
        + [in_vmem for _ in operands],
        out_specs=[in_vmem for _ in out_shapes],
        out_shape=[jax.ShapeDtypeStruct(shape, jnp.float32) for shape in out_shapes],
        scratch_shapes=scratch,
        compiler_params=pltpu.CompilerParams(vmem_limit_bytes=UPDATE_VMEM),
        cost_estimate=pl.CostEstimate(
            flops=spectrum.size * rank * 16, bytes_accessed=spectrum.size * 4, transcendentals=0
        ),
    )(*scalars, spectrum, *operands)


def turned_lanes(values):
    return jnp.roll(jnp.flip(values, -1), 1, -1)


def swap_by(value, axis, mask):
    count = lax.axis_size(axis)
    return lax.ppermute(value, axis, [(i, i ^ mask) for i in range(count)])


def sum_over(value, axis, mask):
    count = lax.axis_size(axis)
    while mask < count:
        masks = [mask] if 2 * mask >= count else [mask, 2 * mask, 3 * mask]
        value = sum([swap_by(value, axis, m) for m in masks], value)
        mask *= 2 if len(masks) == 1 else 4
    return value


def on_device(signal, templates, activations):
    subs, groups, members = (lax.axis_size(axis) for axis in ("freq", "group", "member"))
    blocks = groups * members
    rank, bins_here = templates.shape
    ranks_here, width = activations.shape
    units_here = bins_here // LANES
    exchange = ("freq", "member")
    partners = subs * members
    per_member = units_here * groups
    me_sub, me_group, me_member = (lax.axis_index(axis) for axis in ("freq", "group", "member"))

    kept = units_of_member(units_here, range(groups))
    unit_order = tuple(
        units_here * (sub * blocks + group * members + member) + r
        for sub in range(subs)
        for member in range(members)
        for group, r in kept
    )

    samples = signal.reshape(-1, LANES)
    route = [
        (((sub + 1) % subs) * blocks + block + (sub + 1) // subs, sub * blocks + block)
        for sub in range(subs)
        for block in range(blocks)
        if block + (sub + 1) // subs < blocks
    ]
    trailing = lax.ppermute(samples[:HOP_ROWS], ("freq", "group", "member"), route)
    other = [swap_by(templates, "group", 1)] if groups == 2 else []
    own_rows = activations.reshape(ranks_here, width // LANES, LANES).transpose(1, 0, 2)
    own_rows = own_rows.reshape(ranks_here * width // LANES, LANES)
    spectrum = spectrum_blocks(samples, trailing, own_rows, unit_order, partners)
    spectrum, other = lax.optimization_barrier((spectrum, other))
    spectrum = lax.all_to_all(spectrum, exchange, 0, 0, tiled=True)
    local = width // subs
    frames = partners * local

    own = templates.reshape(rank, units_here, LANES).transpose(1, 0, 2)
    if other:
        remote = other[0].reshape(rank, units_here, LANES).transpose(1, 0, 2)
        by_group = jnp.where(me_group == 0, jnp.stack([own, remote]), jnp.stack([remote, own]))
    else:
        by_group = own[None]
    unit_index = units_here * (
        me_sub * blocks + jnp.arange(groups)[:, None] * members + me_member
    ) + jnp.arange(units_here)[None, :]
    is_turned = (unit_index % 2 == 1)[:, :, None, None]
    by_group = jnp.where(is_turned, turned_lanes(by_group), by_group)
    basis = jnp.concatenate([by_group[group, r][None] for group, r in kept], 0)

    lanes_scratch = pltpu.VMEM((frames, 4 * rank), jnp.bfloat16)
    total_scratch = pltpu.VMEM((frames, 2 * rank), jnp.float32)
    half_shape = (frames // 4 + 8, 2 * rank)
    side = (me_sub % 2).astype(jnp.int32).reshape(1)
    extra = ranks_here * width // LANES
    spectrum_rows = spectrum.shape[1] - extra
    row_groups = spectrum_rows // (per_member * GROUP)
    fetch_sems = pltpu.SemaphoreType.DMA((len(row_steps(per_member)) * row_groups,))
    received = spectrum
    mine, other, activity, spectrum = update_call(
        functools.partial(first_kernel, (subs, members, ranks_here, width)),
        received,
        [half_shape, half_shape, (frames, rank), (partners, spectrum_rows, LANES)],
        [
            lanes_scratch,
            total_scratch,
            pltpu.VMEM((partners, extra, LANES), jnp.float32),
            pltpu.SemaphoreType.DMA,
            fetch_sems,
        ],
        (basis,),
        (side,),
        pltpu.HBM,
    )
    mine = mine + swap_by(other, "freq", 1)
    mine = sum_over(mine, "freq", 2)
    mine = sum_over(mine, "member", 1)
    other = swap_by(mine, "freq", 1)

    middle, numerator = update_call(
        second_kernel,
        spectrum,
        [(frames, rank), (per_member * rank + 8, LANES)],
        [lanes_scratch, pltpu.VMEM((2 * rank, frames), jnp.bfloat16)],
        (basis, activity, mine, other),
        (side,),
    )
    numerators = [numerator]
    if groups == 2:
        numerators.append(swap_by(numerator, "group", 1))
    new_basis, payload = update_call(
        third_kernel,
        received,
        [(per_member, rank, LANES), (subs, members, 2, ranks_here, width)],
        [
            lanes_scratch,
            total_scratch,
            pltpu.VMEM((partners, spectrum_rows, LANES), jnp.float32),
            fetch_sems,
        ],
        (basis, middle, *numerators),
        (),
        pltpu.HBM,
    )
    parts = lax.all_to_all(
        payload.reshape(partners, 2, ranks_here, width), exchange, 0, 0, tiled=True
    )
    summed = jnp.sum(parts, axis=0)
    mine = lax.dynamic_slice(
        middle.reshape(subs, members, local, rank),
        (0, me_member, 0, me_sub * ranks_here),
        (subs, 1, local, ranks_here),
    )
    mine = mine.reshape(width, ranks_here).T
    final_activations = mine * (summed[0] / summed[1])

    back = jnp.stack(
        [
            jnp.stack([new_basis[kept.index((group, r))] for r in range(units_here)])
            for group in range(groups)
        ]
    )
    back = lax.dynamic_index_in_dim(back, me_group, 0, keepdims=False)
    turned_here = lax.dynamic_index_in_dim(is_turned, me_group, 0, keepdims=False)
    back = jnp.where(turned_here, turned_lanes(back), back)
    final_templates = back.transpose(1, 0, 2).reshape(rank, bins_here)
    return (final_activations, final_templates)


def solution(mesh):
    subs, blocks = mesh.devices.shape
    groups = 2 if blocks % 2 == 0 else 1
    grid = Mesh(
        mesh.devices.reshape(subs, groups, blocks // groups), ("freq", "group", "member")
    )
    frames = ("group", "member")
    return jax.shard_map(
        on_device,
        mesh=grid,
        in_specs=(P(frames, "freq", None), P(None, ("freq", *frames)), P("freq", frames)),
        out_specs=(P("freq", frames), P(None, ("freq", *frames))),
        check_vma=False,
    )
```

```python
import functools
import math

import jax
import jax.numpy as jnp
import ml_dtypes
import numpy as np
from jax import lax
from jax.experimental import pallas as pl
from jax.experimental.pallas import tpu as pltpu
from jax.sharding import Mesh
from jax.sharding import PartitionSpec as P

FRAME_LEN = 65536
SPLIT = 256
LANES = 128
GROUP = 8
HOP_ROWS = FRAME_LEN // 2 // LANES
SPECTRUM_VMEM = 24 * 1024 * 1024
UPDATE_VMEM = 24 * 1024 * 1024
NT = (((1,), (1,)), ((), ()))


def high_low(values):
    high = values.astype(np.float32).astype(ml_dtypes.bfloat16)
    low = (values - high.astype(np.float64)).astype(ml_dtypes.bfloat16)
    return high, low


def both_parts_below(values):
    high, low = high_low(values)
    return np.concatenate([high, low], 0)


def units_of_member(units_here, member_blocks):
    order = list(range(units_here))
    if units_here % 8 == 0:
        order.sort(key=lambda r: (row_of_unit(r) % 2, r))
    kept = [(block, r) for block in member_blocks for r in order]
    if units_here % 8 == 0:
        kept.sort(key=lambda pair: row_of_unit(pair[1]) % 2)
    return kept


def row_of_unit(unit):
    return unit // 2 if unit % 2 == 0 else SPLIT - 1 - unit // 2


@functools.lru_cache(maxsize=None)
def tables(unit_order):
    half = SPLIT // 2
    index = np.arange(SPLIT, dtype=np.float64)
    slot = np.arange(half, dtype=np.float64)
    angle = 2.0 * np.pi / SPLIT * np.mod(np.outer(np.arange(half + 1), np.arange(SPLIT)), SPLIT)
    cosine, sine = np.cos(angle), np.sin(angle)
    first = np.concatenate([cosine[:half], cosine[half:], -sine[1:half]], 0)
    turn = 2.0 * np.pi / (SPLIT * SPLIT) * np.outer(slot, index)
    twiddle_cos, twiddle_sin = np.cos(turn), np.sin(turn)
    masked_cos = twiddle_cos.copy()
    masked_cos[0] = 0.0
    twiddle = np.stack([twiddle_cos, twiddle_sin, masked_cos]).astype(np.float32)
    middle = 2.0 * np.pi / (SPLIT * SPLIT) * half * index
    odd = 2.0 * np.pi / SPLIT * slot
    rows = np.zeros((8, SPLIT), np.float32)
    rows[0], rows[1] = np.cos(middle), -np.sin(middle)
    rows[2, :half], rows[3, :half] = np.cos(odd), np.sin(odd)
    seconds, mirrored, places = [], [], []
    for parity in range(2):
        here = [place for place, unit in enumerate(unit_order) if row_of_unit(unit) % 2 == parity]
        turns = np.array([row_of_unit(unit_order[place]) // 2 for place in here])
        phase = 2.0 * np.pi / half * np.mod(np.outer(turns, np.arange(half)), half)
        c, s = np.cos(phase), np.sin(phase)
        seconds.append(
            both_parts_below(np.concatenate([np.concatenate([c, s], 1), np.concatenate([-s, c], 1)], 0))
        )
        flags = np.zeros((half, LANES), np.float32)
        flags[:, 0] = [unit_order[place] % 2 for place in here]
        mirrored.append(flags)
        places.append(tuple(here))
    position = np.arange(FRAME_LEN, dtype=np.float64)
    window = (0.5 - 0.5 * np.cos(2.0 * np.pi / FRAME_LEN * position)).astype(np.float32)
    window = window.reshape(SPLIT, 2, LANES).transpose(1, 0, 2)
    return (
        np.ascontiguousarray(window),
        both_parts_below(first),
        twiddle,
        rows,
        np.stack(seconds),
        np.stack(mirrored),
        tuple(places),
    )


def split_values(values):
    high = values.astype(jnp.bfloat16)
    low = (values - high.astype(jnp.float32)).astype(jnp.bfloat16)
    return high, low


def dot(left, right):
    return jnp.dot(left, right, preferred_element_type=jnp.float32)


def dot_nt(left, right):
    return lax.dot_general(left, right, NT, preferred_element_type=jnp.float32)


def transform_group(hop_rows, places, per_member, table_refs, out_ref, parts_ref, middle_ref, written=None):
    window_ref, first_ref, twiddle_ref, rows_ref, second_ref, mirrored_ref = table_refs
    half = SPLIT // 2
    middle_ref[...] = jnp.zeros_like(middle_ref)

    def even_odd(real, imag):
        even = jnp.concatenate([real[:, :half] + real[:, half:], imag[:, :half] + imag[:, half:]], 1)
        real = real[:, :half] - real[:, half:]
        imag = imag[:, :half] - imag[:, half:]
        c, s = rows_ref[2:3, :half], rows_ref[3:4, :half]
        odd = jnp.concatenate([real * c + imag * s, imag * c - real * s], 1)
        return even, odd

    def in_parts(values):
        return jnp.concatenate(split_values(values), 1)

    def second(parity, parts):
        both = dot_nt(second_ref[parity], parts[:, :SPLIT])
        return both[:SPLIT] + (both[SPLIT:] + dot_nt(second_ref[parity, :SPLIT, :], parts[:, SPLIT:]))

    for g in range(GROUP):
        columns = [
            jnp.concatenate([hop_rows(g, side), hop_rows(g + 1, side)], 0) * window_ref[side]
            for side in range(2)
        ]
        high, low = split_values(jnp.concatenate(columns, 1))
        section = dot(first_ref[...], high)
        section = section[:SPLIT] + (section[SPLIT:] + dot(first_ref[:SPLIT, :], low))
        a, b = section[:half], section[half:]
        real = a * twiddle_ref[0] + b * twiddle_ref[1]
        imag = b * twiddle_ref[2] - a * twiddle_ref[1]
        for parity, values in enumerate(even_odd(real, imag)):
            parts_ref[parity, g * half : (g + 1) * half, :] = in_parts(values)
        nyquist = section[half : half + 1]
        for parity, values in enumerate(even_odd(nyquist * rows_ref[0:1], nyquist * rows_ref[1:2])):
            middle_ref[parity, g : g + 1, :] = values

    def magnitude(values):
        real, imag = values[:half], values[half:]
        return jnp.sqrt(real * real + imag * imag) * (8.0 / SPLIT)

    for parity in range(2):
        middle = magnitude(second(parity, in_parts(middle_ref[parity])))
        is_middle = mirrored_ref[parity] > 0.0
        for pair in range(GROUP // 2):
            values = magnitude(second(parity, parts_ref[parity, pair * SPLIT : (pair + 1) * SPLIT, :]))
            for lane in range(2):
                g = 2 * pair + lane
                block = jnp.where(
                    is_middle, middle[:, g : g + 1], values[:, lane * LANES : (lane + 1) * LANES]
                )
                start = 0
                while start < half:
                    stop = start + 1
                    place = places[parity][start]
                    while (
                        stop < half
                        and stop - start < 8
                        and places[parity][stop] == place + stop - start
                        and places[parity][stop] // per_member == place // per_member
                    ):
                        stop += 1
                    member, row = divmod(place, per_member)
                    out_ref[member, pl.ds(row * GROUP + g, stop - start, stride=GROUP), :] = block[start:stop]
                    start = stop
        if written is not None:
            written(parity)


def early_kernel(
    places, per_member, frames, samples_ref, *rest
):
    table_refs, (out_ref, tail_ref, group_ref) = rest[:6], rest[6:9]
    copies_ref, (hops_ref, parts_ref, middle_ref, sem_ref, out_sem_ref) = rest[9:15], rest[15:]
    groups = frames // GROUP - 1
    group_rows = GROUP * HOP_ROWS
    half = SPLIT // 2

    def fetch(first, count, slot):
        return pltpu.make_async_copy(
            samples_ref.at[pl.ds(first, count), :], hops_ref.at[pl.ds(first, count), :], sem_ref.at[slot]
        )

    tables_in = [
        pltpu.make_async_copy(table_refs[i], copies_ref[i], sem_ref.at[i]) for i in range(len(table_refs))
    ]
    lead = fetch(0, HOP_ROWS, 6)
    tail = pltpu.make_async_copy(
        samples_ref.at[pl.ds(groups * group_rows, group_rows), :], tail_ref, sem_ref.at[7]
    )
    hops = [fetch(HOP_ROWS + i * group_rows, group_rows, 8 + i) for i in range(groups)]
    for copy in [tables_in[1], lead, hops[0], *tables_in[:1], *tables_in[2:], *hops[1:], tail]:
        copy.start()
    lead.wait()
    for copy in tables_in:
        copy.wait()

    def body(i, carry):
        first = pl.multiple_of(i * group_rows, group_rows)
        pltpu.make_async_copy(
            samples_ref.at[pl.ds(HOP_ROWS + first, group_rows), :],
            hops_ref.at[pl.ds(HOP_ROWS + first, group_rows), :],
            sem_ref.at[8 + i],
        ).wait()

        transform_group(
            lambda hop, side: hops_ref[pl.ds(first + hop * HOP_ROWS + side, half, stride=2), :],
            places,
            per_member,
            copies_ref,
            group_ref.at[i],
            parts_ref,
            middle_ref,
        )

        @pl.when(i < groups - 1)
        def _():
            send(i).start()

        return carry

    def send(i):
        count = group_ref.shape[2]
        return pltpu.make_async_copy(
            group_ref.at[i],
            out_ref.at[:, pl.ds(pl.multiple_of(i * count, count), count), :],
            out_sem_ref.at[i],
        )

    lax.fori_loop(0, groups, body, 0)
    tail.wait()
    for i in range(groups - 1):
        send(i).wait()


def late_kernel(places, per_member, frames, done_ref, tail_ref, trailing_ref, activity_ref, *rest):
    table_refs, (_, out_ref, parts_ref, middle_ref, group_ref, sem_ref) = rest[:6], rest[6:]
    count = per_member * GROUP
    before = frames // GROUP - 1
    pass_on = pltpu.make_async_copy(
        done_ref.at[before - 1], out_ref.at[:, pl.ds((before - 1) * count, count), :], sem_ref.at[0]
    )
    pass_on.start()

    def hop_rows(hop, side):
        if hop == GROUP:
            return trailing_ref[pl.ds(side, SPLIT // 2, stride=2), :]
        return tail_ref[pl.ds(hop * HOP_ROWS + side, SPLIT // 2, stride=2), :]

    for member in range(out_ref.shape[0]):
        group_ref[member, count:, :] = activity_ref[...]
    bounds = [0, group_ref.shape[1]]
    if all(place % per_member < per_member // 2 for place in places[0]):
        bounds.insert(1, count // 2)
    sends = []

    def written(parity):
        if parity == 1 or len(bounds) == 3:
            first, last = bounds[len(sends)], bounds[len(sends) + 1]
            sends.append(
                pltpu.make_async_copy(
                    group_ref.at[:, pl.ds(first, last - first), :],
                    out_ref.at[:, pl.ds(before * count + first, last - first), :],
                    sem_ref.at[1 + len(sends)],
                )
            )
            sends[-1].start()

    transform_group(
        hop_rows,
        places,
        per_member,
        table_refs,
        group_ref,
        parts_ref,
        middle_ref,
        written,
    )
    pass_on.wait()
    for send in sends:
        send.wait()


def spectrum_blocks(samples, trailing, activity, unit_order, members):
    *values, places = tables(unit_order)
    per_member = SPLIT // members
    frames = samples.shape[0] // HOP_ROWS
    groups = frames // GROUP - 1
    constants = [jnp.asarray(t) for t in values]
    group_shape = (members, per_member * GROUP, LANES)
    last_shape = (members, per_member * GROUP + activity.shape[0], LANES)
    out_shape = pltpu.HBM((members, per_member * frames + activity.shape[0], LANES), jnp.float32)
    tail_shape = jax.ShapeDtypeStruct((GROUP * HOP_ROWS, LANES), jnp.float32)
    in_vmem = pl.BlockSpec(memory_space=pltpu.VMEM)
    in_hbm = pl.BlockSpec(memory_space=pltpu.HBM)
    scratch = [
        pltpu.VMEM((2, GROUP * LANES, 2 * SPLIT), jnp.bfloat16),
        pltpu.VMEM((2, 16, SPLIT), jnp.float32),
    ]

    def settings(count):
        return dict(
            compiler_params=pltpu.CompilerParams(vmem_limit_bytes=SPECTRUM_VMEM),
            cost_estimate=pl.CostEstimate(
                flops=count * GROUP * 6 * SPLIT * SPLIT * SPLIT * 2,
                bytes_accessed=count * GROUP * FRAME_LEN * 4,
                transcendentals=0,
            ),
        )

    early, tail, done, *copies = pl.pallas_call(
        functools.partial(early_kernel, places, per_member, frames),
        in_specs=[in_hbm] * (1 + len(constants)),
        out_specs=[in_hbm] + [in_vmem] * (2 + len(constants)),
        out_shape=[out_shape, tail_shape, jax.ShapeDtypeStruct((groups, *group_shape), jnp.float32)]
        + [jax.ShapeDtypeStruct(t.shape, t.dtype) for t in constants],
        scratch_shapes=[pltpu.VMEM(((groups * GROUP + 1) * HOP_ROWS, LANES), jnp.float32)]
        + scratch
        + [
            pltpu.SemaphoreType.DMA((8 + groups,)),
            pltpu.SemaphoreType.DMA((groups,)),
        ],
        **settings(groups),
    )(*[pltpu.with_memory_space_constraint(value, pltpu.HBM) for value in (samples, *constants)])
    return pl.pallas_call(
        functools.partial(late_kernel, places, per_member, frames),
        in_specs=[in_vmem] * (4 + len(constants)) + [in_hbm],
        out_specs=in_hbm,
        out_shape=out_shape,
        scratch_shapes=scratch + [pltpu.VMEM(last_shape, jnp.float32), pltpu.SemaphoreType.DMA((3,))],
        input_output_aliases={4 + len(constants): 0},
        **settings(1),
    )(done, tail, trailing, activity, *copies, early)


def lanes_of_activity(activity):
    high, low = split_values(activity)
    return jnp.concatenate([high, high, low, low], 1)


def ratio_of(spectrum_ref, start, activity_lanes, basis):
    frames = activity_lanes.shape[0]
    members = spectrum_ref.shape[0]
    groups = frames // (members * GROUP)
    stride = spectrum_ref.shape[1] // groups
    splits = [split_values(block) for block in basis]
    stacked = jnp.concatenate([jnp.concatenate([h, l, h, l], 0) for h, l in splits], 1)
    approx = dot(activity_lanes, stacked)
    values = jnp.concatenate(
        [
            jnp.stack(
                [
                    spectrum_ref[:, pl.ds(group * stride + (start + row) * GROUP, GROUP), :]
                    for group in range(groups)
                ],
                1,
            ).reshape(frames, LANES)
            for row in range(len(basis))
        ],
        1,
    )
    return values / approx, jnp.concatenate([jnp.concatenate([h, l], 0) for h, l in splits], 1)


def for_activity(ratio, basis):
    high, low = split_values(ratio)
    return dot_nt(high, basis) + dot_nt(low, basis)


def both_parts(values):
    half = values.shape[1] // 2
    return values + pltpu.roll(values, half, 1)


def row_sums(basis):
    return dot_nt(jnp.ones((16, basis.shape[1]), jnp.bfloat16), basis)


def row_steps(per_member, most=8):
    rows = math.gcd(per_member, most)
    return [range(start, start + rows) for start in range(0, per_member, rows)]


def packed(values):
    rows, width = values.shape
    lane = lax.broadcasted_iota(jnp.int32, (rows // 2, width), 1)
    return jnp.where(lane < width // 2, values[: rows // 2], values[rows // 2 :])


def unpacked(values):
    half = values.shape[1] // 2
    return jnp.concatenate([values[:, :half], values[:, half:]], 0)


def gathered_activity(rows_ref, shape):
    subs, members, ranks, width = shape
    local = width // subs
    frames_in = width // LANES
    pieces = {}
    for member in range(members):
        for part in range(frames_in):
            start = part * ranks
            rows = [rows_ref[sub * members + member, start : start + ranks, :] for sub in range(subs)]
            block = jnp.transpose(jnp.concatenate(rows, 0))
            for place in range(LANES // local):
                pieces[part * (LANES // local) + place, member] = block[place * local : (place + 1) * local]
    return jnp.concatenate([pieces[sub, member] for sub in range(subs) for member in range(members)], 0)


def start_fetches(received_ref, spectrum_ref, sem_ref, per_member, steps):
    count = spectrum_ref.shape[1]
    groups = count // (per_member * GROUP)
    copies = []
    for step, rows in enumerate(steps):
        copies.append([])
        for group in range(groups):
            place = pl.ds((group * per_member + rows[0]) * GROUP, len(rows) * GROUP)
            copies[-1].append(
                pltpu.make_async_copy(
                    received_ref.at[:, place, :], spectrum_ref.at[:, place, :], sem_ref.at[step * groups + group]
                )
            )
            copies[-1][-1].start()
    return copies


def first_kernel(
    shape,
    side_ref,
    received_ref,
    basis_ref,
    mine_ref,
    other_ref,
    activity_ref,
    spectrum_ref,
    lanes_ref,
    total_ref,
    rows_ref,
    rows_sem_ref,
    sem_ref,
):
    steps = row_steps(basis_ref.shape[0], 16)
    count = spectrum_ref.shape[1]
    rows_copy = pltpu.make_async_copy(
        received_ref.at[:, pl.ds(count, rows_ref.shape[1]), :], rows_ref, rows_sem_ref
    )
    rows_copy.start()
    copies = start_fetches(received_ref, spectrum_ref, sem_ref, basis_ref.shape[0], steps)
    rows_copy.wait()
    activity = gathered_activity(rows_ref, shape)
    activity_ref[...] = activity
    lanes_ref[...] = lanes_of_activity(activity)
    sums = 0.0
    for step, rows in enumerate(steps):
        for copy in copies[step]:
            copy.wait()
        ratio, basis = ratio_of(spectrum_ref, rows[0], lanes_ref[...], [basis_ref[row] for row in rows])
        part = for_activity(ratio, basis)
        if step == 0:
            total_ref[...] = part
        else:
            total_ref[...] += part
        sums += row_sums(basis)
    total = both_parts(total_ref[...])
    half = total.shape[0] // 2
    quarter = half // 2
    early, late = packed(total[:half]), packed(total[half:])
    first = side_ref[0] == 0
    mine_ref[:quarter, :] = jnp.where(first, early, late)
    other_ref[:quarter, :] = jnp.where(first, late, early)
    sums = both_parts(sums)[:8]
    mine_ref[quarter:, :] = sums
    other_ref[quarter:, :] = sums


def by_owner(values, shape):
    subs, members, ranks, width = shape
    local = width // subs
    blocks = []
    for member in range(members):
        rows = [
            values[(sub * members + member) * local : (sub * members + member + 1) * local]
            for sub in range(subs)
        ]
        blocks.append(jnp.transpose(jnp.concatenate(rows, 0)).reshape(subs, ranks, width))
    return blocks


def second_kernel(
    side_ref,
    spectrum_ref,
    basis_ref,
    activity_ref,
    mine_ref,
    other_ref,
    middle_ref,
    early_ref,
    late_ref,
    lanes_ref,
    turned_ref,
):
    rank = activity_ref.shape[1]
    quarter = activity_ref.shape[0] // 4
    first = side_ref[0] == 0
    mine = mine_ref[:quarter, :] / mine_ref[quarter : quarter + 1, :]
    other = other_ref[:quarter, :] / other_ref[quarter : quarter + 1, :]
    early, late = jnp.where(first, mine, other), jnp.where(first, other, mine)
    middle = activity_ref[...] * jnp.concatenate([unpacked(early), unpacked(late)], 0)
    middle_ref[...] = middle
    lanes_ref[...] = lanes_of_activity(middle)
    turned = jnp.transpose(middle)
    high, low = split_values(turned)
    turned_ref[...] = jnp.concatenate([high, low], 0)
    totals = jnp.sum(middle, axis=0, keepdims=True)
    totals = jnp.broadcast_to(jnp.concatenate([totals] * (LANES // rank), 1), (8, LANES))
    early_ref[early_ref.shape[0] - 8 :, :] = totals
    early_rows = early_ref.shape[0] // rank
    for rows in row_steps(basis_ref.shape[0]):
        ratio, _ = ratio_of(spectrum_ref, rows[0], lanes_ref[...], [basis_ref[row] for row in rows])
        high, low = split_values(ratio)
        total = dot(turned_ref[...], high) + dot(turned_ref[...], low)
        total = total[:rank] + total[rank:]
        for place, row in enumerate(rows):
            out_ref, start = (early_ref, row) if row < early_rows else (late_ref, row - early_rows)
            out_ref[start * rank : (start + 1) * rank, :] = total[:, place * LANES : (place + 1) * LANES]


def renew_and_add(rows, spectrum_ref, basis_ref, lanes_ref, scale, numerators, new_ref, total_ref, sums_ref):
    rank = basis_ref.shape[1]
    blocks = [
        basis_ref[row] * (sum(ref[place * rank : (place + 1) * rank, :] for ref in numerators) * scale)
        for place, row in enumerate(rows)
    ]
    for place, block in enumerate(blocks):
        new_ref[place] = block
    ratio, basis = ratio_of(spectrum_ref, rows[0], lanes_ref[...], blocks)
    total_ref[...] = for_activity(ratio, basis)
    sums_ref[...] = row_sums(basis)


def third_kernel(rows, later, received_ref, basis_ref, middle_ref, *rest):
    numerators = rest[:-7]
    new_ref, total_ref, sums_ref, lanes_ref, scale_ref, spectrum_ref, sem_ref = rest[-7:]
    rank = middle_ref.shape[1]
    copies = start_fetches(received_ref, spectrum_ref, sem_ref, basis_ref.shape[0], [rows, later])
    lanes_ref[...] = lanes_of_activity(middle_ref[...])
    totals = sum(ref[len(rows) * rank :, :] for ref in numerators)
    totals = jnp.transpose(jnp.concatenate([totals] * (LANES // 8), 0))[:rank]
    scale_ref[...] = 1.0 / totals
    for copy in copies[0]:
        copy.wait()
    renew_and_add(
        rows, spectrum_ref, basis_ref, lanes_ref, scale_ref[...], numerators, new_ref, total_ref, sums_ref
    )
    for copy in copies[1]:
        copy.wait()


def last_kernel(rows, spectrum_ref, basis_ref, lanes_ref, scale_ref, before_ref, sums_before_ref, *rest):
    numerators = rest[:-4]
    new_ref, out_ref, total_ref, sums_ref = rest[-4:]
    rank = basis_ref.shape[1]
    renew_and_add(
        rows, spectrum_ref, basis_ref, lanes_ref, scale_ref[...], numerators, new_ref, total_ref, sums_ref
    )
    total = both_parts(before_ref[...] + total_ref[...])[:, :rank]
    sums = both_parts(sums_before_ref[...] + sums_ref[...])
    subs, members, _, ranks, width = out_ref.shape
    sums = jnp.transpose(jnp.broadcast_to(sums[:1], (LANES, 2 * rank)))[:rank]
    sums = jnp.concatenate([sums] * (width // LANES), 1).reshape(subs, ranks, width)
    for member, block in enumerate(by_owner(total, (subs, members, ranks, width))):
        out_ref[:, member, 0] = block
        out_ref[:, member, 1] = sums


def update_call(kernel, spectrum, out_shapes, scratch, operands, scalars=(), place=pltpu.VMEM):
    in_vmem = pl.BlockSpec(memory_space=pltpu.VMEM)
    if place == pltpu.HBM:
        spectrum = pltpu.with_memory_space_constraint(spectrum, place)
    rank = operands[0].shape[1]
    return pl.pallas_call(
        kernel,
        in_specs=[pl.BlockSpec(memory_space=pltpu.SMEM) for _ in scalars]
        + [pl.BlockSpec(memory_space=place)]
        + [in_vmem for _ in operands],
        out_specs=[in_vmem for _ in out_shapes],
        out_shape=[
            shape if hasattr(shape, "dtype") else jax.ShapeDtypeStruct(shape, jnp.float32)
            for shape in out_shapes
        ],
        scratch_shapes=scratch,
        compiler_params=pltpu.CompilerParams(vmem_limit_bytes=UPDATE_VMEM),
        cost_estimate=pl.CostEstimate(
            flops=spectrum.size * rank * 16, bytes_accessed=spectrum.size * 4, transcendentals=0
        ),
    )(*scalars, spectrum, *operands)


def turned_lanes(values):
    return jnp.roll(jnp.flip(values, -1), 1, -1)


def swap_by(value, axis, mask):
    count = lax.axis_size(axis)
    return lax.ppermute(value, axis, [(i, i ^ mask) for i in range(count)])


def sum_over(value, axis, mask):
    count = lax.axis_size(axis)
    while mask < count:
        masks = [mask] if 2 * mask >= count else [mask, 2 * mask, 3 * mask]
        value = sum([swap_by(value, axis, m) for m in masks], value)
        mask *= 2 if len(masks) == 1 else 4
    return value


def on_device(signal, templates, activations):
    subs, groups, members = (lax.axis_size(axis) for axis in ("freq", "group", "member"))
    blocks = groups * members
    rank, bins_here = templates.shape
    ranks_here, width = activations.shape
    units_here = bins_here // LANES
    exchange = ("freq", "member")
    partners = subs * members
    per_member = units_here * groups
    me_sub, me_group, me_member = (lax.axis_index(axis) for axis in ("freq", "group", "member"))

    kept = units_of_member(units_here, range(groups))
    unit_order = tuple(
        units_here * (sub * blocks + group * members + member) + r
        for sub in range(subs)
        for member in range(members)
        for group, r in kept
    )

    samples = signal.reshape(-1, LANES)
    route = [
        (((sub + 1) % subs) * blocks + block + (sub + 1) // subs, sub * blocks + block)
        for sub in range(subs)
        for block in range(blocks)
        if block + (sub + 1) // subs < blocks
    ]
    trailing = lax.ppermute(samples[:HOP_ROWS], ("freq", "group", "member"), route)
    other = [swap_by(templates, "group", 1)] if groups == 2 else []
    own_rows = activations.reshape(ranks_here, width // LANES, LANES).transpose(1, 0, 2)
    own_rows = own_rows.reshape(ranks_here * width // LANES, LANES)
    spectrum = spectrum_blocks(samples, trailing, own_rows, unit_order, partners)
    spectrum, other = lax.optimization_barrier((spectrum, other))
    spectrum = lax.all_to_all(spectrum, exchange, 0, 0, tiled=True)
    local = width // subs
    frames = partners * local

    own = templates.reshape(rank, units_here, LANES).transpose(1, 0, 2)
    if other:
        remote = other[0].reshape(rank, units_here, LANES).transpose(1, 0, 2)
        by_group = jnp.where(me_group == 0, jnp.stack([own, remote]), jnp.stack([remote, own]))
    else:
        by_group = own[None]
    unit_index = units_here * (
        me_sub * blocks + jnp.arange(groups)[:, None] * members + me_member
    ) + jnp.arange(units_here)[None, :]
    is_turned = (unit_index % 2 == 1)[:, :, None, None]
    by_group = jnp.where(is_turned, turned_lanes(by_group), by_group)
    basis = jnp.concatenate([by_group[group, r][None] for group, r in kept], 0)

    lanes_scratch = pltpu.VMEM((frames, 4 * rank), jnp.bfloat16)
    total_scratch = pltpu.VMEM((frames, 2 * rank), jnp.float32)
    half_shape = (frames // 4 + 8, 2 * rank)
    side = (me_sub % 2).astype(jnp.int32).reshape(1)
    extra = ranks_here * width // LANES
    spectrum_rows = spectrum.shape[1] - extra
    row_groups = spectrum_rows // (per_member * GROUP)
    fetch_sems = pltpu.SemaphoreType.DMA((len(row_steps(per_member)) * row_groups,))
    received = spectrum
    mine, other, activity, spectrum = update_call(
        functools.partial(first_kernel, (subs, members, ranks_here, width)),
        received,
        [half_shape, half_shape, (frames, rank), (partners, spectrum_rows, LANES)],
        [
            lanes_scratch,
            total_scratch,
            pltpu.VMEM((partners, extra, LANES), jnp.float32),
            pltpu.SemaphoreType.DMA,
            fetch_sems,
        ],
        (basis,),
        (side,),
        pltpu.HBM,
    )
    mine = mine + swap_by(other, "freq", 1)
    mine = sum_over(mine, "freq", 2)
    mine = sum_over(mine, "member", 1)
    other = swap_by(mine, "freq", 1)

    early_rows = range(max(1, per_member // 2))
    late_rows = range(len(early_rows), per_member)
    middle, *numerators = update_call(
        second_kernel,
        spectrum,
        [(frames, rank), (len(early_rows) * rank + 8, LANES), (len(late_rows) * rank, LANES)],
        [lanes_scratch, pltpu.VMEM((2 * rank, frames), jnp.bfloat16)],
        (basis, activity, mine, other),
        (side,),
    )
    numerators = [[numerator] for numerator in numerators]
    if groups == 2:
        for numerator in numerators:
            numerator.append(swap_by(numerator[0], "group", 1))
    early_new, total, sums, lanes, scale, spectrum = update_call(
        functools.partial(third_kernel, early_rows, late_rows),
        received,
        [
            (len(early_rows), rank, LANES),
            (frames, 2 * rank),
            (16, 2 * rank),
            jax.ShapeDtypeStruct((frames, 4 * rank), jnp.bfloat16),
            (rank, LANES),
            (partners, spectrum_rows, LANES),
        ],
        [pltpu.SemaphoreType.DMA((2 * row_groups,))],
        (basis, middle, *numerators[0]),
        (),
        pltpu.HBM,
    )
    late_new, payload = update_call(
        functools.partial(last_kernel, late_rows),
        spectrum,
        [(len(late_rows), rank, LANES), (subs, members, 2, ranks_here, width)],
        [total_scratch, pltpu.VMEM((16, 2 * rank), jnp.float32)],
        (basis, lanes, scale, total, sums, *numerators[1]),
    )
    new_basis = [*early_new, *late_new]
    parts = lax.all_to_all(
        payload.reshape(partners, 2, ranks_here, width), exchange, 0, 0, tiled=True
    )
    summed = jnp.sum(parts, axis=0)
    mine = lax.dynamic_slice(
        middle.reshape(subs, members, local, rank),
        (0, me_member, 0, me_sub * ranks_here),
        (subs, 1, local, ranks_here),
    )
    mine = mine.reshape(width, ranks_here).T
    final_activations = mine * (summed[0] / summed[1])

    back = jnp.stack(
        [
            jnp.stack([new_basis[kept.index((group, r))] for r in range(units_here)])
            for group in range(groups)
        ]
    )
    back = lax.dynamic_index_in_dim(back, me_group, 0, keepdims=False)
    turned_here = lax.dynamic_index_in_dim(is_turned, me_group, 0, keepdims=False)
    back = jnp.where(turned_here, turned_lanes(back), back)
    final_templates = back.transpose(1, 0, 2).reshape(rank, bins_here)
    return (final_activations, final_templates)


def solution(mesh):
    subs, blocks = mesh.devices.shape
    groups = 2 if blocks % 2 == 0 else 1
    grid = Mesh(
        mesh.devices.reshape(subs, groups, blocks // groups), ("freq", "group", "member")
    )
    frames = ("group", "member")
    return jax.shard_map(
        on_device,
        mesh=grid,
        in_specs=(P(frames, "freq", None), P(None, ("freq", *frames)), P("freq", frames)),
        out_specs=(P("freq", frames), P(None, ("freq", *frames))),
        check_vma=False,
    )
```

```python
import functools
import math

import jax
import jax.numpy as jnp
import ml_dtypes
import numpy as np
from jax import lax
from jax.experimental import pallas as pl
from jax.experimental.pallas import tpu as pltpu
from jax.sharding import Mesh
from jax.sharding import PartitionSpec as P

FRAME_LEN = 65536
SPLIT = 256
LANES = 128
GROUP = 8
HOP_ROWS = FRAME_LEN // 2 // LANES
SPECTRUM_VMEM = 24 * 1024 * 1024
UPDATE_VMEM = 24 * 1024 * 1024
NT = (((1,), (1,)), ((), ()))


def high_low(values):
    high = values.astype(np.float32).astype(ml_dtypes.bfloat16)
    low = (values - high.astype(np.float64)).astype(ml_dtypes.bfloat16)
    return high, low


def both_parts_below(values):
    high, low = high_low(values)
    return np.concatenate([high, low], 0)


def units_of_member(units_here, member_blocks):
    order = list(range(units_here))
    if units_here % 8 == 0:
        order.sort(key=lambda r: (row_of_unit(r) % 2, r))
    kept = [(block, r) for block in member_blocks for r in order]
    if units_here % 8 == 0:
        kept.sort(key=lambda pair: row_of_unit(pair[1]) % 2)
    return kept


def row_of_unit(unit):
    return unit // 2 if unit % 2 == 0 else SPLIT - 1 - unit // 2


@functools.lru_cache(maxsize=None)
def tables(unit_order):
    half = SPLIT // 2
    index = np.arange(SPLIT, dtype=np.float64)
    slot = np.arange(half, dtype=np.float64)
    angle = 2.0 * np.pi / SPLIT * np.mod(np.outer(np.arange(half + 1), np.arange(SPLIT)), SPLIT)
    cosine, sine = np.cos(angle), np.sin(angle)
    first = np.concatenate([cosine[:half], cosine[half:], -sine[1:half]], 0)
    turn = 2.0 * np.pi / (SPLIT * SPLIT) * np.outer(slot, index)
    twiddle_cos, twiddle_sin = np.cos(turn), np.sin(turn)
    masked_cos = twiddle_cos.copy()
    masked_cos[0] = 0.0
    twiddle = np.stack([twiddle_cos, twiddle_sin, masked_cos]).astype(np.float32)
    middle = 2.0 * np.pi / (SPLIT * SPLIT) * half * index
    odd = 2.0 * np.pi / SPLIT * slot
    rows = np.zeros((8, SPLIT), np.float32)
    rows[0], rows[1] = np.cos(middle), -np.sin(middle)
    rows[2, :half], rows[3, :half] = np.cos(odd), np.sin(odd)
    seconds, mirrored, places = [], [], []
    for parity in range(2):
        here = [place for place, unit in enumerate(unit_order) if row_of_unit(unit) % 2 == parity]
        turns = np.array([row_of_unit(unit_order[place]) // 2 for place in here])
        phase = 2.0 * np.pi / half * np.mod(np.outer(turns, np.arange(half)), half)
        c, s = np.cos(phase), np.sin(phase)
        seconds.append(
            both_parts_below(np.concatenate([np.concatenate([c, s], 1), np.concatenate([-s, c], 1)], 0))
        )
        flags = np.zeros((half, LANES), np.float32)
        flags[:, 0] = [unit_order[place] % 2 for place in here]
        mirrored.append(flags)
        places.append(tuple(here))
    position = np.arange(FRAME_LEN, dtype=np.float64)
    window = (0.5 - 0.5 * np.cos(2.0 * np.pi / FRAME_LEN * position)).astype(np.float32)
    window = window.reshape(SPLIT, 2, LANES).transpose(1, 0, 2)
    return (
        np.ascontiguousarray(window),
        both_parts_below(first),
        twiddle,
        rows,
        np.stack(seconds),
        np.stack(mirrored),
        tuple(places),
    )


def split_values(values):
    high = values.astype(jnp.bfloat16)
    low = (values - high.astype(jnp.float32)).astype(jnp.bfloat16)
    return high, low


def dot(left, right):
    return jnp.dot(left, right, preferred_element_type=jnp.float32)


def dot_nt(left, right):
    return lax.dot_general(left, right, NT, preferred_element_type=jnp.float32)


def transform_group(hop_rows, places, per_member, table_refs, out_ref, parts_ref, middle_ref, written=None):
    window_ref, first_ref, twiddle_ref, rows_ref, second_ref, mirrored_ref = table_refs
    half = SPLIT // 2
    middle_ref[...] = jnp.zeros_like(middle_ref)

    def even_odd(real, imag):
        even = jnp.concatenate([real[:, :half] + real[:, half:], imag[:, :half] + imag[:, half:]], 1)
        real = real[:, :half] - real[:, half:]
        imag = imag[:, :half] - imag[:, half:]
        c, s = rows_ref[2:3, :half], rows_ref[3:4, :half]
        odd = jnp.concatenate([real * c + imag * s, imag * c - real * s], 1)
        return even, odd

    def in_parts(values):
        return jnp.concatenate(split_values(values), 1)

    def second(parity, parts):
        both = dot_nt(second_ref[parity], parts[:, :SPLIT])
        return both[:SPLIT] + (both[SPLIT:] + dot_nt(second_ref[parity, :SPLIT, :], parts[:, SPLIT:]))

    for g in range(GROUP):
        columns = [
            jnp.concatenate([hop_rows(g, side), hop_rows(g + 1, side)], 0) * window_ref[side]
            for side in range(2)
        ]
        values = jnp.concatenate(columns, 1)
        high, low = split_values(values)
        rest = ((values - high.astype(jnp.float32)) - low.astype(jnp.float32)).astype(jnp.bfloat16)
        large = dot(first_ref[...], high)
        small = dot(first_ref[...], low)
        section = (small[SPLIT:] + dot(first_ref[:SPLIT, :], rest)) + (large[SPLIT:] + small[:SPLIT])
        section = large[:SPLIT] + section
        a, b = section[:half], section[half:]
        real = a * twiddle_ref[0] + b * twiddle_ref[1]
        imag = b * twiddle_ref[2] - a * twiddle_ref[1]
        for parity, values in enumerate(even_odd(real, imag)):
            parts_ref[parity, g * half : (g + 1) * half, :] = in_parts(values)
        nyquist = section[half : half + 1]
        for parity, values in enumerate(even_odd(nyquist * rows_ref[0:1], nyquist * rows_ref[1:2])):
            middle_ref[parity, g : g + 1, :] = values

    def magnitude(values):
        real, imag = values[:half], values[half:]
        return jnp.sqrt(real * real + imag * imag) * (8.0 / SPLIT)

    for parity in range(2):
        middle = magnitude(second(parity, in_parts(middle_ref[parity])))
        is_middle = mirrored_ref[parity] > 0.0
        for pair in range(GROUP // 2):
            values = magnitude(second(parity, parts_ref[parity, pair * SPLIT : (pair + 1) * SPLIT, :]))
            for lane in range(2):
                g = 2 * pair + lane
                block = jnp.where(
                    is_middle, middle[:, g : g + 1], values[:, lane * LANES : (lane + 1) * LANES]
                )
                start = 0
                while start < half:
                    stop = start + 1
                    place = places[parity][start]
                    while (
                        stop < half
                        and stop - start < 8
                        and places[parity][stop] == place + stop - start
                        and places[parity][stop] // per_member == place // per_member
                    ):
                        stop += 1
                    member, row = divmod(place, per_member)
                    out_ref[member, pl.ds(row * GROUP + g, stop - start, stride=GROUP), :] = block[start:stop]
                    start = stop
        if written is not None:
            written(parity)


def early_kernel(
    places, per_member, frames, samples_ref, *rest
):
    table_refs, (out_ref, tail_ref, group_ref) = rest[:6], rest[6:9]
    copies_ref, (hops_ref, parts_ref, middle_ref, sem_ref, out_sem_ref) = rest[9:15], rest[15:]
    groups = frames // GROUP - 1
    group_rows = GROUP * HOP_ROWS
    half = SPLIT // 2

    def fetch(first, count, slot):
        return pltpu.make_async_copy(
            samples_ref.at[pl.ds(first, count), :], hops_ref.at[pl.ds(first, count), :], sem_ref.at[slot]
        )

    tables_in = [
        pltpu.make_async_copy(table_refs[i], copies_ref[i], sem_ref.at[i]) for i in range(len(table_refs))
    ]
    lead = fetch(0, HOP_ROWS, 6)
    tail = pltpu.make_async_copy(
        samples_ref.at[pl.ds(groups * group_rows, group_rows), :], tail_ref, sem_ref.at[7]
    )
    hops = [fetch(HOP_ROWS + i * group_rows, group_rows, 8 + i) for i in range(groups)]
    for copy in [tables_in[1], lead, hops[0], *tables_in[:1], *tables_in[2:], *hops[1:], tail]:
        copy.start()
    lead.wait()
    for copy in tables_in:
        copy.wait()

    def body(i, carry):
        first = pl.multiple_of(i * group_rows, group_rows)
        pltpu.make_async_copy(
            samples_ref.at[pl.ds(HOP_ROWS + first, group_rows), :],
            hops_ref.at[pl.ds(HOP_ROWS + first, group_rows), :],
            sem_ref.at[8 + i],
        ).wait()

        transform_group(
            lambda hop, side: hops_ref[pl.ds(first + hop * HOP_ROWS + side, half, stride=2), :],
            places,
            per_member,
            copies_ref,
            group_ref.at[i],
            parts_ref,
            middle_ref,
        )

        @pl.when(i < groups - 1)
        def _():
            send(i).start()

        return carry

    def send(i):
        count = group_ref.shape[2]
        return pltpu.make_async_copy(
            group_ref.at[i],
            out_ref.at[:, pl.ds(pl.multiple_of(i * count, count), count), :],
            out_sem_ref.at[i],
        )

    lax.fori_loop(0, groups, body, 0)
    tail.wait()
    for i in range(groups - 1):
        send(i).wait()


def late_kernel(places, per_member, frames, done_ref, tail_ref, trailing_ref, activity_ref, *rest):
    table_refs, (_, out_ref, parts_ref, middle_ref, group_ref, sem_ref) = rest[:6], rest[6:]
    count = per_member * GROUP
    before = frames // GROUP - 1
    pass_on = pltpu.make_async_copy(
        done_ref.at[before - 1], out_ref.at[:, pl.ds((before - 1) * count, count), :], sem_ref.at[0]
    )
    pass_on.start()

    def hop_rows(hop, side):
        if hop == GROUP:
            return trailing_ref[pl.ds(side, SPLIT // 2, stride=2), :]
        return tail_ref[pl.ds(hop * HOP_ROWS + side, SPLIT // 2, stride=2), :]

    for member in range(out_ref.shape[0]):
        group_ref[member, count:, :] = activity_ref[...]
    bounds = [0, group_ref.shape[1]]
    if all(place % per_member < per_member // 2 for place in places[0]):
        bounds.insert(1, count // 2)
    sends = []

    def written(parity):
        if parity == 1 or len(bounds) == 3:
            first, last = bounds[len(sends)], bounds[len(sends) + 1]
            sends.append(
                pltpu.make_async_copy(
                    group_ref.at[:, pl.ds(first, last - first), :],
                    out_ref.at[:, pl.ds(before * count + first, last - first), :],
                    sem_ref.at[1 + len(sends)],
                )
            )
            sends[-1].start()

    transform_group(
        hop_rows,
        places,
        per_member,
        table_refs,
        group_ref,
        parts_ref,
        middle_ref,
        written,
    )
    pass_on.wait()
    for send in sends:
        send.wait()


def spectrum_blocks(samples, trailing, activity, unit_order, members):
    *values, places = tables(unit_order)
    per_member = SPLIT // members
    frames = samples.shape[0] // HOP_ROWS
    groups = frames // GROUP - 1
    constants = [jnp.asarray(t) for t in values]
    group_shape = (members, per_member * GROUP, LANES)
    last_shape = (members, per_member * GROUP + activity.shape[0], LANES)
    out_shape = pltpu.HBM((members, per_member * frames + activity.shape[0], LANES), jnp.float32)
    tail_shape = jax.ShapeDtypeStruct((GROUP * HOP_ROWS, LANES), jnp.float32)
    in_vmem = pl.BlockSpec(memory_space=pltpu.VMEM)
    in_hbm = pl.BlockSpec(memory_space=pltpu.HBM)
    scratch = [
        pltpu.VMEM((2, GROUP * LANES, 2 * SPLIT), jnp.bfloat16),
        pltpu.VMEM((2, 16, SPLIT), jnp.float32),
    ]

    def settings(count):
        return dict(
            compiler_params=pltpu.CompilerParams(vmem_limit_bytes=SPECTRUM_VMEM),
            cost_estimate=pl.CostEstimate(
                flops=count * GROUP * 6 * SPLIT * SPLIT * SPLIT * 2,
                bytes_accessed=count * GROUP * FRAME_LEN * 4,
                transcendentals=0,
            ),
        )

    early, tail, done, *copies = pl.pallas_call(
        functools.partial(early_kernel, places, per_member, frames),
        in_specs=[in_hbm] * (1 + len(constants)),
        out_specs=[in_hbm] + [in_vmem] * (2 + len(constants)),
        out_shape=[out_shape, tail_shape, jax.ShapeDtypeStruct((groups, *group_shape), jnp.float32)]
        + [jax.ShapeDtypeStruct(t.shape, t.dtype) for t in constants],
        scratch_shapes=[pltpu.VMEM(((groups * GROUP + 1) * HOP_ROWS, LANES), jnp.float32)]
        + scratch
        + [
            pltpu.SemaphoreType.DMA((8 + groups,)),
            pltpu.SemaphoreType.DMA((groups,)),
        ],
        **settings(groups),
    )(*[pltpu.with_memory_space_constraint(value, pltpu.HBM) for value in (samples, *constants)])
    return pl.pallas_call(
        functools.partial(late_kernel, places, per_member, frames),
        in_specs=[in_vmem] * (4 + len(constants)) + [in_hbm],
        out_specs=in_hbm,
        out_shape=out_shape,
        scratch_shapes=scratch + [pltpu.VMEM(last_shape, jnp.float32), pltpu.SemaphoreType.DMA((3,))],
        input_output_aliases={4 + len(constants): 0},
        **settings(1),
    )(done, tail, trailing, activity, *copies, early)


def lanes_of_activity(activity):
    high, low = split_values(activity)
    return jnp.concatenate([high, high, low, low], 1)


def ratio_of(spectrum_ref, start, activity_lanes, basis):
    frames = activity_lanes.shape[0]
    members = spectrum_ref.shape[0]
    groups = frames // (members * GROUP)
    stride = spectrum_ref.shape[1] // groups
    splits = [split_values(block) for block in basis]
    stacked = jnp.concatenate([jnp.concatenate([h, l, h, l], 0) for h, l in splits], 1)
    approx = dot(activity_lanes, stacked)
    values = jnp.concatenate(
        [
            jnp.stack(
                [
                    spectrum_ref[:, pl.ds(group * stride + (start + row) * GROUP, GROUP), :]
                    for group in range(groups)
                ],
                1,
            ).reshape(frames, LANES)
            for row in range(len(basis))
        ],
        1,
    )
    return values / approx, jnp.concatenate([jnp.concatenate([h, l], 0) for h, l in splits], 1)


def for_activity(ratio, basis):
    high, low = split_values(ratio)
    return dot_nt(high, basis) + dot_nt(low, basis)


def both_parts(values):
    half = values.shape[1] // 2
    return values + pltpu.roll(values, half, 1)


def row_sums(basis):
    return dot_nt(jnp.ones((16, basis.shape[1]), jnp.bfloat16), basis)


def row_steps(per_member, most=8):
    rows = math.gcd(per_member, most)
    return [range(start, start + rows) for start in range(0, per_member, rows)]


def packed(values):
    rows, width = values.shape
    lane = lax.broadcasted_iota(jnp.int32, (rows // 2, width), 1)
    return jnp.where(lane < width // 2, values[: rows // 2], values[rows // 2 :])


def unpacked(values):
    half = values.shape[1] // 2
    return jnp.concatenate([values[:, :half], values[:, half:]], 0)


def gathered_activity(rows_ref, shape):
    subs, members, ranks, width = shape
    local = width // subs
    frames_in = width // LANES
    pieces = {}
    for member in range(members):
        for part in range(frames_in):
            start = part * ranks
            rows = [rows_ref[sub * members + member, start : start + ranks, :] for sub in range(subs)]
            block = jnp.transpose(jnp.concatenate(rows, 0))
            for place in range(LANES // local):
                pieces[part * (LANES // local) + place, member] = block[place * local : (place + 1) * local]
    return jnp.concatenate([pieces[sub, member] for sub in range(subs) for member in range(members)], 0)


def start_fetches(received_ref, spectrum_ref, sem_ref, per_member, steps):
    count = spectrum_ref.shape[1]
    groups = count // (per_member * GROUP)
    copies = []
    for step, rows in enumerate(steps):
        copies.append([])
        for group in range(groups):
            place = pl.ds((group * per_member + rows[0]) * GROUP, len(rows) * GROUP)
            copies[-1].append(
                pltpu.make_async_copy(
                    received_ref.at[:, place, :], spectrum_ref.at[:, place, :], sem_ref.at[step * groups + group]
                )
            )
            copies[-1][-1].start()
    return copies


def first_kernel(
    shape,
    side_ref,
    received_ref,
    basis_ref,
    mine_ref,
    other_ref,
    activity_ref,
    spectrum_ref,
    lanes_ref,
    total_ref,
    rows_ref,
    rows_sem_ref,
    sem_ref,
):
    steps = row_steps(basis_ref.shape[0], 16)
    count = spectrum_ref.shape[1]
    rows_copy = pltpu.make_async_copy(
        received_ref.at[:, pl.ds(count, rows_ref.shape[1]), :], rows_ref, rows_sem_ref
    )
    rows_copy.start()
    copies = start_fetches(received_ref, spectrum_ref, sem_ref, basis_ref.shape[0], steps)
    rows_copy.wait()
    activity = gathered_activity(rows_ref, shape)
    activity_ref[...] = activity
    lanes_ref[...] = lanes_of_activity(activity)
    sums = 0.0
    for step, rows in enumerate(steps):
        for copy in copies[step]:
            copy.wait()
        ratio, basis = ratio_of(spectrum_ref, rows[0], lanes_ref[...], [basis_ref[row] for row in rows])
        part = for_activity(ratio, basis)
        if step == 0:
            total_ref[...] = part
        else:
            total_ref[...] += part
        sums += row_sums(basis)
    total = both_parts(total_ref[...])
    half = total.shape[0] // 2
    quarter = half // 2
    early, late = packed(total[:half]), packed(total[half:])
    first = side_ref[0] == 0
    mine_ref[:quarter, :] = jnp.where(first, early, late)
    other_ref[:quarter, :] = jnp.where(first, late, early)
    sums = both_parts(sums)[:8]
    mine_ref[quarter:, :] = sums
    other_ref[quarter:, :] = sums


def by_owner(values, shape):
    subs, members, ranks, width = shape
    local = width // subs
    blocks = []
    for member in range(members):
        rows = [
            values[(sub * members + member) * local : (sub * members + member + 1) * local]
            for sub in range(subs)
        ]
        blocks.append(jnp.transpose(jnp.concatenate(rows, 0)).reshape(subs, ranks, width))
    return blocks


def second_kernel(
    side_ref,
    spectrum_ref,
    basis_ref,
    activity_ref,
    mine_ref,
    other_ref,
    middle_ref,
    early_ref,
    late_ref,
    lanes_ref,
    turned_ref,
):
    rank = activity_ref.shape[1]
    quarter = activity_ref.shape[0] // 4
    first = side_ref[0] == 0
    mine = mine_ref[:quarter, :] / mine_ref[quarter : quarter + 1, :]
    other = other_ref[:quarter, :] / other_ref[quarter : quarter + 1, :]
    early, late = jnp.where(first, mine, other), jnp.where(first, other, mine)
    middle = activity_ref[...] * jnp.concatenate([unpacked(early), unpacked(late)], 0)
    middle_ref[...] = middle
    lanes_ref[...] = lanes_of_activity(middle)
    turned = jnp.transpose(middle)
    high, low = split_values(turned)
    turned_ref[...] = jnp.concatenate([high, low], 0)
    totals = jnp.sum(middle, axis=0, keepdims=True)
    totals = jnp.broadcast_to(jnp.concatenate([totals] * (LANES // rank), 1), (8, LANES))
    early_ref[early_ref.shape[0] - 8 :, :] = totals
    early_rows = early_ref.shape[0] // rank
    for rows in row_steps(basis_ref.shape[0]):
        ratio, _ = ratio_of(spectrum_ref, rows[0], lanes_ref[...], [basis_ref[row] for row in rows])
        high, low = split_values(ratio)
        total = dot(turned_ref[...], high) + dot(turned_ref[...], low)
        total = total[:rank] + total[rank:]
        for place, row in enumerate(rows):
            out_ref, start = (early_ref, row) if row < early_rows else (late_ref, row - early_rows)
            out_ref[start * rank : (start + 1) * rank, :] = total[:, place * LANES : (place + 1) * LANES]


def renew_and_add(rows, spectrum_ref, basis_ref, lanes_ref, scale, numerators, new_ref, total_ref, sums_ref):
    rank = basis_ref.shape[1]
    blocks = [
        basis_ref[row] * (sum(ref[place * rank : (place + 1) * rank, :] for ref in numerators) * scale)
        for place, row in enumerate(rows)
    ]
    for place, block in enumerate(blocks):
        new_ref[place] = block
    ratio, basis = ratio_of(spectrum_ref, rows[0], lanes_ref[...], blocks)
    total_ref[...] = for_activity(ratio, basis)
    sums_ref[...] = row_sums(basis)


def third_kernel(rows, later, received_ref, basis_ref, middle_ref, *rest):
    numerators = rest[:-7]
    new_ref, total_ref, sums_ref, lanes_ref, scale_ref, spectrum_ref, sem_ref = rest[-7:]
    rank = middle_ref.shape[1]
    copies = start_fetches(received_ref, spectrum_ref, sem_ref, basis_ref.shape[0], [rows, later])
    lanes_ref[...] = lanes_of_activity(middle_ref[...])
    totals = sum(ref[len(rows) * rank :, :] for ref in numerators)
    totals = jnp.transpose(jnp.concatenate([totals] * (LANES // 8), 0))[:rank]
    scale_ref[...] = 1.0 / totals
    for copy in copies[0]:
        copy.wait()
    renew_and_add(
        rows, spectrum_ref, basis_ref, lanes_ref, scale_ref[...], numerators, new_ref, total_ref, sums_ref
    )
    for copy in copies[1]:
        copy.wait()


def last_kernel(rows, spectrum_ref, basis_ref, lanes_ref, scale_ref, before_ref, sums_before_ref, *rest):
    numerators = rest[:-4]
    new_ref, out_ref, total_ref, sums_ref = rest[-4:]
    rank = basis_ref.shape[1]
    renew_and_add(
        rows, spectrum_ref, basis_ref, lanes_ref, scale_ref[...], numerators, new_ref, total_ref, sums_ref
    )
    total = both_parts(before_ref[...] + total_ref[...])[:, :rank]
    sums = both_parts(sums_before_ref[...] + sums_ref[...])
    subs, members, _, ranks, width = out_ref.shape
    sums = jnp.transpose(jnp.broadcast_to(sums[:1], (LANES, 2 * rank)))[:rank]
    sums = jnp.concatenate([sums] * (width // LANES), 1).reshape(subs, ranks, width)
    for member, block in enumerate(by_owner(total, (subs, members, ranks, width))):
        out_ref[:, member, 0] = block
        out_ref[:, member, 1] = sums


def update_call(kernel, spectrum, out_shapes, scratch, operands, scalars=(), place=pltpu.VMEM):
    in_vmem = pl.BlockSpec(memory_space=pltpu.VMEM)
    if place == pltpu.HBM:
        spectrum = pltpu.with_memory_space_constraint(spectrum, place)
    rank = operands[0].shape[1]
    return pl.pallas_call(
        kernel,
        in_specs=[pl.BlockSpec(memory_space=pltpu.SMEM) for _ in scalars]
        + [pl.BlockSpec(memory_space=place)]
        + [in_vmem for _ in operands],
        out_specs=[in_vmem for _ in out_shapes],
        out_shape=[
            shape if hasattr(shape, "dtype") else jax.ShapeDtypeStruct(shape, jnp.float32)
            for shape in out_shapes
        ],
        scratch_shapes=scratch,
        compiler_params=pltpu.CompilerParams(vmem_limit_bytes=UPDATE_VMEM),
        cost_estimate=pl.CostEstimate(
            flops=spectrum.size * rank * 16, bytes_accessed=spectrum.size * 4, transcendentals=0
        ),
    )(*scalars, spectrum, *operands)


def turned_lanes(values):
    return jnp.roll(jnp.flip(values, -1), 1, -1)


def swap_by(value, axis, mask):
    count = lax.axis_size(axis)
    return lax.ppermute(value, axis, [(i, i ^ mask) for i in range(count)])


def sum_over(value, axis, mask):
    count = lax.axis_size(axis)
    while mask < count:
        masks = [mask] if 2 * mask >= count else [mask, 2 * mask, 3 * mask]
        value = sum([swap_by(value, axis, m) for m in masks], value)
        mask *= 2 if len(masks) == 1 else 4
    return value


def on_device(signal, templates, activations):
    subs, groups, members = (lax.axis_size(axis) for axis in ("freq", "group", "member"))
    blocks = groups * members
    rank, bins_here = templates.shape
    ranks_here, width = activations.shape
    units_here = bins_here // LANES
    exchange = ("freq", "member")
    partners = subs * members
    per_member = units_here * groups
    me_sub, me_group, me_member = (lax.axis_index(axis) for axis in ("freq", "group", "member"))

    kept = units_of_member(units_here, range(groups))
    unit_order = tuple(
        units_here * (sub * blocks + group * members + member) + r
        for sub in range(subs)
        for member in range(members)
        for group, r in kept
    )

    samples = signal.reshape(-1, LANES)
    route = [
        (((sub + 1) % subs) * blocks + block + (sub + 1) // subs, sub * blocks + block)
        for sub in range(subs)
        for block in range(blocks)
        if block + (sub + 1) // subs < blocks
    ]
    trailing = lax.ppermute(samples[:HOP_ROWS], ("freq", "group", "member"), route)
    other = [swap_by(templates, "group", 1)] if groups == 2 else []
    own_rows = activations.reshape(ranks_here, width // LANES, LANES).transpose(1, 0, 2)
    own_rows = own_rows.reshape(ranks_here * width // LANES, LANES)
    spectrum = spectrum_blocks(samples, trailing, own_rows, unit_order, partners)
    spectrum, other = lax.optimization_barrier((spectrum, other))
    spectrum = lax.all_to_all(spectrum, exchange, 0, 0, tiled=True)
    local = width // subs
    frames = partners * local

    own = templates.reshape(rank, units_here, LANES).transpose(1, 0, 2)
    if other:
        remote = other[0].reshape(rank, units_here, LANES).transpose(1, 0, 2)
        by_group = jnp.where(me_group == 0, jnp.stack([own, remote]), jnp.stack([remote, own]))
    else:
        by_group = own[None]
    unit_index = units_here * (
        me_sub * blocks + jnp.arange(groups)[:, None] * members + me_member
    ) + jnp.arange(units_here)[None, :]
    is_turned = (unit_index % 2 == 1)[:, :, None, None]
    by_group = jnp.where(is_turned, turned_lanes(by_group), by_group)
    basis = jnp.concatenate([by_group[group, r][None] for group, r in kept], 0)

    lanes_scratch = pltpu.VMEM((frames, 4 * rank), jnp.bfloat16)
    total_scratch = pltpu.VMEM((frames, 2 * rank), jnp.float32)
    half_shape = (frames // 4 + 8, 2 * rank)
    side = (me_sub % 2).astype(jnp.int32).reshape(1)
    extra = ranks_here * width // LANES
    spectrum_rows = spectrum.shape[1] - extra
    row_groups = spectrum_rows // (per_member * GROUP)
    fetch_sems = pltpu.SemaphoreType.DMA((len(row_steps(per_member)) * row_groups,))
    received = spectrum
    mine, other, activity, spectrum = update_call(
        functools.partial(first_kernel, (subs, members, ranks_here, width)),
        received,
        [half_shape, half_shape, (frames, rank), (partners, spectrum_rows, LANES)],
        [
            lanes_scratch,
            total_scratch,
            pltpu.VMEM((partners, extra, LANES), jnp.float32),
            pltpu.SemaphoreType.DMA,
            fetch_sems,
        ],
        (basis,),
        (side,),
        pltpu.HBM,
    )
    mine = mine + swap_by(other, "freq", 1)
    mine = sum_over(mine, "freq", 2)
    mine = sum_over(mine, "member", 1)
    other = swap_by(mine, "freq", 1)

    early_rows = range(max(1, per_member // 2))
    late_rows = range(len(early_rows), per_member)
    middle, *numerators = update_call(
        second_kernel,
        spectrum,
        [(frames, rank), (len(early_rows) * rank + 8, LANES), (len(late_rows) * rank, LANES)],
        [lanes_scratch, pltpu.VMEM((2 * rank, frames), jnp.bfloat16)],
        (basis, activity, mine, other),
        (side,),
    )
    numerators = [[numerator] for numerator in numerators]
    if groups == 2:
        for numerator in numerators:
            numerator.append(swap_by(numerator[0], "group", 1))
    early_new, total, sums, lanes, scale, spectrum = update_call(
        functools.partial(third_kernel, early_rows, late_rows),
        received,
        [
            (len(early_rows), rank, LANES),
            (frames, 2 * rank),
            (16, 2 * rank),
            jax.ShapeDtypeStruct((frames, 4 * rank), jnp.bfloat16),
            (rank, LANES),
            (partners, spectrum_rows, LANES),
        ],
        [pltpu.SemaphoreType.DMA((2 * row_groups,))],
        (basis, middle, *numerators[0]),
        (),
        pltpu.HBM,
    )
    late_new, payload = update_call(
        functools.partial(last_kernel, late_rows),
        spectrum,
        [(len(late_rows), rank, LANES), (subs, members, 2, ranks_here, width)],
        [total_scratch, pltpu.VMEM((16, 2 * rank), jnp.float32)],
        (basis, lanes, scale, total, sums, *numerators[1]),
    )
    new_basis = [*early_new, *late_new]
    parts = lax.all_to_all(
        payload.reshape(partners, 2, ranks_here, width), exchange, 0, 0, tiled=True
    )
    summed = jnp.sum(parts, axis=0)
    mine = lax.dynamic_slice(
        middle.reshape(subs, members, local, rank),
        (0, me_member, 0, me_sub * ranks_here),
        (subs, 1, local, ranks_here),
    )
    mine = mine.reshape(width, ranks_here).T
    final_activations = mine * (summed[0] / summed[1])

    back = jnp.stack(
        [
            jnp.stack([new_basis[kept.index((group, r))] for r in range(units_here)])
            for group in range(groups)
        ]
    )
    back = lax.dynamic_index_in_dim(back, me_group, 0, keepdims=False)
    turned_here = lax.dynamic_index_in_dim(is_turned, me_group, 0, keepdims=False)
    back = jnp.where(turned_here, turned_lanes(back), back)
    final_templates = back.transpose(1, 0, 2).reshape(rank, bins_here)
    return (final_activations, final_templates)


def solution(mesh):
    subs, blocks = mesh.devices.shape
    groups = 2 if blocks % 2 == 0 else 1
    grid = Mesh(
        mesh.devices.reshape(subs, groups, blocks // groups), ("freq", "group", "member")
    )
    frames = ("group", "member")
    return jax.shard_map(
        on_device,
        mesh=grid,
        in_specs=(P(frames, "freq", None), P(None, ("freq", *frames)), P("freq", frames)),
        out_specs=(P("freq", frames), P(None, ("freq", *frames))),
        check_vma=False,
    )
```

```python
import functools
import math

import jax
import jax.numpy as jnp
import ml_dtypes
import numpy as np
from jax import lax
from jax.experimental import pallas as pl
from jax.experimental.pallas import tpu as pltpu
from jax.sharding import Mesh
from jax.sharding import PartitionSpec as P

FRAME_LEN = 65536
SPLIT = 256
LANES = 128
GROUP = 8
HOP_ROWS = FRAME_LEN // 2 // LANES
SPECTRUM_VMEM = 24 * 1024 * 1024
UPDATE_VMEM = 24 * 1024 * 1024
NT = (((1,), (1,)), ((), ()))


def high_low(values):
    high = values.astype(np.float32).astype(ml_dtypes.bfloat16)
    low = (values - high.astype(np.float64)).astype(ml_dtypes.bfloat16)
    return high, low


def both_parts_below(values):
    high, low = high_low(values)
    return np.concatenate([high, low], 0)


def units_of_member(units_here, member_blocks):
    order = list(range(units_here))
    if units_here % 8 == 0:
        order.sort(key=lambda r: (row_of_unit(r) % 2, r))
    kept = [(block, r) for block in member_blocks for r in order]
    if units_here % 8 == 0:
        kept.sort(key=lambda pair: row_of_unit(pair[1]) % 2)
    return kept


def row_of_unit(unit):
    return unit // 2 if unit % 2 == 0 else SPLIT - 1 - unit // 2


def lane_order():
    return np.concatenate([np.arange(0, SPLIT // 2, 2), np.arange(1, SPLIT // 2, 2)])


@functools.lru_cache(maxsize=None)
def tables(unit_order):
    half = SPLIT // 2
    index = np.arange(SPLIT, dtype=np.float64)
    slot = np.arange(half, dtype=np.float64)
    firsts = []
    for parity in range(2):
        angle = 2.0 * np.pi / SPLIT * np.mod(np.outer(lane_order()[parity * half // 2 :][: half // 2], slot), SPLIT)
        matrix = np.concatenate([np.cos(angle), -np.sin(angle)], 0)
        if parity == 0:
            matrix[half // 2] = np.cos(np.pi * slot)
        firsts.append(high_low(matrix))
    zeros = np.zeros_like(firsts[0][0])
    first = [np.concatenate([np.concatenate([part, part], 1) for part in parts], 0) for parts in firsts]
    first.append(np.block([[firsts[0][0], zeros], [zeros, firsts[1][0]]]))
    turn = 2.0 * np.pi / (SPLIT * SPLIT) * np.outer(lane_order(), index)
    twiddle_cos, twiddle_sin = np.cos(turn), np.sin(turn)
    masked_cos = twiddle_cos.copy()
    masked_cos[0] = 0.0
    twiddle = np.stack([twiddle_cos, twiddle_sin, masked_cos]).astype(np.float32)
    middle = 2.0 * np.pi / (SPLIT * SPLIT) * half * index
    odd = 2.0 * np.pi / SPLIT * slot
    rows = np.zeros((8, SPLIT), np.float32)
    rows[0], rows[1] = np.cos(middle), -np.sin(middle)
    rows[2, :half], rows[3, :half] = np.cos(odd), np.sin(odd)
    seconds, mirrored, places = [], [], []
    for parity in range(2):
        here = [place for place, unit in enumerate(unit_order) if row_of_unit(unit) % 2 == parity]
        turns = np.array([row_of_unit(unit_order[place]) // 2 for place in here])
        phase = 2.0 * np.pi / half * np.mod(np.outer(turns, np.arange(half)), half)
        c, s = np.cos(phase), np.sin(phase)
        seconds.append(
            both_parts_below(np.concatenate([np.concatenate([c, s], 1), np.concatenate([-s, c], 1)], 0))
        )
        flags = np.zeros((half, LANES), np.float32)
        flags[:, 0] = [unit_order[place] % 2 for place in here]
        mirrored.append(flags)
        places.append(tuple(here))
    position = np.arange(FRAME_LEN, dtype=np.float64)
    window = (0.5 - 0.5 * np.cos(2.0 * np.pi / FRAME_LEN * position)).astype(np.float32)
    window = window.reshape(SPLIT, 2, LANES).transpose(1, 0, 2)
    return (
        np.ascontiguousarray(window),
        np.stack(first),
        twiddle,
        rows,
        np.stack(seconds),
        np.stack(mirrored),
        tuple(places),
    )


def split_values(values):
    high = values.astype(jnp.bfloat16)
    low = (values - high.astype(jnp.float32)).astype(jnp.bfloat16)
    return high, low


def dot(left, right):
    return jnp.dot(left, right, preferred_element_type=jnp.float32)


def dot_nt(left, right):
    return lax.dot_general(left, right, NT, preferred_element_type=jnp.float32)


def transform_group(hop_rows, places, per_member, table_refs, out_ref, parts_ref, middle_ref, written=None):
    window_ref, first_ref, twiddle_ref, rows_ref, second_ref, mirrored_ref = table_refs
    half = SPLIT // 2
    middle_ref[...] = jnp.zeros_like(middle_ref)

    def even_odd(real, imag):
        even = jnp.concatenate([real[:, :half] + real[:, half:], imag[:, :half] + imag[:, half:]], 1)
        real = real[:, :half] - real[:, half:]
        imag = imag[:, :half] - imag[:, half:]
        c, s = rows_ref[2:3, :half], rows_ref[3:4, :half]
        odd = jnp.concatenate([real * c + imag * s, imag * c - real * s], 1)
        return even, odd

    def in_parts(values):
        return jnp.concatenate(split_values(values), 1)

    def second(parity, parts):
        both = dot_nt(second_ref[parity], parts[:, :SPLIT])
        return both[:SPLIT] + (both[SPLIT:] + dot_nt(second_ref[parity, :SPLIT, :], parts[:, SPLIT:]))

    for g in range(GROUP):
        top, bottom = (
            jnp.concatenate([hop_rows(g + hop, side) * window_ref[side, rows, :] for side in range(2)], 1)
            for hop, rows in enumerate((slice(0, half), slice(half, SPLIT)))
        )
        sections, rests = [], []
        for parity, values in enumerate((top + bottom, top - bottom)):
            high, low = split_values(values)
            rests.append(
                ((values - high.astype(jnp.float32)) - low.astype(jnp.float32)).astype(jnp.bfloat16)
            )
            sections.append(dot(first_ref[parity], jnp.concatenate([high, low], 0)))
        rest = dot(first_ref[2], jnp.concatenate(rests, 0))
        even, odd = (
            section[:half] + (section[half:] + rest[parity * half : (parity + 1) * half])
            for parity, section in enumerate(sections)
        )
        a = jnp.concatenate([even[: half // 2], odd[: half // 2]], 0)
        b = jnp.concatenate([even[half // 2 :], odd[half // 2 :]], 0)
        real = a * twiddle_ref[0] + b * twiddle_ref[1]
        imag = b * twiddle_ref[2] - a * twiddle_ref[1]
        for parity, values in enumerate(even_odd(real, imag)):
            parts_ref[parity, g * half : (g + 1) * half, :] = in_parts(values)
        nyquist = b[:1]
        for parity, values in enumerate(even_odd(nyquist * rows_ref[0:1], nyquist * rows_ref[1:2])):
            middle_ref[parity, g : g + 1, :] = values

    def magnitude(values):
        real, imag = values[:half], values[half:]
        return jnp.sqrt(real * real + imag * imag) * (8.0 / SPLIT)

    for parity in range(2):
        middle = magnitude(second(parity, in_parts(middle_ref[parity])))
        is_middle = mirrored_ref[parity] > 0.0
        for pair in range(GROUP // 2):
            values = magnitude(second(parity, parts_ref[parity, pair * SPLIT : (pair + 1) * SPLIT, :]))
            for lane in range(2):
                g = 2 * pair + lane
                block = jnp.where(
                    is_middle, middle[:, g : g + 1], values[:, lane * LANES : (lane + 1) * LANES]
                )
                start = 0
                while start < half:
                    stop = start + 1
                    place = places[parity][start]
                    while (
                        stop < half
                        and stop - start < 8
                        and places[parity][stop] == place + stop - start
                        and places[parity][stop] // per_member == place // per_member
                    ):
                        stop += 1
                    member, row = divmod(place, per_member)
                    out_ref[member, pl.ds(row * GROUP + g, stop - start, stride=GROUP), :] = block[start:stop]
                    start = stop
        if written is not None:
            written(parity)


def early_kernel(
    places, per_member, frames, samples_ref, *rest
):
    table_refs, (out_ref, tail_ref, group_ref) = rest[:6], rest[6:9]
    copies_ref, (hops_ref, parts_ref, middle_ref, sem_ref, out_sem_ref) = rest[9:15], rest[15:]
    groups = frames // GROUP - 1
    group_rows = GROUP * HOP_ROWS
    half = SPLIT // 2

    def fetch(first, count, slot):
        return pltpu.make_async_copy(
            samples_ref.at[pl.ds(first, count), :], hops_ref.at[pl.ds(first, count), :], sem_ref.at[slot]
        )

    tables_in = [
        pltpu.make_async_copy(table_refs[i], copies_ref[i], sem_ref.at[i]) for i in range(len(table_refs))
    ]
    lead = fetch(0, HOP_ROWS, 6)
    tail = pltpu.make_async_copy(
        samples_ref.at[pl.ds(groups * group_rows, group_rows), :], tail_ref, sem_ref.at[7]
    )
    hops = [fetch(HOP_ROWS + i * group_rows, group_rows, 8 + i) for i in range(groups)]
    for copy in [tables_in[1], lead, hops[0], *tables_in[:1], *tables_in[2:], *hops[1:], tail]:
        copy.start()
    lead.wait()
    for copy in tables_in:
        copy.wait()

    def body(i, carry):
        first = pl.multiple_of(i * group_rows, group_rows)
        pltpu.make_async_copy(
            samples_ref.at[pl.ds(HOP_ROWS + first, group_rows), :],
            hops_ref.at[pl.ds(HOP_ROWS + first, group_rows), :],
            sem_ref.at[8 + i],
        ).wait()

        transform_group(
            lambda hop, side: hops_ref[pl.ds(first + hop * HOP_ROWS + side, half, stride=2), :],
            places,
            per_member,
            copies_ref,
            group_ref.at[i],
            parts_ref,
            middle_ref,
        )

        @pl.when(i < groups - 1)
        def _():
            send(i).start()

        return carry

    def send(i):
        count = group_ref.shape[2]
        return pltpu.make_async_copy(
            group_ref.at[i],
            out_ref.at[:, pl.ds(pl.multiple_of(i * count, count), count), :],
            out_sem_ref.at[i],
        )

    lax.fori_loop(0, groups, body, 0)
    tail.wait()
    for i in range(groups - 1):
        send(i).wait()


def late_kernel(places, per_member, frames, done_ref, tail_ref, trailing_ref, activity_ref, *rest):
    table_refs, (_, out_ref, parts_ref, middle_ref, group_ref, sem_ref) = rest[:6], rest[6:]
    count = per_member * GROUP
    before = frames // GROUP - 1
    pass_on = pltpu.make_async_copy(
        done_ref.at[before - 1], out_ref.at[:, pl.ds((before - 1) * count, count), :], sem_ref.at[0]
    )
    pass_on.start()

    def hop_rows(hop, side):
        if hop == GROUP:
            return trailing_ref[pl.ds(side, SPLIT // 2, stride=2), :]
        return tail_ref[pl.ds(hop * HOP_ROWS + side, SPLIT // 2, stride=2), :]

    for member in range(out_ref.shape[0]):
        group_ref[member, count:, :] = activity_ref[...]
    bounds = [0, group_ref.shape[1]]
    if all(place % per_member < per_member // 2 for place in places[0]):
        bounds.insert(1, count // 2)
    sends = []

    def written(parity):
        if parity == 1 or len(bounds) == 3:
            first, last = bounds[len(sends)], bounds[len(sends) + 1]
            sends.append(
                pltpu.make_async_copy(
                    group_ref.at[:, pl.ds(first, last - first), :],
                    out_ref.at[:, pl.ds(before * count + first, last - first), :],
                    sem_ref.at[1 + len(sends)],
                )
            )
            sends[-1].start()

    transform_group(
        hop_rows,
        places,
        per_member,
        table_refs,
        group_ref,
        parts_ref,
        middle_ref,
        written,
    )
    pass_on.wait()
    for send in sends:
        send.wait()


def spectrum_blocks(samples, trailing, activity, unit_order, members):
    *values, places = tables(unit_order)
    per_member = SPLIT // members
    frames = samples.shape[0] // HOP_ROWS
    groups = frames // GROUP - 1
    constants = [jnp.asarray(t) for t in values]
    group_shape = (members, per_member * GROUP, LANES)
    last_shape = (members, per_member * GROUP + activity.shape[0], LANES)
    out_shape = pltpu.HBM((members, per_member * frames + activity.shape[0], LANES), jnp.float32)
    tail_shape = jax.ShapeDtypeStruct((GROUP * HOP_ROWS, LANES), jnp.float32)
    in_vmem = pl.BlockSpec(memory_space=pltpu.VMEM)
    in_hbm = pl.BlockSpec(memory_space=pltpu.HBM)
    scratch = [
        pltpu.VMEM((2, GROUP * LANES, 2 * SPLIT), jnp.bfloat16),
        pltpu.VMEM((2, 16, SPLIT), jnp.float32),
    ]

    def settings(count):
        return dict(
            compiler_params=pltpu.CompilerParams(vmem_limit_bytes=SPECTRUM_VMEM),
            cost_estimate=pl.CostEstimate(
                flops=count * GROUP * 6 * SPLIT * SPLIT * SPLIT * 2,
                bytes_accessed=count * GROUP * FRAME_LEN * 4,
                transcendentals=0,
            ),
        )

    early, tail, done, *copies = pl.pallas_call(
        functools.partial(early_kernel, places, per_member, frames),
        in_specs=[in_hbm] * (1 + len(constants)),
        out_specs=[in_hbm] + [in_vmem] * (2 + len(constants)),
        out_shape=[out_shape, tail_shape, jax.ShapeDtypeStruct((groups, *group_shape), jnp.float32)]
        + [jax.ShapeDtypeStruct(t.shape, t.dtype) for t in constants],
        scratch_shapes=[pltpu.VMEM(((groups * GROUP + 1) * HOP_ROWS, LANES), jnp.float32)]
        + scratch
        + [
            pltpu.SemaphoreType.DMA((8 + groups,)),
            pltpu.SemaphoreType.DMA((groups,)),
        ],
        **settings(groups),
    )(*[pltpu.with_memory_space_constraint(value, pltpu.HBM) for value in (samples, *constants)])
    return pl.pallas_call(
        functools.partial(late_kernel, places, per_member, frames),
        in_specs=[in_vmem] * (4 + len(constants)) + [in_hbm],
        out_specs=in_hbm,
        out_shape=out_shape,
        scratch_shapes=scratch + [pltpu.VMEM(last_shape, jnp.float32), pltpu.SemaphoreType.DMA((3,))],
        input_output_aliases={4 + len(constants): 0},
        **settings(1),
    )(done, tail, trailing, activity, *copies, early)


def lanes_of_activity(activity):
    high, low = split_values(activity)
    return jnp.concatenate([high, high, low, low], 1)


def ratio_of(spectrum_ref, start, activity_lanes, basis):
    frames = activity_lanes.shape[0]
    members = spectrum_ref.shape[0]
    groups = frames // (members * GROUP)
    stride = spectrum_ref.shape[1] // groups
    splits = [split_values(block) for block in basis]
    stacked = jnp.concatenate([jnp.concatenate([h, l, h, l], 0) for h, l in splits], 1)
    approx = dot(activity_lanes, stacked)
    values = jnp.concatenate(
        [
            jnp.stack(
                [
                    spectrum_ref[:, pl.ds(group * stride + (start + row) * GROUP, GROUP), :]
                    for group in range(groups)
                ],
                1,
            ).reshape(frames, LANES)
            for row in range(len(basis))
        ],
        1,
    )
    return values / approx, jnp.concatenate([jnp.concatenate([h, l], 0) for h, l in splits], 1)


def for_activity(ratio, basis):
    high, low = split_values(ratio)
    return dot_nt(high, basis) + dot_nt(low, basis)


def both_parts(values):
    half = values.shape[1] // 2
    return values + pltpu.roll(values, half, 1)


def row_sums(basis):
    return dot_nt(jnp.ones((16, basis.shape[1]), jnp.bfloat16), basis)


def row_steps(per_member, most=8):
    rows = math.gcd(per_member, most)
    return [range(start, start + rows) for start in range(0, per_member, rows)]


def packed(values):
    rows, width = values.shape
    lane = lax.broadcasted_iota(jnp.int32, (rows // 2, width), 1)
    return jnp.where(lane < width // 2, values[: rows // 2], values[rows // 2 :])


def unpacked(values):
    half = values.shape[1] // 2
    return jnp.concatenate([values[:, :half], values[:, half:]], 0)


def gathered_activity(rows_ref, shape):
    subs, members, ranks, width = shape
    local = width // subs
    frames_in = width // LANES
    pieces = {}
    for member in range(members):
        for part in range(frames_in):
            start = part * ranks
            rows = [rows_ref[sub * members + member, start : start + ranks, :] for sub in range(subs)]
            block = jnp.transpose(jnp.concatenate(rows, 0))
            for place in range(LANES // local):
                pieces[part * (LANES // local) + place, member] = block[place * local : (place + 1) * local]
    return jnp.concatenate([pieces[sub, member] for sub in range(subs) for member in range(members)], 0)


def start_fetches(received_ref, spectrum_ref, sem_ref, per_member, steps):
    count = spectrum_ref.shape[1]
    groups = count // (per_member * GROUP)
    copies = []
    for step, rows in enumerate(steps):
        copies.append([])
        for group in range(groups):
            place = pl.ds((group * per_member + rows[0]) * GROUP, len(rows) * GROUP)
            copies[-1].append(
                pltpu.make_async_copy(
                    received_ref.at[:, place, :], spectrum_ref.at[:, place, :], sem_ref.at[step * groups + group]
                )
            )
            copies[-1][-1].start()
    return copies


def first_kernel(
    shape,
    side_ref,
    received_ref,
    basis_ref,
    mine_ref,
    other_ref,
    activity_ref,
    spectrum_ref,
    lanes_ref,
    total_ref,
    rows_ref,
    rows_sem_ref,
    sem_ref,
):
    steps = row_steps(basis_ref.shape[0], 16)
    count = spectrum_ref.shape[1]
    rows_copy = pltpu.make_async_copy(
        received_ref.at[:, pl.ds(count, rows_ref.shape[1]), :], rows_ref, rows_sem_ref
    )
    rows_copy.start()
    copies = start_fetches(received_ref, spectrum_ref, sem_ref, basis_ref.shape[0], steps)
    rows_copy.wait()
    activity = gathered_activity(rows_ref, shape)
    activity_ref[...] = activity
    lanes_ref[...] = lanes_of_activity(activity)
    sums = 0.0
    for step, rows in enumerate(steps):
        for copy in copies[step]:
            copy.wait()
        ratio, basis = ratio_of(spectrum_ref, rows[0], lanes_ref[...], [basis_ref[row] for row in rows])
        part = for_activity(ratio, basis)
        if step == 0:
            total_ref[...] = part
        else:
            total_ref[...] += part
        sums += row_sums(basis)
    total = both_parts(total_ref[...])
    half = total.shape[0] // 2
    quarter = half // 2
    early, late = packed(total[:half]), packed(total[half:])
    first = side_ref[0] == 0
    mine_ref[:quarter, :] = jnp.where(first, early, late)
    other_ref[:quarter, :] = jnp.where(first, late, early)
    sums = both_parts(sums)[:8]
    mine_ref[quarter:, :] = sums
    other_ref[quarter:, :] = sums


def by_owner(values, shape):
    subs, members, ranks, width = shape
    local = width // subs
    blocks = []
    for member in range(members):
        rows = [
            values[(sub * members + member) * local : (sub * members + member + 1) * local]
            for sub in range(subs)
        ]
        blocks.append(jnp.transpose(jnp.concatenate(rows, 0)).reshape(subs, ranks, width))
    return blocks


def second_kernel(
    side_ref,
    spectrum_ref,
    basis_ref,
    activity_ref,
    mine_ref,
    other_ref,
    middle_ref,
    early_ref,
    late_ref,
    lanes_ref,
    turned_ref,
):
    rank = activity_ref.shape[1]
    quarter = activity_ref.shape[0] // 4
    first = side_ref[0] == 0
    mine = mine_ref[:quarter, :] / mine_ref[quarter : quarter + 1, :]
    other = other_ref[:quarter, :] / other_ref[quarter : quarter + 1, :]
    early, late = jnp.where(first, mine, other), jnp.where(first, other, mine)
    middle = activity_ref[...] * jnp.concatenate([unpacked(early), unpacked(late)], 0)
    middle_ref[...] = middle
    lanes_ref[...] = lanes_of_activity(middle)
    turned = jnp.transpose(middle)
    high, low = split_values(turned)
    turned_ref[...] = jnp.concatenate([high, low], 0)
    totals = jnp.sum(middle, axis=0, keepdims=True)
    totals = jnp.broadcast_to(jnp.concatenate([totals] * (LANES // rank), 1), (8, LANES))
    early_ref[early_ref.shape[0] - 8 :, :] = totals
    early_rows = early_ref.shape[0] // rank
    for rows in row_steps(basis_ref.shape[0]):
        ratio, _ = ratio_of(spectrum_ref, rows[0], lanes_ref[...], [basis_ref[row] for row in rows])
        high, low = split_values(ratio)
        total = dot(turned_ref[...], high) + dot(turned_ref[...], low)
        total = total[:rank] + total[rank:]
        for place, row in enumerate(rows):
            out_ref, start = (early_ref, row) if row < early_rows else (late_ref, row - early_rows)
            out_ref[start * rank : (start + 1) * rank, :] = total[:, place * LANES : (place + 1) * LANES]


def renew_and_add(rows, spectrum_ref, basis_ref, lanes_ref, scale, numerators, new_ref, total_ref, sums_ref):
    rank = basis_ref.shape[1]
    blocks = [
        basis_ref[row] * (sum(ref[place * rank : (place + 1) * rank, :] for ref in numerators) * scale)
        for place, row in enumerate(rows)
    ]
    for place, block in enumerate(blocks):
        new_ref[place] = block
    ratio, basis = ratio_of(spectrum_ref, rows[0], lanes_ref[...], blocks)
    total_ref[...] = for_activity(ratio, basis)
    sums_ref[...] = row_sums(basis)


def third_kernel(rows, later, received_ref, basis_ref, middle_ref, *rest):
    numerators = rest[:-7]
    new_ref, total_ref, sums_ref, lanes_ref, scale_ref, spectrum_ref, sem_ref = rest[-7:]
    rank = middle_ref.shape[1]
    copies = start_fetches(received_ref, spectrum_ref, sem_ref, basis_ref.shape[0], [rows, later])
    lanes_ref[...] = lanes_of_activity(middle_ref[...])
    totals = sum(ref[len(rows) * rank :, :] for ref in numerators)
    totals = jnp.transpose(jnp.concatenate([totals] * (LANES // 8), 0))[:rank]
    scale_ref[...] = 1.0 / totals
    for copy in copies[0]:
        copy.wait()
    renew_and_add(
        rows, spectrum_ref, basis_ref, lanes_ref, scale_ref[...], numerators, new_ref, total_ref, sums_ref
    )
    for copy in copies[1]:
        copy.wait()


def last_kernel(rows, spectrum_ref, basis_ref, lanes_ref, scale_ref, before_ref, sums_before_ref, *rest):
    numerators = rest[:-4]
    new_ref, out_ref, total_ref, sums_ref = rest[-4:]
    rank = basis_ref.shape[1]
    renew_and_add(
        rows, spectrum_ref, basis_ref, lanes_ref, scale_ref[...], numerators, new_ref, total_ref, sums_ref
    )
    total = both_parts(before_ref[...] + total_ref[...])[:, :rank]
    sums = both_parts(sums_before_ref[...] + sums_ref[...])
    subs, members, _, ranks, width = out_ref.shape
    sums = jnp.transpose(jnp.broadcast_to(sums[:1], (LANES, 2 * rank)))[:rank]
    sums = jnp.concatenate([sums] * (width // LANES), 1).reshape(subs, ranks, width)
    for member, block in enumerate(by_owner(total, (subs, members, ranks, width))):
        out_ref[:, member, 0] = block
        out_ref[:, member, 1] = sums


def update_call(kernel, spectrum, out_shapes, scratch, operands, scalars=(), place=pltpu.VMEM):
    in_vmem = pl.BlockSpec(memory_space=pltpu.VMEM)
    if place == pltpu.HBM:
        spectrum = pltpu.with_memory_space_constraint(spectrum, place)
    rank = operands[0].shape[1]
    return pl.pallas_call(
        kernel,
        in_specs=[pl.BlockSpec(memory_space=pltpu.SMEM) for _ in scalars]
        + [pl.BlockSpec(memory_space=place)]
        + [in_vmem for _ in operands],
        out_specs=[in_vmem for _ in out_shapes],
        out_shape=[
            shape if hasattr(shape, "dtype") else jax.ShapeDtypeStruct(shape, jnp.float32)
            for shape in out_shapes
        ],
        scratch_shapes=scratch,
        compiler_params=pltpu.CompilerParams(vmem_limit_bytes=UPDATE_VMEM),
        cost_estimate=pl.CostEstimate(
            flops=spectrum.size * rank * 16, bytes_accessed=spectrum.size * 4, transcendentals=0
        ),
    )(*scalars, spectrum, *operands)


def reorder(values, is_turned, back):
    order = lane_order()
    places = np.stack([order, -order % LANES])
    moves = np.zeros((2, LANES, LANES), np.float32)
    for move, place in zip(moves, places):
        move[place, np.arange(LANES)] = 1.0
    if back:
        moves = moves.transpose(0, 2, 1)
    moved = [
        lax.dot_general(
            values,
            jnp.asarray(move),
            (((values.ndim - 1,), (0,)), ((), ())),
            precision=lax.Precision.HIGHEST,
            preferred_element_type=jnp.float32,
        )
        for move in moves
    ]
    return jnp.where(is_turned, moved[1], moved[0])


def swap_by(value, axis, mask):
    count = lax.axis_size(axis)
    return lax.ppermute(value, axis, [(i, i ^ mask) for i in range(count)])


def sum_over(value, axis, mask):
    count = lax.axis_size(axis)
    while mask < count:
        masks = [mask] if 2 * mask >= count else [mask, 2 * mask, 3 * mask]
        value = sum([swap_by(value, axis, m) for m in masks], value)
        mask *= 2 if len(masks) == 1 else 4
    return value


def on_device(signal, templates, activations):
    subs, groups, members = (lax.axis_size(axis) for axis in ("freq", "group", "member"))
    blocks = groups * members
    rank, bins_here = templates.shape
    ranks_here, width = activations.shape
    units_here = bins_here // LANES
    exchange = ("freq", "member")
    partners = subs * members
    per_member = units_here * groups
    me_sub, me_group, me_member = (lax.axis_index(axis) for axis in ("freq", "group", "member"))

    kept = units_of_member(units_here, range(groups))
    unit_order = tuple(
        units_here * (sub * blocks + group * members + member) + r
        for sub in range(subs)
        for member in range(members)
        for group, r in kept
    )

    samples = signal.reshape(-1, LANES)
    route = [
        (((sub + 1) % subs) * blocks + block + (sub + 1) // subs, sub * blocks + block)
        for sub in range(subs)
        for block in range(blocks)
        if block + (sub + 1) // subs < blocks
    ]
    trailing = lax.ppermute(samples[:HOP_ROWS], ("freq", "group", "member"), route)
    other = [swap_by(templates, "group", 1)] if groups == 2 else []
    own_rows = activations.reshape(ranks_here, width // LANES, LANES).transpose(1, 0, 2)
    own_rows = own_rows.reshape(ranks_here * width // LANES, LANES)
    spectrum = spectrum_blocks(samples, trailing, own_rows, unit_order, partners)
    spectrum, other = lax.optimization_barrier((spectrum, other))
    spectrum = lax.all_to_all(spectrum, exchange, 0, 0, tiled=True)
    local = width // subs
    frames = partners * local

    own = templates.reshape(rank, units_here, LANES).transpose(1, 0, 2)
    if other:
        remote = other[0].reshape(rank, units_here, LANES).transpose(1, 0, 2)
        by_group = jnp.where(me_group == 0, jnp.stack([own, remote]), jnp.stack([remote, own]))
    else:
        by_group = own[None]
    unit_index = units_here * (
        me_sub * blocks + jnp.arange(groups)[:, None] * members + me_member
    ) + jnp.arange(units_here)[None, :]
    is_turned = (unit_index % 2 == 1)[:, :, None, None]
    by_group = reorder(by_group, is_turned, False)
    basis = jnp.concatenate([by_group[group, r][None] for group, r in kept], 0)

    lanes_scratch = pltpu.VMEM((frames, 4 * rank), jnp.bfloat16)
    total_scratch = pltpu.VMEM((frames, 2 * rank), jnp.float32)
    half_shape = (frames // 4 + 8, 2 * rank)
    side = (me_sub % 2).astype(jnp.int32).reshape(1)
    extra = ranks_here * width // LANES
    spectrum_rows = spectrum.shape[1] - extra
    row_groups = spectrum_rows // (per_member * GROUP)
    fetch_sems = pltpu.SemaphoreType.DMA((len(row_steps(per_member)) * row_groups,))
    received = spectrum
    mine, other, activity, spectrum = update_call(
        functools.partial(first_kernel, (subs, members, ranks_here, width)),
        received,
        [half_shape, half_shape, (frames, rank), (partners, spectrum_rows, LANES)],
        [
            lanes_scratch,
            total_scratch,
            pltpu.VMEM((partners, extra, LANES), jnp.float32),
            pltpu.SemaphoreType.DMA,
            fetch_sems,
        ],
        (basis,),
        (side,),
        pltpu.HBM,
    )
    mine = mine + swap_by(other, "freq", 1)
    mine = sum_over(mine, "freq", 2)
    mine = sum_over(mine, "member", 1)
    other = swap_by(mine, "freq", 1)

    early_rows = range(max(1, per_member // 2))
    late_rows = range(len(early_rows), per_member)
    middle, *numerators = update_call(
        second_kernel,
        spectrum,
        [(frames, rank), (len(early_rows) * rank + 8, LANES), (len(late_rows) * rank, LANES)],
        [lanes_scratch, pltpu.VMEM((2 * rank, frames), jnp.bfloat16)],
        (basis, activity, mine, other),
        (side,),
    )
    numerators = [[numerator] for numerator in numerators]
    if groups == 2:
        for numerator in numerators:
            numerator.append(swap_by(numerator[0], "group", 1))
    early_new, total, sums, lanes, scale, spectrum = update_call(
        functools.partial(third_kernel, early_rows, late_rows),
        received,
        [
            (len(early_rows), rank, LANES),
            (frames, 2 * rank),
            (16, 2 * rank),
            jax.ShapeDtypeStruct((frames, 4 * rank), jnp.bfloat16),
            (rank, LANES),
            (partners, spectrum_rows, LANES),
        ],
        [pltpu.SemaphoreType.DMA((2 * row_groups,))],
        (basis, middle, *numerators[0]),
        (),
        pltpu.HBM,
    )
    late_new, payload = update_call(
        functools.partial(last_kernel, late_rows),
        spectrum,
        [(len(late_rows), rank, LANES), (subs, members, 2, ranks_here, width)],
        [total_scratch, pltpu.VMEM((16, 2 * rank), jnp.float32)],
        (basis, lanes, scale, total, sums, *numerators[1]),
    )
    new_basis = [*early_new, *late_new]
    parts = lax.all_to_all(
        payload.reshape(partners, 2, ranks_here, width), exchange, 0, 0, tiled=True
    )
    summed = jnp.sum(parts, axis=0)
    mine = lax.dynamic_slice(
        middle.reshape(subs, members, local, rank),
        (0, me_member, 0, me_sub * ranks_here),
        (subs, 1, local, ranks_here),
    )
    mine = mine.reshape(width, ranks_here).T
    final_activations = mine * (summed[0] / summed[1])

    back = jnp.stack(
        [
            jnp.stack([new_basis[kept.index((group, r))] for r in range(units_here)])
            for group in range(groups)
        ]
    )
    back = lax.dynamic_index_in_dim(back, me_group, 0, keepdims=False)
    turned_here = lax.dynamic_index_in_dim(is_turned, me_group, 0, keepdims=False)
    back = reorder(back, turned_here, True)
    final_templates = back.transpose(1, 0, 2).reshape(rank, bins_here)
    return (final_activations, final_templates)


def solution(mesh):
    subs, blocks = mesh.devices.shape
    groups = 2 if blocks % 2 == 0 else 1
    grid = Mesh(
        mesh.devices.reshape(subs, groups, blocks // groups), ("freq", "group", "member")
    )
    frames = ("group", "member")
    return jax.shard_map(
        on_device,
        mesh=grid,
        in_specs=(P(frames, "freq", None), P(None, ("freq", *frames)), P("freq", frames)),
        out_specs=(P("freq", frames), P(None, ("freq", *frames))),
        check_vma=False,
    )
```

```python
import functools
import math

import jax
import jax.numpy as jnp
import ml_dtypes
import numpy as np
from jax import lax
from jax.experimental import pallas as pl
from jax.experimental.pallas import tpu as pltpu
from jax.sharding import Mesh
from jax.sharding import PartitionSpec as P

FRAME_LEN = 65536
SPLIT = 256
LANES = 128
GROUP = 8
SPARE = 8
HOP_ROWS = FRAME_LEN // 2 // LANES
SPECTRUM_VMEM = 24 * 1024 * 1024
UPDATE_VMEM = 24 * 1024 * 1024
NT = (((1,), (1,)), ((), ()))


def high_low(values):
    high = values.astype(np.float32).astype(ml_dtypes.bfloat16)
    low = (values - high.astype(np.float64)).astype(ml_dtypes.bfloat16)
    return high, low


def both_parts_below(values):
    high, low = high_low(values)
    return np.concatenate([high, low], 0)


def units_of_member(units_here, member_blocks):
    order = list(range(units_here))
    if units_here % 8 == 0:
        order.sort(key=lambda r: (row_of_unit(r) % 2, r))
    kept = [(block, r) for block in member_blocks for r in order]
    if units_here % 8 == 0:
        kept.sort(key=lambda pair: row_of_unit(pair[1]) % 2)
    return kept


def row_of_unit(unit):
    return unit // 2 if unit % 2 == 0 else SPLIT - 1 - unit // 2


def lane_order():
    return np.concatenate([np.arange(0, SPLIT // 2, 2), np.arange(1, SPLIT // 2, 2)])


@functools.lru_cache(maxsize=None)
def tables(unit_order):
    half = SPLIT // 2
    index = np.arange(SPLIT, dtype=np.float64)
    slot = np.arange(half, dtype=np.float64)
    firsts = []
    for parity in range(2):
        angle = 2.0 * np.pi / SPLIT * np.mod(np.outer(lane_order()[parity * half // 2 :][: half // 2], slot), SPLIT)
        matrix = np.concatenate([np.cos(angle), -np.sin(angle)], 0)
        if parity == 0:
            matrix[half // 2] = np.cos(np.pi * slot)
        firsts.append(high_low(matrix))
    zeros = np.zeros_like(firsts[0][0])
    first = [np.concatenate([np.concatenate([part, part], 1) for part in parts], 0) for parts in firsts]
    first.append(np.block([[firsts[0][0], zeros], [zeros, firsts[1][0]]]))
    turn = 2.0 * np.pi / (SPLIT * SPLIT) * np.outer(lane_order(), index)
    twiddle_cos, twiddle_sin = np.cos(turn), np.sin(turn)
    masked_cos = twiddle_cos.copy()
    masked_cos[0] = 0.0
    twiddle = np.stack([twiddle_cos, twiddle_sin, masked_cos]).astype(np.float32)
    middle = 2.0 * np.pi / (SPLIT * SPLIT) * half * index
    odd = 2.0 * np.pi / SPLIT * slot
    rows = np.zeros((8, SPLIT), np.float32)
    rows[0], rows[1] = np.cos(middle), -np.sin(middle)
    rows[2, :half], rows[3, :half] = np.cos(odd), np.sin(odd)
    seconds, mirrored, places = [], [], []
    for parity in range(2):
        here = [place for place, unit in enumerate(unit_order) if row_of_unit(unit) % 2 == parity]
        turns = np.array([row_of_unit(unit_order[place]) // 2 for place in here])
        phase = 2.0 * np.pi / half * np.mod(np.outer(turns, np.arange(half)), half)
        c, s = np.cos(phase), np.sin(phase)
        seconds.append(
            both_parts_below(np.concatenate([np.concatenate([c, s], 1), np.concatenate([-s, c], 1)], 0))
        )
        flags = np.zeros((half, LANES), np.float32)
        flags[:, 0] = [unit_order[place] % 2 for place in here]
        mirrored.append(flags)
        places.append(tuple(here))
    position = np.arange(FRAME_LEN, dtype=np.float64)
    window = (0.5 - 0.5 * np.cos(2.0 * np.pi / FRAME_LEN * position)).astype(np.float32)
    window = window.reshape(SPLIT, 2, LANES).transpose(1, 0, 2)
    return (
        np.ascontiguousarray(window),
        np.stack(first),
        twiddle,
        rows,
        np.stack(seconds),
        np.stack(mirrored),
        tuple(places),
    )


def split_values(values):
    high = values.astype(jnp.bfloat16)
    low = (values - high.astype(jnp.float32)).astype(jnp.bfloat16)
    return high, low


def dot(left, right):
    return jnp.dot(left, right, preferred_element_type=jnp.float32)


def dot_nt(left, right):
    return lax.dot_general(left, right, NT, preferred_element_type=jnp.float32)


def transform_group(hop_rows, places, per_member, table_refs, out_ref, parts_ref, middle_ref, written=None):
    window_ref, first_ref, twiddle_ref, rows_ref, second_ref, mirrored_ref = table_refs
    half = SPLIT // 2
    middle_ref[...] = jnp.zeros_like(middle_ref)

    def even_odd(real, imag):
        even = jnp.concatenate([real[:, :half] + real[:, half:], imag[:, :half] + imag[:, half:]], 1)
        real = real[:, :half] - real[:, half:]
        imag = imag[:, :half] - imag[:, half:]
        c, s = rows_ref[2:3, :half], rows_ref[3:4, :half]
        odd = jnp.concatenate([real * c + imag * s, imag * c - real * s], 1)
        return even, odd

    def in_parts(values):
        return jnp.concatenate(split_values(values), 1)

    def second(parity, parts):
        both = dot_nt(second_ref[parity], parts[:, :SPLIT])
        return both[:SPLIT] + (both[SPLIT:] + dot_nt(second_ref[parity, :SPLIT, :], parts[:, SPLIT:]))

    for g in range(GROUP):
        top, bottom = (
            jnp.concatenate([hop_rows(g + hop, side) * window_ref[side, rows, :] for side in range(2)], 1)
            for hop, rows in enumerate((slice(0, half), slice(half, SPLIT)))
        )
        sections, rests = [], []
        for parity, values in enumerate((top + bottom, top - bottom)):
            high, low = split_values(values)
            rests.append(
                ((values - high.astype(jnp.float32)) - low.astype(jnp.float32)).astype(jnp.bfloat16)
            )
            sections.append(dot(first_ref[parity], jnp.concatenate([high, low], 0)))
        rest = dot(first_ref[2], jnp.concatenate(rests, 0))
        even, odd = (
            section[:half] + (section[half:] + rest[parity * half : (parity + 1) * half])
            for parity, section in enumerate(sections)
        )
        a = jnp.concatenate([even[: half // 2], odd[: half // 2]], 0)
        b = jnp.concatenate([even[half // 2 :], odd[half // 2 :]], 0)
        real = a * twiddle_ref[0] + b * twiddle_ref[1]
        imag = b * twiddle_ref[2] - a * twiddle_ref[1]
        for parity, values in enumerate(even_odd(real, imag)):
            parts_ref[parity, g * half : (g + 1) * half, :] = in_parts(values)
        nyquist = b[:1]
        for parity, values in enumerate(even_odd(nyquist * rows_ref[0:1], nyquist * rows_ref[1:2])):
            middle_ref[parity, g : g + 1, :] = values

    def magnitude(values):
        real, imag = values[:half], values[half:]
        return jnp.sqrt(real * real + imag * imag) * (8.0 / SPLIT)

    for parity in range(2):
        middle = magnitude(second(parity, in_parts(middle_ref[parity])))
        is_middle = mirrored_ref[parity] > 0.0
        for pair in range(GROUP // 2):
            values = magnitude(second(parity, parts_ref[parity, pair * SPLIT : (pair + 1) * SPLIT, :]))
            for lane in range(2):
                g = 2 * pair + lane
                block = jnp.where(
                    is_middle, middle[:, g : g + 1], values[:, lane * LANES : (lane + 1) * LANES]
                )
                start = 0
                while start < half:
                    stop = start + 1
                    place = places[parity][start]
                    while (
                        stop < half
                        and stop - start < 8
                        and places[parity][stop] == place + stop - start
                        and places[parity][stop] // per_member == place // per_member
                    ):
                        stop += 1
                    member, row = divmod(place, per_member)
                    out_ref[member, pl.ds(row * GROUP + g, stop - start, stride=GROUP), :] = block[start:stop]
                    start = stop
        if written is not None:
            written(parity)


def early_kernel(
    places, per_member, frames, samples_ref, *rest
):
    table_refs, (out_ref, tail_ref, group_ref) = rest[:6], rest[6:9]
    copies_ref, (hops_ref, parts_ref, middle_ref, sem_ref, out_sem_ref) = rest[9:15], rest[15:]
    groups = frames // GROUP - 1
    group_rows = GROUP * HOP_ROWS
    half = SPLIT // 2

    def fetch(first, count, slot):
        return pltpu.make_async_copy(
            samples_ref.at[pl.ds(first, count), :], hops_ref.at[pl.ds(first, count), :], sem_ref.at[slot]
        )

    tables_in = [
        pltpu.make_async_copy(table_refs[i], copies_ref[i], sem_ref.at[i]) for i in range(len(table_refs))
    ]
    lead = fetch(0, HOP_ROWS, 6)
    tail = pltpu.make_async_copy(
        samples_ref.at[pl.ds(groups * group_rows, group_rows), :], tail_ref, sem_ref.at[7]
    )
    hops = [fetch(HOP_ROWS + i * group_rows, group_rows, 8 + i) for i in range(groups)]
    for copy in [tables_in[1], lead, hops[0], *tables_in[:1], *tables_in[2:], *hops[1:], tail]:
        copy.start()
    lead.wait()
    for copy in tables_in:
        copy.wait()

    def body(i, carry):
        first = pl.multiple_of(i * group_rows, group_rows)
        pltpu.make_async_copy(
            samples_ref.at[pl.ds(HOP_ROWS + first, group_rows), :],
            hops_ref.at[pl.ds(HOP_ROWS + first, group_rows), :],
            sem_ref.at[8 + i],
        ).wait()

        transform_group(
            lambda hop, side: hops_ref[pl.ds(first + hop * HOP_ROWS + side, half, stride=2), :],
            places,
            per_member,
            copies_ref,
            group_ref.at[i],
            parts_ref,
            middle_ref,
        )

        @pl.when(i < groups - 1)
        def _():
            send(i).start()

        return carry

    def send(i):
        count = per_member * GROUP
        return pltpu.make_async_copy(
            group_ref.at[i, :, pl.ds(0, count), :],
            out_ref.at[:, pl.ds(pl.multiple_of(i * count, count), count), :],
            out_sem_ref.at[i],
        )

    lax.fori_loop(0, groups, body, 0)
    tail.wait()
    for i in range(groups - 1):
        send(i).wait()


def late_kernel(places, per_member, frames, done_ref, tail_ref, trailing_ref, activity_ref, *rest):
    table_refs, (_, out_ref, parts_ref, middle_ref, group_ref, sem_ref) = rest[:6], rest[6:]
    count = per_member * GROUP
    before = frames // GROUP - 1
    pass_on = pltpu.make_async_copy(
        done_ref.at[before - 1, :, pl.ds(0, count), :], out_ref.at[:, pl.ds((before - 1) * count, count), :], sem_ref.at[0]
    )
    pass_on.start()

    def hop_rows(hop, side):
        if hop == GROUP:
            return trailing_ref[pl.ds(side, SPLIT // 2, stride=2), :]
        return tail_ref[pl.ds(hop * HOP_ROWS + side, SPLIT // 2, stride=2), :]

    for member in range(out_ref.shape[0]):
        group_ref[member, count:, :] = activity_ref[...]
    bounds = [0, group_ref.shape[1]]
    if all(place % per_member < per_member // 2 for place in places[0]):
        bounds.insert(1, count // 2)
    sends = []

    def written(parity):
        if parity == 1 or len(bounds) == 3:
            first, last = bounds[len(sends)], bounds[len(sends) + 1]
            sends.append(
                pltpu.make_async_copy(
                    group_ref.at[:, pl.ds(first, last - first), :],
                    out_ref.at[:, pl.ds(before * count + first, last - first), :],
                    sem_ref.at[1 + len(sends)],
                )
            )
            sends[-1].start()

    transform_group(
        hop_rows,
        places,
        per_member,
        table_refs,
        group_ref,
        parts_ref,
        middle_ref,
        written,
    )
    pass_on.wait()
    for send in sends:
        send.wait()


def spectrum_blocks(samples, trailing, activity, unit_order, members):
    *values, places = tables(unit_order)
    per_member = SPLIT // members
    frames = samples.shape[0] // HOP_ROWS
    groups = frames // GROUP - 1
    constants = [jnp.asarray(t) for t in values]
    group_shape = (members, per_member * GROUP + SPARE, LANES)
    last_shape = (members, per_member * GROUP + activity.shape[0], LANES)
    out_shape = pltpu.HBM((members, per_member * frames + activity.shape[0], LANES), jnp.float32)
    tail_shape = jax.ShapeDtypeStruct((GROUP * HOP_ROWS, LANES), jnp.float32)
    in_vmem = pl.BlockSpec(memory_space=pltpu.VMEM)
    in_hbm = pl.BlockSpec(memory_space=pltpu.HBM)
    scratch = [
        pltpu.VMEM((2, GROUP * LANES, 2 * SPLIT), jnp.bfloat16),
        pltpu.VMEM((2, 16, SPLIT), jnp.float32),
    ]

    def settings(count):
        return dict(
            compiler_params=pltpu.CompilerParams(vmem_limit_bytes=SPECTRUM_VMEM),
            cost_estimate=pl.CostEstimate(
                flops=count * GROUP * 6 * SPLIT * SPLIT * SPLIT * 2,
                bytes_accessed=count * GROUP * FRAME_LEN * 4,
                transcendentals=0,
            ),
        )

    early, tail, done, *copies = pl.pallas_call(
        functools.partial(early_kernel, places, per_member, frames),
        in_specs=[in_hbm] * (1 + len(constants)),
        out_specs=[in_hbm] + [in_vmem] * (2 + len(constants)),
        out_shape=[out_shape, tail_shape, jax.ShapeDtypeStruct((groups, *group_shape), jnp.float32)]
        + [jax.ShapeDtypeStruct(t.shape, t.dtype) for t in constants],
        scratch_shapes=[pltpu.VMEM(((groups * GROUP + 1) * HOP_ROWS + SPARE, LANES), jnp.float32)]
        + scratch
        + [
            pltpu.SemaphoreType.DMA((8 + groups,)),
            pltpu.SemaphoreType.DMA((groups,)),
        ],
        **settings(groups),
    )(*[pltpu.with_memory_space_constraint(value, pltpu.HBM) for value in (samples, *constants)])
    return pl.pallas_call(
        functools.partial(late_kernel, places, per_member, frames),
        in_specs=[in_vmem] * (4 + len(constants)) + [in_hbm],
        out_specs=in_hbm,
        out_shape=out_shape,
        scratch_shapes=scratch + [pltpu.VMEM(last_shape, jnp.float32), pltpu.SemaphoreType.DMA((3,))],
        input_output_aliases={4 + len(constants): 0},
        **settings(1),
    )(done, tail, trailing, activity, *copies, early)


def lanes_of_activity(activity):
    high, low = split_values(activity)
    return jnp.concatenate([high, high, low, low], 1)


def ratio_of(spectrum_ref, start, activity_lanes, basis):
    frames = activity_lanes.shape[0]
    members = spectrum_ref.shape[0]
    groups = frames // (members * GROUP)
    stride = spectrum_ref.shape[1] // groups
    splits = [split_values(block) for block in basis]
    stacked = jnp.concatenate([jnp.concatenate([h, l, h, l], 0) for h, l in splits], 1)
    approx = dot(activity_lanes, stacked)
    values = jnp.concatenate(
        [
            jnp.stack(
                [
                    spectrum_ref[:, pl.ds(group * stride + (start + row) * GROUP, GROUP), :]
                    for group in range(groups)
                ],
                1,
            ).reshape(frames, LANES)
            for row in range(len(basis))
        ],
        1,
    )
    return values / approx, jnp.concatenate([jnp.concatenate([h, l], 0) for h, l in splits], 1)


def for_activity(ratio, basis):
    high, low = split_values(ratio)
    return dot_nt(high, basis) + dot_nt(low, basis)


def both_parts(values):
    half = values.shape[1] // 2
    return values + pltpu.roll(values, half, 1)


def row_sums(basis):
    return dot_nt(jnp.ones((16, basis.shape[1]), jnp.bfloat16), basis)


def row_steps(per_member, most=8):
    rows = math.gcd(per_member, most)
    return [range(start, start + rows) for start in range(0, per_member, rows)]


def packed(values):
    rows, width = values.shape
    lane = lax.broadcasted_iota(jnp.int32, (rows // 2, width), 1)
    return jnp.where(lane < width // 2, values[: rows // 2], values[rows // 2 :])


def unpacked(values):
    half = values.shape[1] // 2
    return jnp.concatenate([values[:, :half], values[:, half:]], 0)


def gathered_activity(rows_ref, shape):
    subs, members, ranks, width = shape
    local = width // subs
    frames_in = width // LANES
    pieces = {}
    for member in range(members):
        for part in range(frames_in):
            start = part * ranks
            rows = [rows_ref[sub * members + member, start : start + ranks, :] for sub in range(subs)]
            block = jnp.transpose(jnp.concatenate(rows, 0))
            for place in range(LANES // local):
                pieces[part * (LANES // local) + place, member] = block[place * local : (place + 1) * local]
    return jnp.concatenate([pieces[sub, member] for sub in range(subs) for member in range(members)], 0)


def start_fetches(received_ref, spectrum_ref, sem_ref, per_member, steps):
    count = spectrum_ref.shape[1]
    groups = count // (per_member * GROUP)
    copies = []
    for step, rows in enumerate(steps):
        copies.append([])
        for group in range(groups):
            place = pl.ds((group * per_member + rows[0]) * GROUP, len(rows) * GROUP)
            copies[-1].append(
                pltpu.make_async_copy(
                    received_ref.at[:, place, :], spectrum_ref.at[:, place, :], sem_ref.at[step * groups + group]
                )
            )
            copies[-1][-1].start()
    return copies


def first_kernel(
    shape,
    side_ref,
    received_ref,
    basis_ref,
    mine_ref,
    other_ref,
    activity_ref,
    spectrum_ref,
    lanes_ref,
    total_ref,
    rows_ref,
    rows_sem_ref,
    sem_ref,
):
    steps = row_steps(basis_ref.shape[0], 16)
    count = spectrum_ref.shape[1]
    rows_copy = pltpu.make_async_copy(
        received_ref.at[:, pl.ds(count, rows_ref.shape[1]), :], rows_ref, rows_sem_ref
    )
    rows_copy.start()
    copies = start_fetches(received_ref, spectrum_ref, sem_ref, basis_ref.shape[0], steps)
    rows_copy.wait()
    activity = gathered_activity(rows_ref, shape)
    activity_ref[...] = activity
    lanes_ref[...] = lanes_of_activity(activity)
    sums = 0.0
    for step, rows in enumerate(steps):
        for copy in copies[step]:
            copy.wait()
        ratio, basis = ratio_of(spectrum_ref, rows[0], lanes_ref[...], [basis_ref[row] for row in rows])
        part = for_activity(ratio, basis)
        if step == 0:
            total_ref[...] = part
        else:
            total_ref[...] += part
        sums += row_sums(basis)
    total = both_parts(total_ref[...])
    half = total.shape[0] // 2
    quarter = half // 2
    early, late = packed(total[:half]), packed(total[half:])
    first = side_ref[0] == 0
    mine_ref[:quarter, :] = jnp.where(first, early, late)
    other_ref[:quarter, :] = jnp.where(first, late, early)
    sums = both_parts(sums)[:8]
    mine_ref[quarter:, :] = sums
    other_ref[quarter:, :] = sums


def by_owner(values, shape):
    subs, members, ranks, width = shape
    local = width // subs
    blocks = []
    for member in range(members):
        rows = [
            values[(sub * members + member) * local : (sub * members + member + 1) * local]
            for sub in range(subs)
        ]
        blocks.append(jnp.transpose(jnp.concatenate(rows, 0)).reshape(subs, ranks, width))
    return blocks


def second_kernel(
    side_ref,
    spectrum_ref,
    basis_ref,
    activity_ref,
    mine_ref,
    other_ref,
    middle_ref,
    early_ref,
    late_ref,
    lanes_ref,
    turned_ref,
):
    rank = activity_ref.shape[1]
    quarter = activity_ref.shape[0] // 4
    first = side_ref[0] == 0
    mine = mine_ref[:quarter, :] / mine_ref[quarter : quarter + 1, :]
    other = other_ref[:quarter, :] / other_ref[quarter : quarter + 1, :]
    early, late = jnp.where(first, mine, other), jnp.where(first, other, mine)
    middle = activity_ref[...] * jnp.concatenate([unpacked(early), unpacked(late)], 0)
    middle_ref[...] = middle
    lanes_ref[...] = lanes_of_activity(middle)
    turned = jnp.transpose(middle)
    high, low = split_values(turned)
    turned_ref[...] = jnp.concatenate([high, low], 0)
    totals = jnp.sum(middle, axis=0, keepdims=True)
    totals = jnp.broadcast_to(jnp.concatenate([totals] * (LANES // rank), 1), (8, LANES))
    early_ref[early_ref.shape[0] - 8 :, :] = totals
    early_rows = early_ref.shape[0] // rank
    for rows in row_steps(basis_ref.shape[0]):
        ratio, _ = ratio_of(spectrum_ref, rows[0], lanes_ref[...], [basis_ref[row] for row in rows])
        high, low = split_values(ratio)
        total = dot(turned_ref[...], high) + dot(turned_ref[...], low)
        total = total[:rank] + total[rank:]
        for place, row in enumerate(rows):
            out_ref, start = (early_ref, row) if row < early_rows else (late_ref, row - early_rows)
            out_ref[start * rank : (start + 1) * rank, :] = total[:, place * LANES : (place + 1) * LANES]


def renew_and_add(rows, spectrum_ref, basis_ref, lanes_ref, scale, numerators, new_ref, total_ref, sums_ref):
    rank = basis_ref.shape[1]
    blocks = [
        basis_ref[row] * (sum(ref[place * rank : (place + 1) * rank, :] for ref in numerators) * scale)
        for place, row in enumerate(rows)
    ]
    for place, block in enumerate(blocks):
        new_ref[place] = block
    ratio, basis = ratio_of(spectrum_ref, rows[0], lanes_ref[...], blocks)
    total_ref[...] = for_activity(ratio, basis)
    sums_ref[...] = row_sums(basis)


def third_kernel(rows, later, received_ref, basis_ref, middle_ref, *rest):
    numerators = rest[:-7]
    new_ref, total_ref, sums_ref, lanes_ref, scale_ref, spectrum_ref, sem_ref = rest[-7:]
    rank = middle_ref.shape[1]
    copies = start_fetches(received_ref, spectrum_ref, sem_ref, basis_ref.shape[0], [rows, later])
    lanes_ref[...] = lanes_of_activity(middle_ref[...])
    totals = sum(ref[len(rows) * rank :, :] for ref in numerators)
    totals = jnp.transpose(jnp.concatenate([totals] * (LANES // 8), 0))[:rank]
    scale_ref[...] = 1.0 / totals
    for copy in copies[0]:
        copy.wait()
    renew_and_add(
        rows, spectrum_ref, basis_ref, lanes_ref, scale_ref[...], numerators, new_ref, total_ref, sums_ref
    )
    for copy in copies[1]:
        copy.wait()


def last_kernel(rows, spectrum_ref, basis_ref, lanes_ref, scale_ref, before_ref, sums_before_ref, *rest):
    numerators = rest[:-4]
    new_ref, out_ref, total_ref, sums_ref = rest[-4:]
    rank = basis_ref.shape[1]
    renew_and_add(
        rows, spectrum_ref, basis_ref, lanes_ref, scale_ref[...], numerators, new_ref, total_ref, sums_ref
    )
    total = both_parts(before_ref[...] + total_ref[...])[:, :rank]
    sums = both_parts(sums_before_ref[...] + sums_ref[...])
    subs, members, _, ranks, width = out_ref.shape
    sums = jnp.transpose(jnp.broadcast_to(sums[:1], (LANES, 2 * rank)))[:rank]
    sums = jnp.concatenate([sums] * (width // LANES), 1).reshape(subs, ranks, width)
    for member, block in enumerate(by_owner(total, (subs, members, ranks, width))):
        out_ref[:, member, 0] = block
        out_ref[:, member, 1] = sums


def update_call(kernel, spectrum, out_shapes, scratch, operands, scalars=(), place=pltpu.VMEM):
    in_vmem = pl.BlockSpec(memory_space=pltpu.VMEM)
    if place == pltpu.HBM:
        spectrum = pltpu.with_memory_space_constraint(spectrum, place)
    rank = operands[0].shape[1]
    return pl.pallas_call(
        kernel,
        in_specs=[pl.BlockSpec(memory_space=pltpu.SMEM) for _ in scalars]
        + [pl.BlockSpec(memory_space=place)]
        + [in_vmem for _ in operands],
        out_specs=[in_vmem for _ in out_shapes],
        out_shape=[
            shape if hasattr(shape, "dtype") else jax.ShapeDtypeStruct(shape, jnp.float32)
            for shape in out_shapes
        ],
        scratch_shapes=scratch,
        compiler_params=pltpu.CompilerParams(vmem_limit_bytes=UPDATE_VMEM),
        cost_estimate=pl.CostEstimate(
            flops=spectrum.size * rank * 16, bytes_accessed=spectrum.size * 4, transcendentals=0
        ),
    )(*scalars, spectrum, *operands)


def reorder(values, is_turned, back):
    order = lane_order()
    places = np.stack([order, -order % LANES])
    moves = np.zeros((2, LANES, LANES), np.float32)
    for move, place in zip(moves, places):
        move[place, np.arange(LANES)] = 1.0
    if back:
        moves = moves.transpose(0, 2, 1)
    moved = [
        lax.dot_general(
            values,
            jnp.asarray(move),
            (((values.ndim - 1,), (0,)), ((), ())),
            precision=lax.Precision.HIGHEST,
            preferred_element_type=jnp.float32,
        )
        for move in moves
    ]
    return jnp.where(is_turned, moved[1], moved[0])


def swap_by(value, axis, mask):
    count = lax.axis_size(axis)
    return lax.ppermute(value, axis, [(i, i ^ mask) for i in range(count)])


def sum_over(value, axis, mask):
    count = lax.axis_size(axis)
    while mask < count:
        masks = [mask] if 2 * mask >= count else [mask, 2 * mask, 3 * mask]
        value = sum([swap_by(value, axis, m) for m in masks], value)
        mask *= 2 if len(masks) == 1 else 4
    return value


def on_device(signal, templates, activations):
    subs, groups, members = (lax.axis_size(axis) for axis in ("freq", "group", "member"))
    blocks = groups * members
    rank, bins_here = templates.shape
    ranks_here, width = activations.shape
    units_here = bins_here // LANES
    exchange = ("freq", "member")
    partners = subs * members
    per_member = units_here * groups
    me_sub, me_group, me_member = (lax.axis_index(axis) for axis in ("freq", "group", "member"))

    kept = units_of_member(units_here, range(groups))
    unit_order = tuple(
        units_here * (sub * blocks + group * members + member) + r
        for sub in range(subs)
        for member in range(members)
        for group, r in kept
    )

    samples = signal.reshape(-1, LANES)
    route = [
        (((sub + 1) % subs) * blocks + block + (sub + 1) // subs, sub * blocks + block)
        for sub in range(subs)
        for block in range(blocks)
        if block + (sub + 1) // subs < blocks
    ]
    trailing = lax.ppermute(samples[:HOP_ROWS], ("freq", "group", "member"), route)
    other = [swap_by(templates, "group", 1)] if groups == 2 else []
    own_rows = activations.reshape(ranks_here, width // LANES, LANES).transpose(1, 0, 2)
    own_rows = own_rows.reshape(ranks_here * width // LANES, LANES)
    spectrum = spectrum_blocks(samples, trailing, own_rows, unit_order, partners)
    spectrum, other = lax.optimization_barrier((spectrum, other))
    spectrum = lax.all_to_all(spectrum, exchange, 0, 0, tiled=True)
    local = width // subs
    frames = partners * local

    own = templates.reshape(rank, units_here, LANES).transpose(1, 0, 2)
    if other:
        remote = other[0].reshape(rank, units_here, LANES).transpose(1, 0, 2)
        by_group = jnp.where(me_group == 0, jnp.stack([own, remote]), jnp.stack([remote, own]))
    else:
        by_group = own[None]
    unit_index = units_here * (
        me_sub * blocks + jnp.arange(groups)[:, None] * members + me_member
    ) + jnp.arange(units_here)[None, :]
    is_turned = (unit_index % 2 == 1)[:, :, None, None]
    by_group = reorder(by_group, is_turned, False)
    basis = jnp.concatenate([by_group[group, r][None] for group, r in kept], 0)

    lanes_scratch = pltpu.VMEM((frames, 4 * rank), jnp.bfloat16)
    total_scratch = pltpu.VMEM((frames, 2 * rank), jnp.float32)
    half_shape = (frames // 4 + 8, 2 * rank)
    side = (me_sub % 2).astype(jnp.int32).reshape(1)
    extra = ranks_here * width // LANES
    spectrum_rows = spectrum.shape[1] - extra
    row_groups = spectrum_rows // (per_member * GROUP)
    fetch_sems = pltpu.SemaphoreType.DMA((len(row_steps(per_member)) * row_groups,))
    received = spectrum
    mine, other, activity, spectrum = update_call(
        functools.partial(first_kernel, (subs, members, ranks_here, width)),
        received,
        [half_shape, half_shape, (frames, rank), (partners, spectrum_rows, LANES)],
        [
            lanes_scratch,
            total_scratch,
            pltpu.VMEM((partners, extra, LANES), jnp.float32),
            pltpu.SemaphoreType.DMA,
            fetch_sems,
        ],
        (basis,),
        (side,),
        pltpu.HBM,
    )
    mine = mine + swap_by(other, "freq", 1)
    mine = sum_over(mine, "freq", 2)
    mine = sum_over(mine, "member", 1)
    other = swap_by(mine, "freq", 1)

    early_rows = range(max(1, per_member // 2))
    late_rows = range(len(early_rows), per_member)
    middle, *numerators = update_call(
        second_kernel,
        spectrum,
        [(frames, rank), (len(early_rows) * rank + 8, LANES), (len(late_rows) * rank, LANES)],
        [lanes_scratch, pltpu.VMEM((2 * rank, frames), jnp.bfloat16)],
        (basis, activity, mine, other),
        (side,),
    )
    numerators = [[numerator] for numerator in numerators]
    if groups == 2:
        for numerator in numerators:
            numerator.append(swap_by(numerator[0], "group", 1))
    early_new, total, sums, lanes, scale, spectrum = update_call(
        functools.partial(third_kernel, early_rows, late_rows),
        received,
        [
            (len(early_rows), rank, LANES),
            (frames, 2 * rank),
            (16, 2 * rank),
            jax.ShapeDtypeStruct((frames, 4 * rank), jnp.bfloat16),
            (rank, LANES),
            (partners, spectrum_rows, LANES),
        ],
        [pltpu.SemaphoreType.DMA((2 * row_groups,))],
        (basis, middle, *numerators[0]),
        (),
        pltpu.HBM,
    )
    late_new, payload = update_call(
        functools.partial(last_kernel, late_rows),
        spectrum,
        [(len(late_rows), rank, LANES), (subs, members, 2, ranks_here, width)],
        [total_scratch, pltpu.VMEM((16, 2 * rank), jnp.float32)],
        (basis, lanes, scale, total, sums, *numerators[1]),
    )
    new_basis = [*early_new, *late_new]
    parts = lax.all_to_all(
        payload.reshape(partners, 2, ranks_here, width), exchange, 0, 0, tiled=True
    )
    summed = jnp.sum(parts, axis=0)
    mine = lax.dynamic_slice(
        middle.reshape(subs, members, local, rank),
        (0, me_member, 0, me_sub * ranks_here),
        (subs, 1, local, ranks_here),
    )
    mine = mine.reshape(width, ranks_here).T
    final_activations = mine * (summed[0] / summed[1])

    back = jnp.stack(
        [
            jnp.stack([new_basis[kept.index((group, r))] for r in range(units_here)])
            for group in range(groups)
        ]
    )
    back = lax.dynamic_index_in_dim(back, me_group, 0, keepdims=False)
    turned_here = lax.dynamic_index_in_dim(is_turned, me_group, 0, keepdims=False)
    back = reorder(back, turned_here, True)
    final_templates = back.transpose(1, 0, 2).reshape(rank, bins_here)
    return (final_activations, final_templates)


def solution(mesh):
    subs, blocks = mesh.devices.shape
    groups = 2 if blocks % 2 == 0 else 1
    grid = Mesh(
        mesh.devices.reshape(subs, groups, blocks // groups), ("freq", "group", "member")
    )
    frames = ("group", "member")
    return jax.shard_map(
        on_device,
        mesh=grid,
        in_specs=(P(frames, "freq", None), P(None, ("freq", *frames)), P("freq", frames)),
        out_specs=(P("freq", frames), P(None, ("freq", *frames))),
        check_vma=False,
    )
```

```python
import functools
import math

import jax
import jax.numpy as jnp
import ml_dtypes
import numpy as np
from jax import lax
from jax.experimental import pallas as pl
from jax.experimental.pallas import tpu as pltpu
from jax.sharding import Mesh
from jax.sharding import PartitionSpec as P

FRAME_LEN = 65536
SPLIT = 256
LANES = 128
GROUP = 8
SPARE = 8
HOP_ROWS = FRAME_LEN // 2 // LANES
SPECTRUM_VMEM = 24 * 1024 * 1024
UPDATE_VMEM = 24 * 1024 * 1024
NT = (((1,), (1,)), ((), ()))


def high_low(values):
    high = values.astype(np.float32).astype(ml_dtypes.bfloat16)
    low = (values - high.astype(np.float64)).astype(ml_dtypes.bfloat16)
    return high, low


def both_parts_below(values):
    high, low = high_low(values)
    return np.concatenate([high, low], 0)


def units_of_member(units_here, member_blocks):
    order = list(range(units_here))
    if units_here % 8 == 0:
        order.sort(key=lambda r: (row_of_unit(r) % 2, r))
    kept = [(block, r) for block in member_blocks for r in order]
    if units_here % 8 == 0:
        kept.sort(key=lambda pair: row_of_unit(pair[1]) % 2)
    return kept


def row_of_unit(unit):
    return unit // 2 if unit % 2 == 0 else SPLIT - 1 - unit // 2


def lane_order():
    return np.concatenate([np.arange(0, SPLIT // 2, 2), np.arange(1, SPLIT // 2, 2)])


@functools.lru_cache(maxsize=None)
def tables(unit_order):
    half = SPLIT // 2
    index = np.arange(SPLIT, dtype=np.float64)
    slot = np.arange(half, dtype=np.float64)
    firsts = []
    for parity in range(2):
        angle = 2.0 * np.pi / SPLIT * np.mod(np.outer(lane_order()[parity * half // 2 :][: half // 2], slot), SPLIT)
        matrix = np.concatenate([np.cos(angle), -np.sin(angle)], 0)
        if parity == 0:
            matrix[half // 2] = np.cos(np.pi * slot)
        firsts.append(high_low(matrix))
    zeros = np.zeros_like(firsts[0][0])
    first = [np.concatenate([np.concatenate([part, part], 1) for part in parts], 0) for parts in firsts]
    first.append(np.block([[firsts[0][0], zeros], [zeros, firsts[1][0]]]))
    turn = 2.0 * np.pi / (SPLIT * SPLIT) * np.outer(lane_order(), index)
    twiddle_cos, twiddle_sin = np.cos(turn), np.sin(turn)
    masked_cos = twiddle_cos.copy()
    masked_cos[0] = 0.0
    twiddle = np.stack([twiddle_cos, twiddle_sin, masked_cos]).astype(np.float32)
    middle = 2.0 * np.pi / (SPLIT * SPLIT) * half * index
    odd = 2.0 * np.pi / SPLIT * slot
    rows = np.zeros((8, SPLIT), np.float32)
    rows[0], rows[1] = np.cos(middle), -np.sin(middle)
    rows[2, :half], rows[3, :half] = np.cos(odd), np.sin(odd)
    seconds, mirrored, places = [], [], []
    for parity in range(2):
        here = [place for place, unit in enumerate(unit_order) if row_of_unit(unit) % 2 == parity]
        turns = np.array([row_of_unit(unit_order[place]) // 2 for place in here])
        phase = 2.0 * np.pi / half * np.mod(np.outer(turns, np.arange(half)), half)
        c, s = np.cos(phase), np.sin(phase)
        seconds.append(
            both_parts_below(np.concatenate([np.concatenate([c, s], 1), np.concatenate([-s, c], 1)], 0))
        )
        flags = np.zeros((half, LANES), np.float32)
        flags[:, 0] = [unit_order[place] % 2 for place in here]
        mirrored.append(flags)
        places.append(tuple(here))
    position = np.arange(FRAME_LEN, dtype=np.float64)
    window = (0.5 - 0.5 * np.cos(2.0 * np.pi / FRAME_LEN * position)).astype(np.float32)
    window = window.reshape(SPLIT, 2, LANES).transpose(1, 0, 2)
    return (
        np.ascontiguousarray(window),
        np.stack(first),
        twiddle,
        rows,
        np.stack(seconds),
        np.stack(mirrored),
        tuple(places),
    )


def split_values(values):
    high = values.astype(jnp.bfloat16)
    low = (values - high.astype(jnp.float32)).astype(jnp.bfloat16)
    return high, low


def dot(left, right):
    return jnp.dot(left, right, preferred_element_type=jnp.float32)


def dot_nt(left, right):
    return lax.dot_general(left, right, NT, preferred_element_type=jnp.float32)


def transform_group(hop_rows, places, per_member, table_refs, out_ref, parts_ref, middle_ref, written=None):
    window_ref, first_ref, twiddle_ref, rows_ref, second_ref, mirrored_ref = table_refs
    half = SPLIT // 2
    middle_ref[...] = jnp.zeros_like(middle_ref)

    def even_odd(real, imag):
        even = jnp.concatenate([real[:, :half] + real[:, half:], imag[:, :half] + imag[:, half:]], 1)
        real = real[:, :half] - real[:, half:]
        imag = imag[:, :half] - imag[:, half:]
        c, s = rows_ref[2:3, :half], rows_ref[3:4, :half]
        odd = jnp.concatenate([real * c + imag * s, imag * c - real * s], 1)
        return even, odd

    def in_parts(values):
        return jnp.concatenate(split_values(values), 1)

    def second(parity, parts):
        both = dot_nt(second_ref[parity], parts[:, :SPLIT])
        return both[:SPLIT] + (both[SPLIT:] + dot_nt(second_ref[parity, :SPLIT, :], parts[:, SPLIT:]))

    for g in range(GROUP):
        top, bottom = (
            jnp.concatenate([hop_rows(g + hop, side) * window_ref[side, rows, :] for side in range(2)], 1)
            for hop, rows in enumerate((slice(0, half), slice(half, SPLIT)))
        )
        sections, rests = [], []
        for parity, values in enumerate((top + bottom, top - bottom)):
            high, low = split_values(values)
            rests.append(
                ((values - high.astype(jnp.float32)) - low.astype(jnp.float32)).astype(jnp.bfloat16)
            )
            sections.append(dot(first_ref[parity], jnp.concatenate([high, low], 0)))
        rest = dot(first_ref[2], jnp.concatenate(rests, 0))
        even, odd = (
            section[:half] + (section[half:] + rest[parity * half : (parity + 1) * half])
            for parity, section in enumerate(sections)
        )
        a = jnp.concatenate([even[: half // 2], odd[: half // 2]], 0)
        b = jnp.concatenate([even[half // 2 :], odd[half // 2 :]], 0)
        real = a * twiddle_ref[0] + b * twiddle_ref[1]
        imag = b * twiddle_ref[2] - a * twiddle_ref[1]
        for parity, values in enumerate(even_odd(real, imag)):
            parts_ref[parity, g * half : (g + 1) * half, :] = in_parts(values)
        nyquist = b[:1]
        for parity, values in enumerate(even_odd(nyquist * rows_ref[0:1], nyquist * rows_ref[1:2])):
            middle_ref[parity, g : g + 1, :] = values

    def magnitude(values):
        real, imag = values[:half], values[half:]
        return jnp.sqrt(real * real + imag * imag) * (8.0 / SPLIT)

    for parity in range(2):
        middle = magnitude(second(parity, in_parts(middle_ref[parity])))
        is_middle = mirrored_ref[parity] > 0.0
        for pair in range(GROUP // 2):
            values = magnitude(second(parity, parts_ref[parity, pair * SPLIT : (pair + 1) * SPLIT, :]))
            for lane in range(2):
                g = 2 * pair + lane
                block = jnp.where(
                    is_middle, middle[:, g : g + 1], values[:, lane * LANES : (lane + 1) * LANES]
                )
                start = 0
                while start < half:
                    stop = start + 1
                    place = places[parity][start]
                    while (
                        stop < half
                        and stop - start < 8
                        and places[parity][stop] == place + stop - start
                        and places[parity][stop] // per_member == place // per_member
                    ):
                        stop += 1
                    member, row = divmod(place, per_member)
                    out_ref[member, pl.ds(row * GROUP + g, stop - start, stride=GROUP), :] = block[start:stop]
                    start = stop
        if written is not None:
            written(parity)


def early_kernel(
    places, per_member, frames, samples_ref, *rest
):
    table_refs, (out_ref, tail_ref, group_ref) = rest[:6], rest[6:9]
    copies_ref, (hops_ref, parts_ref, middle_ref, sem_ref, out_sem_ref) = rest[9:15], rest[15:]
    groups = frames // GROUP - 1
    group_rows = GROUP * HOP_ROWS
    half = SPLIT // 2

    def fetch(first, count, slot):
        return pltpu.make_async_copy(
            samples_ref.at[pl.ds(first, count), :], hops_ref.at[pl.ds(first, count), :], sem_ref.at[slot]
        )

    tables_in = [
        pltpu.make_async_copy(table_refs[i], copies_ref[i], sem_ref.at[i]) for i in range(len(table_refs))
    ]
    lead = fetch(0, HOP_ROWS, 6)
    tail = pltpu.make_async_copy(
        samples_ref.at[pl.ds(groups * group_rows, group_rows), :], tail_ref, sem_ref.at[7]
    )
    hops = [fetch(HOP_ROWS + i * group_rows, group_rows, 8 + i) for i in range(groups)]
    for copy in [tables_in[1], lead, hops[0], *tables_in[:1], *tables_in[2:], *hops[1:], tail]:
        copy.start()
    lead.wait()
    for copy in tables_in:
        copy.wait()

    def body(i, carry):
        first = pl.multiple_of(i * group_rows, group_rows)
        pltpu.make_async_copy(
            samples_ref.at[pl.ds(HOP_ROWS + first, group_rows), :],
            hops_ref.at[pl.ds(HOP_ROWS + first, group_rows), :],
            sem_ref.at[8 + i],
        ).wait()

        transform_group(
            lambda hop, side: hops_ref[pl.ds(first + hop * HOP_ROWS + side, half, stride=2), :],
            places,
            per_member,
            copies_ref,
            group_ref.at[i],
            parts_ref,
            middle_ref,
        )

        @pl.when(i < groups - 1)
        def _():
            send(i).start()

        return carry

    def send(i):
        count = per_member * GROUP
        return pltpu.make_async_copy(
            group_ref.at[i, :, pl.ds(0, count), :],
            out_ref.at[:, pl.ds(pl.multiple_of(i * count, count), count), :],
            out_sem_ref.at[i],
        )

    lax.fori_loop(0, groups, body, 0)
    tail.wait()
    for i in range(groups - 1):
        send(i).wait()


def late_kernel(places, per_member, frames, done_ref, tail_ref, trailing_ref, activity_ref, *rest):
    table_refs, (_, out_ref, parts_ref, middle_ref, group_ref, sem_ref) = rest[:6], rest[6:]
    count = per_member * GROUP
    before = frames // GROUP - 1
    pass_on = pltpu.make_async_copy(
        done_ref.at[before - 1, :, pl.ds(0, count), :], out_ref.at[:, pl.ds((before - 1) * count, count), :], sem_ref.at[0]
    )
    pass_on.start()

    def hop_rows(hop, side):
        if hop == GROUP:
            return trailing_ref[pl.ds(side, SPLIT // 2, stride=2), :]
        return tail_ref[pl.ds(hop * HOP_ROWS + side, SPLIT // 2, stride=2), :]

    for member in range(out_ref.shape[0]):
        group_ref[member, count:, :] = activity_ref[...]
    bounds = [0, group_ref.shape[1]]
    if all(place % per_member < per_member // 2 for place in places[0]):
        bounds.insert(1, count // 2)
    sends = []

    def written(parity):
        if parity == 1 or len(bounds) == 3:
            first, last = bounds[len(sends)], bounds[len(sends) + 1]
            sends.append(
                pltpu.make_async_copy(
                    group_ref.at[:, pl.ds(first, last - first), :],
                    out_ref.at[:, pl.ds(before * count + first, last - first), :],
                    sem_ref.at[1 + len(sends)],
                )
            )
            sends[-1].start()

    transform_group(
        hop_rows,
        places,
        per_member,
        table_refs,
        group_ref,
        parts_ref,
        middle_ref,
        written,
    )
    pass_on.wait()
    for send in sends:
        send.wait()


def spectrum_blocks(samples, trailing, activity, unit_order, members):
    *values, places = tables(unit_order)
    per_member = SPLIT // members
    frames = samples.shape[0] // HOP_ROWS
    groups = frames // GROUP - 1
    constants = [jnp.asarray(t) for t in values]
    group_shape = (members, per_member * GROUP + SPARE, LANES)
    last_shape = (members, per_member * GROUP + activity.shape[0], LANES)
    out_shape = pltpu.HBM((members, per_member * frames + activity.shape[0], LANES), jnp.float32)
    tail_shape = jax.ShapeDtypeStruct((GROUP * HOP_ROWS, LANES), jnp.float32)
    in_vmem = pl.BlockSpec(memory_space=pltpu.VMEM)
    in_hbm = pl.BlockSpec(memory_space=pltpu.HBM)
    scratch = [
        pltpu.VMEM((2, GROUP * LANES, 2 * SPLIT), jnp.bfloat16),
        pltpu.VMEM((2, 16, SPLIT), jnp.float32),
    ]

    def settings(count):
        return dict(
            compiler_params=pltpu.CompilerParams(vmem_limit_bytes=SPECTRUM_VMEM),
            cost_estimate=pl.CostEstimate(
                flops=count * GROUP * 6 * SPLIT * SPLIT * SPLIT * 2,
                bytes_accessed=count * GROUP * FRAME_LEN * 4,
                transcendentals=0,
            ),
        )

    early, tail, done, *copies = pl.pallas_call(
        functools.partial(early_kernel, places, per_member, frames),
        in_specs=[in_hbm] * (1 + len(constants)),
        out_specs=[in_hbm] + [in_vmem] * (2 + len(constants)),
        out_shape=[out_shape, tail_shape, jax.ShapeDtypeStruct((groups, *group_shape), jnp.float32)]
        + [jax.ShapeDtypeStruct(t.shape, t.dtype) for t in constants],
        scratch_shapes=[pltpu.VMEM(((groups * GROUP + 1) * HOP_ROWS + SPARE, LANES), jnp.float32)]
        + scratch
        + [
            pltpu.SemaphoreType.DMA((8 + groups,)),
            pltpu.SemaphoreType.DMA((groups,)),
        ],
        **settings(groups),
    )(*[pltpu.with_memory_space_constraint(value, pltpu.HBM) for value in (samples, *constants)])
    return pl.pallas_call(
        functools.partial(late_kernel, places, per_member, frames),
        in_specs=[in_vmem] * (4 + len(constants)) + [in_hbm],
        out_specs=in_hbm,
        out_shape=out_shape,
        scratch_shapes=scratch + [pltpu.VMEM(last_shape, jnp.float32), pltpu.SemaphoreType.DMA((3,))],
        input_output_aliases={4 + len(constants): 0},
        **settings(1),
    )(done, tail, trailing, activity, *copies, early)


def lanes_of_activity(activity):
    high, low = split_values(activity)
    return jnp.concatenate([high, high, low, low], 1)


def ratio_of(spectrum_ref, start, activity_lanes, basis):
    frames = activity_lanes.shape[0]
    members = spectrum_ref.shape[0]
    groups = frames // (members * GROUP)
    stride = spectrum_ref.shape[1] // groups
    splits = [split_values(block) for block in basis]
    stacked = jnp.concatenate([jnp.concatenate([h, l, h, l], 0) for h, l in splits], 1)
    approx = dot(activity_lanes, stacked)
    values = jnp.concatenate(
        [
            jnp.stack(
                [
                    spectrum_ref[:, pl.ds(group * stride + (start + row) * GROUP, GROUP), :]
                    for group in range(groups)
                ],
                1,
            ).reshape(frames, LANES)
            for row in range(len(basis))
        ],
        1,
    )
    return values / approx, jnp.concatenate([jnp.concatenate([h, l], 0) for h, l in splits], 1)


def for_activity(ratio, basis):
    high, low = split_values(ratio)
    return dot_nt(high, basis) + dot_nt(low, basis)


def both_parts(values):
    half = values.shape[1] // 2
    return values + pltpu.roll(values, half, 1)


def row_sums(basis):
    return dot_nt(jnp.ones((16, basis.shape[1]), jnp.bfloat16), basis)


def row_steps(per_member, most=8):
    rows = math.gcd(per_member, most)
    return [range(start, start + rows) for start in range(0, per_member, rows)]


def packed(values):
    rows, width = values.shape
    lane = lax.broadcasted_iota(jnp.int32, (rows // 2, width), 1)
    return jnp.where(lane < width // 2, values[: rows // 2], values[rows // 2 :])


def unpacked(values):
    half = values.shape[1] // 2
    return jnp.concatenate([values[:, :half], values[:, half:]], 0)


def gathered_activity(rows_ref, shape):
    subs, members, ranks, width = shape
    local = width // subs
    frames_in = width // LANES
    pieces = {}
    for member in range(members):
        for part in range(frames_in):
            start = part * ranks
            rows = [rows_ref[sub * members + member, start : start + ranks, :] for sub in range(subs)]
            block = jnp.transpose(jnp.concatenate(rows, 0))
            for place in range(LANES // local):
                pieces[part * (LANES // local) + place, member] = block[place * local : (place + 1) * local]
    return jnp.concatenate([pieces[sub, member] for sub in range(subs) for member in range(members)], 0)


def start_fetches(received_ref, spectrum_ref, sem_ref, per_member, steps):
    count = spectrum_ref.shape[1]
    groups = count // (per_member * GROUP)
    copies = []
    for step, rows in enumerate(steps):
        copies.append([])
        for group in range(groups):
            place = pl.ds((group * per_member + rows[0]) * GROUP, len(rows) * GROUP)
            copies[-1].append(
                pltpu.make_async_copy(
                    received_ref.at[:, place, :], spectrum_ref.at[:, place, :], sem_ref.at[step * groups + group]
                )
            )
            copies[-1][-1].start()
    return copies


def first_kernel(
    shape,
    side_ref,
    received_ref,
    basis_ref,
    mine_ref,
    other_ref,
    activity_ref,
    spectrum_ref,
    lanes_ref,
    total_ref,
    rows_ref,
    rows_sem_ref,
    sem_ref,
):
    steps = row_steps(basis_ref.shape[0], 16)
    count = spectrum_ref.shape[1]
    rows_copy = pltpu.make_async_copy(
        received_ref.at[:, pl.ds(count, rows_ref.shape[1]), :], rows_ref, rows_sem_ref
    )
    rows_copy.start()
    copies = start_fetches(received_ref, spectrum_ref, sem_ref, basis_ref.shape[0], steps)
    rows_copy.wait()
    activity = gathered_activity(rows_ref, shape)
    activity_ref[...] = activity
    lanes_ref[...] = lanes_of_activity(activity)
    sums = 0.0
    for step, rows in enumerate(steps):
        for copy in copies[step]:
            copy.wait()
        ratio, basis = ratio_of(spectrum_ref, rows[0], lanes_ref[...], [basis_ref[row] for row in rows])
        part = for_activity(ratio, basis)
        if step == 0:
            total_ref[...] = part
        else:
            total_ref[...] += part
        sums += row_sums(basis)
    total = both_parts(total_ref[...])
    half = total.shape[0] // 2
    quarter = half // 2
    early, late = packed(total[:half]), packed(total[half:])
    first = side_ref[0] == 0
    mine_ref[:quarter, :] = jnp.where(first, early, late)
    other_ref[:quarter, :] = jnp.where(first, late, early)
    sums = both_parts(sums)[:8]
    mine_ref[quarter:, :] = sums
    other_ref[quarter:, :] = sums


def by_owner(values, shape):
    subs, members, ranks, width = shape
    local = width // subs
    blocks = []
    for member in range(members):
        rows = [
            values[(sub * members + member) * local : (sub * members + member + 1) * local]
            for sub in range(subs)
        ]
        blocks.append(jnp.transpose(jnp.concatenate(rows, 0)).reshape(subs, ranks, width))
    return blocks


def sums_for_basis(rows, spectrum_ref, basis_ref, lanes_ref, turned_ref, out_ref):
    rank = basis_ref.shape[1]
    ratio, _ = ratio_of(spectrum_ref, rows[0], lanes_ref[...], [basis_ref[row] for row in rows])
    high, low = split_values(ratio)
    total = dot(turned_ref[...], high) + dot(turned_ref[...], low)
    total = total[:rank] + total[rank:]
    for place in range(len(rows)):
        out_ref[place * rank : (place + 1) * rank, :] = total[:, place * LANES : (place + 1) * LANES]


def second_kernel(
    rows,
    side_ref,
    spectrum_ref,
    basis_ref,
    activity_ref,
    mine_ref,
    other_ref,
    middle_ref,
    early_ref,
    lanes_ref,
    turned_ref,
):
    rank = activity_ref.shape[1]
    quarter = activity_ref.shape[0] // 4
    first = side_ref[0] == 0
    mine = mine_ref[:quarter, :] / mine_ref[quarter : quarter + 1, :]
    other = other_ref[:quarter, :] / other_ref[quarter : quarter + 1, :]
    early, late = jnp.where(first, mine, other), jnp.where(first, other, mine)
    middle = activity_ref[...] * jnp.concatenate([unpacked(early), unpacked(late)], 0)
    middle_ref[...] = middle
    lanes_ref[...] = lanes_of_activity(middle)
    turned = jnp.transpose(middle)
    high, low = split_values(turned)
    turned_ref[...] = jnp.concatenate([high, low], 0)
    totals = jnp.sum(middle, axis=0, keepdims=True)
    totals = jnp.broadcast_to(jnp.concatenate([totals] * (LANES // rank), 1), (8, LANES))
    early_ref[early_ref.shape[0] - 8 :, :] = totals
    sums_for_basis(rows, spectrum_ref, basis_ref, lanes_ref, turned_ref, early_ref)


def second_late_kernel(rows, spectrum_ref, basis_ref, lanes_ref, turned_ref, late_ref):
    sums_for_basis(rows, spectrum_ref, basis_ref, lanes_ref, turned_ref, late_ref)


def renew_and_add(rows, spectrum_ref, basis_ref, lanes_ref, scale, numerators, new_ref, total_ref, sums_ref):
    rank = basis_ref.shape[1]
    blocks = [
        basis_ref[row] * (sum(ref[place * rank : (place + 1) * rank, :] for ref in numerators) * scale)
        for place, row in enumerate(rows)
    ]
    for place, block in enumerate(blocks):
        new_ref[place] = block
    ratio, basis = ratio_of(spectrum_ref, rows[0], lanes_ref[...], blocks)
    total_ref[...] = for_activity(ratio, basis)
    sums_ref[...] = row_sums(basis)


def third_kernel(rows, later, received_ref, basis_ref, middle_ref, *rest):
    numerators = rest[:-7]
    new_ref, total_ref, sums_ref, lanes_ref, scale_ref, spectrum_ref, sem_ref = rest[-7:]
    rank = middle_ref.shape[1]
    copies = start_fetches(received_ref, spectrum_ref, sem_ref, basis_ref.shape[0], [rows, later])
    lanes_ref[...] = lanes_of_activity(middle_ref[...])
    totals = sum(ref[len(rows) * rank :, :] for ref in numerators)
    totals = jnp.transpose(jnp.concatenate([totals] * (LANES // 8), 0))[:rank]
    scale_ref[...] = 1.0 / totals
    for copy in copies[0]:
        copy.wait()
    renew_and_add(
        rows, spectrum_ref, basis_ref, lanes_ref, scale_ref[...], numerators, new_ref, total_ref, sums_ref
    )
    for copy in copies[1]:
        copy.wait()


def last_kernel(rows, spectrum_ref, basis_ref, lanes_ref, scale_ref, before_ref, sums_before_ref, *rest):
    numerators = rest[:-4]
    new_ref, out_ref, total_ref, sums_ref = rest[-4:]
    rank = basis_ref.shape[1]
    renew_and_add(
        rows, spectrum_ref, basis_ref, lanes_ref, scale_ref[...], numerators, new_ref, total_ref, sums_ref
    )
    total = both_parts(before_ref[...] + total_ref[...])[:, :rank]
    sums = both_parts(sums_before_ref[...] + sums_ref[...])
    subs, members, _, ranks, width = out_ref.shape
    sums = jnp.transpose(jnp.broadcast_to(sums[:1], (LANES, 2 * rank)))[:rank]
    sums = jnp.concatenate([sums] * (width // LANES), 1).reshape(subs, ranks, width)
    for member, block in enumerate(by_owner(total, (subs, members, ranks, width))):
        out_ref[:, member, 0] = block
        out_ref[:, member, 1] = sums


def update_call(kernel, spectrum, out_shapes, scratch, operands, scalars=(), place=pltpu.VMEM):
    in_vmem = pl.BlockSpec(memory_space=pltpu.VMEM)
    if place == pltpu.HBM:
        spectrum = pltpu.with_memory_space_constraint(spectrum, place)
    rank = operands[0].shape[1]
    return pl.pallas_call(
        kernel,
        in_specs=[pl.BlockSpec(memory_space=pltpu.SMEM) for _ in scalars]
        + [pl.BlockSpec(memory_space=place)]
        + [in_vmem for _ in operands],
        out_specs=[in_vmem for _ in out_shapes],
        out_shape=[
            shape if hasattr(shape, "dtype") else jax.ShapeDtypeStruct(shape, jnp.float32)
            for shape in out_shapes
        ],
        scratch_shapes=scratch,
        compiler_params=pltpu.CompilerParams(vmem_limit_bytes=UPDATE_VMEM),
        cost_estimate=pl.CostEstimate(
            flops=spectrum.size * rank * 16, bytes_accessed=spectrum.size * 4, transcendentals=0
        ),
    )(*scalars, spectrum, *operands)


def reorder(values, is_turned, back):
    order = lane_order()
    places = np.stack([order, -order % LANES])
    moves = np.zeros((2, LANES, LANES), np.float32)
    for move, place in zip(moves, places):
        move[place, np.arange(LANES)] = 1.0
    if back:
        moves = moves.transpose(0, 2, 1)
    moved = [
        lax.dot_general(
            values,
            jnp.asarray(move),
            (((values.ndim - 1,), (0,)), ((), ())),
            precision=lax.Precision.HIGHEST,
            preferred_element_type=jnp.float32,
        )
        for move in moves
    ]
    return jnp.where(is_turned, moved[1], moved[0])


def swap_by(value, axis, mask):
    count = lax.axis_size(axis)
    return lax.ppermute(value, axis, [(i, i ^ mask) for i in range(count)])


def sum_over(value, axis, mask):
    count = lax.axis_size(axis)
    while mask < count:
        masks = [mask] if 2 * mask >= count else [mask, 2 * mask, 3 * mask]
        value = sum([swap_by(value, axis, m) for m in masks], value)
        mask *= 2 if len(masks) == 1 else 4
    return value


def on_device(signal, templates, activations):
    subs, groups, members = (lax.axis_size(axis) for axis in ("freq", "group", "member"))
    blocks = groups * members
    rank, bins_here = templates.shape
    ranks_here, width = activations.shape
    units_here = bins_here // LANES
    exchange = ("freq", "member")
    partners = subs * members
    per_member = units_here * groups
    me_sub, me_group, me_member = (lax.axis_index(axis) for axis in ("freq", "group", "member"))

    kept = units_of_member(units_here, range(groups))
    unit_order = tuple(
        units_here * (sub * blocks + group * members + member) + r
        for sub in range(subs)
        for member in range(members)
        for group, r in kept
    )

    samples = signal.reshape(-1, LANES)
    route = [
        (((sub + 1) % subs) * blocks + block + (sub + 1) // subs, sub * blocks + block)
        for sub in range(subs)
        for block in range(blocks)
        if block + (sub + 1) // subs < blocks
    ]
    trailing = lax.ppermute(samples[:HOP_ROWS], ("freq", "group", "member"), route)
    other = [swap_by(templates, "group", 1)] if groups == 2 else []
    own_rows = activations.reshape(ranks_here, width // LANES, LANES).transpose(1, 0, 2)
    own_rows = own_rows.reshape(ranks_here * width // LANES, LANES)
    spectrum = spectrum_blocks(samples, trailing, own_rows, unit_order, partners)
    spectrum, other = lax.optimization_barrier((spectrum, other))
    spectrum = lax.all_to_all(spectrum, exchange, 0, 0, tiled=True)
    local = width // subs
    frames = partners * local

    own = templates.reshape(rank, units_here, LANES).transpose(1, 0, 2)
    if other:
        remote = other[0].reshape(rank, units_here, LANES).transpose(1, 0, 2)
        by_group = jnp.where(me_group == 0, jnp.stack([own, remote]), jnp.stack([remote, own]))
    else:
        by_group = own[None]
    unit_index = units_here * (
        me_sub * blocks + jnp.arange(groups)[:, None] * members + me_member
    ) + jnp.arange(units_here)[None, :]
    is_turned = (unit_index % 2 == 1)[:, :, None, None]
    by_group = reorder(by_group, is_turned, False)
    basis = jnp.concatenate([by_group[group, r][None] for group, r in kept], 0)

    lanes_scratch = pltpu.VMEM((frames, 4 * rank), jnp.bfloat16)
    total_scratch = pltpu.VMEM((frames, 2 * rank), jnp.float32)
    half_shape = (frames // 4 + 8, 2 * rank)
    side = (me_sub % 2).astype(jnp.int32).reshape(1)
    extra = ranks_here * width // LANES
    spectrum_rows = spectrum.shape[1] - extra
    row_groups = spectrum_rows // (per_member * GROUP)
    fetch_sems = pltpu.SemaphoreType.DMA((len(row_steps(per_member)) * row_groups,))
    received = spectrum
    mine, other, activity, spectrum = update_call(
        functools.partial(first_kernel, (subs, members, ranks_here, width)),
        received,
        [half_shape, half_shape, (frames, rank), (partners, spectrum_rows, LANES)],
        [
            lanes_scratch,
            total_scratch,
            pltpu.VMEM((partners, extra, LANES), jnp.float32),
            pltpu.SemaphoreType.DMA,
            fetch_sems,
        ],
        (basis,),
        (side,),
        pltpu.HBM,
    )
    mine = mine + swap_by(other, "freq", 1)
    mine = sum_over(mine, "freq", 2)
    mine = sum_over(mine, "member", 1)
    other = swap_by(mine, "freq", 1)

    early_rows = range(max(1, per_member // 2))
    late_rows = range(len(early_rows), per_member)
    middle, early_sums, lanes, turned = update_call(
        functools.partial(second_kernel, early_rows),
        spectrum,
        [
            (frames, rank),
            (len(early_rows) * rank + 8, LANES),
            jax.ShapeDtypeStruct((frames, 4 * rank), jnp.bfloat16),
            jax.ShapeDtypeStruct((2 * rank, frames), jnp.bfloat16),
        ],
        [],
        (basis, activity, mine, other),
        (side,),
    )
    (late_sums,) = update_call(
        functools.partial(second_late_kernel, late_rows),
        spectrum,
        [(len(late_rows) * rank, LANES)],
        [],
        (basis, lanes, turned),
    )
    numerators = [early_sums, late_sums]
    numerators = [[numerator] for numerator in numerators]
    if groups == 2:
        for numerator in numerators:
            numerator.append(swap_by(numerator[0], "group", 1))
    early_new, total, sums, lanes, scale, spectrum = update_call(
        functools.partial(third_kernel, early_rows, late_rows),
        received,
        [
            (len(early_rows), rank, LANES),
            (frames, 2 * rank),
            (16, 2 * rank),
            jax.ShapeDtypeStruct((frames, 4 * rank), jnp.bfloat16),
            (rank, LANES),
            (partners, spectrum_rows, LANES),
        ],
        [pltpu.SemaphoreType.DMA((2 * row_groups,))],
        (basis, middle, *numerators[0]),
        (),
        pltpu.HBM,
    )
    late_new, payload = update_call(
        functools.partial(last_kernel, late_rows),
        spectrum,
        [(len(late_rows), rank, LANES), (subs, members, 2, ranks_here, width)],
        [total_scratch, pltpu.VMEM((16, 2 * rank), jnp.float32)],
        (basis, lanes, scale, total, sums, *numerators[1]),
    )
    new_basis = [*early_new, *late_new]
    parts = lax.all_to_all(
        payload.reshape(partners, 2, ranks_here, width), exchange, 0, 0, tiled=True
    )
    summed = jnp.sum(parts, axis=0)
    mine = lax.dynamic_slice(
        middle.reshape(subs, members, local, rank),
        (0, me_member, 0, me_sub * ranks_here),
        (subs, 1, local, ranks_here),
    )
    mine = mine.reshape(width, ranks_here).T
    final_activations = mine * (summed[0] / summed[1])

    back = jnp.stack(
        [
            jnp.stack([new_basis[kept.index((group, r))] for r in range(units_here)])
            for group in range(groups)
        ]
    )
    back = lax.dynamic_index_in_dim(back, me_group, 0, keepdims=False)
    turned_here = lax.dynamic_index_in_dim(is_turned, me_group, 0, keepdims=False)
    back = reorder(back, turned_here, True)
    final_templates = back.transpose(1, 0, 2).reshape(rank, bins_here)
    return (final_activations, final_templates)


def solution(mesh):
    subs, blocks = mesh.devices.shape
    groups = 2 if blocks % 2 == 0 else 1
    grid = Mesh(
        mesh.devices.reshape(subs, groups, blocks // groups), ("freq", "group", "member")
    )
    frames = ("group", "member")
    return jax.shard_map(
        on_device,
        mesh=grid,
        in_specs=(P(frames, "freq", None), P(None, ("freq", *frames)), P("freq", frames)),
        out_specs=(P("freq", frames), P(None, ("freq", *frames))),
        check_vma=False,
    )
```

```python
import functools
import math

import jax
import jax.numpy as jnp
import ml_dtypes
import numpy as np
from jax import lax
from jax.experimental import pallas as pl
from jax.experimental.pallas import tpu as pltpu
from jax.sharding import Mesh
from jax.sharding import PartitionSpec as P

FRAME_LEN = 65536
SPLIT = 256
LANES = 128
GROUP = 8
SPARE = 8
HOP_ROWS = FRAME_LEN // 2 // LANES
SPECTRUM_VMEM = 24 * 1024 * 1024
UPDATE_VMEM = 24 * 1024 * 1024
NT = (((1,), (1,)), ((), ()))


def high_low(values):
    high = values.astype(np.float32).astype(ml_dtypes.bfloat16)
    low = (values - high.astype(np.float64)).astype(ml_dtypes.bfloat16)
    return high, low


def both_parts_below(values):
    high, low = high_low(values)
    return np.concatenate([high, low], 0)


def units_of_member(units_here, member_blocks):
    order = list(range(units_here))
    if units_here % 8 == 0:
        order.sort(key=lambda r: (row_of_unit(r) % 2, r))
    kept = [(block, r) for block in member_blocks for r in order]
    if units_here % 8 == 0:
        kept.sort(key=lambda pair: row_of_unit(pair[1]) % 2)
    return kept


def row_of_unit(unit):
    return unit // 2 if unit % 2 == 0 else SPLIT - 1 - unit // 2


def lane_order():
    return np.concatenate([np.arange(0, SPLIT // 2, 2), np.arange(1, SPLIT // 2, 2)])


@functools.lru_cache(maxsize=None)
def tables(unit_order):
    half = SPLIT // 2
    index = np.arange(SPLIT, dtype=np.float64)
    slot = np.arange(half, dtype=np.float64)
    firsts = []
    for parity in range(2):
        angle = 2.0 * np.pi / SPLIT * np.mod(np.outer(lane_order()[parity * half // 2 :][: half // 2], slot), SPLIT)
        matrix = np.concatenate([np.cos(angle), -np.sin(angle)], 0)
        if parity == 0:
            matrix[half // 2] = np.cos(np.pi * slot)
        firsts.append(high_low(matrix))
    zeros = np.zeros_like(firsts[0][0])
    first = [np.concatenate([np.concatenate([part, part], 1) for part in parts], 0) for parts in firsts]
    first.append(np.block([[firsts[0][0], zeros], [zeros, firsts[1][0]]]))
    turn = 2.0 * np.pi / (SPLIT * SPLIT) * np.outer(lane_order(), index)
    twiddle_cos, twiddle_sin = np.cos(turn), np.sin(turn)
    masked_cos = twiddle_cos.copy()
    masked_cos[0] = 0.0
    twiddle = np.stack([twiddle_cos, twiddle_sin, masked_cos]).astype(np.float32)
    middle = 2.0 * np.pi / (SPLIT * SPLIT) * half * index
    odd = 2.0 * np.pi / SPLIT * slot
    rows = np.zeros((8, SPLIT), np.float32)
    rows[0], rows[1] = np.cos(middle), -np.sin(middle)
    rows[2, :half], rows[3, :half] = np.cos(odd), np.sin(odd)
    seconds, mirrored, places = [], [], []
    for parity in range(2):
        here = [place for place, unit in enumerate(unit_order) if row_of_unit(unit) % 2 == parity]
        turns = np.array([row_of_unit(unit_order[place]) // 2 for place in here])
        phase = 2.0 * np.pi / half * np.mod(np.outer(turns, np.arange(half)), half)
        c, s = np.cos(phase), np.sin(phase)
        seconds.append(
            both_parts_below(np.concatenate([np.concatenate([c, s], 1), np.concatenate([-s, c], 1)], 0))
        )
        flags = np.zeros((half, LANES), np.float32)
        flags[:, 0] = [unit_order[place] % 2 for place in here]
        mirrored.append(flags)
        places.append(tuple(here))
    position = np.arange(FRAME_LEN, dtype=np.float64)
    window = (0.5 - 0.5 * np.cos(2.0 * np.pi / FRAME_LEN * position)).astype(np.float32)
    window = window.reshape(SPLIT, 2, LANES).transpose(1, 0, 2)
    return (
        np.ascontiguousarray(window),
        np.stack(first),
        twiddle,
        rows,
        np.stack(seconds),
        np.stack(mirrored),
        tuple(places),
    )


def split_values(values):
    high = values.astype(jnp.bfloat16)
    low = (values - high.astype(jnp.float32)).astype(jnp.bfloat16)
    return high, low


def dot(left, right):
    return jnp.dot(left, right, preferred_element_type=jnp.float32)


def dot_nt(left, right):
    return lax.dot_general(left, right, NT, preferred_element_type=jnp.float32)


def transform_group(hop_rows, places, per_member, table_refs, out_ref, parts_ref, middle_ref, written=None):
    window_ref, first_ref, twiddle_ref, rows_ref, second_ref, mirrored_ref = table_refs
    half = SPLIT // 2
    middle_ref[...] = jnp.zeros_like(middle_ref)

    def even_odd(real, imag):
        even = jnp.concatenate([real[:, :half] + real[:, half:], imag[:, :half] + imag[:, half:]], 1)
        real = real[:, :half] - real[:, half:]
        imag = imag[:, :half] - imag[:, half:]
        c, s = rows_ref[2:3, :half], rows_ref[3:4, :half]
        odd = jnp.concatenate([real * c + imag * s, imag * c - real * s], 1)
        return even, odd

    def in_parts(values):
        return jnp.concatenate(split_values(values), 1)

    def second(parity, parts):
        both = dot_nt(second_ref[parity], parts[:, :SPLIT])
        return both[:SPLIT] + (both[SPLIT:] + dot_nt(second_ref[parity, :SPLIT, :], parts[:, SPLIT:]))

    for g in range(GROUP):
        top, bottom = (
            jnp.concatenate([hop_rows(g + hop, side) * window_ref[side, rows, :] for side in range(2)], 1)
            for hop, rows in enumerate((slice(0, half), slice(half, SPLIT)))
        )
        sections, rests = [], []
        for parity, values in enumerate((top + bottom, top - bottom)):
            high, low = split_values(values)
            rests.append(
                ((values - high.astype(jnp.float32)) - low.astype(jnp.float32)).astype(jnp.bfloat16)
            )
            sections.append(dot(first_ref[parity], jnp.concatenate([high, low], 0)))
        rest = dot(first_ref[2], jnp.concatenate(rests, 0))
        even, odd = (
            section[:half] + (section[half:] + rest[parity * half : (parity + 1) * half])
            for parity, section in enumerate(sections)
        )
        a = jnp.concatenate([even[: half // 2], odd[: half // 2]], 0)
        b = jnp.concatenate([even[half // 2 :], odd[half // 2 :]], 0)
        real = a * twiddle_ref[0] + b * twiddle_ref[1]
        imag = b * twiddle_ref[2] - a * twiddle_ref[1]
        for parity, values in enumerate(even_odd(real, imag)):
            parts_ref[parity, g * half : (g + 1) * half, :] = in_parts(values)
        nyquist = b[:1]
        for parity, values in enumerate(even_odd(nyquist * rows_ref[0:1], nyquist * rows_ref[1:2])):
            middle_ref[parity, g : g + 1, :] = values

    def magnitude(values):
        real, imag = values[:half], values[half:]
        return jnp.sqrt(real * real + imag * imag) * (8.0 / SPLIT)

    for parity in range(2):
        middle = magnitude(second(parity, in_parts(middle_ref[parity])))
        is_middle = mirrored_ref[parity] > 0.0
        for pair in range(GROUP // 2):
            values = magnitude(second(parity, parts_ref[parity, pair * SPLIT : (pair + 1) * SPLIT, :]))
            for lane in range(2):
                g = 2 * pair + lane
                block = jnp.where(
                    is_middle, middle[:, g : g + 1], values[:, lane * LANES : (lane + 1) * LANES]
                )
                start = 0
                while start < half:
                    stop = start + 1
                    place = places[parity][start]
                    while (
                        stop < half
                        and stop - start < 8
                        and places[parity][stop] == place + stop - start
                        and places[parity][stop] // per_member == place // per_member
                    ):
                        stop += 1
                    member, row = divmod(place, per_member)
                    out_ref[member, pl.ds(row * GROUP + g, stop - start, stride=GROUP), :] = block[start:stop]
                    start = stop
        if written is not None:
            written(parity)


def early_kernel(
    places, per_member, frames, samples_ref, *rest
):
    table_refs, (out_ref, tail_ref, group_ref) = rest[:6], rest[6:9]
    copies_ref, (hops_ref, parts_ref, middle_ref, sem_ref, out_sem_ref) = rest[9:15], rest[15:]
    groups = frames // GROUP - 1
    group_rows = GROUP * HOP_ROWS
    half = SPLIT // 2

    def fetch(first, count, slot):
        return pltpu.make_async_copy(
            samples_ref.at[pl.ds(first, count), :], hops_ref.at[pl.ds(first, count), :], sem_ref.at[slot]
        )

    tables_in = [
        pltpu.make_async_copy(table_refs[i], copies_ref[i], sem_ref.at[i]) for i in range(len(table_refs))
    ]
    lead = fetch(0, HOP_ROWS, 6)
    tail = pltpu.make_async_copy(
        samples_ref.at[pl.ds(groups * group_rows, group_rows), :], tail_ref, sem_ref.at[7]
    )
    hops = [fetch(HOP_ROWS + i * group_rows, group_rows, 8 + i) for i in range(groups)]
    for copy in [tables_in[1], lead, hops[0], *tables_in[:1], *tables_in[2:], *hops[1:], tail]:
        copy.start()
    lead.wait()
    for copy in tables_in:
        copy.wait()

    def body(i, carry):
        first = pl.multiple_of(i * group_rows, group_rows)
        pltpu.make_async_copy(
            samples_ref.at[pl.ds(HOP_ROWS + first, group_rows), :],
            hops_ref.at[pl.ds(HOP_ROWS + first, group_rows), :],
            sem_ref.at[8 + i],
        ).wait()

        transform_group(
            lambda hop, side: hops_ref[pl.ds(first + hop * HOP_ROWS + side, half, stride=2), :],
            places,
            per_member,
            copies_ref,
            group_ref.at[i],
            parts_ref,
            middle_ref,
        )

        @pl.when(i < groups - 1)
        def _():
            send(i).start()

        return carry

    def send(i):
        count = per_member * GROUP
        return pltpu.make_async_copy(
            group_ref.at[i, :, pl.ds(0, count), :],
            out_ref.at[:, pl.ds(pl.multiple_of(i * count, count), count), :],
            out_sem_ref.at[i],
        )

    lax.fori_loop(0, groups, body, 0)
    tail.wait()
    for i in range(groups - 1):
        send(i).wait()


def late_kernel(places, per_member, frames, done_ref, tail_ref, trailing_ref, activity_ref, *rest):
    table_refs, (_, out_ref, parts_ref, middle_ref, group_ref, sem_ref) = rest[:6], rest[6:]
    count = per_member * GROUP
    before = frames // GROUP - 1
    pass_on = pltpu.make_async_copy(
        done_ref.at[before - 1, :, pl.ds(0, count), :], out_ref.at[:, pl.ds((before - 1) * count, count), :], sem_ref.at[0]
    )
    pass_on.start()

    def hop_rows(hop, side):
        if hop == GROUP:
            return trailing_ref[pl.ds(side, SPLIT // 2, stride=2), :]
        return tail_ref[pl.ds(hop * HOP_ROWS + side, SPLIT // 2, stride=2), :]

    for member in range(out_ref.shape[0]):
        group_ref[member, count:, :] = activity_ref[...]
    bounds = [0, group_ref.shape[1]]
    if all(place % per_member < per_member // 2 for place in places[0]):
        bounds.insert(1, count // 2)
    sends = []

    def written(parity):
        if parity == 1 or len(bounds) == 3:
            first, last = bounds[len(sends)], bounds[len(sends) + 1]
            sends.append(
                pltpu.make_async_copy(
                    group_ref.at[:, pl.ds(first, last - first), :],
                    out_ref.at[:, pl.ds(before * count + first, last - first), :],
                    sem_ref.at[1 + len(sends)],
                )
            )
            sends[-1].start()

    transform_group(
        hop_rows,
        places,
        per_member,
        table_refs,
        group_ref,
        parts_ref,
        middle_ref,
        written,
    )
    pass_on.wait()
    for send in sends:
        send.wait()


def spectrum_blocks(samples, trailing, activity, unit_order, members):
    *values, places = tables(unit_order)
    per_member = SPLIT // members
    frames = samples.shape[0] // HOP_ROWS
    groups = frames // GROUP - 1
    constants = [jnp.asarray(t) for t in values]
    group_shape = (members, per_member * GROUP + SPARE, LANES)
    last_shape = (members, per_member * GROUP + activity.shape[0], LANES)
    out_shape = pltpu.HBM((members, per_member * frames + activity.shape[0], LANES), jnp.float32)
    tail_shape = jax.ShapeDtypeStruct((GROUP * HOP_ROWS, LANES), jnp.float32)
    in_vmem = pl.BlockSpec(memory_space=pltpu.VMEM)
    in_hbm = pl.BlockSpec(memory_space=pltpu.HBM)
    scratch = [
        pltpu.VMEM((2, GROUP * LANES, 2 * SPLIT), jnp.bfloat16),
        pltpu.VMEM((2, 16, SPLIT), jnp.float32),
    ]

    def settings(count):
        return dict(
            compiler_params=pltpu.CompilerParams(vmem_limit_bytes=SPECTRUM_VMEM),
            cost_estimate=pl.CostEstimate(
                flops=count * GROUP * 6 * SPLIT * SPLIT * SPLIT * 2,
                bytes_accessed=count * GROUP * FRAME_LEN * 4,
                transcendentals=0,
            ),
        )

    early, tail, done, *copies = pl.pallas_call(
        functools.partial(early_kernel, places, per_member, frames),
        in_specs=[in_hbm] * (1 + len(constants)),
        out_specs=[in_hbm] + [in_vmem] * (2 + len(constants)),
        out_shape=[out_shape, tail_shape, jax.ShapeDtypeStruct((groups, *group_shape), jnp.float32)]
        + [jax.ShapeDtypeStruct(t.shape, t.dtype) for t in constants],
        scratch_shapes=[pltpu.VMEM(((groups * GROUP + 1) * HOP_ROWS + SPARE, LANES), jnp.float32)]
        + scratch
        + [
            pltpu.SemaphoreType.DMA((8 + groups,)),
            pltpu.SemaphoreType.DMA((groups,)),
        ],
        **settings(groups),
    )(*[pltpu.with_memory_space_constraint(value, pltpu.HBM) for value in (samples, *constants)])
    return pl.pallas_call(
        functools.partial(late_kernel, places, per_member, frames),
        in_specs=[in_vmem] * (4 + len(constants)) + [in_hbm],
        out_specs=in_hbm,
        out_shape=out_shape,
        scratch_shapes=scratch + [pltpu.VMEM(last_shape, jnp.float32), pltpu.SemaphoreType.DMA((3,))],
        input_output_aliases={4 + len(constants): 0},
        **settings(1),
    )(done, tail, trailing, activity, *copies, early)


def lanes_of_activity(activity):
    high, low = split_values(activity)
    return jnp.concatenate([high, high, low, low], 1)


def ratio_of(spectrum_ref, start, activity_lanes, basis):
    frames = activity_lanes.shape[0]
    members = spectrum_ref.shape[0]
    groups = frames // (members * GROUP)
    stride = spectrum_ref.shape[1] // groups
    splits = [split_values(block) for block in basis]
    stacked = jnp.concatenate([jnp.concatenate([h, l, h, l], 0) for h, l in splits], 1)
    approx = dot(activity_lanes, stacked)
    values = jnp.concatenate(
        [
            jnp.stack(
                [
                    spectrum_ref[:, pl.ds(group * stride + (start + row) * GROUP, GROUP), :]
                    for group in range(groups)
                ],
                1,
            ).reshape(frames, LANES)
            for row in range(len(basis))
        ],
        1,
    )
    return values / approx, jnp.concatenate([jnp.concatenate([h, l], 0) for h, l in splits], 1)


def for_activity(ratio, basis):
    high, low = split_values(ratio)
    return dot_nt(high, basis) + dot_nt(low, basis)


def both_parts(values):
    half = values.shape[1] // 2
    return values + pltpu.roll(values, half, 1)


def row_sums(basis):
    return dot_nt(jnp.ones((16, basis.shape[1]), jnp.bfloat16), basis)


def row_steps(per_member, most=8):
    rows = math.gcd(per_member, most)
    return [range(start, start + rows) for start in range(0, per_member, rows)]


def packed(values):
    rows, width = values.shape
    lane = lax.broadcasted_iota(jnp.int32, (rows // 2, width), 1)
    return jnp.where(lane < width // 2, values[: rows // 2], values[rows // 2 :])


def unpacked(values):
    half = values.shape[1] // 2
    return jnp.concatenate([values[:, :half], values[:, half:]], 0)


def gathered_activity(rows_ref, shape):
    subs, members, ranks, width = shape
    local = width // subs
    frames_in = width // LANES
    pieces = {}
    for member in range(members):
        for part in range(frames_in):
            start = part * ranks
            rows = [rows_ref[sub * members + member, start : start + ranks, :] for sub in range(subs)]
            block = jnp.transpose(jnp.concatenate(rows, 0))
            for place in range(LANES // local):
                pieces[part * (LANES // local) + place, member] = block[place * local : (place + 1) * local]
    return jnp.concatenate([pieces[sub, member] for sub in range(subs) for member in range(members)], 0)


def start_fetches(received_ref, spectrum_ref, sem_ref, per_member, steps):
    count = spectrum_ref.shape[1]
    groups = count // (per_member * GROUP)
    copies = []
    for step, rows in enumerate(steps):
        copies.append([])
        for group in range(groups):
            place = pl.ds((group * per_member + rows[0]) * GROUP, len(rows) * GROUP)
            copies[-1].append(
                pltpu.make_async_copy(
                    received_ref.at[:, place, :], spectrum_ref.at[:, place, :], sem_ref.at[step * groups + group]
                )
            )
            copies[-1][-1].start()
    return copies


def first_kernel(
    shape,
    side_ref,
    received_ref,
    basis_ref,
    mine_ref,
    other_ref,
    activity_ref,
    spectrum_ref,
    lanes_ref,
    total_ref,
    rows_ref,
    rows_sem_ref,
    sem_ref,
):
    steps = row_steps(basis_ref.shape[0], 16)
    count = spectrum_ref.shape[1]
    rows_copy = pltpu.make_async_copy(
        received_ref.at[:, pl.ds(count, rows_ref.shape[1]), :], rows_ref, rows_sem_ref
    )
    rows_copy.start()
    copies = start_fetches(received_ref, spectrum_ref, sem_ref, basis_ref.shape[0], steps)
    rows_copy.wait()
    activity = gathered_activity(rows_ref, shape)
    activity_ref[...] = activity
    lanes_ref[...] = lanes_of_activity(activity)
    sums = 0.0
    for step, rows in enumerate(steps):
        for copy in copies[step]:
            copy.wait()
        ratio, basis = ratio_of(spectrum_ref, rows[0], lanes_ref[...], [basis_ref[row] for row in rows])
        part = for_activity(ratio, basis)
        if step == 0:
            total_ref[...] = part
        else:
            total_ref[...] += part
        sums += row_sums(basis)
    total = both_parts(total_ref[...])
    half = total.shape[0] // 2
    quarter = half // 2
    early, late = packed(total[:half]), packed(total[half:])
    first = side_ref[0] == 0
    mine_ref[:quarter, :] = jnp.where(first, early, late)
    other_ref[:quarter, :] = jnp.where(first, late, early)
    sums = both_parts(sums)[:8]
    mine_ref[quarter:, :] = sums
    other_ref[quarter:, :] = sums


def by_owner(values, shape):
    subs, members, ranks, width = shape
    local = width // subs
    blocks = []
    for member in range(members):
        rows = [
            values[(sub * members + member) * local : (sub * members + member + 1) * local]
            for sub in range(subs)
        ]
        blocks.append(jnp.transpose(jnp.concatenate(rows, 0)).reshape(subs, ranks, width))
    return blocks


def sums_for_basis(rows, spectrum_ref, basis_ref, lanes_ref, turned_ref, out_ref):
    rank = basis_ref.shape[1]
    ratio, _ = ratio_of(spectrum_ref, rows[0], lanes_ref[...], [basis_ref[row] for row in rows])
    high, low = split_values(ratio)
    total = dot(turned_ref[...], high) + dot(turned_ref[...], low)
    total = total[:rank] + total[rank:]
    for place in range(len(rows)):
        out_ref[place * rank : (place + 1) * rank, :] = total[:, place * LANES : (place + 1) * LANES]


def second_kernel(
    rows,
    side_ref,
    spectrum_ref,
    basis_ref,
    activity_ref,
    mine_ref,
    other_ref,
    middle_ref,
    early_ref,
    lanes_ref,
    turned_ref,
):
    rank = activity_ref.shape[1]
    quarter = activity_ref.shape[0] // 4
    first = side_ref[0] == 0
    mine = mine_ref[:quarter, :] / mine_ref[quarter : quarter + 1, :]
    other = other_ref[:quarter, :] / other_ref[quarter : quarter + 1, :]
    early, late = jnp.where(first, mine, other), jnp.where(first, other, mine)
    middle = activity_ref[...] * jnp.concatenate([unpacked(early), unpacked(late)], 0)
    middle_ref[...] = middle
    lanes_ref[...] = lanes_of_activity(middle)
    turned = jnp.transpose(middle)
    high, low = split_values(turned)
    turned_ref[...] = jnp.concatenate([high, low], 0)
    totals = jnp.sum(middle, axis=0, keepdims=True)
    totals = jnp.broadcast_to(jnp.concatenate([totals] * (LANES // rank), 1), (8, LANES))
    early_ref[early_ref.shape[0] - 8 :, :] = totals
    sums_for_basis(rows, spectrum_ref, basis_ref, lanes_ref, turned_ref, early_ref)


def second_late_kernel(rows, received_ref, basis_ref, lanes_ref, turned_ref, late_ref, spectrum_ref, sem_ref):
    for copy in start_fetches(received_ref, spectrum_ref, sem_ref, basis_ref.shape[0], [rows])[0]:
        copy.wait()
    sums_for_basis(rows, spectrum_ref, basis_ref, lanes_ref, turned_ref, late_ref)


def renew_and_add(rows, spectrum_ref, basis_ref, lanes_ref, scale, numerators, new_ref, total_ref, sums_ref):
    rank = basis_ref.shape[1]
    blocks = [
        basis_ref[row] * (sum(ref[place * rank : (place + 1) * rank, :] for ref in numerators) * scale)
        for place, row in enumerate(rows)
    ]
    for place, block in enumerate(blocks):
        new_ref[place] = block
    ratio, basis = ratio_of(spectrum_ref, rows[0], lanes_ref[...], blocks)
    total_ref[...] = for_activity(ratio, basis)
    sums_ref[...] = row_sums(basis)


def third_kernel(rows, later, received_ref, basis_ref, middle_ref, *rest):
    numerators = rest[:-7]
    new_ref, total_ref, sums_ref, lanes_ref, scale_ref, spectrum_ref, sem_ref = rest[-7:]
    rank = middle_ref.shape[1]
    copies = start_fetches(received_ref, spectrum_ref, sem_ref, basis_ref.shape[0], [rows, later])
    lanes_ref[...] = lanes_of_activity(middle_ref[...])
    totals = sum(ref[len(rows) * rank :, :] for ref in numerators)
    totals = jnp.transpose(jnp.concatenate([totals] * (LANES // 8), 0))[:rank]
    scale_ref[...] = 1.0 / totals
    for copy in copies[0]:
        copy.wait()
    renew_and_add(
        rows, spectrum_ref, basis_ref, lanes_ref, scale_ref[...], numerators, new_ref, total_ref, sums_ref
    )
    for copy in copies[1]:
        copy.wait()


def last_kernel(rows, spectrum_ref, basis_ref, lanes_ref, scale_ref, before_ref, sums_before_ref, *rest):
    numerators = rest[:-4]
    new_ref, out_ref, total_ref, sums_ref = rest[-4:]
    rank = basis_ref.shape[1]
    renew_and_add(
        rows, spectrum_ref, basis_ref, lanes_ref, scale_ref[...], numerators, new_ref, total_ref, sums_ref
    )
    total = both_parts(before_ref[...] + total_ref[...])[:, :rank]
    sums = both_parts(sums_before_ref[...] + sums_ref[...])
    subs, members, _, ranks, width = out_ref.shape
    sums = jnp.transpose(jnp.broadcast_to(sums[:1], (LANES, 2 * rank)))[:rank]
    sums = jnp.concatenate([sums] * (width // LANES), 1).reshape(subs, ranks, width)
    for member, block in enumerate(by_owner(total, (subs, members, ranks, width))):
        out_ref[:, member, 0] = block
        out_ref[:, member, 1] = sums


def update_call(kernel, spectrum, out_shapes, scratch, operands, scalars=(), place=pltpu.VMEM):
    in_vmem = pl.BlockSpec(memory_space=pltpu.VMEM)
    if place == pltpu.HBM:
        spectrum = pltpu.with_memory_space_constraint(spectrum, place)
    rank = operands[0].shape[1]
    return pl.pallas_call(
        kernel,
        in_specs=[pl.BlockSpec(memory_space=pltpu.SMEM) for _ in scalars]
        + [pl.BlockSpec(memory_space=place)]
        + [in_vmem for _ in operands],
        out_specs=[in_vmem for _ in out_shapes],
        out_shape=[
            shape if hasattr(shape, "dtype") else jax.ShapeDtypeStruct(shape, jnp.float32)
            for shape in out_shapes
        ],
        scratch_shapes=scratch,
        compiler_params=pltpu.CompilerParams(vmem_limit_bytes=UPDATE_VMEM),
        cost_estimate=pl.CostEstimate(
            flops=spectrum.size * rank * 16, bytes_accessed=spectrum.size * 4, transcendentals=0
        ),
    )(*scalars, spectrum, *operands)


def reorder(values, is_turned, back):
    order = lane_order()
    places = np.stack([order, -order % LANES])
    moves = np.zeros((2, LANES, LANES), np.float32)
    for move, place in zip(moves, places):
        move[place, np.arange(LANES)] = 1.0
    if back:
        moves = moves.transpose(0, 2, 1)
    moved = [
        lax.dot_general(
            values,
            jnp.asarray(move),
            (((values.ndim - 1,), (0,)), ((), ())),
            precision=lax.Precision.HIGHEST,
            preferred_element_type=jnp.float32,
        )
        for move in moves
    ]
    return jnp.where(is_turned, moved[1], moved[0])


def swap_by(value, axis, mask):
    count = lax.axis_size(axis)
    return lax.ppermute(value, axis, [(i, i ^ mask) for i in range(count)])


def sum_over(value, axis, mask):
    count = lax.axis_size(axis)
    while mask < count:
        masks = [mask] if 2 * mask >= count else [mask, 2 * mask, 3 * mask]
        value = sum([swap_by(value, axis, m) for m in masks], value)
        mask *= 2 if len(masks) == 1 else 4
    return value


def on_device(signal, templates, activations):
    subs, groups, members = (lax.axis_size(axis) for axis in ("freq", "group", "member"))
    blocks = groups * members
    rank, bins_here = templates.shape
    ranks_here, width = activations.shape
    units_here = bins_here // LANES
    exchange = ("freq", "member")
    partners = subs * members
    per_member = units_here * groups
    me_sub, me_group, me_member = (lax.axis_index(axis) for axis in ("freq", "group", "member"))

    kept = units_of_member(units_here, range(groups))
    unit_order = tuple(
        units_here * (sub * blocks + group * members + member) + r
        for sub in range(subs)
        for member in range(members)
        for group, r in kept
    )

    samples = signal.reshape(-1, LANES)
    route = [
        (((sub + 1) % subs) * blocks + block + (sub + 1) // subs, sub * blocks + block)
        for sub in range(subs)
        for block in range(blocks)
        if block + (sub + 1) // subs < blocks
    ]
    trailing = lax.ppermute(samples[:HOP_ROWS], ("freq", "group", "member"), route)
    other = [swap_by(templates, "group", 1)] if groups == 2 else []
    own_rows = activations.reshape(ranks_here, width // LANES, LANES).transpose(1, 0, 2)
    own_rows = own_rows.reshape(ranks_here * width // LANES, LANES)
    spectrum = spectrum_blocks(samples, trailing, own_rows, unit_order, partners)
    spectrum, other = lax.optimization_barrier((spectrum, other))
    spectrum = lax.all_to_all(spectrum, exchange, 0, 0, tiled=True)
    local = width // subs
    frames = partners * local

    own = templates.reshape(rank, units_here, LANES).transpose(1, 0, 2)
    if other:
        remote = other[0].reshape(rank, units_here, LANES).transpose(1, 0, 2)
        by_group = jnp.where(me_group == 0, jnp.stack([own, remote]), jnp.stack([remote, own]))
    else:
        by_group = own[None]
    unit_index = units_here * (
        me_sub * blocks + jnp.arange(groups)[:, None] * members + me_member
    ) + jnp.arange(units_here)[None, :]
    is_turned = (unit_index % 2 == 1)[:, :, None, None]
    by_group = reorder(by_group, is_turned, False)
    basis = jnp.concatenate([by_group[group, r][None] for group, r in kept], 0)

    lanes_scratch = pltpu.VMEM((frames, 4 * rank), jnp.bfloat16)
    total_scratch = pltpu.VMEM((frames, 2 * rank), jnp.float32)
    half_shape = (frames // 4 + 8, 2 * rank)
    side = (me_sub % 2).astype(jnp.int32).reshape(1)
    extra = ranks_here * width // LANES
    spectrum_rows = spectrum.shape[1] - extra
    row_groups = spectrum_rows // (per_member * GROUP)
    fetch_sems = pltpu.SemaphoreType.DMA((len(row_steps(per_member)) * row_groups,))
    received = spectrum
    mine, other, activity, spectrum = update_call(
        functools.partial(first_kernel, (subs, members, ranks_here, width)),
        received,
        [half_shape, half_shape, (frames, rank), (partners, spectrum_rows, LANES)],
        [
            lanes_scratch,
            total_scratch,
            pltpu.VMEM((partners, extra, LANES), jnp.float32),
            pltpu.SemaphoreType.DMA,
            fetch_sems,
        ],
        (basis,),
        (side,),
        pltpu.HBM,
    )
    mine = mine + swap_by(other, "freq", 1)
    mine = sum_over(mine, "freq", 2)
    mine = sum_over(mine, "member", 1)
    other = swap_by(mine, "freq", 1)

    early_rows = range(max(1, per_member // 2))
    late_rows = range(len(early_rows), per_member)
    middle, early_sums, lanes, turned = update_call(
        functools.partial(second_kernel, early_rows),
        spectrum,
        [
            (frames, rank),
            (len(early_rows) * rank + 8, LANES),
            jax.ShapeDtypeStruct((frames, 4 * rank), jnp.bfloat16),
            jax.ShapeDtypeStruct((2 * rank, frames), jnp.bfloat16),
        ],
        [],
        (basis, activity, mine, other),
        (side,),
    )
    (late_sums,) = update_call(
        functools.partial(second_late_kernel, late_rows),
        received,
        [(len(late_rows) * rank, LANES)],
        [
            pltpu.VMEM((partners, spectrum_rows, LANES), jnp.float32),
            pltpu.SemaphoreType.DMA((row_groups,)),
        ],
        (basis, lanes, turned),
        (),
        pltpu.HBM,
    )
    numerators = [early_sums, late_sums]
    numerators = [[numerator] for numerator in numerators]
    if groups == 2:
        for numerator in numerators:
            numerator.append(swap_by(numerator[0], "group", 1))
    early_new, total, sums, lanes, scale, spectrum = update_call(
        functools.partial(third_kernel, early_rows, late_rows),
        received,
        [
            (len(early_rows), rank, LANES),
            (frames, 2 * rank),
            (16, 2 * rank),
            jax.ShapeDtypeStruct((frames, 4 * rank), jnp.bfloat16),
            (rank, LANES),
            (partners, spectrum_rows, LANES),
        ],
        [pltpu.SemaphoreType.DMA((2 * row_groups,))],
        (basis, middle, *numerators[0]),
        (),
        pltpu.HBM,
    )
    late_new, payload = update_call(
        functools.partial(last_kernel, late_rows),
        spectrum,
        [(len(late_rows), rank, LANES), (subs, members, 2, ranks_here, width)],
        [total_scratch, pltpu.VMEM((16, 2 * rank), jnp.float32)],
        (basis, lanes, scale, total, sums, *numerators[1]),
    )
    new_basis = [*early_new, *late_new]
    parts = lax.all_to_all(
        payload.reshape(partners, 2, ranks_here, width), exchange, 0, 0, tiled=True
    )
    summed = jnp.sum(parts, axis=0)
    mine = lax.dynamic_slice(
        middle.reshape(subs, members, local, rank),
        (0, me_member, 0, me_sub * ranks_here),
        (subs, 1, local, ranks_here),
    )
    mine = mine.reshape(width, ranks_here).T
    final_activations = mine * (summed[0] / summed[1])

    back = jnp.stack(
        [
            jnp.stack([new_basis[kept.index((group, r))] for r in range(units_here)])
            for group in range(groups)
        ]
    )
    back = lax.dynamic_index_in_dim(back, me_group, 0, keepdims=False)
    turned_here = lax.dynamic_index_in_dim(is_turned, me_group, 0, keepdims=False)
    back = reorder(back, turned_here, True)
    final_templates = back.transpose(1, 0, 2).reshape(rank, bins_here)
    return (final_activations, final_templates)


def solution(mesh):
    subs, blocks = mesh.devices.shape
    groups = 2 if blocks % 2 == 0 else 1
    grid = Mesh(
        mesh.devices.reshape(subs, groups, blocks // groups), ("freq", "group", "member")
    )
    frames = ("group", "member")
    return jax.shard_map(
        on_device,
        mesh=grid,
        in_specs=(P(frames, "freq", None), P(None, ("freq", *frames)), P("freq", frames)),
        out_specs=(P("freq", frames), P(None, ("freq", *frames))),
        check_vma=False,
    )
```

```python
import functools
import math

import jax
import jax.numpy as jnp
import ml_dtypes
import numpy as np
from jax import lax
from jax.experimental import pallas as pl
from jax.experimental.pallas import tpu as pltpu
from jax.sharding import Mesh
from jax.sharding import PartitionSpec as P

FRAME_LEN = 65536
SPLIT = 256
LANES = 128
GROUP = 8
SPARE = 8
HOP_ROWS = FRAME_LEN // 2 // LANES
SPECTRUM_VMEM = 24 * 1024 * 1024
UPDATE_VMEM = 16 * 1024 * 1024
NT = (((1,), (1,)), ((), ()))


def high_low(values):
    high = values.astype(np.float32).astype(ml_dtypes.bfloat16)
    low = (values - high.astype(np.float64)).astype(ml_dtypes.bfloat16)
    return high, low


def both_parts_below(values):
    high, low = high_low(values)
    return np.concatenate([high, low], 0)


def units_of_member(units_here, member_blocks):
    order = list(range(units_here))
    if units_here % 8 == 0:
        order.sort(key=lambda r: (row_of_unit(r) % 2, r))
    kept = [(block, r) for block in member_blocks for r in order]
    if units_here % 8 == 0:
        kept.sort(key=lambda pair: row_of_unit(pair[1]) % 2)
    return kept


def row_of_unit(unit):
    return unit // 2 if unit % 2 == 0 else SPLIT - 1 - unit // 2


def lane_order():
    return np.concatenate([np.arange(0, SPLIT // 2, 2), np.arange(1, SPLIT // 2, 2)])


@functools.lru_cache(maxsize=None)
def tables(unit_order):
    half = SPLIT // 2
    index = np.arange(SPLIT, dtype=np.float64)
    slot = np.arange(half, dtype=np.float64)
    firsts = []
    for parity in range(2):
        angle = 2.0 * np.pi / SPLIT * np.mod(np.outer(lane_order()[parity * half // 2 :][: half // 2], slot), SPLIT)
        matrix = np.concatenate([np.cos(angle), -np.sin(angle)], 0)
        if parity == 0:
            matrix[half // 2] = np.cos(np.pi * slot)
        firsts.append(high_low(matrix))
    zeros = np.zeros_like(firsts[0][0])
    first = [np.concatenate([np.concatenate([part, part], 1) for part in parts], 0) for parts in firsts]
    first.append(np.block([[firsts[0][0], zeros], [zeros, firsts[1][0]]]))
    turn = 2.0 * np.pi / (SPLIT * SPLIT) * np.outer(lane_order(), index)
    twiddle_cos, twiddle_sin = np.cos(turn), np.sin(turn)
    masked_cos = twiddle_cos.copy()
    masked_cos[0] = 0.0
    twiddle = np.stack([twiddle_cos, twiddle_sin, masked_cos]).astype(np.float32)
    middle = 2.0 * np.pi / (SPLIT * SPLIT) * half * index
    odd = 2.0 * np.pi / SPLIT * slot
    rows = np.zeros((8, SPLIT), np.float32)
    rows[0], rows[1] = np.cos(middle), -np.sin(middle)
    rows[2, :half], rows[3, :half] = np.cos(odd), np.sin(odd)
    seconds, mirrored, places = [], [], []
    for parity in range(2):
        here = [place for place, unit in enumerate(unit_order) if row_of_unit(unit) % 2 == parity]
        turns = np.array([row_of_unit(unit_order[place]) // 2 for place in here])
        phase = 2.0 * np.pi / half * np.mod(np.outer(turns, np.arange(half)), half)
        c, s = np.cos(phase), np.sin(phase)
        seconds.append(
            both_parts_below(np.concatenate([np.concatenate([c, s], 1), np.concatenate([-s, c], 1)], 0))
        )
        flags = np.zeros((half, LANES), np.float32)
        flags[:, 0] = [unit_order[place] % 2 for place in here]
        mirrored.append(flags)
        places.append(tuple(here))
    position = np.arange(FRAME_LEN, dtype=np.float64)
    window = (0.5 - 0.5 * np.cos(2.0 * np.pi / FRAME_LEN * position)).astype(np.float32)
    window = window.reshape(SPLIT, 2, LANES).transpose(1, 0, 2)
    return (
        np.ascontiguousarray(window),
        np.stack(first),
        twiddle,
        rows,
        np.stack(seconds),
        np.stack(mirrored),
        tuple(places),
    )


def split_values(values):
    high = values.astype(jnp.bfloat16)
    low = (values - high.astype(jnp.float32)).astype(jnp.bfloat16)
    return high, low


def dot(left, right):
    return jnp.dot(left, right, preferred_element_type=jnp.float32)


def dot_nt(left, right):
    return lax.dot_general(left, right, NT, preferred_element_type=jnp.float32)


def transform_group(hop_rows, places, per_member, table_refs, out_ref, parts_ref, middle_ref, written=None):
    window_ref, first_ref, twiddle_ref, rows_ref, second_ref, mirrored_ref = table_refs
    half = SPLIT // 2
    middle_ref[...] = jnp.zeros_like(middle_ref)

    def even_odd(real, imag):
        even = jnp.concatenate([real[:, :half] + real[:, half:], imag[:, :half] + imag[:, half:]], 1)
        real = real[:, :half] - real[:, half:]
        imag = imag[:, :half] - imag[:, half:]
        c, s = rows_ref[2:3, :half], rows_ref[3:4, :half]
        odd = jnp.concatenate([real * c + imag * s, imag * c - real * s], 1)
        return even, odd

    def in_parts(values):
        return jnp.concatenate(split_values(values), 1)

    def second(parity, parts):
        both = dot_nt(second_ref[parity], parts[:, :SPLIT])
        return both[:SPLIT] + (both[SPLIT:] + dot_nt(second_ref[parity, :SPLIT, :], parts[:, SPLIT:]))

    for g in range(GROUP):
        top, bottom = (
            jnp.concatenate([hop_rows(g + hop, side) * window_ref[side, rows, :] for side in range(2)], 1)
            for hop, rows in enumerate((slice(0, half), slice(half, SPLIT)))
        )
        sections, rests = [], []
        for parity, values in enumerate((top + bottom, top - bottom)):
            high, low = split_values(values)
            rests.append(
                ((values - high.astype(jnp.float32)) - low.astype(jnp.float32)).astype(jnp.bfloat16)
            )
            sections.append(dot(first_ref[parity], jnp.concatenate([high, low], 0)))
        rest = dot(first_ref[2], jnp.concatenate(rests, 0))
        even, odd = (
            section[:half] + (section[half:] + rest[parity * half : (parity + 1) * half])
            for parity, section in enumerate(sections)
        )
        a = jnp.concatenate([even[: half // 2], odd[: half // 2]], 0)
        b = jnp.concatenate([even[half // 2 :], odd[half // 2 :]], 0)
        real = a * twiddle_ref[0] + b * twiddle_ref[1]
        imag = b * twiddle_ref[2] - a * twiddle_ref[1]
        for parity, values in enumerate(even_odd(real, imag)):
            parts_ref[parity, g * half : (g + 1) * half, :] = in_parts(values)
        nyquist = b[:1]
        for parity, values in enumerate(even_odd(nyquist * rows_ref[0:1], nyquist * rows_ref[1:2])):
            middle_ref[parity, g : g + 1, :] = values

    def magnitude(values):
        real, imag = values[:half], values[half:]
        return jnp.sqrt(real * real + imag * imag) * (8.0 / SPLIT)

    for parity in range(2):
        middle = magnitude(second(parity, in_parts(middle_ref[parity])))
        is_middle = mirrored_ref[parity] > 0.0
        for pair in range(GROUP // 2):
            values = magnitude(second(parity, parts_ref[parity, pair * SPLIT : (pair + 1) * SPLIT, :]))
            for lane in range(2):
                g = 2 * pair + lane
                block = jnp.where(
                    is_middle, middle[:, g : g + 1], values[:, lane * LANES : (lane + 1) * LANES]
                )
                start = 0
                while start < half:
                    stop = start + 1
                    place = places[parity][start]
                    while (
                        stop < half
                        and stop - start < 8
                        and places[parity][stop] == place + stop - start
                        and places[parity][stop] // per_member == place // per_member
                    ):
                        stop += 1
                    member, row = divmod(place, per_member)
                    out_ref[member, pl.ds(row * GROUP + g, stop - start, stride=GROUP), :] = block[start:stop]
                    start = stop
        if written is not None:
            written(parity)


def early_kernel(
    places, per_member, frames, samples_ref, *rest
):
    table_refs, (out_ref, tail_ref, group_ref) = rest[:6], rest[6:9]
    copies_ref, (hops_ref, parts_ref, middle_ref, sem_ref, out_sem_ref) = rest[9:15], rest[15:]
    groups = frames // GROUP - 1
    group_rows = GROUP * HOP_ROWS
    half = SPLIT // 2

    def fetch(first, count, slot):
        return pltpu.make_async_copy(
            samples_ref.at[pl.ds(first, count), :], hops_ref.at[pl.ds(first, count), :], sem_ref.at[slot]
        )

    tables_in = [
        pltpu.make_async_copy(table_refs[i], copies_ref[i], sem_ref.at[i]) for i in range(len(table_refs))
    ]
    lead = fetch(0, HOP_ROWS, 6)
    tail = pltpu.make_async_copy(
        samples_ref.at[pl.ds(groups * group_rows, group_rows), :], tail_ref, sem_ref.at[7]
    )
    hops = [fetch(HOP_ROWS + i * group_rows, group_rows, 8 + i) for i in range(groups)]
    for copy in [tables_in[1], lead, hops[0], *tables_in[:1], *tables_in[2:], *hops[1:], tail]:
        copy.start()
    lead.wait()
    for copy in tables_in:
        copy.wait()

    def body(i, carry):
        first = pl.multiple_of(i * group_rows, group_rows)
        pltpu.make_async_copy(
            samples_ref.at[pl.ds(HOP_ROWS + first, group_rows), :],
            hops_ref.at[pl.ds(HOP_ROWS + first, group_rows), :],
            sem_ref.at[8 + i],
        ).wait()

        transform_group(
            lambda hop, side: hops_ref[pl.ds(first + hop * HOP_ROWS + side, half, stride=2), :],
            places,
            per_member,
            copies_ref,
            group_ref.at[i],
            parts_ref,
            middle_ref,
        )

        @pl.when(i < groups - 1)
        def _():
            send(i).start()

        return carry

    def send(i):
        count = per_member * GROUP
        return pltpu.make_async_copy(
            group_ref.at[i, :, pl.ds(0, count), :],
            out_ref.at[:, pl.ds(pl.multiple_of(i * count, count), count), :],
            out_sem_ref.at[i],
        )

    lax.fori_loop(0, groups, body, 0)
    tail.wait()
    for i in range(groups - 1):
        send(i).wait()


def late_kernel(places, per_member, frames, done_ref, tail_ref, trailing_ref, activity_ref, *rest):
    table_refs, (_, out_ref, parts_ref, middle_ref, group_ref, sem_ref) = rest[:6], rest[6:]
    count = per_member * GROUP
    before = frames // GROUP - 1
    pass_on = pltpu.make_async_copy(
        done_ref.at[before - 1, :, pl.ds(0, count), :], out_ref.at[:, pl.ds((before - 1) * count, count), :], sem_ref.at[0]
    )
    pass_on.start()

    def hop_rows(hop, side):
        if hop == GROUP:
            return trailing_ref[pl.ds(side, SPLIT // 2, stride=2), :]
        return tail_ref[pl.ds(hop * HOP_ROWS + side, SPLIT // 2, stride=2), :]

    for member in range(out_ref.shape[0]):
        group_ref[member, count:, :] = activity_ref[...]
    bounds = [0, group_ref.shape[1]]
    if all(place % per_member < per_member // 2 for place in places[0]):
        bounds.insert(1, count // 2)
    sends = []

    def written(parity):
        if parity == 1 or len(bounds) == 3:
            first, last = bounds[len(sends)], bounds[len(sends) + 1]
            sends.append(
                pltpu.make_async_copy(
                    group_ref.at[:, pl.ds(first, last - first), :],
                    out_ref.at[:, pl.ds(before * count + first, last - first), :],
                    sem_ref.at[1 + len(sends)],
                )
            )
            sends[-1].start()

    transform_group(
        hop_rows,
        places,
        per_member,
        table_refs,
        group_ref,
        parts_ref,
        middle_ref,
        written,
    )
    pass_on.wait()
    for send in sends:
        send.wait()


def spectrum_blocks(samples, trailing, activity, unit_order, members):
    *values, places = tables(unit_order)
    per_member = SPLIT // members
    frames = samples.shape[0] // HOP_ROWS
    groups = frames // GROUP - 1
    constants = [jnp.asarray(t) for t in values]
    group_shape = (members, per_member * GROUP + SPARE, LANES)
    last_shape = (members, per_member * GROUP + activity.shape[0], LANES)
    out_shape = pltpu.HBM((members, per_member * frames + activity.shape[0], LANES), jnp.float32)
    tail_shape = jax.ShapeDtypeStruct((GROUP * HOP_ROWS, LANES), jnp.float32)
    in_vmem = pl.BlockSpec(memory_space=pltpu.VMEM)
    in_hbm = pl.BlockSpec(memory_space=pltpu.HBM)
    scratch = [
        pltpu.VMEM((2, GROUP * LANES, 2 * SPLIT), jnp.bfloat16),
        pltpu.VMEM((2, 16, SPLIT), jnp.float32),
    ]

    def settings(count):
        return dict(
            compiler_params=pltpu.CompilerParams(vmem_limit_bytes=SPECTRUM_VMEM),
            cost_estimate=pl.CostEstimate(
                flops=count * GROUP * 6 * SPLIT * SPLIT * SPLIT * 2,
                bytes_accessed=count * GROUP * FRAME_LEN * 4,
                transcendentals=0,
            ),
        )

    early, tail, done, *copies = pl.pallas_call(
        functools.partial(early_kernel, places, per_member, frames),
        in_specs=[in_hbm] * (1 + len(constants)),
        out_specs=[in_hbm] + [in_vmem] * (2 + len(constants)),
        out_shape=[out_shape, tail_shape, jax.ShapeDtypeStruct((groups, *group_shape), jnp.float32)]
        + [jax.ShapeDtypeStruct(t.shape, t.dtype) for t in constants],
        scratch_shapes=[pltpu.VMEM(((groups * GROUP + 1) * HOP_ROWS + SPARE, LANES), jnp.float32)]
        + scratch
        + [
            pltpu.SemaphoreType.DMA((8 + groups,)),
            pltpu.SemaphoreType.DMA((groups,)),
        ],
        **settings(groups),
    )(*[pltpu.with_memory_space_constraint(value, pltpu.HBM) for value in (samples, *constants)])
    return pl.pallas_call(
        functools.partial(late_kernel, places, per_member, frames),
        in_specs=[in_vmem] * (4 + len(constants)) + [in_hbm],
        out_specs=in_hbm,
        out_shape=out_shape,
        scratch_shapes=scratch + [pltpu.VMEM(last_shape, jnp.float32), pltpu.SemaphoreType.DMA((3,))],
        input_output_aliases={4 + len(constants): 0},
        **settings(1),
    )(done, tail, trailing, activity, *copies, early)


def lanes_of_activity(activity):
    high, low = split_values(activity)
    return jnp.concatenate([high, high, low, low], 1)


def ratio_of(spectrum_ref, start, activity_lanes, basis):
    frames = activity_lanes.shape[0]
    members = spectrum_ref.shape[0]
    groups = frames // (members * GROUP)
    stride = spectrum_ref.shape[1] // groups
    splits = [split_values(block) for block in basis]
    stacked = jnp.concatenate([jnp.concatenate([h, l, h, l], 0) for h, l in splits], 1)
    approx = dot(activity_lanes, stacked)
    values = jnp.concatenate(
        [
            jnp.stack(
                [
                    spectrum_ref[:, pl.ds(group * stride + (start + row) * GROUP, GROUP), :]
                    for group in range(groups)
                ],
                1,
            ).reshape(frames, LANES)
            for row in range(len(basis))
        ],
        1,
    )
    return values / approx, jnp.concatenate([jnp.concatenate([h, l], 0) for h, l in splits], 1)


def for_activity(ratio, basis):
    high, low = split_values(ratio)
    return dot_nt(high, basis) + dot_nt(low, basis)


def both_parts(values):
    half = values.shape[1] // 2
    return values + pltpu.roll(values, half, 1)


def row_sums(basis):
    return dot_nt(jnp.ones((16, basis.shape[1]), jnp.bfloat16), basis)


def row_steps(per_member, most=8):
    rows = math.gcd(per_member, most)
    return [range(start, start + rows) for start in range(0, per_member, rows)]


def packed(values):
    rows, width = values.shape
    lane = lax.broadcasted_iota(jnp.int32, (rows // 2, width), 1)
    return jnp.where(lane < width // 2, values[: rows // 2], values[rows // 2 :])


def unpacked(values):
    half = values.shape[1] // 2
    return jnp.concatenate([values[:, :half], values[:, half:]], 0)


def gathered_activity(rows_ref, shape):
    subs, members, ranks, width = shape
    local = width // subs
    frames_in = width // LANES
    pieces = {}
    for member in range(members):
        for part in range(frames_in):
            start = part * ranks
            rows = [rows_ref[sub * members + member, start : start + ranks, :] for sub in range(subs)]
            block = jnp.transpose(jnp.concatenate(rows, 0))
            for place in range(LANES // local):
                pieces[part * (LANES // local) + place, member] = block[place * local : (place + 1) * local]
    return jnp.concatenate([pieces[sub, member] for sub in range(subs) for member in range(members)], 0)


def start_fetches(received_ref, spectrum_ref, sem_ref, per_member, steps):
    count = spectrum_ref.shape[1]
    groups = count // (per_member * GROUP)
    copies = []
    for step, rows in enumerate(steps):
        copies.append([])
        for group in range(groups):
            place = pl.ds((group * per_member + rows[0]) * GROUP, len(rows) * GROUP)
            copies[-1].append(
                pltpu.make_async_copy(
                    received_ref.at[:, place, :], spectrum_ref.at[:, place, :], sem_ref.at[step * groups + group]
                )
            )
            copies[-1][-1].start()
    return copies


def first_kernel(
    shape,
    side_ref,
    received_ref,
    basis_ref,
    mine_ref,
    other_ref,
    activity_ref,
    spectrum_ref,
    lanes_ref,
    total_ref,
    rows_ref,
    rows_sem_ref,
    sem_ref,
):
    steps = row_steps(basis_ref.shape[0], 16)
    count = spectrum_ref.shape[1]
    rows_copy = pltpu.make_async_copy(
        received_ref.at[:, pl.ds(count, rows_ref.shape[1]), :], rows_ref, rows_sem_ref
    )
    rows_copy.start()
    copies = start_fetches(received_ref, spectrum_ref, sem_ref, basis_ref.shape[0], steps)
    rows_copy.wait()
    activity = gathered_activity(rows_ref, shape)
    activity_ref[...] = activity
    lanes_ref[...] = lanes_of_activity(activity)
    sums = 0.0
    for step, rows in enumerate(steps):
        for copy in copies[step]:
            copy.wait()
        ratio, basis = ratio_of(spectrum_ref, rows[0], lanes_ref[...], [basis_ref[row] for row in rows])
        part = for_activity(ratio, basis)
        if step == 0:
            total_ref[...] = part
        else:
            total_ref[...] += part
        sums += row_sums(basis)
    total = both_parts(total_ref[...])
    half = total.shape[0] // 2
    quarter = half // 2
    early, late = packed(total[:half]), packed(total[half:])
    first = side_ref[0] == 0
    mine_ref[:quarter, :] = jnp.where(first, early, late)
    other_ref[:quarter, :] = jnp.where(first, late, early)
    sums = both_parts(sums)[:8]
    mine_ref[quarter:, :] = sums
    other_ref[quarter:, :] = sums


def by_owner(values, shape):
    subs, members, ranks, width = shape
    local = width // subs
    blocks = []
    for member in range(members):
        rows = [
            values[(sub * members + member) * local : (sub * members + member + 1) * local]
            for sub in range(subs)
        ]
        blocks.append(jnp.transpose(jnp.concatenate(rows, 0)).reshape(subs, ranks, width))
    return blocks


def sums_for_basis(rows, spectrum_ref, basis_ref, lanes_ref, turned_ref, out_ref):
    rank = basis_ref.shape[1]
    ratio, _ = ratio_of(spectrum_ref, rows[0], lanes_ref[...], [basis_ref[row] for row in rows])
    high, low = split_values(ratio)
    total = dot(turned_ref[...], high) + dot(turned_ref[...], low)
    total = total[:rank] + total[rank:]
    for place in range(len(rows)):
        out_ref[place * rank : (place + 1) * rank, :] = total[:, place * LANES : (place + 1) * LANES]


def second_kernel(
    rows,
    side_ref,
    spectrum_ref,
    basis_ref,
    activity_ref,
    mine_ref,
    other_ref,
    middle_ref,
    early_ref,
    lanes_ref,
    turned_ref,
):
    rank = activity_ref.shape[1]
    quarter = activity_ref.shape[0] // 4
    first = side_ref[0] == 0
    mine = mine_ref[:quarter, :] / mine_ref[quarter : quarter + 1, :]
    other = other_ref[:quarter, :] / other_ref[quarter : quarter + 1, :]
    early, late = jnp.where(first, mine, other), jnp.where(first, other, mine)
    middle = activity_ref[...] * jnp.concatenate([unpacked(early), unpacked(late)], 0)
    middle_ref[...] = middle
    lanes_ref[...] = lanes_of_activity(middle)
    turned = jnp.transpose(middle)
    high, low = split_values(turned)
    turned_ref[...] = jnp.concatenate([high, low], 0)
    totals = jnp.sum(middle, axis=0, keepdims=True)
    totals = jnp.broadcast_to(jnp.concatenate([totals] * (LANES // rank), 1), (8, LANES))
    early_ref[early_ref.shape[0] - 8 :, :] = totals
    sums_for_basis(rows, spectrum_ref, basis_ref, lanes_ref, turned_ref, early_ref)


def second_late_kernel(rows, received_ref, basis_ref, lanes_ref, turned_ref, late_ref, spectrum_ref, sem_ref):
    for copy in start_fetches(received_ref, spectrum_ref, sem_ref, basis_ref.shape[0], [rows])[0]:
        copy.wait()
    sums_for_basis(rows, spectrum_ref, basis_ref, lanes_ref, turned_ref, late_ref)


def renew_and_add(rows, spectrum_ref, basis_ref, lanes_ref, scale, numerators, new_ref, total_ref, sums_ref):
    rank = basis_ref.shape[1]
    blocks = [
        basis_ref[row] * (sum(ref[place * rank : (place + 1) * rank, :] for ref in numerators) * scale)
        for place, row in enumerate(rows)
    ]
    for place, block in enumerate(blocks):
        new_ref[place] = block
    ratio, basis = ratio_of(spectrum_ref, rows[0], lanes_ref[...], blocks)
    total_ref[...] = for_activity(ratio, basis)
    sums_ref[...] = row_sums(basis)


def third_kernel(rows, later, received_ref, basis_ref, middle_ref, *rest):
    numerators = rest[:-7]
    new_ref, total_ref, sums_ref, lanes_ref, scale_ref, spectrum_ref, sem_ref = rest[-7:]
    rank = middle_ref.shape[1]
    copies = start_fetches(received_ref, spectrum_ref, sem_ref, basis_ref.shape[0], [rows, later])
    lanes_ref[...] = lanes_of_activity(middle_ref[...])
    totals = sum(ref[len(rows) * rank :, :] for ref in numerators)
    totals = jnp.transpose(jnp.concatenate([totals] * (LANES // 8), 0))[:rank]
    scale_ref[...] = 1.0 / totals
    for copy in copies[0]:
        copy.wait()
    renew_and_add(
        rows, spectrum_ref, basis_ref, lanes_ref, scale_ref[...], numerators, new_ref, total_ref, sums_ref
    )
    for copy in copies[1]:
        copy.wait()


def last_kernel(rows, spectrum_ref, basis_ref, lanes_ref, scale_ref, before_ref, sums_before_ref, *rest):
    numerators = rest[:-4]
    new_ref, out_ref, total_ref, sums_ref = rest[-4:]
    rank = basis_ref.shape[1]
    renew_and_add(
        rows, spectrum_ref, basis_ref, lanes_ref, scale_ref[...], numerators, new_ref, total_ref, sums_ref
    )
    total = both_parts(before_ref[...] + total_ref[...])[:, :rank]
    sums = both_parts(sums_before_ref[...] + sums_ref[...])
    subs, members, _, ranks, width = out_ref.shape
    sums = jnp.transpose(jnp.broadcast_to(sums[:1], (LANES, 2 * rank)))[:rank]
    sums = jnp.concatenate([sums] * (width // LANES), 1).reshape(subs, ranks, width)
    for member, block in enumerate(by_owner(total, (subs, members, ranks, width))):
        out_ref[:, member, 0] = block
        out_ref[:, member, 1] = sums


def update_call(kernel, spectrum, out_shapes, scratch, operands, scalars=(), place=pltpu.VMEM):
    in_vmem = pl.BlockSpec(memory_space=pltpu.VMEM)
    if place == pltpu.HBM:
        spectrum = pltpu.with_memory_space_constraint(spectrum, place)
    rank = operands[0].shape[1]
    return pl.pallas_call(
        kernel,
        in_specs=[pl.BlockSpec(memory_space=pltpu.SMEM) for _ in scalars]
        + [pl.BlockSpec(memory_space=place)]
        + [in_vmem for _ in operands],
        out_specs=[in_vmem for _ in out_shapes],
        out_shape=[
            shape if hasattr(shape, "dtype") else jax.ShapeDtypeStruct(shape, jnp.float32)
            for shape in out_shapes
        ],
        scratch_shapes=scratch,
        compiler_params=pltpu.CompilerParams(vmem_limit_bytes=UPDATE_VMEM),
        cost_estimate=pl.CostEstimate(
            flops=spectrum.size * rank * 16, bytes_accessed=spectrum.size * 4, transcendentals=0
        ),
    )(*scalars, spectrum, *operands)


def reorder(values, is_turned, back):
    order = lane_order()
    places = np.stack([order, -order % LANES])
    moves = np.zeros((2, LANES, LANES), np.float32)
    for move, place in zip(moves, places):
        move[place, np.arange(LANES)] = 1.0
    if back:
        moves = moves.transpose(0, 2, 1)
    moved = [
        lax.dot_general(
            values,
            jnp.asarray(move),
            (((values.ndim - 1,), (0,)), ((), ())),
            precision=lax.Precision.HIGHEST,
            preferred_element_type=jnp.float32,
        )
        for move in moves
    ]
    return jnp.where(is_turned, moved[1], moved[0])


def swap_by(value, axis, mask):
    count = lax.axis_size(axis)
    return lax.ppermute(value, axis, [(i, i ^ mask) for i in range(count)])


def sum_over(value, axis, mask):
    count = lax.axis_size(axis)
    while mask < count:
        masks = [mask] if 2 * mask >= count else [mask, 2 * mask, 3 * mask]
        value = sum([swap_by(value, axis, m) for m in masks], value)
        mask *= 2 if len(masks) == 1 else 4
    return value


def on_device(signal, templates, activations):
    subs, groups, members = (lax.axis_size(axis) for axis in ("freq", "group", "member"))
    blocks = groups * members
    rank, bins_here = templates.shape
    ranks_here, width = activations.shape
    units_here = bins_here // LANES
    exchange = ("freq", "member")
    partners = subs * members
    per_member = units_here * groups
    me_sub, me_group, me_member = (lax.axis_index(axis) for axis in ("freq", "group", "member"))

    kept = units_of_member(units_here, range(groups))
    unit_order = tuple(
        units_here * (sub * blocks + group * members + member) + r
        for sub in range(subs)
        for member in range(members)
        for group, r in kept
    )

    samples = signal.reshape(-1, LANES)
    route = [
        (((sub + 1) % subs) * blocks + block + (sub + 1) // subs, sub * blocks + block)
        for sub in range(subs)
        for block in range(blocks)
        if block + (sub + 1) // subs < blocks
    ]
    trailing = lax.ppermute(samples[:HOP_ROWS], ("freq", "group", "member"), route)
    other = [swap_by(templates, "group", 1)] if groups == 2 else []
    own_rows = activations.reshape(ranks_here, width // LANES, LANES).transpose(1, 0, 2)
    own_rows = own_rows.reshape(ranks_here * width // LANES, LANES)
    spectrum = spectrum_blocks(samples, trailing, own_rows, unit_order, partners)
    spectrum, other = lax.optimization_barrier((spectrum, other))
    spectrum = lax.all_to_all(spectrum, exchange, 0, 0, tiled=True)
    local = width // subs
    frames = partners * local

    own = templates.reshape(rank, units_here, LANES).transpose(1, 0, 2)
    if other:
        remote = other[0].reshape(rank, units_here, LANES).transpose(1, 0, 2)
        by_group = jnp.where(me_group == 0, jnp.stack([own, remote]), jnp.stack([remote, own]))
    else:
        by_group = own[None]
    unit_index = units_here * (
        me_sub * blocks + jnp.arange(groups)[:, None] * members + me_member
    ) + jnp.arange(units_here)[None, :]
    is_turned = (unit_index % 2 == 1)[:, :, None, None]
    by_group = reorder(by_group, is_turned, False)
    basis = jnp.concatenate([by_group[group, r][None] for group, r in kept], 0)

    lanes_scratch = pltpu.VMEM((frames, 4 * rank), jnp.bfloat16)
    total_scratch = pltpu.VMEM((frames, 2 * rank), jnp.float32)
    half_shape = (frames // 4 + 8, 2 * rank)
    side = (me_sub % 2).astype(jnp.int32).reshape(1)
    extra = ranks_here * width // LANES
    spectrum_rows = spectrum.shape[1] - extra
    row_groups = spectrum_rows // (per_member * GROUP)
    fetch_sems = pltpu.SemaphoreType.DMA((len(row_steps(per_member)) * row_groups,))
    received = spectrum
    mine, other, activity, spectrum = update_call(
        functools.partial(first_kernel, (subs, members, ranks_here, width)),
        received,
        [half_shape, half_shape, (frames, rank), (partners, spectrum_rows, LANES)],
        [
            lanes_scratch,
            total_scratch,
            pltpu.VMEM((partners, extra, LANES), jnp.float32),
            pltpu.SemaphoreType.DMA,
            fetch_sems,
        ],
        (basis,),
        (side,),
        pltpu.HBM,
    )
    mine = mine + swap_by(other, "freq", 1)
    mine = sum_over(mine, "freq", 2)
    mine = sum_over(mine, "member", 1)
    other = swap_by(mine, "freq", 1)

    early_rows = range(max(1, per_member // 2))
    late_rows = range(len(early_rows), per_member)
    middle, early_sums, lanes, turned = update_call(
        functools.partial(second_kernel, early_rows),
        spectrum,
        [
            (frames, rank),
            (len(early_rows) * rank + 8, LANES),
            jax.ShapeDtypeStruct((frames, 4 * rank), jnp.bfloat16),
            jax.ShapeDtypeStruct((2 * rank, frames), jnp.bfloat16),
        ],
        [],
        (basis, activity, mine, other),
        (side,),
    )
    (late_sums,) = update_call(
        functools.partial(second_late_kernel, late_rows),
        received,
        [(len(late_rows) * rank, LANES)],
        [
            pltpu.VMEM((partners, spectrum_rows, LANES), jnp.float32),
            pltpu.SemaphoreType.DMA((row_groups,)),
        ],
        (basis, lanes, turned),
        (),
        pltpu.HBM,
    )
    numerators = [early_sums, late_sums]
    numerators = [[numerator] for numerator in numerators]
    if groups == 2:
        for numerator in numerators:
            numerator.append(swap_by(numerator[0], "group", 1))
    early_new, total, sums, lanes, scale, spectrum = update_call(
        functools.partial(third_kernel, early_rows, late_rows),
        received,
        [
            (len(early_rows), rank, LANES),
            (frames, 2 * rank),
            (16, 2 * rank),
            jax.ShapeDtypeStruct((frames, 4 * rank), jnp.bfloat16),
            (rank, LANES),
            (partners, spectrum_rows, LANES),
        ],
        [pltpu.SemaphoreType.DMA((2 * row_groups,))],
        (basis, middle, *numerators[0]),
        (),
        pltpu.HBM,
    )
    late_new, payload = update_call(
        functools.partial(last_kernel, late_rows),
        spectrum,
        [(len(late_rows), rank, LANES), (subs, members, 2, ranks_here, width)],
        [total_scratch, pltpu.VMEM((16, 2 * rank), jnp.float32)],
        (basis, lanes, scale, total, sums, *numerators[1]),
    )
    new_basis = [*early_new, *late_new]
    parts = lax.all_to_all(
        payload.reshape(partners, 2, ranks_here, width), exchange, 0, 0, tiled=True
    )
    summed = jnp.sum(parts, axis=0)
    mine = lax.dynamic_slice(
        middle.reshape(subs, members, local, rank),
        (0, me_member, 0, me_sub * ranks_here),
        (subs, 1, local, ranks_here),
    )
    mine = mine.reshape(width, ranks_here).T
    final_activations = mine * (summed[0] / summed[1])

    back = jnp.stack(
        [
            jnp.stack([new_basis[kept.index((group, r))] for r in range(units_here)])
            for group in range(groups)
        ]
    )
    back = lax.dynamic_index_in_dim(back, me_group, 0, keepdims=False)
    turned_here = lax.dynamic_index_in_dim(is_turned, me_group, 0, keepdims=False)
    back = reorder(back, turned_here, True)
    final_templates = back.transpose(1, 0, 2).reshape(rank, bins_here)
    return (final_activations, final_templates)


def solution(mesh):
    subs, blocks = mesh.devices.shape
    groups = 2 if blocks % 2 == 0 else 1
    grid = Mesh(
        mesh.devices.reshape(subs, groups, blocks // groups), ("freq", "group", "member")
    )
    frames = ("group", "member")
    return jax.shard_map(
        on_device,
        mesh=grid,
        in_specs=(P(frames, "freq", None), P(None, ("freq", *frames)), P("freq", frames)),
        out_specs=(P("freq", frames), P(None, ("freq", *frames))),
        check_vma=False,
    )
```
